32 devices in a mesh: dp: 2 (over x), centers: 16 (over z, y, core).
Axes of the slice: x: 2, y: 2, z: 4, core: 2. Of those that a mesh axis runs over, the one named last changes fastest.
Arguments:
- features: bfloat16 [64, 8192], P(None, 'dp'), may hold values from -8 to 8
- prices: float32 [8192], P('dp'), may hold values from -6 to 6
- slots: int32 [8192], P('dp'), may hold values from 0 to 7
- center_idx: int32 [8192], P('centers'), may hold values from 0 to 8191
- center_scale: float32 [8192], P('centers'), may hold values from 0.5 to 18
Outputs:
- coefficients: float32 [8, 8192], P(None, 'centers')
- residual: float32 [8, 8192], P(None, 'centers')
The draws below stay inside these ranges and needn't reach their ends.
All inputs are finite; a program needn't handle non-finite values.
Results may differ from the reference program's by a relative error of at most 0.00195.
Values may be sent and summed in bfloat16 or wider, within the bound.
No kernel may reach another device: no remote copies, remote signals or barrier semaphores. Data moves between devices by JAX's collectives and lax.ppermute only.
A program may use at most 64 MiB of HBM per device.

```python
import math
import jax
import jax.numpy as jnp
from jax import lax

F = 64
SLOTS = 8
ITERS = 2
NN = 8192
M = 8192


cluster_count = 256


def draw_features(key, part):
    key = jax.random.fold_in(key, 5)
    mean_key, member_key, noise_key = jax.random.split(key, 3)
    member = jax.random.randint(member_key, (NN,), 0, cluster_count)
    centres = 1.2 * jax.random.normal(mean_key, (F, cluster_count), jnp.float32)
    noise = jax.random.normal(noise_key, (F, NN), jnp.float32)
    return jnp.clip(jnp.take(centres, member, axis=1) + noise, -8.0, 8.0).astype(jnp.bfloat16)


def draw_center_scale(key, part):
    key = jax.random.fold_in(key, 11)
    position = jnp.arange(M, dtype=jnp.float32) / jnp.float32(max(M - 1, 1))
    factor = jnp.exp(jax.random.uniform(key, (M,), jnp.float32, -0.69, 0.69))
    return 3.0 ** position * factor


def place_ends(array, own_key, smallest, high):
    spot = [jax.random.randint(jax.random.fold_in(own_key, axis), (), 0, length) for axis, length in enumerate(array.shape)]
    widest = array.shape.index(max(array.shape))
    beside = spot[:widest] + [(spot[widest] + 1) % array.shape[widest]] + spot[widest + 1:]
    return array.at[tuple(spot)].set(smallest).at[tuple(beside)].set(high)


def level_of(own_key, shape, cuts, low, top_value):
    level, own = 1.0, jax.random.fold_in(own_key, 6)
    for dim, parts in cuts:
        draws = jnp.exp(jax.random.uniform(jax.random.fold_in(own, dim), (parts,), jnp.float32, low / len(cuts), top_value / len(cuts)))
        level = level * jnp.repeat(draws, shape[dim] // parts).reshape([-1 if axis == dim else 1 for axis in range(len(shape))])
    return level


def gaussian(rng, extent, spread, most, pieces=(), kind=jnp.bfloat16):
    drawn = spread * jax.random.normal(rng, extent, jnp.float32)
    if pieces:
        drawn = drawn * level_of(rng, extent, pieces, -0.22, 0.18)
    return jnp.clip(drawn, -most, most).astype(kind)


def setup_inputs(seed: int = 0) -> dict:
    streams_of = jax.random.split(jax.random.key(seed), 6)
    return {
        "features": draw_features(jax.random.fold_in(streams_of[5], 71), 0),
        "prices": gaussian(streams_of[1], (NN,), 1.0, 6.0, ((0, 2),), jnp.float32),
        "slots": place_ends(jax.random.randint(streams_of[2], (NN,), 0, SLOTS), jax.random.fold_in(streams_of[2], 1), 0, SLOTS - 1).astype(jnp.int32),
        "center_idx": place_ends(jax.random.randint(streams_of[3], (M,), 0, NN), jax.random.fold_in(streams_of[3], 1), 0, NN - 1).astype(jnp.int32),
        "center_scale": draw_center_scale(jax.random.fold_in(streams_of[5], 71), 0),
    }


highest_prec = lax.Precision.HIGHEST
ridge_shift = 0.5

def kernel_block(columns, center_f, center_norm):
    inner_prod = jnp.dot(columns.T, center_f, precision=highest_prec)
    row_norm = lax.optimization_barrier(jnp.sum(columns * columns, axis=0))
    return jnp.exp(-(row_norm[:, None] + center_norm[None, :] - 2.0 * inner_prod) / (2.0 * F))

def reference(features, prices, slots, center_idx, center_scale):
    feat32 = features.astype(jnp.float32)
    center_f = jnp.take(feat32, center_idx.astype(jnp.int32), axis=1)
    center_norm = lax.optimization_barrier(jnp.sum(center_f * center_f, axis=0))
    slot_mask = (slots[:, None] == jnp.arange(SLOTS, dtype=jnp.int32)[None, :]).astype(jnp.float32)
    block_len = math.gcd(NN, 1024)
    blocks = NN // block_len
    feat_blocks = jnp.transpose(feat32.reshape(F, blocks, block_len), (1, 0, 2))
    mask_blocks = slot_mask.reshape(blocks, block_len, SLOTS)
    price_blocks = prices.reshape(blocks, block_len)

    def full_pass(scaled, use_prices):

        def visit(summed, items):
            columns, masks, block_price = items
            kernel_tile = kernel_block(columns, center_f, center_norm)
            if use_prices:
                weights = masks * block_price[:, None]
            else:
                weights = masks * jnp.dot(kernel_tile, scaled.T, precision=highest_prec)
            return (summed + jnp.dot(weights.T, kernel_tile, precision=highest_prec), None)
        start_sum = jnp.zeros((SLOTS, M), jnp.float32)
        summed, unused = lax.scan(visit, start_sum, (feat_blocks, mask_blocks, price_blocks))
        return summed
    target_side = center_scale[None, :] * full_pass(jnp.zeros((SLOTS, M), jnp.float32), True) / jnp.sqrt(jnp.float32(NN))

    def hessian_apply(vector):
        summed = full_pass(center_scale[None, :] * vector, False)
        return center_scale[None, :] * summed / jnp.float32(NN) + ridge_shift * vector
    coefficients = jnp.zeros((SLOTS, M), jnp.float32)
    residual = target_side
    direction = target_side
    norm_now = lax.optimization_barrier(jnp.sum(residual * residual, axis=1))
    for iteration in range(ITERS):
        applied = hessian_apply(direction)
        step_size = norm_now / lax.optimization_barrier(jnp.sum(direction * applied, axis=1))
        coefficients = coefficients + step_size[:, None] * direction
        residual = residual - step_size[:, None] * applied
        norm_next = lax.optimization_barrier(jnp.sum(residual * residual, axis=1))
        direction = residual + (norm_next / norm_now)[:, None] * direction
        norm_now = norm_next
    return (coefficients, residual)
```

```python
import functools
import math

import jax
import jax.numpy as jnp
from jax import lax
from jax.experimental import pallas as pl
from jax.experimental.pallas import tpu as pltpu
from jax.sharding import PartitionSpec as P

SLOTS = 8
RIDGE = 0.5
CHUNK = 512
EXTRA = 128
f32 = jnp.float32
bf16 = jnp.bfloat16


def split3(value):
    high = value.astype(bf16).astype(f32)
    rest = value - high
    mid = rest.astype(bf16).astype(f32)
    return high, mid, rest - mid


def stack3(value):
    return jnp.concatenate(split3(value), axis=0).astype(bf16)


def unstack3(value):
    return value[0:8] + (value[8:16] + value[16:24])


def pair_total(parts):
    while len(parts) > 1:
        parts = [parts[i] + parts[i + 1] for i in range(0, len(parts), 2)]
    return parts[0]


def total_of(refs):
    return pair_total([ref[...] for ref in refs])


def slot_mask(slots_ref, begin):
    row = lax.broadcasted_iota(jnp.int32, (SLOTS, CHUNK), 0)
    return slots_ref[:, begin : begin + CHUNK] == row


def with_norms(feat, feat_first):
    feat32 = feat.astype(f32)
    half = -0.5 * jnp.sum(feat32 * feat32, axis=0, keepdims=True)
    high, mid, low = split3(half)
    row = lax.broadcasted_iota(jnp.int32, (16, feat.shape[1]), 0)
    base = 0 if feat_first else 3
    extra = jnp.where(row < 6, 1.0, 0.0)
    for place, part in enumerate((high, mid, low)):
        extra = jnp.where(row == base + place, part, extra)
    return jnp.concatenate([feat, extra.astype(bf16)], axis=0)


def pick_body(feat_ref, idx_ref, out_ref):
    total = jnp.zeros(out_ref.shape, f32)
    count = out_ref.shape[1]
    for begin in range(0, feat_ref.shape[1], CHUNK):
        row = lax.broadcasted_iota(jnp.int32, (CHUNK, count), 0)
        hit = row == (idx_ref[...] - begin)
        one_hot = jnp.where(hit, 1.0, 0.0).astype(bf16)
        total += jnp.dot(
            feat_ref[:, begin : begin + CHUNK], one_hot, preferred_element_type=f32
        )
    out_ref[...] = total.astype(bf16)


def kernel_body(parts, feat_ref, prices_ref, slots_ref, *refs):
    center_refs, (high_ref, low_ref, out_ref) = refs[:parts], refs[parts:]
    center = with_norms(total_of(center_refs), True)
    count = center.shape[1]
    total = jnp.zeros((24, count), f32)
    for begin in range(0, feat_ref.shape[1], CHUNK):
        here = slice(begin, begin + CHUNK)
        columns = with_norms(feat_ref[:, here], False)
        inner = lax.dot_general(
            center, columns, (((0,), (0,)), ((), ())), preferred_element_type=f32
        )
        value = jnp.exp2(inner * (math.log2(math.e) / 64.0))
        high = value.astype(bf16)
        low = (value - high.astype(f32)).astype(bf16)
        high_ref[:, here] = high
        low_ref[:, here] = low
        weight = stack3(jnp.where(slot_mask(slots_ref, begin), prices_ref[:, here], 0.0))
        for piece in (high, low):
            total += lax.dot_general(
                weight, piece, (((1,), (1,)), ((), ())), preferred_element_type=f32
            )
    out_ref[...] = unstack3(total)


def apply_rows(scaled, high_ref, low_ref, slots_ref, out_ref):
    stacked = stack3(scaled)
    for turn, begin in enumerate(range(0, high_ref.shape[1], CHUNK)):
        here = slice(begin, begin + CHUNK)
        value = jnp.dot(stacked, high_ref[:, here], preferred_element_type=f32)
        value += jnp.dot(stacked, low_ref[:, here], preferred_element_type=f32)
        own = jnp.where(slot_mask(slots_ref, begin), unstack3(value), 0.0)
        out_ref[turn : turn + 1, 0:CHUNK] = jnp.sum(own, axis=0, keepdims=True)


def fold_rows(row_weights, high_ref, low_ref, out_ref):
    count = high_ref.shape[0]
    total = jnp.zeros((24, count), f32)
    square = jnp.zeros((SLOTS, 1), f32)
    for turn, begin in enumerate(range(0, high_ref.shape[1], CHUNK)):
        here = slice(begin, begin + CHUNK)
        weight = row_weights(turn, begin)
        square += jnp.sum(weight * weight, axis=1, keepdims=True)
        weight = stack3(weight)
        for ref in (high_ref, low_ref):
            total += lax.dot_general(
                weight, ref[:, here], (((1,), (1,)), ((), ())), preferred_element_type=f32
            )
    out_ref[:, 0:count] = unstack3(total)
    out_ref[:, count : count + EXTRA] = jnp.broadcast_to(square, (SLOTS, EXTRA))


def row_sum(value):
    return jnp.sum(value, axis=1, keepdims=True)


def first_apply_body(parts, scale_over_root, *refs):
    first_refs = refs[:parts]
    scale_ref, slots_ref, high_ref, low_ref, target_ref, out_ref = refs[parts:]
    scale = scale_ref[...]
    target = scale * total_of(first_refs) * scale_over_root
    target_ref[...] = target
    out_ref[:, CHUNK:] = jnp.broadcast_to(row_sum(target * target), (SLOTS, EXTRA))
    apply_rows(scale * target, high_ref, low_ref, slots_ref, out_ref)


def first_fold_body(parts, *refs):
    row_refs = refs[:parts]
    slots_ref, high_ref, low_ref, rows_ref, out_ref = refs[parts:]
    rows_ref[...] = total_of(row_refs)

    def row_weights(turn, begin):
        value = rows_ref[turn : turn + 1, 0:CHUNK]
        return jnp.where(slot_mask(slots_ref, begin), value, 0.0)

    fold_rows(row_weights, high_ref, low_ref, out_ref)


def second_apply_body(parts, inv_rows, *refs):
    fold_refs = refs[:parts]
    (scale_ref, slots_ref, high_ref, low_ref, target_ref, rows_ref,
     residual_ref, step_ref, out_ref) = refs[parts:]
    count = scale_ref.shape[1]
    folded = total_of(fold_refs)
    scale = scale_ref[...]
    target = target_ref[...]
    norm = rows_ref[:, CHUNK : CHUNK + 1]
    applied = scale * folded[:, 0:count] * inv_rows + RIDGE * target
    step = norm / (folded[:, count : count + 1] * inv_rows + RIDGE * norm)
    residual = target - step * applied
    residual_ref[...] = residual
    step_ref[...] = jnp.broadcast_to(step, step_ref.shape)
    lane = lax.broadcasted_iota(jnp.int32, (SLOTS, EXTRA), 1)
    out_ref[:, CHUNK:] = jnp.where(
        lane == 0, row_sum(residual * residual), row_sum(residual * target)
    )
    apply_rows(scale * residual, high_ref, low_ref, slots_ref, out_ref)


def second_fold_body(parts, *refs):
    row_refs = refs[:parts]
    slots_ref, high_ref, low_ref, rows_ref, sums_ref, out_ref = refs[parts:]
    latest = total_of(row_refs)
    sums_ref[...] = latest[:, CHUNK:]
    ratio = latest[:, CHUNK : CHUNK + 1] / rows_ref[:, CHUNK : CHUNK + 1]

    def row_weights(turn, begin):
        value = latest[turn : turn + 1, 0:CHUNK] + ratio * rows_ref[turn : turn + 1, 0:CHUNK]
        return jnp.where(slot_mask(slots_ref, begin), value, 0.0)

    fold_rows(row_weights, high_ref, low_ref, out_ref)


def finish_body(parts, inv_rows, *refs):
    fold_refs = refs[:parts]
    (scale_ref, target_ref, residual_ref, step_ref, rows_ref, sums_ref,
     coefficients_ref, out_ref) = refs[parts:]
    count = scale_ref.shape[1]
    folded = total_of(fold_refs)
    target = target_ref[...]
    residual = residual_ref[...]
    first_norm = rows_ref[:, CHUNK : CHUNK + 1]
    norm = sums_ref[:, 0:1]
    cross = sums_ref[:, 1:2]
    ratio = norm / first_norm
    direction = residual + ratio * target
    square = norm + 2.0 * ratio * cross + ratio * ratio * first_norm
    applied = scale_ref[...] * folded[:, 0:count] * inv_rows + RIDGE * direction
    step = norm / (folded[:, count : count + 1] * inv_rows + RIDGE * square)
    coefficients_ref[...] = step_ref[:, 0:1] * target + step * direction
    out_ref[...] = residual - step * applied


def call(body, out_shape, *args):
    return pl.pallas_call(
        body,
        out_shape=out_shape,
        in_specs=[pl.BlockSpec(memory_space=pltpu.VMEM)] * len(args),
        out_specs=jax.tree.map(lambda _: pl.BlockSpec(memory_space=pltpu.VMEM), out_shape),
        compiler_params=pltpu.CompilerParams(vmem_limit_bytes=40 * 1024 * 1024),
    )(*args)


def exchange(value, axis):
    size = lax.axis_size(axis)
    parts = [value]
    stride = 1
    while stride < size:
        value = pair_total(parts)
        parts = [value]
        span = min(4, size // stride)
        for offset in range(1, span):
            pairs = [(i, i ^ (offset * stride)) for i in range(size)]
            parts.append(lax.ppermute(value, axis, pairs))
        stride *= span
    return parts


def shaped(shape, dtype=f32):
    return jax.ShapeDtypeStruct(shape, dtype)


def per_device(features, prices, slots, center_idx, center_scale):
    row_count = features.shape[1]
    count = center_idx.shape[0]
    all_rows = row_count * lax.axis_size("dp")
    local_idx = (center_idx - lax.axis_index("dp") * row_count).reshape(1, count)
    prices = prices.reshape(1, row_count)
    slots = slots.reshape(1, row_count)
    scale = center_scale.reshape(1, count)
    turns = row_count // CHUNK
    part = functools.partial

    picked = call(pick_body, shaped((features.shape[0], count), bf16), features, local_idx)
    centers = exchange(picked, "dp")
    block = shaped((count, row_count), bf16)
    high, low, first = call(
        part(kernel_body, len(centers)),
        (block, block, shaped((SLOTS, count))),
        features, prices, slots, *centers,
    )
    firsts = exchange(first, "dp")
    row_shape = shaped((turns, CHUNK + EXTRA))
    fold_shape = shaped((SLOTS, count + EXTRA))
    vector = shaped((SLOTS, count))
    narrow = shaped((SLOTS, EXTRA))
    target, rows = call(
        part(first_apply_body, len(firsts), 1.0 / math.sqrt(all_rows)),
        (vector, row_shape),
        *firsts, scale, slots, high, low,
    )
    rows = exchange(rows, "centers")
    rows, folded = call(
        part(first_fold_body, len(rows)), (row_shape, fold_shape), *rows, slots, high, low
    )
    folds = exchange(folded, "dp")
    residual, step, latest = call(
        part(second_apply_body, len(folds), 1.0 / all_rows),
        (vector, narrow, row_shape),
        *folds, scale, slots, high, low, target, rows,
    )
    latest = exchange(latest, "centers")
    sums, folded = call(
        part(second_fold_body, len(latest)),
        (narrow, fold_shape),
        *latest, slots, high, low, rows,
    )
    folds = exchange(folded, "dp")
    return call(
        part(finish_body, len(folds), 1.0 / all_rows),
        (vector, vector),
        *folds, scale, target, residual, step, rows, sums,
    )


def solution(mesh):
    return jax.shard_map(
        per_device,
        mesh=mesh,
        in_specs=(P(None, "dp"), P("dp"), P("dp"), P("centers"), P("centers")),
        out_specs=(P(None, "centers"), P(None, "centers")),
        check_vma=False,
    )
```

```python
import functools
import math

import jax
import jax.numpy as jnp
from jax import lax
from jax.experimental import pallas as pl
from jax.experimental.pallas import tpu as pltpu
from jax.sharding import PartitionSpec as P

SLOTS = 8
RIDGE = 0.5
CHUNK = 512
EXTRA = 128
f32 = jnp.float32
bf16 = jnp.bfloat16


def split3(value):
    high = value.astype(bf16).astype(f32)
    rest = value - high
    mid = rest.astype(bf16).astype(f32)
    return high, mid, rest - mid


def stack3(value):
    return jnp.concatenate(split3(value), axis=0).astype(bf16)


def unstack3(value):
    return value[0:8] + (value[8:16] + value[16:24])


def pair_total(parts):
    while len(parts) > 1:
        parts = [parts[i] + parts[i + 1] for i in range(0, len(parts), 2)]
    return parts[0]


def total_of(refs):
    return pair_total([ref[i] for ref in refs for i in range(ref.shape[0])])


def slot_mask(small_ref, begin):
    row = lax.broadcasted_iota(jnp.int32, (SLOTS, CHUNK), 0).astype(f32)
    return small_ref[:, begin : begin + CHUNK] == row


def scale_of(small_ref, count):
    return small_ref[:, -2 * count : -count]


def with_norms(feat, feat_first):
    feat32 = feat.astype(f32)
    half = -0.5 * jnp.sum(feat32 * feat32, axis=0, keepdims=True)
    high, mid, low = split3(half)
    row = lax.broadcasted_iota(jnp.int32, (16, feat.shape[1]), 0)
    base = 0 if feat_first else 3
    extra = jnp.where(row < 6, 1.0, 0.0)
    for place, part in enumerate((high, mid, low)):
        extra = jnp.where(row == base + place, part, extra)
    return jnp.concatenate([feat, extra.astype(bf16)], axis=0)


def pick_body(feat_ref, small_ref, out_ref):
    total = jnp.zeros(out_ref.shape, f32)
    count = out_ref.shape[1]
    local_idx = small_ref[:, -count:]
    for begin in range(0, feat_ref.shape[1], CHUNK):
        row = lax.broadcasted_iota(jnp.int32, (CHUNK, count), 0).astype(f32)
        one_hot = jnp.where(row == local_idx - float(begin), 1.0, 0.0).astype(bf16)
        total += jnp.dot(
            feat_ref[:, begin : begin + CHUNK], one_hot, preferred_element_type=f32
        )
    out_ref[...] = total.astype(bf16)


def kernel_body(parts, feat_ref, small_ref, *refs):
    center_refs, (high_ref, low_ref, out_ref) = refs[:parts], refs[parts:]
    center = with_norms(total_of(center_refs), True)
    count = center.shape[1]
    total = jnp.zeros((24, count), f32)
    for begin in range(0, feat_ref.shape[1], CHUNK):
        here = slice(begin, begin + CHUNK)
        columns = with_norms(feat_ref[:, here], False)
        inner = lax.dot_general(
            center, columns, (((0,), (0,)), ((), ())), preferred_element_type=f32
        )
        value = jnp.exp2(inner * (math.log2(math.e) / 64.0))
        high = value.astype(bf16)
        low = (value - high.astype(f32)).astype(bf16)
        high_ref[:, here] = high
        low_ref[:, here] = low
        rows = feat_ref.shape[1]
        price = small_ref[:, rows + begin : rows + begin + CHUNK]
        weight = stack3(jnp.where(slot_mask(small_ref, begin), price, 0.0))
        for piece in (high, low):
            total += lax.dot_general(
                weight, piece, (((1,), (1,)), ((), ())), preferred_element_type=f32
            )
    out_ref[...] = unstack3(total)


def apply_rows(scaled, high_ref, low_ref, small_ref, out_ref):
    stacked = stack3(scaled)
    for turn, begin in enumerate(range(0, high_ref.shape[1], CHUNK)):
        here = slice(begin, begin + CHUNK)
        value = jnp.dot(stacked, high_ref[:, here], preferred_element_type=f32)
        value += jnp.dot(stacked, low_ref[:, here], preferred_element_type=f32)
        own = jnp.where(slot_mask(small_ref, begin), unstack3(value), 0.0)
        out_ref[turn : turn + 1, 0:CHUNK] = jnp.sum(own, axis=0, keepdims=True)


def fold_rows(row_weights, high_ref, low_ref, out_ref):
    count = high_ref.shape[0]
    total = jnp.zeros((24, count), f32)
    square = jnp.zeros((SLOTS, 1), f32)
    for turn, begin in enumerate(range(0, high_ref.shape[1], CHUNK)):
        here = slice(begin, begin + CHUNK)
        weight = row_weights(turn, begin)
        square += jnp.sum(weight * weight, axis=1, keepdims=True)
        weight = stack3(weight)
        for ref in (high_ref, low_ref):
            total += lax.dot_general(
                weight, ref[:, here], (((1,), (1,)), ((), ())), preferred_element_type=f32
            )
    out_ref[:, 0:count] = unstack3(total)
    out_ref[:, count : count + EXTRA] = jnp.broadcast_to(square, (SLOTS, EXTRA))


def row_sum(value):
    return jnp.sum(value, axis=1, keepdims=True)


def first_apply_body(parts, scale_over_root, *refs):
    first_refs = refs[:parts]
    small_ref, high_ref, low_ref, target_ref, out_ref = refs[parts:]
    scale = scale_of(small_ref, target_ref.shape[1])
    target = scale * total_of(first_refs) * scale_over_root
    target_ref[...] = target
    out_ref[:, CHUNK:] = jnp.broadcast_to(row_sum(target * target), (SLOTS, EXTRA))
    apply_rows(scale * target, high_ref, low_ref, small_ref, out_ref)


def first_fold_body(parts, *refs):
    row_refs = refs[:parts]
    small_ref, high_ref, low_ref, rows_ref, out_ref = refs[parts:]
    rows_ref[...] = total_of(row_refs)

    def row_weights(turn, begin):
        value = rows_ref[turn : turn + 1, 0:CHUNK]
        return jnp.where(slot_mask(small_ref, begin), value, 0.0)

    fold_rows(row_weights, high_ref, low_ref, out_ref)


def second_apply_body(parts, inv_rows, *refs):
    fold_refs = refs[:parts]
    (small_ref, high_ref, low_ref, target_ref, rows_ref,
     residual_ref, step_ref, out_ref) = refs[parts:]
    count = target_ref.shape[1]
    folded = total_of(fold_refs)
    scale = scale_of(small_ref, count)
    target = target_ref[...]
    norm = rows_ref[:, CHUNK : CHUNK + 1]
    applied = scale * folded[:, 0:count] * inv_rows + RIDGE * target
    step = norm / (folded[:, count : count + 1] * inv_rows + RIDGE * norm)
    residual = target - step * applied
    residual_ref[...] = residual
    step_ref[...] = jnp.broadcast_to(step, step_ref.shape)
    lane = lax.broadcasted_iota(jnp.int32, (SLOTS, EXTRA), 1)
    out_ref[:, CHUNK:] = jnp.where(
        lane == 0, row_sum(residual * residual), row_sum(residual * target)
    )
    apply_rows(scale * residual, high_ref, low_ref, small_ref, out_ref)


def second_fold_body(parts, *refs):
    row_refs = refs[:parts]
    small_ref, high_ref, low_ref, rows_ref, sums_ref, out_ref = refs[parts:]
    latest = total_of(row_refs)
    sums_ref[...] = latest[:, CHUNK:]
    ratio = latest[:, CHUNK : CHUNK + 1] / rows_ref[:, CHUNK : CHUNK + 1]

    def row_weights(turn, begin):
        value = latest[turn : turn + 1, 0:CHUNK] + ratio * rows_ref[turn : turn + 1, 0:CHUNK]
        return jnp.where(slot_mask(small_ref, begin), value, 0.0)

    fold_rows(row_weights, high_ref, low_ref, out_ref)


def finish_body(parts, inv_rows, *refs):
    fold_refs = refs[:parts]
    (small_ref, target_ref, residual_ref, step_ref, rows_ref, sums_ref,
     coefficients_ref, out_ref) = refs[parts:]
    count = target_ref.shape[1]
    folded = total_of(fold_refs)
    target = target_ref[...]
    residual = residual_ref[...]
    first_norm = rows_ref[:, CHUNK : CHUNK + 1]
    norm = sums_ref[:, 0:1]
    cross = sums_ref[:, 1:2]
    ratio = norm / first_norm
    direction = residual + ratio * target
    square = norm + 2.0 * ratio * cross + ratio * ratio * first_norm
    applied = scale_of(small_ref, count) * folded[:, 0:count] * inv_rows + RIDGE * direction
    step = norm / (folded[:, count : count + 1] * inv_rows + RIDGE * square)
    coefficients_ref[...] = step_ref[:, 0:1] * target + step * direction
    out_ref[...] = residual - step * applied


def call(body, out_shape, *args):
    return pl.pallas_call(
        body,
        out_shape=out_shape,
        in_specs=[pl.BlockSpec(memory_space=pltpu.VMEM)] * len(args),
        out_specs=jax.tree.map(lambda _: pl.BlockSpec(memory_space=pltpu.VMEM), out_shape),
        compiler_params=pltpu.CompilerParams(vmem_limit_bytes=40 * 1024 * 1024),
    )(*args)


def exchange(value, axis):
    size = lax.axis_size(axis)
    parts = [value]
    stride = 1
    while stride < size:
        value = pair_total(parts)
        span = min(4, size // stride)
        parts = [value]
        if span == 2:
            pairs = [(i, i ^ stride) for i in range(size)]
            parts.append(lax.ppermute(value, axis, pairs))
        else:
            groups = [
                [first + offset * stride for offset in range(span)]
                for first in range(size)
                if (first // stride) % span == 0
            ]
            copies = jnp.broadcast_to(value[None], (span, *value.shape))
            got = lax.all_to_all(copies, axis, 0, 0, axis_index_groups=groups, tiled=True)
            parts = [got[i] for i in range(span)]
        stride *= span
    if len(parts) == 4:
        return [got]
    return [part[None] for part in parts]


def shaped(shape, dtype=f32):
    return jax.ShapeDtypeStruct(shape, dtype)


def per_device(features, prices, slots, center_idx, center_scale):
    row_count = features.shape[1]
    count = center_idx.shape[0]
    all_rows = row_count * lax.axis_size("dp")
    local_idx = center_idx - lax.axis_index("dp") * row_count
    small = jnp.concatenate(
        [slots.astype(f32), prices, center_scale, local_idx.astype(f32)]
    ).reshape(1, -1)
    turns = row_count // CHUNK
    part = functools.partial

    picked = call(pick_body, shaped((features.shape[0], count), bf16), features, small)
    centers = exchange(picked, "dp")
    block = shaped((count, row_count), bf16)
    high, low, first = call(
        part(kernel_body, len(centers)),
        (block, block, shaped((SLOTS, count))),
        features, small, *centers,
    )
    firsts = exchange(first, "dp")
    row_shape = shaped((turns, CHUNK + EXTRA))
    fold_shape = shaped((SLOTS, count + EXTRA))
    vector = shaped((SLOTS, count))
    narrow = shaped((SLOTS, EXTRA))
    target, rows = call(
        part(first_apply_body, len(firsts), 1.0 / math.sqrt(all_rows)),
        (vector, row_shape),
        *firsts, small, high, low,
    )
    rows = exchange(rows, "centers")
    rows, folded = call(
        part(first_fold_body, len(rows)), (row_shape, fold_shape), *rows, small, high, low
    )
    folds = exchange(folded, "dp")
    residual, step, latest = call(
        part(second_apply_body, len(folds), 1.0 / all_rows),
        (vector, narrow, row_shape),
        *folds, small, high, low, target, rows,
    )
    latest = exchange(latest, "centers")
    sums, folded = call(
        part(second_fold_body, len(latest)),
        (narrow, fold_shape),
        *latest, small, high, low, rows,
    )
    folds = exchange(folded, "dp")
    return call(
        part(finish_body, len(folds), 1.0 / all_rows),
        (vector, vector),
        *folds, small, target, residual, step, rows, sums,
    )


def solution(mesh):
    return jax.shard_map(
        per_device,
        mesh=mesh,
        in_specs=(P(None, "dp"), P("dp"), P("dp"), P("centers"), P("centers")),
        out_specs=(P(None, "centers"), P(None, "centers")),
        check_vma=False,
    )
```

```python
import math
from functools import partial

import jax
import jax.numpy as jnp
from jax import lax
from jax.experimental import pallas as pl
from jax.experimental.pallas import tpu as pltpu
from jax.sharding import PartitionSpec as P

SLOTS = 8
RIDGE = 0.5
CHUNK = 512
EXTRA = 128
DEPTH = 128
f32 = jnp.float32
bf16 = jnp.bfloat16
VMEM = pl.BlockSpec(memory_space=pltpu.VMEM)
HBM = pl.BlockSpec(memory_space=pltpu.HBM)


def split3(value):
    high = value.astype(bf16).astype(f32)
    rest = value - high
    mid = rest.astype(bf16).astype(f32)
    return high, mid, rest - mid


def stack3(value):
    return jnp.concatenate(split3(value), axis=0).astype(bf16)


def unstack3(value):
    return value[0:8] + (value[8:16] + value[16:24])


def pair_total(parts):
    while len(parts) > 1:
        parts = [parts[i] + parts[i + 1] for i in range(0, len(parts), 2)]
    return parts[0]


def total_of(refs):
    return pair_total([ref[...] for ref in refs])


def row_sum(value):
    return jnp.sum(value, axis=1, keepdims=True)


def slot_mask(slots):
    row = lax.broadcasted_iota(jnp.int32, (SLOTS, slots.shape[1]), 0)
    return slots == row


def with_norms(feat, feat_first):
    feat32 = feat.astype(f32)
    half = -0.5 * jnp.sum(feat32 * feat32, axis=0, keepdims=True)
    rows = DEPTH - feat.shape[0]
    row = lax.broadcasted_iota(jnp.int32, (rows, feat.shape[1]), 0)
    base = 0 if feat_first else 3
    extra = jnp.where(row < 6, 1.0, 0.0)
    for place, part in enumerate(split3(half)):
        extra = jnp.where(row == base + place, part, extra)
    return jnp.concatenate([feat32, extra], axis=0)


def kernel_parts(left, right):
    inner = jnp.dot(left, right, preferred_element_type=f32)
    value = jnp.exp2(inner * (math.log2(math.e) / 64.0))
    high = value.astype(bf16)
    return high, (value - high.astype(f32)).astype(bf16)


def pick_body(feat_hbm, *refs):
    small_hbm, refs = refs[:4], refs[4:]
    feat_ref, idx_ref, slots_ref, prices_ref, scale_ref, out_ref, sems = refs
    row_count = feat_ref.shape[1]
    copies = []
    for source, target in zip(small_hbm, (idx_ref, slots_ref, prices_ref, scale_ref)):
        copies.append(pltpu.make_async_copy(source, target, sems.at[len(copies)]))
    for begin in range(0, row_count, CHUNK):
        here = pl.ds(begin, CHUNK)
        copies.append(
            pltpu.make_async_copy(feat_hbm.at[:, here], feat_ref.at[:, here], sems.at[len(copies)])
        )
    for copy in copies:
        copy.start()
    total = jnp.zeros(out_ref.shape, f32)
    count = out_ref.shape[1]
    copies[0].wait()
    local_idx = idx_ref[...] - lax.axis_index("dp") * row_count
    for turn, begin in enumerate(range(0, row_count, CHUNK)):
        row = lax.broadcasted_iota(jnp.int32, (CHUNK, count), 0)
        one_hot = jnp.where(row == local_idx - begin, 1.0, 0.0).astype(bf16)
        copies[4 + turn].wait()
        total += jnp.dot(
            feat_ref[:, begin : begin + CHUNK], one_hot, preferred_element_type=f32
        )
    out_ref[...] = total.astype(bf16)
    for copy in copies[1:4]:
        copy.wait()


def columns_body(feat_ref, slots_ref, prices_ref, columns_ref, turned_ref, weight_ref):
    for begin in range(0, feat_ref.shape[1], CHUNK):
        here = slice(begin, begin + CHUNK)
        columns = with_norms(feat_ref[:, here], False)
        columns_ref[:, here] = columns.astype(bf16)
        turned_ref[here, :] = columns.T.astype(bf16)
        weight = jnp.where(slot_mask(slots_ref[:, here]), prices_ref[:, here], 0.0)
        weight_ref[:, here] = stack3(weight)


def rows_body(parts, turned_ref, weight_ref, *refs):
    center_refs, (block_ref, center_ref, out_ref) = refs[:parts], refs[parts:]
    center = with_norms(total_of(center_refs), True).astype(bf16)
    center_ref[...] = center
    total = jnp.zeros((24, center.shape[1]), f32)
    for begin in range(0, turned_ref.shape[0], CHUNK):
        here = slice(begin, begin + CHUNK)
        high, low = kernel_parts(turned_ref[here, :], center)
        block_ref[2 * begin : 2 * begin + CHUNK, :] = high
        block_ref[2 * begin + CHUNK : 2 * begin + 2 * CHUNK, :] = low
        weight = weight_ref[:, here]
        total += jnp.dot(weight, high, preferred_element_type=f32)
        total += jnp.dot(weight, low, preferred_element_type=f32)
    out_ref[...] = unstack3(total)


def turned_body(columns_ref, center_ref, block_ref):
    center = center_ref[...].astype(f32).T.astype(bf16)
    count = center.shape[0]
    for begin in range(0, columns_ref.shape[1], CHUNK):
        here = slice(begin, begin + CHUNK)
        high, low = kernel_parts(center, columns_ref[:, here])
        block_ref[0:count, here] = high
        block_ref[count:, here] = low


def apply_rows(scaled, turned_ref, slots_ref, out_ref):
    stacked = stack3(scaled)
    stacked = jnp.concatenate([stacked, stacked], axis=1)
    for turn, begin in enumerate(range(0, turned_ref.shape[1], CHUNK)):
        here = slice(begin, begin + CHUNK)
        value = jnp.dot(stacked, turned_ref[:, here], preferred_element_type=f32)
        own = jnp.where(slot_mask(slots_ref[:, here]), unstack3(value), 0.0)
        out_ref[turn : turn + 1, 0:CHUNK] = jnp.sum(own, axis=0, keepdims=True)


def fold_rows(row_weights, block_ref, slots_ref, out_ref):
    count = block_ref.shape[1]
    total = jnp.zeros((24, count), f32)
    square = jnp.zeros((SLOTS, 1), f32)
    for turn, begin in enumerate(range(0, slots_ref.shape[1], CHUNK)):
        mask = slot_mask(slots_ref[:, begin : begin + CHUNK])
        weight = jnp.where(mask, row_weights(turn), 0.0)
        square += row_sum(weight * weight)
        weight = stack3(weight)
        weight = jnp.concatenate([weight, weight], axis=1)
        block = block_ref[2 * begin : 2 * begin + 2 * CHUNK, :]
        total += jnp.dot(weight, block, preferred_element_type=f32)
    out_ref[:, 0:count] = unstack3(total)
    out_ref[:, count : count + EXTRA] = jnp.broadcast_to(square, (SLOTS, EXTRA))


def first_apply_body(parts, scale_over_root, *refs):
    first_refs = refs[:parts]
    scale_ref, slots_ref, turned_ref, target_ref, out_ref = refs[parts:]
    scale = scale_ref[...]
    target = scale * total_of(first_refs) * scale_over_root
    target_ref[...] = target
    out_ref[:, CHUNK:] = jnp.broadcast_to(row_sum(target * target), (SLOTS, EXTRA))
    apply_rows(scale * target, turned_ref, slots_ref, out_ref)


def first_fold_body(parts, *refs):
    row_refs = refs[:parts]
    slots_ref, block_ref, rows_ref, out_ref = refs[parts:]
    rows = total_of(row_refs)
    rows_ref[...] = rows
    fold_rows(lambda turn: rows[turn : turn + 1, 0:CHUNK], block_ref, slots_ref, out_ref)


def second_apply_body(parts, inv_rows, *refs):
    fold_refs = refs[:parts]
    (scale_ref, slots_ref, turned_ref, target_ref, rows_ref,
     residual_ref, step_ref, out_ref) = refs[parts:]
    count = scale_ref.shape[1]
    folded = total_of(fold_refs)
    scale = scale_ref[...]
    target = target_ref[...]
    norm = rows_ref[:, CHUNK : CHUNK + 1]
    applied = scale * folded[:, 0:count] * inv_rows + RIDGE * target
    step = norm / (folded[:, count : count + 1] * inv_rows + RIDGE * norm)
    residual = target - step * applied
    residual_ref[...] = residual
    step_ref[...] = jnp.broadcast_to(step, step_ref.shape)
    lane = lax.broadcasted_iota(jnp.int32, (SLOTS, EXTRA), 1)
    out_ref[:, CHUNK:] = jnp.where(
        lane == 0, row_sum(residual * residual), row_sum(residual * target)
    )
    apply_rows(scale * residual, turned_ref, slots_ref, out_ref)


def second_fold_body(parts, *refs):
    row_refs = refs[:parts]
    slots_ref, block_ref, rows_ref, sums_ref, out_ref = refs[parts:]
    latest = total_of(row_refs)
    sums_ref[...] = latest[:, CHUNK:]
    rows = rows_ref[...]
    ratio = latest[:, CHUNK : CHUNK + 1] / rows[:, CHUNK : CHUNK + 1]

    def row_weights(turn):
        return latest[turn : turn + 1, 0:CHUNK] + ratio * rows[turn : turn + 1, 0:CHUNK]

    fold_rows(row_weights, block_ref, slots_ref, out_ref)


def finish_body(parts, inv_rows, *refs):
    fold_refs = refs[:parts]
    (scale_ref, target_ref, residual_ref, step_ref, rows_ref, sums_ref,
     coefficients_ref, out_ref) = refs[parts:]
    count = scale_ref.shape[1]
    folded = total_of(fold_refs)
    target = target_ref[...]
    residual = residual_ref[...]
    first_norm = rows_ref[:, CHUNK : CHUNK + 1]
    norm = sums_ref[:, 0:1]
    cross = sums_ref[:, 1:2]
    ratio = norm / first_norm
    direction = residual + ratio * target
    square = norm + 2.0 * ratio * cross + ratio * ratio * first_norm
    applied = scale_ref[...] * folded[:, 0:count] * inv_rows + RIDGE * direction
    step = norm / (folded[:, count : count + 1] * inv_rows + RIDGE * square)
    coefficients_ref[...] = step_ref[:, 0:1] * target + step * direction
    out_ref[...] = residual - step * applied


def call(body, out_shape, *args, source=VMEM, flops=0, bytes_accessed=0, **more):
    return pl.pallas_call(
        body,
        out_shape=out_shape,
        in_specs=[source] * len(args),
        out_specs=jax.tree.map(lambda _: VMEM, out_shape),
        compiler_params=pltpu.CompilerParams(vmem_limit_bytes=36 * 1024 * 1024),
        cost_estimate=pl.CostEstimate(
            flops=flops, bytes_accessed=bytes_accessed, transcendentals=0
        ),
        **more,
    )(*args)


def exchange(value, axis):
    size = lax.axis_size(axis)
    parts = [value]
    stride = 1
    while stride < size:
        value = pair_total(parts)
        parts = [value]
        span = min(4, size // stride)
        for offset in range(1, span):
            pairs = [(i, i ^ (offset * stride)) for i in range(size)]
            parts.append(lax.ppermute(value, axis, pairs))
        stride *= span
    return parts


def shaped(shape, dtype=f32):
    return jax.ShapeDtypeStruct(shape, dtype)


def per_device(features, prices, slots, center_idx, center_scale):
    depth, row_count = features.shape
    count = center_idx.shape[0]
    all_rows = row_count * lax.axis_size("dp")
    turns = row_count // CHUNK
    row_shape = shaped((turns, CHUNK + EXTRA))
    fold_shape = shaped((SLOTS, count + EXTRA))
    vector = shaped((SLOTS, count))
    narrow = shaped((SLOTS, EXTRA))
    pass_cost = dict(flops=64 * row_count * count, bytes_accessed=4 * row_count * count)

    inputs = [
        pltpu.with_memory_space_constraint(array, pltpu.HBM)
        for array in (
            features,
            center_idx.reshape(1, count),
            slots.reshape(1, row_count),
            prices.reshape(1, row_count),
            center_scale.reshape(1, count),
        )
    ]
    features, _, slots, prices, scale, picked = call(
        pick_body,
        (
            shaped(features.shape, bf16),
            shaped((1, count), jnp.int32),
            shaped((1, row_count), jnp.int32),
            shaped((1, row_count)),
            shaped((1, count)),
            shaped((depth, count), bf16),
        ),
        *inputs,
        source=HBM,
        scratch_shapes=[pltpu.SemaphoreType.DMA((4 + turns,))],
    )
    centers = exchange(picked, "dp")
    columns, turned_columns, weight = call(
        columns_body,
        (
            shaped((DEPTH, row_count), bf16),
            shaped((row_count, DEPTH), bf16),
            shaped((24, row_count), bf16),
        ),
        features, slots, prices,
        flops=1000 * row_count,
        bytes_accessed=1024 * row_count,
    )
    block, center, first = call(
        partial(rows_body, len(centers)),
        (shaped((2 * row_count, count), bf16), shaped((DEPTH, count), bf16), vector),
        turned_columns, weight, *centers,
        **pass_cost,
    )
    firsts = exchange(first, "dp")
    turned = call(
        turned_body, shaped((2 * count, row_count), bf16), columns, center, **pass_cost
    )
    target, rows = call(
        partial(first_apply_body, len(firsts), 1.0 / math.sqrt(all_rows)),
        (vector, row_shape),
        *firsts, scale, slots, turned,
    )
    rows = exchange(rows, "centers")
    rows, folded = call(
        partial(first_fold_body, len(rows)), (row_shape, fold_shape), *rows, slots, block
    )
    folds = exchange(folded, "dp")
    residual, step, latest = call(
        partial(second_apply_body, len(folds), 1.0 / all_rows),
        (vector, narrow, row_shape),
        *folds, scale, slots, turned, target, rows,
    )
    latest = exchange(latest, "centers")
    sums, folded = call(
        partial(second_fold_body, len(latest)),
        (narrow, fold_shape),
        *latest, slots, block, rows,
    )
    folds = exchange(folded, "dp")
    return call(
        partial(finish_body, len(folds), 1.0 / all_rows),
        (vector, vector),
        *folds, scale, target, residual, step, rows, sums,
    )


def solution(mesh):
    return jax.shard_map(
        per_device,
        mesh=mesh,
        in_specs=(P(None, "dp"), P("dp"), P("dp"), P("centers"), P("centers")),
        out_specs=(P(None, "centers"), P(None, "centers")),
        check_vma=False,
    )
```

```python
import math
from functools import partial

import jax
import jax.numpy as jnp
from jax import lax
from jax.experimental import pallas as pl
from jax.experimental.pallas import tpu as pltpu
from jax.sharding import PartitionSpec as P

SLOTS = 8
RIDGE = 0.5
CHUNK = 512
EXTRA = 128
DEPTH = 256
STEP = 256
FACTOR = math.log2(math.e) / 64.0
f32 = jnp.float32
bf16 = jnp.bfloat16
VMEM = pl.BlockSpec(memory_space=pltpu.VMEM)
HBM = pl.BlockSpec(memory_space=pltpu.HBM)


def split3(value):
    high = value.astype(bf16).astype(f32)
    rest = value - high
    mid = rest.astype(bf16).astype(f32)
    return high, mid, rest - mid


def stack3(value):
    return jnp.concatenate(split3(value), axis=0).astype(bf16)


def unstack3(value):
    return value[0:8] + (value[8:16] + value[16:24])


def pair_total(parts):
    while len(parts) > 1:
        parts = [parts[i] + parts[i + 1] for i in range(0, len(parts), 2)]
    return parts[0]


def total_of(refs):
    return pair_total([ref[...] for ref in refs])


def row_sum(value):
    return jnp.sum(value, axis=1, keepdims=True)


def slot_mask(slots):
    row = lax.broadcasted_iota(jnp.int32, (SLOTS, slots.shape[1]), 0)
    return slots == row


def norm_rows(feat32, base):
    half = (-0.5 * FACTOR) * jnp.sum(feat32 * feat32, axis=0, keepdims=True)
    row = lax.broadcasted_iota(jnp.int32, (feat32.shape[0], feat32.shape[1]), 0)
    extra = jnp.where(row < 6, 1.0, 0.0)
    for place, part in enumerate(split3(half)):
        extra = jnp.where(row == base + place, part, extra)
    return extra


def kernel_parts(left, right):
    value = jnp.exp2(jnp.dot(left, right, preferred_element_type=f32))
    high = value.astype(bf16)
    return high, (value - high.astype(f32)).astype(bf16)


def pick_body(feat_hbm, idx_hbm, slots_hbm, prices_hbm, scale_hbm, *refs):
    feat_ref, slots_ref, prices_ref, scale_ref, out_ref, idx_ref, hit_ref, sems = refs
    row_count = feat_ref.shape[1]
    count = out_ref.shape[1]
    sources = (idx_hbm, feat_hbm, slots_hbm, prices_hbm, scale_hbm)
    targets = (idx_ref, feat_ref, slots_ref, prices_ref, scale_ref)
    copies = [
        pltpu.make_async_copy(source, target, sems.at[place])
        for place, (source, target) in enumerate(zip(sources, targets))
    ]
    for copy in copies:
        copy.start()
    copies[0].wait()
    local_idx = idx_ref[...] - lax.axis_index("dp") * row_count
    for begin in range(0, row_count, CHUNK):
        row = lax.broadcasted_iota(jnp.int32, (CHUNK, count), 0)
        hit = jnp.where(row == local_idx - begin, 1.0, 0.0)
        hit_ref[begin : begin + CHUNK, :] = hit.astype(bf16)
    copies[1].wait()
    out_ref[...] = jnp.dot(
        feat_ref[...], hit_ref[...], preferred_element_type=f32
    ).astype(bf16)
    for copy in copies[2:]:
        copy.wait()


def columns_body(feat_ref, slots_ref, prices_ref, columns_ref, turned_ref, weight_ref):
    for begin in range(0, feat_ref.shape[1], CHUNK):
        here = slice(begin, begin + CHUNK)
        feat32 = feat_ref[:, here].astype(f32)
        pair = jnp.concatenate([feat32, feat32], axis=0)
        last = jnp.concatenate([feat32, norm_rows(feat32, 3)], axis=0)
        columns_ref[0:128, here] = pair.astype(bf16)
        columns_ref[128:256, here] = last.astype(bf16)
        turned_ref[here, 0:128] = pair.T.astype(bf16)
        turned_ref[here, 128:256] = last.T.astype(bf16)
        weight = jnp.where(slot_mask(slots_ref[:, here]), prices_ref[:, here], 0.0)
        weight_ref[:, here] = stack3(weight)


def rows_body(parts, turned_ref, weight_ref, *refs):
    center_refs, (block_ref, center_ref, out_ref) = refs[:parts], refs[parts:]
    center = total_of(center_refs).astype(f32)
    center = jnp.concatenate(
        [*split3(center * FACTOR), norm_rows(center, 0)], axis=0
    ).astype(bf16)
    center_ref[...] = center
    total = jnp.zeros((24, center.shape[1]), f32)

    def fold(begin):
        weight = weight_ref[:, begin : begin + STEP]
        weight = jnp.concatenate([weight, weight], axis=1)
        block = block_ref[2 * begin : 2 * begin + 2 * STEP, :]
        return jnp.dot(weight, block, preferred_element_type=f32)

    row_count = turned_ref.shape[0]
    for begin in range(0, row_count, STEP):
        high, low = kernel_parts(turned_ref[begin : begin + STEP, :], center)
        block_ref[2 * begin : 2 * begin + STEP, :] = high
        block_ref[2 * begin + STEP : 2 * begin + 2 * STEP, :] = low
        if begin > 0:
            total += fold(begin - STEP)
    out_ref[...] = unstack3(total + fold(row_count - STEP))


def turned_body(columns_ref, center_ref, block_ref):
    center = center_ref[...].astype(f32).T.astype(bf16)
    count = center.shape[0]
    for begin in range(0, columns_ref.shape[1], CHUNK):
        here = slice(begin, begin + CHUNK)
        high, low = kernel_parts(center, columns_ref[:, here])
        block_ref[0:count, here] = high
        block_ref[count:, here] = low


def apply_rows(scaled, turned_ref, slots_ref, out_ref):
    stacked = stack3(scaled)
    stacked = jnp.concatenate([stacked, stacked], axis=1)
    value = jnp.dot(stacked, turned_ref[...], preferred_element_type=f32)
    own = jnp.where(slot_mask(slots_ref[...]), unstack3(value), 0.0)
    own = jnp.sum(own, axis=0, keepdims=True)
    for turn, begin in enumerate(range(0, turned_ref.shape[1], CHUNK)):
        out_ref[turn : turn + 1, 0:CHUNK] = own[:, begin : begin + CHUNK]


def fold_rows(row_weights, block_ref, slots_ref, out_ref):
    count = block_ref.shape[1]
    square = jnp.zeros((SLOTS, 1), f32)
    weights = []
    for turn, begin in enumerate(range(0, slots_ref.shape[1], CHUNK)):
        mask = slot_mask(slots_ref[:, begin : begin + CHUNK])
        weight = jnp.where(mask, row_weights(turn), 0.0)
        square += row_sum(weight * weight)
        weight = stack3(weight)
        for inner in range(0, CHUNK, STEP):
            weights += [weight[:, inner : inner + STEP]] * 2
    total = jnp.dot(
        jnp.concatenate(weights, axis=1), block_ref[...], preferred_element_type=f32
    )
    out_ref[:, 0:count] = unstack3(total)
    out_ref[:, count : count + EXTRA] = jnp.broadcast_to(square, (SLOTS, EXTRA))


def first_apply_body(parts, scale_over_root, *refs):
    first_refs = refs[:parts]
    scale_ref, slots_ref, turned_ref, target_ref, out_ref = refs[parts:]
    scale = scale_ref[...]
    target = scale * total_of(first_refs) * scale_over_root
    target_ref[...] = target
    out_ref[:, CHUNK:] = jnp.broadcast_to(row_sum(target * target), (SLOTS, EXTRA))
    apply_rows(scale * target, turned_ref, slots_ref, out_ref)


def first_fold_body(parts, *refs):
    row_refs = refs[:parts]
    slots_ref, block_ref, rows_ref, out_ref = refs[parts:]
    rows = total_of(row_refs)
    rows_ref[...] = rows
    fold_rows(lambda turn: rows[turn : turn + 1, 0:CHUNK], block_ref, slots_ref, out_ref)


def second_apply_body(parts, inv_rows, *refs):
    fold_refs = refs[:parts]
    (scale_ref, slots_ref, turned_ref, target_ref, rows_ref,
     residual_ref, step_ref, out_ref) = refs[parts:]
    count = scale_ref.shape[1]
    folded = total_of(fold_refs)
    scale = scale_ref[...]
    target = target_ref[...]
    norm = rows_ref[:, CHUNK : CHUNK + 1]
    applied = scale * folded[:, 0:count] * inv_rows + RIDGE * target
    step = norm / (folded[:, count : count + 1] * inv_rows + RIDGE * norm)
    residual = target - step * applied
    residual_ref[...] = residual
    step_ref[...] = jnp.broadcast_to(step, step_ref.shape)
    lane = lax.broadcasted_iota(jnp.int32, (SLOTS, EXTRA), 1)
    out_ref[:, CHUNK:] = jnp.where(
        lane == 0, row_sum(residual * residual), row_sum(residual * target)
    )
    apply_rows(scale * residual, turned_ref, slots_ref, out_ref)


def second_fold_body(parts, *refs):
    row_refs = refs[:parts]
    slots_ref, block_ref, rows_ref, sums_ref, out_ref = refs[parts:]
    latest = total_of(row_refs)
    sums_ref[...] = latest[:, CHUNK:]
    rows = rows_ref[...]
    ratio = latest[:, CHUNK : CHUNK + 1] / rows[:, CHUNK : CHUNK + 1]

    def row_weights(turn):
        return latest[turn : turn + 1, 0:CHUNK] + ratio * rows[turn : turn + 1, 0:CHUNK]

    fold_rows(row_weights, block_ref, slots_ref, out_ref)


def finish_body(parts, inv_rows, *refs):
    fold_refs = refs[:parts]
    (scale_ref, target_ref, residual_ref, step_ref, rows_ref, sums_ref,
     coefficients_ref, out_ref) = refs[parts:]
    count = scale_ref.shape[1]
    folded = total_of(fold_refs)
    target = target_ref[...]
    residual = residual_ref[...]
    first_norm = rows_ref[:, CHUNK : CHUNK + 1]
    norm = sums_ref[:, 0:1]
    cross = sums_ref[:, 1:2]
    ratio = norm / first_norm
    direction = residual + ratio * target
    square = norm + 2.0 * ratio * cross + ratio * ratio * first_norm
    applied = scale_ref[...] * folded[:, 0:count] * inv_rows + RIDGE * direction
    step = norm / (folded[:, count : count + 1] * inv_rows + RIDGE * square)
    coefficients_ref[...] = step_ref[:, 0:1] * target + step * direction
    out_ref[...] = residual - step * applied


def call(body, out_shape, *args, source=VMEM, flops=0, bytes_accessed=0, **more):
    return pl.pallas_call(
        body,
        out_shape=out_shape,
        in_specs=[source] * len(args),
        out_specs=jax.tree.map(lambda _: VMEM, out_shape),
        compiler_params=pltpu.CompilerParams(vmem_limit_bytes=36 * 1024 * 1024),
        cost_estimate=pl.CostEstimate(
            flops=flops, bytes_accessed=bytes_accessed, transcendentals=0
        ),
        **more,
    )(*args)


def exchange(value, axis):
    size = lax.axis_size(axis)
    parts = [value]
    stride = 1
    while stride < size:
        value = pair_total(parts)
        parts = [value]
        span = min(4, size // stride)
        for offset in range(1, span):
            pairs = [(i, i ^ (offset * stride)) for i in range(size)]
            parts.append(lax.ppermute(value, axis, pairs))
        stride *= span
    return parts


def shaped(shape, dtype=f32):
    return jax.ShapeDtypeStruct(shape, dtype)


def per_device(features, prices, slots, center_idx, center_scale):
    depth, row_count = features.shape
    count = center_idx.shape[0]
    all_rows = row_count * lax.axis_size("dp")
    turns = row_count // CHUNK
    row_shape = shaped((turns, CHUNK + EXTRA))
    fold_shape = shaped((SLOTS, count + EXTRA))
    vector = shaped((SLOTS, count))
    narrow = shaped((SLOTS, EXTRA))
    pass_cost = dict(flops=64 * row_count * count, bytes_accessed=4 * row_count * count)

    inputs = [
        pltpu.with_memory_space_constraint(array, pltpu.HBM)
        for array in (
            features,
            center_idx.reshape(1, count),
            slots.reshape(1, row_count),
            prices.reshape(1, row_count),
            center_scale.reshape(1, count),
        )
    ]
    features, slots, prices, scale, picked = call(
        pick_body,
        (
            shaped(features.shape, bf16),
            shaped((1, row_count), jnp.int32),
            shaped((1, row_count)),
            shaped((1, count)),
            shaped((depth, count), bf16),
        ),
        *inputs,
        source=HBM,
        scratch_shapes=[
            pltpu.VMEM((1, count), jnp.int32),
            pltpu.VMEM((row_count, count), bf16),
            pltpu.SemaphoreType.DMA((5,)),
        ],
    )
    centers = exchange(picked, "dp")
    columns, turned_columns, weight = call(
        columns_body,
        (
            shaped((DEPTH, row_count), bf16),
            shaped((row_count, DEPTH), bf16),
            shaped((24, row_count), bf16),
        ),
        features, slots, prices,
        flops=1000 * row_count,
        bytes_accessed=1024 * row_count,
    )
    block, center, first = call(
        partial(rows_body, len(centers)),
        (shaped((2 * row_count, count), bf16), shaped((DEPTH, count), bf16), vector),
        turned_columns, weight, *centers,
        **pass_cost,
    )
    firsts = exchange(first, "dp")
    turned = call(
        turned_body, shaped((2 * count, row_count), bf16), columns, center, **pass_cost
    )
    target, rows = call(
        partial(first_apply_body, len(firsts), 1.0 / math.sqrt(all_rows)),
        (vector, row_shape),
        *firsts, scale, slots, turned,
    )
    rows = exchange(rows, "centers")
    rows, folded = call(
        partial(first_fold_body, len(rows)), (row_shape, fold_shape), *rows, slots, block
    )
    folds = exchange(folded, "dp")
    residual, step, latest = call(
        partial(second_apply_body, len(folds), 1.0 / all_rows),
        (vector, narrow, row_shape),
        *folds, scale, slots, turned, target, rows,
    )
    latest = exchange(latest, "centers")
    sums, folded = call(
        partial(second_fold_body, len(latest)),
        (narrow, fold_shape),
        *latest, slots, block, rows,
    )
    folds = exchange(folded, "dp")
    return call(
        partial(finish_body, len(folds), 1.0 / all_rows),
        (vector, vector),
        *folds, scale, target, residual, step, rows, sums,
    )


def solution(mesh):
    return jax.shard_map(
        per_device,
        mesh=mesh,
        in_specs=(P(None, "dp"), P("dp"), P("dp"), P("centers"), P("centers")),
        out_specs=(P(None, "centers"), P(None, "centers")),
        check_vma=False,
    )
```

```python
import math
from functools import partial

import jax
import jax.numpy as jnp
from jax import lax
from jax.experimental import pallas as pl
from jax.experimental.pallas import tpu as pltpu
from jax.sharding import PartitionSpec as P

SLOTS = 8
RIDGE = 0.5
CHUNK = 512
EXTRA = 128
DEPTH = 256
STEP = 256
FACTOR = math.log2(math.e) / 64.0
f32 = jnp.float32
bf16 = jnp.bfloat16
VMEM = pl.BlockSpec(memory_space=pltpu.VMEM)
HBM = pl.BlockSpec(memory_space=pltpu.HBM)


def split3(value):
    high = value.astype(bf16).astype(f32)
    rest = value - high
    mid = rest.astype(bf16).astype(f32)
    return high, mid, rest - mid


def stack3(value):
    return jnp.concatenate(split3(value), axis=0).astype(bf16)


def unstack3(value):
    return value[0:8] + (value[8:16] + value[16:24])


def pair_total(parts):
    while len(parts) > 1:
        parts = [parts[i] + parts[i + 1] for i in range(0, len(parts), 2)]
    return parts[0]


def total_of(refs):
    return pair_total([ref[...] for ref in refs])


def row_sum(value):
    return jnp.sum(value, axis=1, keepdims=True)


def slot_mask(slots):
    row = lax.broadcasted_iota(jnp.int32, (SLOTS, slots.shape[1]), 0)
    return slots == row


def norm_rows(feat32, base):
    half = (-0.5 * FACTOR) * jnp.sum(feat32 * feat32, axis=0, keepdims=True)
    row = lax.broadcasted_iota(jnp.int32, (feat32.shape[0], feat32.shape[1]), 0)
    extra = jnp.where(row < 6, 1.0, 0.0)
    for place, part in enumerate(split3(half)):
        extra = jnp.where(row == base + place, part, extra)
    return extra


def kernel_parts(left, right):
    value = jnp.exp2(jnp.dot(left, right, preferred_element_type=f32))
    high = value.astype(bf16)
    return high, (value - high.astype(f32)).astype(bf16)


def pick_body(feat_hbm, idx_hbm, slots_hbm, prices_hbm, scale_hbm, *refs):
    feat_ref, slots_ref, prices_ref, scale_ref, out_ref, idx_ref, hit_ref, sems = refs
    row_count = feat_ref.shape[1]
    count = out_ref.shape[1]
    sources = (idx_hbm, feat_hbm, slots_hbm, prices_hbm, scale_hbm)
    targets = (idx_ref, feat_ref, slots_ref, prices_ref, scale_ref)
    copies = [
        pltpu.make_async_copy(source, target, sems.at[place])
        for place, (source, target) in enumerate(zip(sources, targets))
    ]
    for copy in copies:
        copy.start()
    copies[0].wait()
    local_idx = idx_ref[...] - lax.axis_index("dp") * row_count
    row = lax.broadcasted_iota(jnp.int32, (STEP, count), 0).astype(f32).astype(bf16)
    block = lax.div(local_idx, STEP)
    place = (local_idx - block * STEP).astype(f32)

    def hits(begin):
        own = jnp.where(block == begin // STEP, place, -1.0).astype(bf16)
        return jnp.where(row == own, jnp.ones_like(row), jnp.zeros_like(row))

    half = row_count // 2
    for begin in range(0, half, STEP):
        hit_ref[begin : begin + STEP, :] = hits(begin)
    copies[1].wait()
    total = jnp.dot(feat_ref[:, :half], hit_ref[...], preferred_element_type=f32)
    for begin in range(half, row_count, STEP):
        total += jnp.dot(
            feat_ref[:, begin : begin + STEP], hits(begin), preferred_element_type=f32
        )
    out_ref[...] = total.astype(bf16)
    for copy in copies[2:]:
        copy.wait()


def columns_body(feat_ref, slots_ref, prices_ref, columns_ref, turned_ref, weight_ref):
    for begin in range(0, feat_ref.shape[1], CHUNK):
        here = slice(begin, begin + CHUNK)
        feat32 = feat_ref[:, here].astype(f32)
        pair = jnp.concatenate([feat32, feat32], axis=0)
        last = jnp.concatenate([feat32, norm_rows(feat32, 3)], axis=0)
        columns_ref[0:128, here] = pair.astype(bf16)
        columns_ref[128:256, here] = last.astype(bf16)
        turned_ref[here, 0:128] = pair.T.astype(bf16)
        turned_ref[here, 128:256] = last.T.astype(bf16)
        weight = jnp.where(slot_mask(slots_ref[:, here]), prices_ref[:, here], 0.0)
        weight_ref[:, here] = stack3(weight)


def rows_body(parts, turned_ref, weight_ref, *refs):
    center_refs, (block_ref, center_ref, out_ref) = refs[:parts], refs[parts:]
    center = total_of(center_refs).astype(f32)
    center = jnp.concatenate(
        [*split3(center * FACTOR), norm_rows(center, 0)], axis=0
    ).astype(bf16)
    center_ref[...] = center
    total = jnp.zeros((24, center.shape[1]), f32)

    def fold(begin):
        weight = weight_ref[:, begin : begin + STEP]
        weight = jnp.concatenate([weight, weight], axis=1)
        block = block_ref[2 * begin : 2 * begin + 2 * STEP, :]
        return jnp.dot(weight, block, preferred_element_type=f32)

    row_count = turned_ref.shape[0]
    for begin in range(0, row_count, STEP):
        high, low = kernel_parts(turned_ref[begin : begin + STEP, :], center)
        block_ref[2 * begin : 2 * begin + STEP, :] = high
        block_ref[2 * begin + STEP : 2 * begin + 2 * STEP, :] = low
        if begin > 0:
            total += fold(begin - STEP)
    out_ref[...] = unstack3(total + fold(row_count - STEP))


def turned_body(columns_ref, center_ref, block_ref):
    center = center_ref[...].astype(f32).T.astype(bf16)
    count = center.shape[0]
    for begin in range(0, columns_ref.shape[1], CHUNK):
        here = slice(begin, begin + CHUNK)
        high, low = kernel_parts(center, columns_ref[:, here])
        block_ref[0:count, here] = high
        block_ref[count:, here] = low


def apply_rows(scaled, turned_ref, slots_ref, out_ref):
    stacked = stack3(scaled)
    stacked = jnp.concatenate([stacked, stacked], axis=1)
    value = jnp.dot(stacked, turned_ref[...], preferred_element_type=f32)
    own = jnp.where(slot_mask(slots_ref[...]), unstack3(value), 0.0)
    own = jnp.sum(own, axis=0, keepdims=True)
    for turn, begin in enumerate(range(0, turned_ref.shape[1], CHUNK)):
        out_ref[turn : turn + 1, 0:CHUNK] = own[:, begin : begin + CHUNK]


def fold_rows(row_weights, block_ref, slots_ref, out_ref):
    count = block_ref.shape[1]
    square = jnp.zeros((SLOTS, 1), f32)
    weights = []
    for turn, begin in enumerate(range(0, slots_ref.shape[1], CHUNK)):
        mask = slot_mask(slots_ref[:, begin : begin + CHUNK])
        weight = jnp.where(mask, row_weights(turn), 0.0)
        square += row_sum(weight * weight)
        weight = stack3(weight)
        for inner in range(0, CHUNK, STEP):
            weights += [weight[:, inner : inner + STEP]] * 2
    total = jnp.dot(
        jnp.concatenate(weights, axis=1), block_ref[...], preferred_element_type=f32
    )
    out_ref[:, 0:count] = unstack3(total)
    out_ref[:, count : count + EXTRA] = jnp.broadcast_to(square, (SLOTS, EXTRA))


def first_apply_body(parts, scale_over_root, *refs):
    first_refs = refs[:parts]
    scale_ref, slots_ref, turned_ref, target_ref, out_ref = refs[parts:]
    scale = scale_ref[...]
    target = scale * total_of(first_refs) * scale_over_root
    target_ref[...] = target
    out_ref[:, CHUNK:] = jnp.broadcast_to(row_sum(target * target), (SLOTS, EXTRA))
    apply_rows(scale * target, turned_ref, slots_ref, out_ref)


def first_fold_body(parts, *refs):
    row_refs = refs[:parts]
    slots_ref, block_ref, rows_ref, out_ref = refs[parts:]
    rows = total_of(row_refs)
    rows_ref[...] = rows
    fold_rows(lambda turn: rows[turn : turn + 1, 0:CHUNK], block_ref, slots_ref, out_ref)


def second_apply_body(parts, inv_rows, *refs):
    fold_refs = refs[:parts]
    (scale_ref, slots_ref, turned_ref, target_ref, rows_ref,
     residual_ref, step_ref, out_ref) = refs[parts:]
    count = scale_ref.shape[1]
    folded = total_of(fold_refs)
    scale = scale_ref[...]
    target = target_ref[...]
    norm = rows_ref[:, CHUNK : CHUNK + 1]
    applied = scale * folded[:, 0:count] * inv_rows + RIDGE * target
    step = norm / (folded[:, count : count + 1] * inv_rows + RIDGE * norm)
    residual = target - step * applied
    residual_ref[...] = residual
    step_ref[...] = jnp.broadcast_to(step, step_ref.shape)
    lane = lax.broadcasted_iota(jnp.int32, (SLOTS, EXTRA), 1)
    out_ref[:, CHUNK:] = jnp.where(
        lane == 0, row_sum(residual * residual), row_sum(residual * target)
    )
    apply_rows(scale * residual, turned_ref, slots_ref, out_ref)


def second_fold_body(parts, *refs):
    row_refs = refs[:parts]
    slots_ref, block_ref, rows_ref, sums_ref, out_ref = refs[parts:]
    latest = total_of(row_refs)
    sums_ref[...] = latest[:, CHUNK:]
    rows = rows_ref[...]
    ratio = latest[:, CHUNK : CHUNK + 1] / rows[:, CHUNK : CHUNK + 1]

    def row_weights(turn):
        return latest[turn : turn + 1, 0:CHUNK] + ratio * rows[turn : turn + 1, 0:CHUNK]

    fold_rows(row_weights, block_ref, slots_ref, out_ref)


def finish_body(parts, inv_rows, *refs):
    fold_refs = refs[:parts]
    (scale_ref, target_ref, residual_ref, step_ref, rows_ref, sums_ref,
     coefficients_ref, out_ref) = refs[parts:]
    count = scale_ref.shape[1]
    folded = total_of(fold_refs)
    target = target_ref[...]
    residual = residual_ref[...]
    first_norm = rows_ref[:, CHUNK : CHUNK + 1]
    norm = sums_ref[:, 0:1]
    cross = sums_ref[:, 1:2]
    ratio = norm / first_norm
    direction = residual + ratio * target
    square = norm + 2.0 * ratio * cross + ratio * ratio * first_norm
    applied = scale_ref[...] * folded[:, 0:count] * inv_rows + RIDGE * direction
    step = norm / (folded[:, count : count + 1] * inv_rows + RIDGE * square)
    coefficients_ref[...] = step_ref[:, 0:1] * target + step * direction
    out_ref[...] = residual - step * applied


def call(body, out_shape, *args, source=VMEM, flops=0, bytes_accessed=0, **more):
    return pl.pallas_call(
        body,
        out_shape=out_shape,
        in_specs=[source] * len(args),
        out_specs=jax.tree.map(lambda _: VMEM, out_shape),
        compiler_params=pltpu.CompilerParams(vmem_limit_bytes=36 * 1024 * 1024),
        cost_estimate=pl.CostEstimate(
            flops=flops, bytes_accessed=bytes_accessed, transcendentals=0
        ),
        **more,
    )(*args)


def exchange(value, axis):
    size = lax.axis_size(axis)
    parts = [value]
    stride = 1
    while stride < size:
        value = pair_total(parts)
        parts = [value]
        span = min(4, size // stride)
        side = 0 if stride == 1 else 1
        got = []
        for offset in reversed(range(1, span)):
            pairs = [(i, i ^ (offset * stride) ^ side) for i in range(size)]
            got.append(lax.ppermute(value, axis, pairs))
        parts = got + parts
        stride *= span
    return parts


def shaped(shape, dtype=f32):
    return jax.ShapeDtypeStruct(shape, dtype)


def per_device(features, prices, slots, center_idx, center_scale):
    depth, row_count = features.shape
    count = center_idx.shape[0]
    all_rows = row_count * lax.axis_size("dp")
    turns = row_count // CHUNK
    row_shape = shaped((turns, CHUNK + EXTRA))
    fold_shape = shaped((SLOTS, count + EXTRA))
    vector = shaped((SLOTS, count))
    narrow = shaped((SLOTS, EXTRA))
    pass_cost = dict(flops=64 * row_count * count, bytes_accessed=4 * row_count * count)

    inputs = [
        pltpu.with_memory_space_constraint(array, pltpu.HBM)
        for array in (
            features,
            center_idx.reshape(1, count),
            slots.reshape(1, row_count),
            prices.reshape(1, row_count),
            center_scale.reshape(1, count),
        )
    ]
    features, slots, prices, scale, picked = call(
        pick_body,
        (
            shaped(features.shape, bf16),
            shaped((1, row_count), jnp.int32),
            shaped((1, row_count)),
            shaped((1, count)),
            shaped((depth, count), bf16),
        ),
        *inputs,
        source=HBM,
        scratch_shapes=[
            pltpu.VMEM((1, count), jnp.int32),
            pltpu.VMEM((row_count // 2, count), bf16),
            pltpu.SemaphoreType.DMA((5,)),
        ],
    )
    centers = exchange(picked, "dp")
    columns, turned_columns, weight = call(
        columns_body,
        (
            shaped((DEPTH, row_count), bf16),
            shaped((row_count, DEPTH), bf16),
            shaped((24, row_count), bf16),
        ),
        features, slots, prices,
        flops=1000 * row_count,
        bytes_accessed=1024 * row_count,
    )
    block, center, first = call(
        partial(rows_body, len(centers)),
        (shaped((2 * row_count, count), bf16), shaped((DEPTH, count), bf16), vector),
        turned_columns, weight, *centers,
        **pass_cost,
    )
    firsts = exchange(first, "dp")
    turned = call(
        turned_body, shaped((2 * count, row_count), bf16), columns, center, **pass_cost
    )
    target, rows = call(
        partial(first_apply_body, len(firsts), 1.0 / math.sqrt(all_rows)),
        (vector, row_shape),
        *firsts, scale, slots, turned,
    )
    rows = exchange(rows, "centers")
    rows, folded = call(
        partial(first_fold_body, len(rows)), (row_shape, fold_shape), *rows, slots, block
    )
    folds = exchange(folded, "dp")
    residual, step, latest = call(
        partial(second_apply_body, len(folds), 1.0 / all_rows),
        (vector, narrow, row_shape),
        *folds, scale, slots, turned, target, rows,
    )
    latest = exchange(latest, "centers")
    sums, folded = call(
        partial(second_fold_body, len(latest)),
        (narrow, fold_shape),
        *latest, slots, block, rows,
    )
    folds = exchange(folded, "dp")
    return call(
        partial(finish_body, len(folds), 1.0 / all_rows),
        (vector, vector),
        *folds, scale, target, residual, step, rows, sums,
    )


def solution(mesh):
    return jax.shard_map(
        per_device,
        mesh=mesh,
        in_specs=(P(None, "dp"), P("dp"), P("dp"), P("centers"), P("centers")),
        out_specs=(P(None, "centers"), P(None, "centers")),
        check_vma=False,
    )
```

```python
import math
from functools import partial

import jax
import jax.numpy as jnp
from jax import lax
from jax.experimental import pallas as pl
from jax.experimental.pallas import tpu as pltpu
from jax.sharding import PartitionSpec as P

SLOTS = 8
RIDGE = 0.5
CHUNK = 512
EXTRA = 128
DEPTH = 256
STEP = 256
FACTOR = math.log2(math.e) / 64.0
f32 = jnp.float32
bf16 = jnp.bfloat16
VMEM = pl.BlockSpec(memory_space=pltpu.VMEM)
HBM = pl.BlockSpec(memory_space=pltpu.HBM)


def split3(value):
    high = value.astype(bf16).astype(f32)
    rest = value - high
    mid = rest.astype(bf16).astype(f32)
    return high, mid, rest - mid


def stack2(value):
    high = value.astype(bf16).astype(f32)
    return jnp.concatenate([high, value - high], axis=0).astype(bf16)


def unstack2(value):
    return value[0:8] + value[8:16]


def pair_total(parts):
    while len(parts) > 1:
        parts = [parts[i] + parts[i + 1] for i in range(0, len(parts), 2)]
    return parts[0]


def total_of(refs):
    return pair_total([ref[...] for ref in refs])


def row_sum(value):
    return jnp.sum(value, axis=1, keepdims=True)


def slot_mask(slots):
    row = lax.broadcasted_iota(jnp.int32, (SLOTS, slots.shape[1]), 0)
    return slots == row


def norm_rows(feat32, base):
    half = (-0.5 * FACTOR) * jnp.sum(feat32 * feat32, axis=0, keepdims=True)
    row = lax.broadcasted_iota(jnp.int32, (feat32.shape[0], feat32.shape[1]), 0)
    extra = jnp.where(row < 6, 1.0, 0.0)
    for place, part in enumerate(split3(half)):
        extra = jnp.where(row == base + place, part, extra)
    return extra


def kernel_parts(left, right):
    value = jnp.exp2(jnp.dot(left, right, preferred_element_type=f32))
    high = value.astype(bf16)
    return high, (value - high.astype(f32)).astype(bf16)


def pick_body(feat_hbm, idx_hbm, slots_hbm, prices_hbm, scale_hbm, *refs):
    feat_ref, slots_ref, prices_ref, scale_ref, out_ref, idx_ref, hit_ref, sems = refs
    row_count = feat_ref.shape[1]
    count = out_ref.shape[1]
    sources = (idx_hbm, feat_hbm, slots_hbm, prices_hbm, scale_hbm)
    targets = (idx_ref, feat_ref, slots_ref, prices_ref, scale_ref)
    copies = [
        pltpu.make_async_copy(source, target, sems.at[place])
        for place, (source, target) in enumerate(zip(sources, targets))
    ]
    for copy in copies:
        copy.start()
    copies[0].wait()
    local_idx = idx_ref[...] - lax.axis_index("dp") * row_count
    row = lax.broadcasted_iota(jnp.int32, (STEP, count), 0).astype(f32).astype(bf16)
    block = lax.div(local_idx, STEP)
    place = (local_idx - block * STEP).astype(f32)

    def hits(begin):
        own = jnp.where(block == begin // STEP, place, -1.0).astype(bf16)
        return jnp.where(row == own, jnp.ones_like(row), jnp.zeros_like(row))

    half = row_count // 2
    for begin in range(0, half, STEP):
        hit_ref[begin : begin + STEP, :] = hits(begin)
    copies[1].wait()
    total = jnp.dot(feat_ref[:, :half], hit_ref[...], preferred_element_type=f32)
    for begin in range(half, row_count, STEP):
        total += jnp.dot(
            feat_ref[:, begin : begin + STEP], hits(begin), preferred_element_type=f32
        )
    out_ref[...] = total.astype(bf16)
    for copy in copies[2:]:
        copy.wait()


def columns_body(feat_ref, slots_ref, prices_ref, columns_ref, turned_ref, weight_ref):
    for begin in range(0, feat_ref.shape[1], CHUNK):
        here = slice(begin, begin + CHUNK)
        feat32 = feat_ref[:, here].astype(f32)
        pair = jnp.concatenate([feat32, feat32], axis=0)
        last = jnp.concatenate([feat32, norm_rows(feat32, 3)], axis=0)
        columns_ref[0:128, here] = pair.astype(bf16)
        columns_ref[128:256, here] = last.astype(bf16)
        turned_ref[here, 0:128] = pair.T.astype(bf16)
        turned_ref[here, 128:256] = last.T.astype(bf16)
        weight = jnp.where(slot_mask(slots_ref[:, here]), prices_ref[:, here], 0.0)
        weight_ref[:, here] = stack2(weight)


def rows_body(parts, turned_ref, weight_ref, *refs):
    center_refs, (block_ref, center_ref, out_ref) = refs[:parts], refs[parts:]
    center = total_of(center_refs).astype(f32)
    center = jnp.concatenate(
        [*split3(center * FACTOR), norm_rows(center, 0)], axis=0
    ).astype(bf16)
    center_ref[...] = center
    total = jnp.zeros((16, center.shape[1]), f32)

    def build(begin):
        high, low = kernel_parts(turned_ref[pl.ds(begin, STEP), :], center)
        block_ref[pl.ds(2 * begin, STEP), :] = high
        block_ref[pl.ds(2 * begin + STEP, STEP), :] = low

    def fold(begin):
        weight = weight_ref[:, pl.ds(begin, STEP)]
        weight = jnp.concatenate([weight, weight], axis=1)
        block = block_ref[pl.ds(2 * begin, 2 * STEP), :]
        return jnp.dot(weight, block, preferred_element_type=f32)

    def visit(turn, total):
        begin = pl.multiple_of(turn * STEP, STEP)
        build(begin)
        return total + fold(pl.multiple_of(begin - STEP, STEP))

    row_count = turned_ref.shape[0]
    build(0)
    total = lax.fori_loop(1, row_count // STEP, visit, total)
    out_ref[...] = unstack2(total + fold(row_count - STEP))


def turned_body(columns_ref, center_ref, block_ref):
    center = center_ref[...].astype(f32).T.astype(bf16)
    count = center.shape[0]
    for begin in range(0, columns_ref.shape[1], CHUNK):
        here = slice(begin, begin + CHUNK)
        high, low = kernel_parts(center, columns_ref[:, here])
        block_ref[0:count, here] = high
        block_ref[count:, here] = low


def apply_rows(scaled, turned_ref, slots_ref, out_ref):
    stacked = stack2(scaled)
    stacked = jnp.concatenate([stacked, stacked], axis=1)
    value = jnp.dot(stacked, turned_ref[...], preferred_element_type=f32)
    own = jnp.where(slot_mask(slots_ref[...]), unstack2(value), 0.0)
    own = jnp.sum(own, axis=0, keepdims=True)
    for turn, begin in enumerate(range(0, turned_ref.shape[1], CHUNK)):
        out_ref[turn : turn + 1, 0:CHUNK] = own[:, begin : begin + CHUNK]


def fold_rows(row_weights, block_ref, slots_ref, out_ref):
    count = block_ref.shape[1]
    square = jnp.zeros((SLOTS, 1), f32)
    weights = []
    for turn, begin in enumerate(range(0, slots_ref.shape[1], CHUNK)):
        mask = slot_mask(slots_ref[:, begin : begin + CHUNK])
        weight = jnp.where(mask, row_weights(turn), 0.0)
        square += row_sum(weight * weight)
        weight = stack2(weight)
        for inner in range(0, CHUNK, STEP):
            weights += [weight[:, inner : inner + STEP]] * 2
    total = jnp.dot(
        jnp.concatenate(weights, axis=1), block_ref[...], preferred_element_type=f32
    )
    out_ref[:, 0:count] = unstack2(total)
    out_ref[:, count : count + EXTRA] = jnp.broadcast_to(square, (SLOTS, EXTRA))


def first_apply_body(parts, scale_over_root, *refs):
    first_refs = refs[:parts]
    scale_ref, slots_ref, turned_ref, target_ref, out_ref = refs[parts:]
    scale = scale_ref[...]
    target = scale * total_of(first_refs) * scale_over_root
    target_ref[...] = target
    out_ref[:, CHUNK:] = jnp.broadcast_to(row_sum(target * target), (SLOTS, EXTRA))
    apply_rows(scale * target, turned_ref, slots_ref, out_ref)


def first_fold_body(parts, *refs):
    row_refs = refs[:parts]
    slots_ref, block_ref, rows_ref, out_ref = refs[parts:]
    rows = total_of(row_refs)
    rows_ref[...] = rows
    fold_rows(lambda turn: rows[turn : turn + 1, 0:CHUNK], block_ref, slots_ref, out_ref)


def second_apply_body(parts, inv_rows, *refs):
    fold_refs = refs[:parts]
    (scale_ref, slots_ref, turned_ref, target_ref, rows_ref,
     residual_ref, step_ref, out_ref) = refs[parts:]
    count = scale_ref.shape[1]
    folded = total_of(fold_refs)
    scale = scale_ref[...]
    target = target_ref[...]
    norm = rows_ref[:, CHUNK : CHUNK + 1]
    applied = scale * folded[:, 0:count] * inv_rows + RIDGE * target
    step = norm / (folded[:, count : count + 1] * inv_rows + RIDGE * norm)
    residual = target - step * applied
    residual_ref[...] = residual
    step_ref[...] = jnp.broadcast_to(step, step_ref.shape)
    lane = lax.broadcasted_iota(jnp.int32, (SLOTS, EXTRA), 1)
    out_ref[:, CHUNK:] = jnp.where(
        lane == 0, row_sum(residual * residual), row_sum(residual * target)
    )
    apply_rows(scale * residual, turned_ref, slots_ref, out_ref)


def second_fold_body(parts, *refs):
    row_refs = refs[:parts]
    slots_ref, block_ref, rows_ref, sums_ref, out_ref = refs[parts:]
    latest = total_of(row_refs)
    sums_ref[...] = latest[:, CHUNK:]
    rows = rows_ref[...]
    ratio = latest[:, CHUNK : CHUNK + 1] / rows[:, CHUNK : CHUNK + 1]

    def row_weights(turn):
        return latest[turn : turn + 1, 0:CHUNK] + ratio * rows[turn : turn + 1, 0:CHUNK]

    fold_rows(row_weights, block_ref, slots_ref, out_ref)


def finish_body(parts, inv_rows, *refs):
    fold_refs = refs[:parts]
    (scale_ref, target_ref, residual_ref, step_ref, rows_ref, sums_ref,
     coefficients_ref, out_ref) = refs[parts:]
    count = scale_ref.shape[1]
    folded = total_of(fold_refs)
    target = target_ref[...]
    residual = residual_ref[...]
    first_norm = rows_ref[:, CHUNK : CHUNK + 1]
    norm = sums_ref[:, 0:1]
    cross = sums_ref[:, 1:2]
    ratio = norm / first_norm
    direction = residual + ratio * target
    square = norm + 2.0 * ratio * cross + ratio * ratio * first_norm
    applied = scale_ref[...] * folded[:, 0:count] * inv_rows + RIDGE * direction
    step = norm / (folded[:, count : count + 1] * inv_rows + RIDGE * square)
    coefficients_ref[...] = step_ref[:, 0:1] * target + step * direction
    out_ref[...] = residual - step * applied


def call(body, out_shape, *args, source=VMEM, flops=0, bytes_accessed=0, **more):
    return pl.pallas_call(
        body,
        out_shape=out_shape,
        in_specs=[source] * len(args),
        out_specs=jax.tree.map(lambda _: VMEM, out_shape),
        compiler_params=pltpu.CompilerParams(vmem_limit_bytes=36 * 1024 * 1024),
        cost_estimate=pl.CostEstimate(
            flops=flops, bytes_accessed=bytes_accessed, transcendentals=0
        ),
        **more,
    )(*args)


def exchange(value, axis, near_first=False):
    size = lax.axis_size(axis)
    parts = [value]
    stride = 1
    while stride < size:
        value = pair_total(parts)
        parts = [value]
        span = min(4, size // stride)
        side = 0 if stride == 1 else 1
        got = []
        for offset in reversed(range(1, span)):
            pairs = [(i, i ^ (offset * stride) ^ side) for i in range(size)]
            got.append(lax.ppermute(value, axis, pairs))
        parts = got + parts
        if near_first and stride == 1:
            parts = parts[-2:] + parts[:-2]
        stride *= span
    return parts


def shaped(shape, dtype=f32):
    return jax.ShapeDtypeStruct(shape, dtype)


def per_device(features, prices, slots, center_idx, center_scale):
    depth, row_count = features.shape
    count = center_idx.shape[0]
    all_rows = row_count * lax.axis_size("dp")
    turns = row_count // CHUNK
    row_shape = shaped((turns, CHUNK + EXTRA))
    fold_shape = shaped((SLOTS, count + EXTRA))
    vector = shaped((SLOTS, count))
    narrow = shaped((SLOTS, EXTRA))
    pass_cost = dict(flops=64 * row_count * count, bytes_accessed=4 * row_count * count)

    inputs = [
        pltpu.with_memory_space_constraint(array, pltpu.HBM)
        for array in (
            features,
            center_idx.reshape(1, count),
            slots.reshape(1, row_count),
            prices.reshape(1, row_count),
            center_scale.reshape(1, count),
        )
    ]
    features, slots, prices, scale, picked = call(
        pick_body,
        (
            shaped(features.shape, bf16),
            shaped((1, row_count), jnp.int32),
            shaped((1, row_count)),
            shaped((1, count)),
            shaped((depth, count), bf16),
        ),
        *inputs,
        source=HBM,
        scratch_shapes=[
            pltpu.VMEM((1, count), jnp.int32),
            pltpu.VMEM((row_count // 2, count), bf16),
            pltpu.SemaphoreType.DMA((5,)),
        ],
    )
    centers = exchange(picked, "dp")
    columns, turned_columns, weight = call(
        columns_body,
        (
            shaped((DEPTH, row_count), bf16),
            shaped((row_count, DEPTH), bf16),
            shaped((16, row_count), bf16),
        ),
        features, slots, prices,
        flops=1000 * row_count,
        bytes_accessed=1024 * row_count,
    )
    block, center, first = call(
        partial(rows_body, len(centers)),
        (shaped((2 * row_count, count), bf16), shaped((DEPTH, count), bf16), vector),
        turned_columns, weight, *centers,
        **pass_cost,
    )
    firsts = exchange(first, "dp")
    turned = call(
        turned_body, shaped((2 * count, row_count), bf16), columns, center, **pass_cost
    )
    target, rows = call(
        partial(first_apply_body, len(firsts), 1.0 / math.sqrt(all_rows)),
        (vector, row_shape),
        *firsts, scale, slots, turned,
    )
    rows = exchange(rows, "centers")
    rows, folded = call(
        partial(first_fold_body, len(rows)), (row_shape, fold_shape), *rows, slots, block
    )
    folds = exchange(folded, "dp")
    residual, step, latest = call(
        partial(second_apply_body, len(folds), 1.0 / all_rows),
        (vector, narrow, row_shape),
        *folds, scale, slots, turned, target, rows,
    )
    latest = exchange(latest, "centers", True)
    sums, folded = call(
        partial(second_fold_body, len(latest)),
        (narrow, fold_shape),
        *latest, slots, block, rows,
    )
    folds = exchange(folded, "dp")
    return call(
        partial(finish_body, len(folds), 1.0 / all_rows),
        (vector, vector),
        *folds, scale, target, residual, step, rows, sums,
    )


def solution(mesh):
    return jax.shard_map(
        per_device,
        mesh=mesh,
        in_specs=(P(None, "dp"), P("dp"), P("dp"), P("centers"), P("centers")),
        out_specs=(P(None, "centers"), P(None, "centers")),
        check_vma=False,
    )
```

```python
import math
from functools import partial

import jax
import jax.numpy as jnp
from jax import lax
from jax.experimental import pallas as pl
from jax.experimental.pallas import tpu as pltpu
from jax.sharding import PartitionSpec as P

SLOTS = 8
RIDGE = 0.5
CHUNK = 512
EXTRA = 128
DEPTH = 256
STEP = 256
FACTOR = math.log2(math.e) / 64.0
f32 = jnp.float32
bf16 = jnp.bfloat16
VMEM = pl.BlockSpec(memory_space=pltpu.VMEM)
HBM = pl.BlockSpec(memory_space=pltpu.HBM)


def split3(value):
    high = value.astype(bf16).astype(f32)
    rest = value - high
    mid = rest.astype(bf16).astype(f32)
    return high, mid, rest - mid


def stack2(value):
    high = value.astype(bf16).astype(f32)
    return jnp.concatenate([high, value - high], axis=0).astype(bf16)


def unstack2(value):
    return value[0:8] + value[8:16]


def pair_total(parts):
    while len(parts) > 1:
        parts = [parts[i] + parts[i + 1] for i in range(0, len(parts), 2)]
    return parts[0]


def total_of(refs):
    return pair_total([ref[...] for ref in refs])


def row_sum(value):
    return jnp.sum(value, axis=1, keepdims=True)


def slot_mask(slots):
    row = lax.broadcasted_iota(jnp.int32, (SLOTS, slots.shape[1]), 0)
    return slots == row


def norm_rows(feat32, base):
    half = (-0.5 * FACTOR) * jnp.sum(feat32 * feat32, axis=0, keepdims=True)
    row = lax.broadcasted_iota(jnp.int32, (feat32.shape[0], feat32.shape[1]), 0)
    extra = jnp.where(row < 6, 1.0, 0.0)
    for place, part in enumerate(split3(half)):
        extra = jnp.where(row == base + place, part, extra)
    return extra


def kernel_parts(left, right):
    value = jnp.exp2(jnp.dot(left, right, preferred_element_type=f32))
    high = value.astype(bf16)
    return high, (value - high.astype(f32)).astype(bf16)


def pick_body(feat_hbm, idx_hbm, slots_hbm, prices_hbm, scale_hbm, *refs):
    feat_ref, slots_ref, prices_ref, scale_ref, out_ref, idx_ref, hit_ref, sems = refs
    row_count = feat_ref.shape[1]
    count = out_ref.shape[1]
    sources = (idx_hbm, feat_hbm, slots_hbm, prices_hbm, scale_hbm)
    targets = (idx_ref, feat_ref, slots_ref, prices_ref, scale_ref)
    copies = [
        pltpu.make_async_copy(source, target, sems.at[place])
        for place, (source, target) in enumerate(zip(sources, targets))
    ]
    for copy in copies:
        copy.start()
    copies[0].wait()
    local_idx = idx_ref[...] - lax.axis_index("dp") * row_count
    row = lax.broadcasted_iota(jnp.int32, (STEP, count), 0).astype(f32).astype(bf16)
    block = lax.div(local_idx, STEP)
    place = (local_idx - block * STEP).astype(f32)

    def hits(begin):
        own = jnp.where(block == begin // STEP, place, -1.0).astype(bf16)
        return jnp.where(row == own, jnp.ones_like(row), jnp.zeros_like(row))

    half = row_count // 2
    for begin in range(0, half, STEP):
        hit_ref[begin : begin + STEP, :] = hits(begin)
    copies[1].wait()
    total = jnp.dot(feat_ref[:, :half], hit_ref[...], preferred_element_type=f32)
    for begin in range(half, row_count, STEP):
        total += jnp.dot(
            feat_ref[:, begin : begin + STEP], hits(begin), preferred_element_type=f32
        )
    out_ref[...] = total.astype(bf16)
    for copy in copies[2:]:
        copy.wait()


def columns_body(feat_ref, slots_ref, prices_ref, columns_ref, turned_ref, weight_ref):
    for begin in range(0, feat_ref.shape[1], CHUNK):
        here = slice(begin, begin + CHUNK)
        feat32 = feat_ref[:, here].astype(f32)
        pair = jnp.concatenate([feat32, feat32], axis=0)
        last = jnp.concatenate([feat32, norm_rows(feat32, 3)], axis=0)
        columns_ref[0:128, here] = pair.astype(bf16)
        columns_ref[128:256, here] = last.astype(bf16)
        turned_ref[here, 0:128] = pair.T.astype(bf16)
        turned_ref[here, 128:256] = last.T.astype(bf16)
        weight = jnp.where(slot_mask(slots_ref[:, here]), prices_ref[:, here], 0.0)
        weight_ref[:, here] = stack2(weight)


def rows_body(parts, turned_ref, weight_ref, *refs):
    center_refs, (block_ref, center_ref, out_ref) = refs[:parts], refs[parts:]
    center = total_of(center_refs).astype(f32)
    center = jnp.concatenate(
        [*split3(center * FACTOR), norm_rows(center, 0)], axis=0
    ).astype(bf16)
    center_ref[...] = center
    total = jnp.zeros((16, center.shape[1]), f32)

    def fold(begin):
        weight = weight_ref[:, begin : begin + CHUNK]
        weight = jnp.concatenate([weight, weight], axis=1)
        block = block_ref[2 * begin : 2 * begin + 2 * CHUNK, :]
        return jnp.dot(weight, block, preferred_element_type=f32)

    row_count = turned_ref.shape[0]
    for begin in range(0, row_count, CHUNK):
        high, low = kernel_parts(turned_ref[begin : begin + CHUNK, :], center)
        block_ref[2 * begin : 2 * begin + CHUNK, :] = high
        block_ref[2 * begin + CHUNK : 2 * begin + 2 * CHUNK, :] = low
        if begin > 0:
            total += fold(begin - CHUNK)
    out_ref[...] = unstack2(total + fold(row_count - CHUNK))


def turned_body(columns_ref, center_ref, block_ref):
    center = center_ref[...].astype(f32).T.astype(bf16)
    count = center.shape[0]
    for begin in range(0, columns_ref.shape[1], CHUNK):
        here = slice(begin, begin + CHUNK)
        high, low = kernel_parts(center, columns_ref[:, here])
        block_ref[0:count, here] = high
        block_ref[count:, here] = low


def apply_rows(scaled, turned_ref, slots_ref, out_ref):
    stacked = stack2(scaled)
    stacked = jnp.concatenate([stacked, stacked], axis=1)
    value = jnp.dot(stacked, turned_ref[...], preferred_element_type=f32)
    own = jnp.where(slot_mask(slots_ref[...]), unstack2(value), 0.0)
    own = jnp.sum(own, axis=0, keepdims=True)
    for turn, begin in enumerate(range(0, turned_ref.shape[1], CHUNK)):
        out_ref[turn : turn + 1, 0:CHUNK] = own[:, begin : begin + CHUNK]


def fold_rows(row_weights, block_ref, slots_ref, out_ref):
    count = block_ref.shape[1]
    square = jnp.zeros((SLOTS, 1), f32)
    weights = []
    for turn, begin in enumerate(range(0, slots_ref.shape[1], CHUNK)):
        mask = slot_mask(slots_ref[:, begin : begin + CHUNK])
        weight = jnp.where(mask, row_weights(turn), 0.0)
        square += row_sum(weight * weight)
        weight = stack2(weight)
        weights += [weight, weight]
    total = jnp.dot(
        jnp.concatenate(weights, axis=1), block_ref[...], preferred_element_type=f32
    )
    out_ref[:, 0:count] = unstack2(total)
    out_ref[:, count : count + EXTRA] = jnp.broadcast_to(square, (SLOTS, EXTRA))


def first_apply_body(parts, scale_over_root, *refs):
    first_refs = refs[:parts]
    scale_ref, slots_ref, turned_ref, target_ref, out_ref = refs[parts:]
    scale = scale_ref[...]
    target = scale * total_of(first_refs) * scale_over_root
    target_ref[...] = target
    out_ref[:, CHUNK:] = jnp.broadcast_to(row_sum(target * target), (SLOTS, EXTRA))
    apply_rows(scale * target, turned_ref, slots_ref, out_ref)


def first_fold_body(parts, *refs):
    row_refs = refs[:parts]
    slots_ref, block_ref, rows_ref, out_ref = refs[parts:]
    rows = total_of(row_refs)
    rows_ref[...] = rows
    fold_rows(lambda turn: rows[turn : turn + 1, 0:CHUNK], block_ref, slots_ref, out_ref)


def second_apply_body(parts, inv_rows, *refs):
    fold_refs = refs[:parts]
    (scale_ref, slots_ref, turned_ref, target_ref, rows_ref,
     residual_ref, step_ref, out_ref) = refs[parts:]
    count = scale_ref.shape[1]
    folded = total_of(fold_refs)
    scale = scale_ref[...]
    target = target_ref[...]
    norm = rows_ref[:, CHUNK : CHUNK + 1]
    applied = scale * folded[:, 0:count] * inv_rows + RIDGE * target
    step = norm / (folded[:, count : count + 1] * inv_rows + RIDGE * norm)
    residual = target - step * applied
    residual_ref[...] = residual
    step_ref[...] = jnp.broadcast_to(step, step_ref.shape)
    lane = lax.broadcasted_iota(jnp.int32, (SLOTS, EXTRA), 1)
    out_ref[:, CHUNK:] = jnp.where(
        lane == 0, row_sum(residual * residual), row_sum(residual * target)
    )
    apply_rows(scale * residual, turned_ref, slots_ref, out_ref)


def second_fold_body(parts, *refs):
    row_refs = refs[:parts]
    slots_ref, block_ref, rows_ref, sums_ref, out_ref = refs[parts:]
    latest = total_of(row_refs)
    sums_ref[...] = latest[:, CHUNK:]
    rows = rows_ref[...]
    ratio = latest[:, CHUNK : CHUNK + 1] / rows[:, CHUNK : CHUNK + 1]

    def row_weights(turn):
        return latest[turn : turn + 1, 0:CHUNK] + ratio * rows[turn : turn + 1, 0:CHUNK]

    fold_rows(row_weights, block_ref, slots_ref, out_ref)


def finish_body(parts, inv_rows, *refs):
    fold_refs = refs[:parts]
    (scale_ref, target_ref, residual_ref, step_ref, rows_ref, sums_ref,
     coefficients_ref, out_ref) = refs[parts:]
    count = scale_ref.shape[1]
    folded = total_of(fold_refs)
    target = target_ref[...]
    residual = residual_ref[...]
    first_norm = rows_ref[:, CHUNK : CHUNK + 1]
    norm = sums_ref[:, 0:1]
    cross = sums_ref[:, 1:2]
    ratio = norm / first_norm
    direction = residual + ratio * target
    square = norm + 2.0 * ratio * cross + ratio * ratio * first_norm
    applied = scale_ref[...] * folded[:, 0:count] * inv_rows + RIDGE * direction
    step = norm / (folded[:, count : count + 1] * inv_rows + RIDGE * square)
    coefficients_ref[...] = step_ref[:, 0:1] * target + step * direction
    out_ref[...] = residual - step * applied


def call(body, out_shape, *args, source=VMEM, flops=0, bytes_accessed=0, **more):
    return pl.pallas_call(
        body,
        out_shape=out_shape,
        in_specs=[source] * len(args),
        out_specs=jax.tree.map(lambda _: VMEM, out_shape),
        compiler_params=pltpu.CompilerParams(vmem_limit_bytes=36 * 1024 * 1024),
        cost_estimate=pl.CostEstimate(
            flops=flops, bytes_accessed=bytes_accessed, transcendentals=0
        ),
        **more,
    )(*args)


def exchange(value, axis, near_first=False):
    size = lax.axis_size(axis)
    parts = [value]
    stride = 1
    while stride < size:
        value = pair_total(parts)
        parts = [value]
        span = min(4, size // stride)
        side = 0 if stride == 1 else 1
        got = []
        for offset in reversed(range(1, span)):
            pairs = [(i, i ^ (offset * stride) ^ side) for i in range(size)]
            got.append(lax.ppermute(value, axis, pairs))
        parts = got + parts
        if near_first and stride == 1:
            parts = parts[-2:] + parts[:-2]
        stride *= span
    return parts


def shaped(shape, dtype=f32):
    return jax.ShapeDtypeStruct(shape, dtype)


def per_device(features, prices, slots, center_idx, center_scale):
    depth, row_count = features.shape
    count = center_idx.shape[0]
    all_rows = row_count * lax.axis_size("dp")
    turns = row_count // CHUNK
    row_shape = shaped((turns, CHUNK + EXTRA))
    fold_shape = shaped((SLOTS, count + EXTRA))
    vector = shaped((SLOTS, count))
    narrow = shaped((SLOTS, EXTRA))
    pass_cost = dict(flops=64 * row_count * count, bytes_accessed=4 * row_count * count)

    inputs = [
        pltpu.with_memory_space_constraint(array, pltpu.HBM)
        for array in (
            features,
            center_idx.reshape(1, count),
            slots.reshape(1, row_count),
            prices.reshape(1, row_count),
            center_scale.reshape(1, count),
        )
    ]
    features, slots, prices, scale, picked = call(
        pick_body,
        (
            shaped(features.shape, bf16),
            shaped((1, row_count), jnp.int32),
            shaped((1, row_count)),
            shaped((1, count)),
            shaped((depth, count), bf16),
        ),
        *inputs,
        source=HBM,
        scratch_shapes=[
            pltpu.VMEM((1, count), jnp.int32),
            pltpu.VMEM((row_count // 2, count), bf16),
            pltpu.SemaphoreType.DMA((5,)),
        ],
    )
    centers = exchange(picked, "dp")
    columns, turned_columns, weight = call(
        columns_body,
        (
            shaped((DEPTH, row_count), bf16),
            shaped((row_count, DEPTH), bf16),
            shaped((16, row_count), bf16),
        ),
        features, slots, prices,
        flops=1000 * row_count,
        bytes_accessed=1024 * row_count,
    )
    block, center, first = call(
        partial(rows_body, len(centers)),
        (shaped((2 * row_count, count), bf16), shaped((DEPTH, count), bf16), vector),
        turned_columns, weight, *centers,
        **pass_cost,
    )
    firsts = exchange(first, "dp")
    turned = call(
        turned_body, shaped((2 * count, row_count), bf16), columns, center, **pass_cost
    )
    target, rows = call(
        partial(first_apply_body, len(firsts), 1.0 / math.sqrt(all_rows)),
        (vector, row_shape),
        *firsts, scale, slots, turned,
    )
    rows = exchange(rows, "centers")
    rows, folded = call(
        partial(first_fold_body, len(rows)), (row_shape, fold_shape), *rows, slots, block
    )
    folds = exchange(folded, "dp")
    residual, step, latest = call(
        partial(second_apply_body, len(folds), 1.0 / all_rows),
        (vector, narrow, row_shape),
        *folds, scale, slots, turned, target, rows,
    )
    latest = exchange(latest, "centers", True)
    sums, folded = call(
        partial(second_fold_body, len(latest)),
        (narrow, fold_shape),
        *latest, slots, block, rows,
    )
    folds = exchange(folded, "dp")
    return call(
        partial(finish_body, len(folds), 1.0 / all_rows),
        (vector, vector),
        *folds, scale, target, residual, step, rows, sums,
    )


def solution(mesh):
    return jax.shard_map(
        per_device,
        mesh=mesh,
        in_specs=(P(None, "dp"), P("dp"), P("dp"), P("centers"), P("centers")),
        out_specs=(P(None, "centers"), P(None, "centers")),
        check_vma=False,
    )
```

```python
import math
from functools import partial

import jax
import jax.numpy as jnp
from jax import lax
from jax.experimental import pallas as pl
from jax.experimental.pallas import tpu as pltpu
from jax.sharding import PartitionSpec as P

SLOTS = 8
RIDGE = 0.5
CHUNK = 512
EXTRA = 128
DEPTH = 256
STEP = 256
FACTOR = math.log2(math.e) / 64.0
f32 = jnp.float32
bf16 = jnp.bfloat16
VMEM = pl.BlockSpec(memory_space=pltpu.VMEM)
HBM = pl.BlockSpec(memory_space=pltpu.HBM)


def split3(value):
    high = value.astype(bf16).astype(f32)
    rest = value - high
    mid = rest.astype(bf16).astype(f32)
    return high, mid, rest - mid


def stack2(value):
    high = value.astype(bf16).astype(f32)
    return jnp.concatenate([high, value - high], axis=0).astype(bf16)


def product(stacked, high_block, low_block):
    main = jnp.dot(stacked, high_block, preferred_element_type=f32)
    rest = jnp.dot(stacked[0:SLOTS], low_block, preferred_element_type=f32)
    return main[0:SLOTS] + (main[SLOTS:] + rest)


def slot_lanes(first):
    lane = lax.broadcasted_iota(jnp.int32, (SLOTS, EXTRA), 1)
    return lane == lax.broadcasted_iota(jnp.int32, (SLOTS, EXTRA), 0) + first


def to_lanes(column, first):
    return jnp.sum(jnp.where(slot_lanes(first), column, 0.0), axis=0, keepdims=True)


def from_lanes(row, first):
    return jnp.sum(jnp.where(slot_lanes(first), row, 0.0), axis=1, keepdims=True)


def pair_total(parts):
    while len(parts) > 1:
        parts = [parts[i] + parts[i + 1] for i in range(0, len(parts), 2)]
    return parts[0]


def total_of(refs):
    return pair_total([ref[...] for ref in refs])


def row_sum(value):
    return jnp.sum(value, axis=1, keepdims=True)


def slot_mask(slots):
    row = lax.broadcasted_iota(jnp.int32, (SLOTS, slots.shape[1]), 0)
    return slots == row


def norm_rows(feat32, base):
    half = (-0.5 * FACTOR) * jnp.sum(feat32 * feat32, axis=0, keepdims=True)
    row = lax.broadcasted_iota(jnp.int32, (feat32.shape[0], feat32.shape[1]), 0)
    extra = jnp.where(row < 6, 1.0, 0.0)
    for place, part in enumerate(split3(half)):
        extra = jnp.where(row == base + place, part, extra)
    return extra


def kernel_parts(left, right):
    value = jnp.exp2(jnp.dot(left, right, preferred_element_type=f32))
    high = value.astype(bf16)
    return high, (value - high.astype(f32)).astype(bf16)


def pick_body(feat_hbm, idx_hbm, slots_hbm, prices_hbm, scale_hbm, *refs):
    feat_ref, slots_ref, prices_ref, scale_ref, out_ref, idx_ref, hit_ref, sems = refs
    row_count = feat_ref.shape[1]
    count = out_ref.shape[1]
    half = row_count // 2
    left, right = pl.ds(0, half), pl.ds(half, half)
    sources = (
        idx_hbm, feat_hbm.at[:, left], feat_hbm.at[:, right], slots_hbm, prices_hbm, scale_hbm
    )
    targets = (
        idx_ref, feat_ref.at[:, left], feat_ref.at[:, right], slots_ref, prices_ref, scale_ref
    )
    copies = [
        pltpu.make_async_copy(source, target, sems.at[place])
        for place, (source, target) in enumerate(zip(sources, targets))
    ]
    for copy in copies:
        copy.start()
    copies[0].wait()
    local_idx = idx_ref[...] - lax.axis_index("dp") * row_count
    row = lax.broadcasted_iota(jnp.int32, (STEP, count), 0).astype(f32).astype(bf16)
    block = lax.div(local_idx, STEP)
    place = (local_idx - block * STEP).astype(f32)

    def hits(begin):
        own = jnp.where(block == begin // STEP, place, -1.0).astype(bf16)
        return jnp.where(row == own, jnp.ones_like(row), jnp.zeros_like(row))

    for begin in range(0, half, STEP):
        hit_ref[begin : begin + STEP, :] = hits(begin)
    copies[1].wait()
    total = jnp.dot(feat_ref[:, :half], hit_ref[...], preferred_element_type=f32)
    copies[2].wait()
    for begin in range(half, row_count, STEP):
        total += jnp.dot(
            feat_ref[:, begin : begin + STEP], hits(begin), preferred_element_type=f32
        )
    out_ref[...] = total.astype(bf16)
    for copy in copies[3:]:
        copy.wait()


def columns_body(feat_ref, slots_ref, prices_ref, columns_ref, turned_ref, weight_ref):
    for begin in range(0, feat_ref.shape[1], CHUNK):
        here = slice(begin, begin + CHUNK)
        feat32 = feat_ref[:, here].astype(f32)
        pair = jnp.concatenate([feat32, feat32], axis=0)
        last = jnp.concatenate([feat32, norm_rows(feat32, 3)], axis=0)
        columns_ref[0:128, here] = pair.astype(bf16)
        columns_ref[128:256, here] = last.astype(bf16)
        turned_ref[here, 0:128] = pair.T.astype(bf16)
        turned_ref[here, 128:256] = last.T.astype(bf16)
        weight = jnp.where(slot_mask(slots_ref[:, here]), prices_ref[:, here], 0.0)
        weight_ref[:, here] = stack2(weight)


def rows_body(parts, turned_ref, weight_ref, *refs):
    center_refs, (block_ref, center_ref, out_ref) = refs[:parts], refs[parts:]
    center = total_of(center_refs).astype(f32)
    center = jnp.concatenate(
        [*split3(center * FACTOR), norm_rows(center, 0)], axis=0
    ).astype(bf16)
    center_ref[...] = center
    row_count = turned_ref.shape[0]
    total = jnp.zeros(out_ref.shape, f32)

    def fold(begin):
        end = begin + CHUNK
        return product(
            weight_ref[:, begin:end],
            block_ref[begin:end, :],
            block_ref[row_count + begin : row_count + end, :],
        )

    for begin in range(0, row_count, CHUNK):
        high, low = kernel_parts(turned_ref[begin : begin + CHUNK, :], center)
        block_ref[begin : begin + CHUNK, :] = high
        block_ref[row_count + begin : row_count + begin + CHUNK, :] = low
        if begin > 0:
            total += fold(begin - CHUNK)
    out_ref[...] = total + fold(row_count - CHUNK)


def turned_body(columns_ref, center_ref, block_ref):
    center = center_ref[...].astype(f32).T.astype(bf16)
    count = center.shape[0]
    for begin in range(0, columns_ref.shape[1], CHUNK):
        here = slice(begin, begin + CHUNK)
        high, low = kernel_parts(center, columns_ref[:, here])
        block_ref[0:count, here] = high
        block_ref[count:, here] = low


def apply_rows(scaled, turned_ref, slots_ref, out_ref):
    count, row_count = scaled.shape[1], turned_ref.shape[1]
    value = product(stack2(scaled), turned_ref[0:count, :], turned_ref[count:, :])
    own = jnp.where(slot_mask(slots_ref[...]), value, 0.0)
    out_ref[:, 0:row_count] = jnp.sum(own, axis=0, keepdims=True)


def fold_rows(rows, block_ref, slots_ref, out_ref):
    row_count, count = slots_ref.shape[1], block_ref.shape[1]
    weight = jnp.where(slot_mask(slots_ref[...]), rows, 0.0)
    out_ref[:, 0:count] = product(
        stack2(weight), block_ref[0:row_count, :], block_ref[row_count:, :]
    )
    square = row_sum(weight * weight)
    out_ref[:, count : count + EXTRA] = jnp.broadcast_to(square, (SLOTS, EXTRA))


def first_apply_body(parts, scale_over_root, *refs):
    first_refs = refs[:parts]
    scale_ref, slots_ref, turned_ref, target_ref, out_ref = refs[parts:]
    scale = scale_ref[...]
    target = scale * total_of(first_refs) * scale_over_root
    target_ref[...] = target
    out_ref[:, turned_ref.shape[1] :] = to_lanes(row_sum(target * target), 0)
    apply_rows(scale * target, turned_ref, slots_ref, out_ref)


def first_fold_body(parts, *refs):
    row_refs = refs[:parts]
    slots_ref, block_ref, rows_ref, out_ref = refs[parts:]
    rows = total_of(row_refs)
    rows_ref[...] = rows
    fold_rows(rows[:, 0 : slots_ref.shape[1]], block_ref, slots_ref, out_ref)


def second_apply_body(parts, inv_rows, *refs):
    fold_refs = refs[:parts]
    (scale_ref, slots_ref, turned_ref, target_ref, rows_ref,
     residual_ref, step_ref, out_ref) = refs[parts:]
    row_count, count = turned_ref.shape[1], scale_ref.shape[1]
    folded = total_of(fold_refs)
    scale = scale_ref[...]
    target = target_ref[...]
    norm = from_lanes(rows_ref[:, row_count:], 0)
    applied = scale * folded[:, 0:count] * inv_rows + RIDGE * target
    step = norm / (folded[:, count : count + 1] * inv_rows + RIDGE * norm)
    residual = target - step * applied
    residual_ref[...] = residual
    step_ref[...] = jnp.broadcast_to(step, step_ref.shape)
    out_ref[:, row_count:] = to_lanes(row_sum(residual * residual), 0) + to_lanes(
        row_sum(residual * target), SLOTS
    )
    apply_rows(scale * residual, turned_ref, slots_ref, out_ref)


def second_fold_body(parts, *refs):
    row_refs = refs[:parts]
    slots_ref, block_ref, rows_ref, sums_ref, out_ref = refs[parts:]
    row_count = slots_ref.shape[1]
    latest = total_of(row_refs)
    first_norm = from_lanes(rows_ref[:, row_count:], 0)
    norm = from_lanes(latest[:, row_count:], 0)
    cross = from_lanes(latest[:, row_count:], SLOTS)
    lane = lax.broadcasted_iota(jnp.int32, (SLOTS, EXTRA), 1)
    sums_ref[...] = jnp.where(lane == 0, first_norm, jnp.where(lane == 1, norm, cross))
    rows = latest[:, 0:row_count] + (norm / first_norm) * rows_ref[:, 0:row_count]
    fold_rows(rows, block_ref, slots_ref, out_ref)


def finish_body(parts, inv_rows, *refs):
    fold_refs = refs[:parts]
    (scale_ref, target_ref, residual_ref, step_ref, sums_ref,
     coefficients_ref, out_ref) = refs[parts:]
    count = scale_ref.shape[1]
    folded = total_of(fold_refs)
    target = target_ref[...]
    residual = residual_ref[...]
    first_norm, norm, cross = (sums_ref[:, i : i + 1] for i in range(3))
    ratio = norm / first_norm
    direction = residual + ratio * target
    square = norm + 2.0 * ratio * cross + ratio * ratio * first_norm
    applied = scale_ref[...] * folded[:, 0:count] * inv_rows + RIDGE * direction
    step = norm / (folded[:, count : count + 1] * inv_rows + RIDGE * square)
    coefficients_ref[...] = step_ref[:, 0:1] * target + step * direction
    out_ref[...] = residual - step * applied


def call(body, out_shape, *args, source=VMEM, flops=0, bytes_accessed=0, **more):
    return pl.pallas_call(
        body,
        out_shape=out_shape,
        in_specs=[source] * len(args),
        out_specs=jax.tree.map(lambda _: VMEM, out_shape),
        compiler_params=pltpu.CompilerParams(vmem_limit_bytes=36 * 1024 * 1024),
        cost_estimate=pl.CostEstimate(
            flops=flops, bytes_accessed=bytes_accessed, transcendentals=0
        ),
        **more,
    )(*args)


def exchange(value, axis, near_first=False):
    size = lax.axis_size(axis)
    parts = [value]
    stride = 1
    while stride < size:
        value = pair_total(parts)
        parts = [value]
        span = min(4, size // stride)
        side = 0 if stride == 1 else 1
        got = []
        for offset in reversed(range(1, span)):
            pairs = [(i, i ^ (offset * stride) ^ side) for i in range(size)]
            got.append(lax.ppermute(value, axis, pairs))
        parts = got + parts
        if near_first and stride == 1:
            parts = parts[-2:] + parts[:-2]
        stride *= span
    return parts


def shaped(shape, dtype=f32):
    return jax.ShapeDtypeStruct(shape, dtype)


def per_device(features, prices, slots, center_idx, center_scale):
    depth, row_count = features.shape
    count = center_idx.shape[0]
    all_rows = row_count * lax.axis_size("dp")
    row_shape = shaped((1, row_count + EXTRA))
    fold_shape = shaped((SLOTS, count + EXTRA))
    vector = shaped((SLOTS, count))
    narrow = shaped((SLOTS, EXTRA))
    pass_cost = dict(flops=64 * row_count * count, bytes_accessed=4 * row_count * count)

    inputs = [
        pltpu.with_memory_space_constraint(array, pltpu.HBM)
        for array in (
            features,
            center_idx.reshape(1, count),
            slots.reshape(1, row_count),
            prices.reshape(1, row_count),
            center_scale.reshape(1, count),
        )
    ]
    features, slots, prices, scale, picked = call(
        pick_body,
        (
            shaped(features.shape, bf16),
            shaped((1, row_count), jnp.int32),
            shaped((1, row_count)),
            shaped((1, count)),
            shaped((depth, count), bf16),
        ),
        *inputs,
        source=HBM,
        scratch_shapes=[
            pltpu.VMEM((1, count), jnp.int32),
            pltpu.VMEM((row_count // 2, count), bf16),
            pltpu.SemaphoreType.DMA((6,)),
        ],
    )
    centers = exchange(picked, "dp")
    columns, turned_columns, weight = call(
        columns_body,
        (
            shaped((DEPTH, row_count), bf16),
            shaped((row_count, DEPTH), bf16),
            shaped((16, row_count), bf16),
        ),
        features, slots, prices,
        flops=1000 * row_count,
        bytes_accessed=1024 * row_count,
    )
    block, center, first = call(
        partial(rows_body, len(centers)),
        (shaped((2 * row_count, count), bf16), shaped((DEPTH, count), bf16), vector),
        turned_columns, weight, *centers,
        **pass_cost,
    )
    firsts = exchange(first, "dp")
    turned = call(
        turned_body, shaped((2 * count, row_count), bf16), columns, center, **pass_cost
    )
    target, rows = call(
        partial(first_apply_body, len(firsts), 1.0 / math.sqrt(all_rows)),
        (vector, row_shape),
        *firsts, scale, slots, turned,
    )
    rows = exchange(rows, "centers")
    rows, folded = call(
        partial(first_fold_body, len(rows)), (row_shape, fold_shape), *rows, slots, block
    )
    folds = exchange(folded, "dp")
    residual, step, latest = call(
        partial(second_apply_body, len(folds), 1.0 / all_rows),
        (vector, narrow, row_shape),
        *folds, scale, slots, turned, target, rows,
    )
    latest = exchange(latest, "centers", True)
    sums, folded = call(
        partial(second_fold_body, len(latest)),
        (narrow, fold_shape),
        *latest, slots, block, rows,
    )
    folds = exchange(folded, "dp")
    return call(
        partial(finish_body, len(folds), 1.0 / all_rows),
        (vector, vector),
        *folds, scale, target, residual, step, sums,
    )


def solution(mesh):
    return jax.shard_map(
        per_device,
        mesh=mesh,
        in_specs=(P(None, "dp"), P("dp"), P("dp"), P("centers"), P("centers")),
        out_specs=(P(None, "centers"), P(None, "centers")),
        check_vma=False,
    )
```

```python
import math
from functools import partial

import jax
import jax.numpy as jnp
from jax import lax
from jax.experimental import pallas as pl
from jax.experimental.pallas import tpu as pltpu
from jax.sharding import PartitionSpec as P

SLOTS = 8
RIDGE = 0.5
CHUNK = 512
EXTRA = 128
DEPTH = 256
STEP = 256
FACTOR = math.log2(math.e) / 64.0
f32 = jnp.float32
bf16 = jnp.bfloat16
VMEM = pl.BlockSpec(memory_space=pltpu.VMEM)
HBM = pl.BlockSpec(memory_space=pltpu.HBM)


def split3(value):
    high = value.astype(bf16).astype(f32)
    rest = value - high
    mid = rest.astype(bf16).astype(f32)
    return high, mid, rest - mid


def stack2(value):
    high = value.astype(bf16).astype(f32)
    return jnp.concatenate([high, value - high], axis=0).astype(bf16)


def product(stacked, high_block, low_block):
    main = jnp.dot(stacked, high_block, preferred_element_type=f32)
    rest = jnp.dot(stacked[0:SLOTS], low_block, preferred_element_type=f32)
    return main[0:SLOTS] + (main[SLOTS:] + rest)


def slot_lanes(first):
    lane = lax.broadcasted_iota(jnp.int32, (SLOTS, EXTRA), 1)
    return lane == lax.broadcasted_iota(jnp.int32, (SLOTS, EXTRA), 0) + first


def to_lanes(column, first):
    return jnp.sum(jnp.where(slot_lanes(first), column, 0.0), axis=0, keepdims=True)


def from_lanes(row, first):
    return jnp.sum(jnp.where(slot_lanes(first), row, 0.0), axis=1, keepdims=True)


def spread(column):
    return jnp.broadcast_to(column, (SLOTS, EXTRA))


def wide(narrow, count):
    return jnp.concatenate([narrow] * (count // EXTRA), axis=1)


def pair_total(parts):
    while len(parts) > 1:
        parts = [parts[i] + parts[i + 1] for i in range(0, len(parts), 2)]
    return parts[0]


def total_of(refs):
    return pair_total([ref[...] for ref in refs])


def row_sum(value):
    return jnp.sum(value, axis=1, keepdims=True)


def slot_mask(slots):
    row = lax.broadcasted_iota(jnp.int32, (SLOTS, slots.shape[1]), 0)
    return slots == row


def norm_rows(feat32, base):
    half = (-0.5 * FACTOR) * jnp.sum(feat32 * feat32, axis=0, keepdims=True)
    row = lax.broadcasted_iota(jnp.int32, (feat32.shape[0], feat32.shape[1]), 0)
    extra = jnp.where(row < 6, 1.0, 0.0)
    for place, part in enumerate(split3(half)):
        extra = jnp.where(row == base + place, part, extra)
    return extra


def kernel_parts(left, right):
    value = jnp.exp2(jnp.dot(left, right, preferred_element_type=f32))
    high = value.astype(bf16)
    return high, (value - high.astype(f32)).astype(bf16)


def pick_body(feat_hbm, idx_hbm, slots_hbm, prices_hbm, scale_hbm, *refs):
    feat_ref, slots_ref, prices_ref, scale_ref, out_ref, idx_ref, hit_ref, sems = refs
    row_count = feat_ref.shape[1]
    count = out_ref.shape[1]
    half = row_count // 2
    left, right = pl.ds(0, half), pl.ds(half, half)
    sources = (
        idx_hbm, feat_hbm.at[:, left], feat_hbm.at[:, right], slots_hbm, prices_hbm, scale_hbm
    )
    targets = (
        idx_ref, feat_ref.at[:, left], feat_ref.at[:, right], slots_ref, prices_ref, scale_ref
    )
    copies = [
        pltpu.make_async_copy(source, target, sems.at[place])
        for place, (source, target) in enumerate(zip(sources, targets))
    ]
    for copy in copies:
        copy.start()
    copies[0].wait()
    local_idx = idx_ref[...] - lax.axis_index("dp") * row_count
    row = lax.broadcasted_iota(jnp.int32, (STEP, count), 0).astype(f32).astype(bf16)
    block = lax.div(local_idx, STEP)
    place = (local_idx - block * STEP).astype(f32)

    def hits(begin):
        own = jnp.where(block == begin // STEP, place, -1.0).astype(bf16)
        return jnp.where(row == own, jnp.ones_like(row), jnp.zeros_like(row))

    for begin in range(0, half, STEP):
        hit_ref[begin : begin + STEP, :] = hits(begin)
    copies[1].wait()
    total = jnp.dot(feat_ref[:, :half], hit_ref[...], preferred_element_type=f32)
    copies[2].wait()
    for begin in range(half, row_count, STEP):
        total += jnp.dot(
            feat_ref[:, begin : begin + STEP], hits(begin), preferred_element_type=f32
        )
    out_ref[...] = total.astype(bf16)
    for copy in copies[3:]:
        copy.wait()


def columns_body(feat_ref, slots_ref, prices_ref, columns_ref, turned_ref, weight_ref):
    for begin in range(0, feat_ref.shape[1], CHUNK):
        here = slice(begin, begin + CHUNK)
        feat32 = feat_ref[:, here].astype(f32)
        pair = jnp.concatenate([feat32, feat32], axis=0)
        last = jnp.concatenate([feat32, norm_rows(feat32, 3)], axis=0)
        columns_ref[0:128, here] = pair.astype(bf16)
        columns_ref[128:256, here] = last.astype(bf16)
        turned_ref[here, 0:128] = pair.T.astype(bf16)
        turned_ref[here, 128:256] = last.T.astype(bf16)
        weight = jnp.where(slot_mask(slots_ref[:, here]), prices_ref[:, here], 0.0)
        weight_ref[:, here] = stack2(weight)


def rows_body(parts, turned_ref, weight_ref, *refs):
    center_refs, (block_ref, center_ref, out_ref) = refs[:parts], refs[parts:]
    center = total_of(center_refs).astype(f32)
    center = jnp.concatenate(
        [*split3(center * FACTOR), norm_rows(center, 0)], axis=0
    ).astype(bf16)
    center_ref[...] = center
    row_count = turned_ref.shape[0]
    total = jnp.zeros(out_ref.shape, f32)

    def fold(begin):
        end = begin + CHUNK
        return product(
            weight_ref[:, begin:end],
            block_ref[begin:end, :],
            block_ref[row_count + begin : row_count + end, :],
        )

    for begin in range(0, row_count, CHUNK):
        high, low = kernel_parts(turned_ref[begin : begin + CHUNK, :], center)
        block_ref[begin : begin + CHUNK, :] = high
        block_ref[row_count + begin : row_count + begin + CHUNK, :] = low
        if begin > 0:
            total += fold(begin - CHUNK)
    out_ref[...] = total + fold(row_count - CHUNK)


def turned_body(columns_ref, center_ref, block_ref):
    center = center_ref[...].astype(f32).T.astype(bf16)
    count = center.shape[0]
    for begin in range(0, columns_ref.shape[1], CHUNK):
        here = slice(begin, begin + CHUNK)
        high, low = kernel_parts(center, columns_ref[:, here])
        block_ref[0:count, here] = high
        block_ref[count:, here] = low


def apply_rows(scaled, turned_ref, slots_ref, out_ref):
    count, row_count = scaled.shape[1], turned_ref.shape[1]
    value = product(stack2(scaled), turned_ref[0:count, :], turned_ref[count:, :])
    own = jnp.where(slot_mask(slots_ref[...]), value, 0.0)
    out_ref[:, 0:row_count] = jnp.sum(own, axis=0, keepdims=True)


def fold_rows(rows, block_ref, slots_ref, out_ref):
    row_count, count = slots_ref.shape[1], block_ref.shape[1]
    weight = jnp.where(slot_mask(slots_ref[...]), rows, 0.0)
    out_ref[:, 0:count] = product(
        stack2(weight), block_ref[0:row_count, :], block_ref[row_count:, :]
    )
    square = row_sum(weight * weight)
    out_ref[:, count : count + EXTRA] = spread(square)


def first_apply_body(parts, scale_over_root, *refs):
    first_refs = refs[:parts]
    scale_ref, slots_ref, turned_ref, target_ref, out_ref = refs[parts:]
    scale = scale_ref[...]
    target = scale * total_of(first_refs) * scale_over_root
    target_ref[...] = target
    out_ref[:, turned_ref.shape[1] :] = to_lanes(row_sum(target * target), 0)
    apply_rows(scale * target, turned_ref, slots_ref, out_ref)


def first_fold_body(parts, *refs):
    row_refs = refs[:parts]
    slots_ref, block_ref, rows_ref, norm_ref, out_ref = refs[parts:]
    row_count = slots_ref.shape[1]
    rows = total_of(row_refs)
    rows_ref[...] = rows
    norm_ref[...] = spread(from_lanes(rows[:, row_count:], 0))
    fold_rows(rows[:, 0:row_count], block_ref, slots_ref, out_ref)


def second_apply_body(parts, inv_rows, *refs):
    fold_refs = refs[:parts]
    (scale_ref, slots_ref, turned_ref, target_ref, norm_ref,
     residual_ref, step_ref, out_ref) = refs[parts:]
    row_count, count = turned_ref.shape[1], scale_ref.shape[1]
    folded = total_of(fold_refs)
    scale = scale_ref[...]
    target = target_ref[...]
    norm = norm_ref[...]
    applied = scale * folded[:, 0:count] * inv_rows + RIDGE * target
    step = norm / (folded[:, count:] * inv_rows + RIDGE * norm)
    residual = target - wide(step, count) * applied
    residual_ref[...] = residual
    step_ref[...] = step
    out_ref[:, row_count:] = to_lanes(row_sum(residual * residual), 0) + to_lanes(
        row_sum(residual * target), SLOTS
    )
    apply_rows(scale * residual, turned_ref, slots_ref, out_ref)


def second_fold_body(parts, *refs):
    row_refs = refs[:parts]
    slots_ref, block_ref, rows_ref, norm_ref, sums_ref, out_ref = refs[parts:]
    row_count = slots_ref.shape[1]
    latest = total_of(row_refs)
    norm = spread(from_lanes(latest[:, row_count:], 0))
    ratio = norm / norm_ref[...]
    sums_ref[:, 0:EXTRA] = norm
    sums_ref[:, EXTRA:] = spread(from_lanes(latest[:, row_count:], SLOTS))
    rows = latest[:, 0:row_count] + wide(ratio, row_count) * rows_ref[:, 0:row_count]
    fold_rows(rows, block_ref, slots_ref, out_ref)


def finish_body(parts, inv_rows, *refs):
    fold_refs = refs[:parts]
    (scale_ref, target_ref, residual_ref, step_ref, norm_ref, sums_ref,
     coefficients_ref, out_ref) = refs[parts:]
    count = scale_ref.shape[1]
    folded = total_of(fold_refs)
    target = target_ref[...]
    residual = residual_ref[...]
    first_norm = norm_ref[...]
    norm, cross = sums_ref[:, 0:EXTRA], sums_ref[:, EXTRA:]
    ratio = norm / first_norm
    direction = residual + wide(ratio, count) * target
    square = norm + 2.0 * ratio * cross + ratio * ratio * first_norm
    applied = scale_ref[...] * folded[:, 0:count] * inv_rows + RIDGE * direction
    step = wide(norm / (folded[:, count:] * inv_rows + RIDGE * square), count)
    coefficients_ref[...] = wide(step_ref[...], count) * target + step * direction
    out_ref[...] = residual - step * applied


def call(body, out_shape, *args, source=VMEM, flops=0, bytes_accessed=0, **more):
    return pl.pallas_call(
        body,
        out_shape=out_shape,
        in_specs=[source] * len(args),
        out_specs=jax.tree.map(lambda _: VMEM, out_shape),
        compiler_params=pltpu.CompilerParams(vmem_limit_bytes=36 * 1024 * 1024),
        cost_estimate=pl.CostEstimate(
            flops=flops, bytes_accessed=bytes_accessed, transcendentals=0
        ),
        **more,
    )(*args)


def exchange(value, axis, near_first=False):
    size = lax.axis_size(axis)
    bits = size.bit_length() - 1
    parts = [value]
    for low in range((bits + 1) // 2):
        value = pair_total(parts)
        near, far = 1 << low, 1 << (bits - 1 - low)
        side = 0 if low == 0 else 1
        parts = [value]
        for step in (near, far, near | far) if near != far else (near,):
            pairs = [(i, i ^ step ^ side) for i in range(size)]
            parts.insert(0, lax.ppermute(value, axis, pairs))
        if near_first and low == 0:
            parts = parts[-2:] + parts[:-2]
    return parts


def shaped(shape, dtype=f32):
    return jax.ShapeDtypeStruct(shape, dtype)


def per_device(features, prices, slots, center_idx, center_scale):
    depth, row_count = features.shape
    count = center_idx.shape[0]
    all_rows = row_count * lax.axis_size("dp")
    row_shape = shaped((1, row_count + EXTRA))
    fold_shape = shaped((SLOTS, count + EXTRA))
    vector = shaped((SLOTS, count))
    narrow = shaped((SLOTS, EXTRA))
    pass_cost = dict(flops=64 * row_count * count, bytes_accessed=4 * row_count * count)

    inputs = [
        pltpu.with_memory_space_constraint(array, pltpu.HBM)
        for array in (
            features,
            center_idx.reshape(1, count),
            slots.reshape(1, row_count),
            prices.reshape(1, row_count),
            center_scale.reshape(1, count),
        )
    ]
    features, slots, prices, scale, picked = call(
        pick_body,
        (
            shaped(features.shape, bf16),
            shaped((1, row_count), jnp.int32),
            shaped((1, row_count)),
            shaped((1, count)),
            shaped((depth, count), bf16),
        ),
        *inputs,
        source=HBM,
        scratch_shapes=[
            pltpu.VMEM((1, count), jnp.int32),
            pltpu.VMEM((row_count // 2, count), bf16),
            pltpu.SemaphoreType.DMA((6,)),
        ],
    )
    centers = exchange(picked, "dp")
    columns, turned_columns, weight = call(
        columns_body,
        (
            shaped((DEPTH, row_count), bf16),
            shaped((row_count, DEPTH), bf16),
            shaped((16, row_count), bf16),
        ),
        features, slots, prices,
        flops=1000 * row_count,
        bytes_accessed=1024 * row_count,
    )
    block, center, first = call(
        partial(rows_body, len(centers)),
        (shaped((2 * row_count, count), bf16), shaped((DEPTH, count), bf16), vector),
        turned_columns, weight, *centers,
        **pass_cost,
    )
    firsts = exchange(first, "dp")
    turned = call(
        turned_body, shaped((2 * count, row_count), bf16), columns, center, **pass_cost
    )
    target, rows = call(
        partial(first_apply_body, len(firsts), 1.0 / math.sqrt(all_rows)),
        (vector, row_shape),
        *firsts, scale, slots, turned,
    )
    rows = exchange(rows, "centers")
    rows, norm, folded = call(
        partial(first_fold_body, len(rows)), (row_shape, narrow, fold_shape), *rows, slots, block
    )
    folds = exchange(folded, "dp")
    residual, step, latest = call(
        partial(second_apply_body, len(folds), 1.0 / all_rows),
        (vector, narrow, row_shape),
        *folds, scale, slots, turned, target, norm,
    )
    latest = exchange(latest, "centers", True)
    sums, folded = call(
        partial(second_fold_body, len(latest)),
        (shaped((SLOTS, 2 * EXTRA)), fold_shape),
        *latest, slots, block, rows, norm,
    )
    folds = exchange(folded, "dp")
    return call(
        partial(finish_body, len(folds), 1.0 / all_rows),
        (vector, vector),
        *folds, scale, target, residual, step, norm, sums,
    )


def solution(mesh):
    return jax.shard_map(
        per_device,
        mesh=mesh,
        in_specs=(P(None, "dp"), P("dp"), P("dp"), P("centers"), P("centers")),
        out_specs=(P(None, "centers"), P(None, "centers")),
        check_vma=False,
    )
```

```python
import math
from functools import partial

import jax
import jax.numpy as jnp
from jax import lax
from jax.experimental import pallas as pl
from jax.experimental.pallas import tpu as pltpu
from jax.sharding import PartitionSpec as P

SLOTS = 8
RIDGE = 0.5
CHUNK = 512
EXTRA = 128
DEPTH = 256
STEP = 256
FACTOR = math.log2(math.e) / 64.0
f32 = jnp.float32
bf16 = jnp.bfloat16
VMEM = pl.BlockSpec(memory_space=pltpu.VMEM)
HBM = pl.BlockSpec(memory_space=pltpu.HBM)


def split3(value):
    high = value.astype(bf16).astype(f32)
    rest = value - high
    mid = rest.astype(bf16).astype(f32)
    return high, mid, rest - mid


def stack2(value):
    high = value.astype(bf16).astype(f32)
    return jnp.concatenate([high, value - high], axis=0).astype(bf16)


def product(stacked, high_block, low_block):
    main = jnp.dot(stacked, high_block, preferred_element_type=f32)
    rest = jnp.dot(stacked[0:SLOTS], low_block, preferred_element_type=f32)
    return main[0:SLOTS] + (main[SLOTS:] + rest)


def slot_lanes(first):
    lane = lax.broadcasted_iota(jnp.int32, (SLOTS, EXTRA), 1)
    return lane == lax.broadcasted_iota(jnp.int32, (SLOTS, EXTRA), 0) + first


def to_lanes(column, first):
    return jnp.sum(jnp.where(slot_lanes(first), column, 0.0), axis=0, keepdims=True)


def from_lanes(row, first):
    return jnp.sum(jnp.where(slot_lanes(first), row, 0.0), axis=1, keepdims=True)


def spread(column):
    return jnp.broadcast_to(column, (SLOTS, EXTRA))


def wide(narrow, count):
    return jnp.concatenate([narrow] * (count // EXTRA), axis=1)


def pair_total(parts):
    while len(parts) > 1:
        parts = [parts[i] + parts[i + 1] for i in range(0, len(parts), 2)]
    return parts[0]


def total_of(refs):
    return pair_total([ref[...] for ref in refs])


def row_sum(value):
    return jnp.sum(value, axis=1, keepdims=True)


def slot_mask(slots):
    row = lax.broadcasted_iota(jnp.int32, (SLOTS, slots.shape[1]), 0)
    return slots == row


def norm_rows(feat32, base):
    half = (-0.5 * FACTOR) * jnp.sum(feat32 * feat32, axis=0, keepdims=True)
    row = lax.broadcasted_iota(jnp.int32, (feat32.shape[0], feat32.shape[1]), 0)
    extra = jnp.where(row < 6, 1.0, 0.0)
    for place, part in enumerate(split3(half)):
        extra = jnp.where(row == base + place, part, extra)
    return extra


def kernel_parts(left, right):
    value = jnp.exp2(jnp.dot(left, right, preferred_element_type=f32))
    high = value.astype(bf16)
    return high, (value - high.astype(f32)).astype(bf16)


def pick_body(feat_hbm, idx_hbm, slots_hbm, prices_hbm, scale_hbm, *refs):
    feat_ref, slots_ref, prices_ref, scale_ref, out_ref, idx_ref, hit_ref, sems = refs
    row_count = feat_ref.shape[1]
    count = out_ref.shape[1]
    half = row_count // 2
    left, right = pl.ds(0, half), pl.ds(half, half)
    sources = (
        idx_hbm, feat_hbm.at[:, left], feat_hbm.at[:, right], slots_hbm, prices_hbm, scale_hbm
    )
    targets = (
        idx_ref, feat_ref.at[:, left], feat_ref.at[:, right], slots_ref, prices_ref, scale_ref
    )
    copies = [
        pltpu.make_async_copy(source, target, sems.at[place])
        for place, (source, target) in enumerate(zip(sources, targets))
    ]
    for copy in copies:
        copy.start()
    copies[0].wait()
    local_idx = idx_ref[...] - lax.axis_index("dp") * row_count
    row = lax.broadcasted_iota(jnp.int32, (STEP, count), 0).astype(f32).astype(bf16)
    block = lax.div(local_idx, STEP)
    place = (local_idx - block * STEP).astype(f32)

    def hits(begin):
        own = jnp.where(block == begin // STEP, place, -1.0).astype(bf16)
        return jnp.where(row == own, jnp.ones_like(row), jnp.zeros_like(row))

    for begin in range(0, half, STEP):
        hit_ref[begin : begin + STEP, :] = hits(begin)
    copies[1].wait()
    total = jnp.dot(feat_ref[:, :half], hit_ref[...], preferred_element_type=f32)
    copies[2].wait()
    for begin in range(half, row_count, STEP):
        total += jnp.dot(
            feat_ref[:, begin : begin + STEP], hits(begin), preferred_element_type=f32
        )
    out_ref[...] = total.astype(bf16)
    for copy in copies[3:]:
        copy.wait()


def columns_body(feat_ref, slots_ref, prices_ref, columns_ref, turned_ref, weight_ref):
    for begin in range(0, feat_ref.shape[1], CHUNK):
        here = slice(begin, begin + CHUNK)
        feat32 = feat_ref[:, here].astype(f32)
        pair = jnp.concatenate([feat32, feat32], axis=0)
        last = jnp.concatenate([feat32, norm_rows(feat32, 3)], axis=0)
        columns_ref[0:128, here] = pair.astype(bf16)
        columns_ref[128:256, here] = last.astype(bf16)
        turned_ref[here, 0:128] = pair.T.astype(bf16)
        turned_ref[here, 128:256] = last.T.astype(bf16)
        weight = jnp.where(slot_mask(slots_ref[:, here]), prices_ref[:, here], 0.0)
        weight_ref[:, here] = stack2(weight)


def rows_body(parts, turned_ref, weight_ref, *refs):
    center_refs, (block_ref, center_ref, out_ref) = refs[:parts], refs[parts:]
    center = total_of(center_refs).astype(f32)
    center = jnp.concatenate(
        [*split3(center * FACTOR), norm_rows(center, 0)], axis=0
    ).astype(bf16)
    center_ref[...] = center
    row_count = turned_ref.shape[0]
    total = jnp.zeros(out_ref.shape, f32)

    def fold(begin):
        end = begin + CHUNK
        return product(
            weight_ref[:, begin:end],
            block_ref[begin:end, :],
            block_ref[row_count + begin : row_count + end, :],
        )

    for begin in range(0, row_count, CHUNK):
        high, low = kernel_parts(turned_ref[begin : begin + CHUNK, :], center)
        block_ref[begin : begin + CHUNK, :] = high
        block_ref[row_count + begin : row_count + begin + CHUNK, :] = low
        if begin > 0:
            total += fold(begin - CHUNK)
    out_ref[...] = total + fold(row_count - CHUNK)


def turned_body(columns_ref, center_ref, block_ref):
    center = center_ref[...].astype(f32).T.astype(bf16)
    count = center.shape[0]
    for begin in range(0, columns_ref.shape[1], CHUNK):
        here = slice(begin, begin + CHUNK)
        high, low = kernel_parts(center, columns_ref[:, here])
        block_ref[0:count, here] = high
        block_ref[count:, here] = low


def apply_rows(scaled, turned_ref, slots_ref, out_ref):
    count, row_count = scaled.shape[1], turned_ref.shape[1]
    value = product(stack2(scaled), turned_ref[0:count, :], turned_ref[count:, :])
    own = jnp.where(slot_mask(slots_ref[...]), value, 0.0)
    out_ref[:, 0:row_count] = jnp.sum(own, axis=0, keepdims=True)


def fold_rows(rows, block_ref, slots_ref, out_ref):
    row_count, count = slots_ref.shape[1], block_ref.shape[1]
    weight = jnp.where(slot_mask(slots_ref[...]), rows, 0.0)
    out_ref[:, 0:count] = product(
        stack2(weight), block_ref[0:row_count, :], block_ref[row_count:, :]
    )
    square = row_sum(weight * weight)
    out_ref[:, count : count + EXTRA] = spread(square)


def first_apply_body(parts, scale_over_root, *refs):
    first_refs = refs[:parts]
    scale_ref, slots_ref, turned_ref, target_ref, out_ref = refs[parts:]
    scale = scale_ref[...]
    target = scale * total_of(first_refs) * scale_over_root
    target_ref[...] = target
    out_ref[:, turned_ref.shape[1] :] = to_lanes(row_sum(target * target), 0)
    apply_rows(scale * target, turned_ref, slots_ref, out_ref)


def first_fold_body(parts, *refs):
    row_refs = refs[:parts]
    slots_ref, block_ref, rows_ref, norm_ref, out_ref = refs[parts:]
    row_count = slots_ref.shape[1]
    rows = total_of(row_refs)
    rows_ref[...] = rows
    norm_ref[...] = spread(from_lanes(rows[:, row_count:], 0))
    fold_rows(rows[:, 0:row_count], block_ref, slots_ref, out_ref)


def second_apply_body(parts, inv_rows, *refs):
    fold_refs = refs[:parts]
    (scale_ref, slots_ref, turned_ref, target_ref, norm_ref,
     residual_ref, step_ref, out_ref) = refs[parts:]
    row_count, count = turned_ref.shape[1], scale_ref.shape[1]
    folded = total_of(fold_refs)
    scale = scale_ref[...]
    target = target_ref[...]
    norm = norm_ref[...]
    applied = scale * folded[:, 0:count] * inv_rows + RIDGE * target
    step = norm / (folded[:, count:] * inv_rows + RIDGE * norm)
    residual = target - wide(step, count) * applied
    residual_ref[...] = residual
    step_ref[...] = step
    out_ref[:, row_count:] = to_lanes(row_sum(residual * residual), 0) + to_lanes(
        row_sum(residual * target), SLOTS
    )
    apply_rows(scale * residual, turned_ref, slots_ref, out_ref)


def second_fold_body(parts, *refs):
    row_refs = refs[:parts]
    slots_ref, block_ref, rows_ref, norm_ref, sums_ref, out_ref = refs[parts:]
    row_count = slots_ref.shape[1]
    latest = total_of(row_refs)
    norm = spread(from_lanes(latest[:, row_count:], 0))
    ratio = norm / norm_ref[...]
    sums_ref[:, 0:EXTRA] = norm
    sums_ref[:, EXTRA:] = spread(from_lanes(latest[:, row_count:], SLOTS))
    rows = latest[:, 0:row_count] + wide(ratio, row_count) * rows_ref[:, 0:row_count]
    fold_rows(rows, block_ref, slots_ref, out_ref)


def finish_body(parts, inv_rows, *refs):
    fold_refs = refs[:parts]
    (scale_ref, target_ref, residual_ref, step_ref, norm_ref, sums_ref,
     coefficients_ref, out_ref) = refs[parts:]
    count = scale_ref.shape[1]
    folded = total_of(fold_refs)
    target = target_ref[...]
    residual = residual_ref[...]
    first_norm = norm_ref[...]
    norm, cross = sums_ref[:, 0:EXTRA], sums_ref[:, EXTRA:]
    ratio = norm / first_norm
    direction = residual + wide(ratio, count) * target
    square = norm + 2.0 * ratio * cross + ratio * ratio * first_norm
    applied = scale_ref[...] * folded[:, 0:count] * inv_rows + RIDGE * direction
    step = wide(norm / (folded[:, count:] * inv_rows + RIDGE * square), count)
    coefficients_ref[...] = wide(step_ref[...], count) * target + step * direction
    out_ref[...] = residual - step * applied


def call(body, out_shape, *args, source=VMEM, flops=0, bytes_accessed=0, **more):
    return pl.pallas_call(
        body,
        out_shape=out_shape,
        in_specs=[source] * len(args),
        out_specs=jax.tree.map(lambda _: VMEM, out_shape),
        compiler_params=pltpu.CompilerParams(vmem_limit_bytes=36 * 1024 * 1024),
        cost_estimate=pl.CostEstimate(
            flops=flops, bytes_accessed=bytes_accessed, transcendentals=0
        ),
        **more,
    )(*args)


def exchange(value, axis):
    size = lax.axis_size(axis)
    parts = [value]
    stride = 1
    while stride < size:
        value = pair_total(parts)
        span = 2 if stride < 4 else min(4, size // stride)
        side = 0 if stride == 1 else 1
        parts = [value]
        for offset in range(1, span):
            pairs = [(i, i ^ (offset * stride) ^ side) for i in range(size)]
            parts.insert(0, lax.ppermute(value, axis, pairs))
        stride *= span
    return parts


def shaped(shape, dtype=f32):
    return jax.ShapeDtypeStruct(shape, dtype)


def per_device(features, prices, slots, center_idx, center_scale):
    depth, row_count = features.shape
    count = center_idx.shape[0]
    all_rows = row_count * lax.axis_size("dp")
    row_shape = shaped((1, row_count + EXTRA))
    fold_shape = shaped((SLOTS, count + EXTRA))
    vector = shaped((SLOTS, count))
    narrow = shaped((SLOTS, EXTRA))
    pass_cost = dict(flops=64 * row_count * count, bytes_accessed=4 * row_count * count)

    inputs = [
        pltpu.with_memory_space_constraint(array, pltpu.HBM)
        for array in (
            features,
            center_idx.reshape(1, count),
            slots.reshape(1, row_count),
            prices.reshape(1, row_count),
            center_scale.reshape(1, count),
        )
    ]
    features, slots, prices, scale, picked = call(
        pick_body,
        (
            shaped(features.shape, bf16),
            shaped((1, row_count), jnp.int32),
            shaped((1, row_count)),
            shaped((1, count)),
            shaped((depth, count), bf16),
        ),
        *inputs,
        source=HBM,
        scratch_shapes=[
            pltpu.VMEM((1, count), jnp.int32),
            pltpu.VMEM((row_count // 2, count), bf16),
            pltpu.SemaphoreType.DMA((6,)),
        ],
    )
    centers = exchange(picked, "dp")
    columns, turned_columns, weight = call(
        columns_body,
        (
            shaped((DEPTH, row_count), bf16),
            shaped((row_count, DEPTH), bf16),
            shaped((16, row_count), bf16),
        ),
        features, slots, prices,
        flops=1000 * row_count,
        bytes_accessed=1024 * row_count,
    )
    block, center, first = call(
        partial(rows_body, len(centers)),
        (shaped((2 * row_count, count), bf16), shaped((DEPTH, count), bf16), vector),
        turned_columns, weight, *centers,
        **pass_cost,
    )
    firsts = exchange(first, "dp")
    turned = call(
        turned_body, shaped((2 * count, row_count), bf16), columns, center, **pass_cost
    )
    target, rows = call(
        partial(first_apply_body, len(firsts), 1.0 / math.sqrt(all_rows)),
        (vector, row_shape),
        *firsts, scale, slots, turned,
    )
    rows = exchange(rows, "centers")
    rows, norm, folded = call(
        partial(first_fold_body, len(rows)), (row_shape, narrow, fold_shape), *rows, slots, block
    )
    folds = exchange(folded, "dp")
    residual, step, latest = call(
        partial(second_apply_body, len(folds), 1.0 / all_rows),
        (vector, narrow, row_shape),
        *folds, scale, slots, turned, target, norm,
    )
    latest = exchange(latest, "centers")
    sums, folded = call(
        partial(second_fold_body, len(latest)),
        (shaped((SLOTS, 2 * EXTRA)), fold_shape),
        *latest, slots, block, rows, norm,
    )
    folds = exchange(folded, "dp")
    return call(
        partial(finish_body, len(folds), 1.0 / all_rows),
        (vector, vector),
        *folds, scale, target, residual, step, norm, sums,
    )


def solution(mesh):
    return jax.shard_map(
        per_device,
        mesh=mesh,
        in_specs=(P(None, "dp"), P("dp"), P("dp"), P("centers"), P("centers")),
        out_specs=(P(None, "centers"), P(None, "centers")),
        check_vma=False,
    )
```

```python
import math
from functools import partial

import jax
import jax.numpy as jnp
from jax import lax
from jax.experimental import pallas as pl
from jax.experimental.pallas import tpu as pltpu
from jax.sharding import PartitionSpec as P

SLOTS = 8
RIDGE = 0.5
CHUNK = 512
EXTRA = 128
DEPTH = 256
STEP = 256
FACTOR = math.log2(math.e) / 64.0
f32 = jnp.float32
bf16 = jnp.bfloat16
VMEM = pl.BlockSpec(memory_space=pltpu.VMEM)
HBM = pl.BlockSpec(memory_space=pltpu.HBM)


def split3(value):
    high = value.astype(bf16).astype(f32)
    rest = value - high
    mid = rest.astype(bf16).astype(f32)
    return high, mid, rest - mid


def stack2(value):
    high = value.astype(bf16).astype(f32)
    return jnp.concatenate([high, value - high], axis=0).astype(bf16)


def product(stacked, high_block, low_block):
    main = jnp.dot(stacked, high_block, preferred_element_type=f32)
    rest = jnp.dot(stacked[0:SLOTS], low_block, preferred_element_type=f32)
    return main[0:SLOTS] + (main[SLOTS:] + rest)


def slot_lanes(first):
    lane = lax.broadcasted_iota(jnp.int32, (SLOTS, EXTRA), 1)
    return lane == lax.broadcasted_iota(jnp.int32, (SLOTS, EXTRA), 0) + first


def to_lanes(column, first):
    return jnp.sum(jnp.where(slot_lanes(first), column, 0.0), axis=0, keepdims=True)


def from_lanes(row, first):
    return jnp.sum(jnp.where(slot_lanes(first), row, 0.0), axis=1, keepdims=True)


def spread(column):
    return jnp.broadcast_to(column, (SLOTS, EXTRA))


def wide(narrow, count):
    return jnp.concatenate([narrow] * (count // EXTRA), axis=1)


def pair_total(parts):
    while len(parts) > 1:
        parts = [parts[i] + parts[i + 1] for i in range(0, len(parts), 2)]
    return parts[0]


def total_of(refs):
    return pair_total([ref[...] for ref in refs])


def row_sum(value):
    return jnp.sum(value, axis=1, keepdims=True)


def slot_mask(slots):
    row = lax.broadcasted_iota(jnp.int32, (SLOTS, slots.shape[1]), 0)
    return slots == row


def norm_rows(feat32, base):
    half = (-0.5 * FACTOR) * jnp.sum(feat32 * feat32, axis=0, keepdims=True)
    row = lax.broadcasted_iota(jnp.int32, (feat32.shape[0], feat32.shape[1]), 0)
    extra = jnp.where(row < 6, 1.0, 0.0)
    for place, part in enumerate(split3(half)):
        extra = jnp.where(row == base + place, part, extra)
    return extra


def kernel_parts(left, right):
    value = jnp.exp2(jnp.dot(left, right, preferred_element_type=f32))
    high = value.astype(bf16)
    return high, (value - high.astype(f32)).astype(bf16)


def pick_body(feat_hbm, idx_hbm, slots_hbm, prices_hbm, scale_hbm, *refs):
    feat_ref, slots_ref, prices_ref, scale_ref, out_ref, idx_ref, hit_ref, sems = refs
    row_count = feat_ref.shape[1]
    count = out_ref.shape[1]
    sources = (idx_hbm, feat_hbm, slots_hbm, prices_hbm, scale_hbm)
    targets = (idx_ref, feat_ref, slots_ref, prices_ref, scale_ref)
    copies = [
        pltpu.make_async_copy(source, target, sems.at[place])
        for place, (source, target) in enumerate(zip(sources, targets))
    ]
    for copy in copies:
        copy.start()
    copies[0].wait()
    local_idx = idx_ref[...] - lax.axis_index("dp") * row_count
    row = lax.broadcasted_iota(jnp.int32, (STEP, count), 0).astype(f32).astype(bf16)
    block = lax.div(local_idx, STEP)
    place = (local_idx - block * STEP).astype(f32)

    def hits(begin):
        own = jnp.where(block == begin // STEP, place, -1.0).astype(bf16)
        return jnp.where(row == own, jnp.ones_like(row), jnp.zeros_like(row))

    for begin in range(0, row_count, STEP):
        hit_ref[begin : begin + STEP, :] = hits(begin)
    copies[1].wait()
    out_ref[...] = jnp.dot(
        feat_ref[...], hit_ref[...], preferred_element_type=f32
    ).astype(bf16)
    for copy in copies[2:]:
        copy.wait()


def columns_body(feat_ref, slots_ref, prices_ref, columns_ref, turned_ref, weight_ref):
    for begin in range(0, feat_ref.shape[1], CHUNK):
        here = slice(begin, begin + CHUNK)
        feat32 = feat_ref[:, here].astype(f32)
        pair = jnp.concatenate([feat32, feat32], axis=0)
        last = jnp.concatenate([feat32, norm_rows(feat32, 3)], axis=0)
        columns_ref[0:128, here] = pair.astype(bf16)
        columns_ref[128:256, here] = last.astype(bf16)
        turned_ref[here, 0:128] = pair.T.astype(bf16)
        turned_ref[here, 128:256] = last.T.astype(bf16)
        weight = jnp.where(slot_mask(slots_ref[:, here]), prices_ref[:, here], 0.0)
        weight_ref[:, here] = stack2(weight)


def rows_body(parts, turned_ref, weight_ref, *refs):
    center_refs, (block_ref, center_ref, out_ref) = refs[:parts], refs[parts:]
    center = total_of(center_refs).astype(f32)
    center = jnp.concatenate(
        [*split3(center * FACTOR), norm_rows(center, 0)], axis=0
    ).astype(bf16)
    center_ref[...] = center
    row_count = turned_ref.shape[0]
    total = jnp.zeros(out_ref.shape, f32)

    def fold(begin):
        end = begin + CHUNK
        return product(
            weight_ref[:, begin:end],
            block_ref[begin:end, :],
            block_ref[row_count + begin : row_count + end, :],
        )

    for begin in range(0, row_count, CHUNK):
        high, low = kernel_parts(turned_ref[begin : begin + CHUNK, :], center)
        block_ref[begin : begin + CHUNK, :] = high
        block_ref[row_count + begin : row_count + begin + CHUNK, :] = low
        if begin > 0:
            total += fold(begin - CHUNK)
    out_ref[...] = total + fold(row_count - CHUNK)


def turned_body(columns_ref, center_ref, block_ref):
    center = center_ref[...].astype(f32).T.astype(bf16)
    count = center.shape[0]
    for begin in range(0, columns_ref.shape[1], CHUNK):
        here = slice(begin, begin + CHUNK)
        high, low = kernel_parts(center, columns_ref[:, here])
        block_ref[0:count, here] = high
        block_ref[count:, here] = low


def apply_rows(scaled, turned_ref, slots_ref, out_ref):
    count, row_count = scaled.shape[1], turned_ref.shape[1]
    value = product(stack2(scaled), turned_ref[0:count, :], turned_ref[count:, :])
    own = jnp.where(slot_mask(slots_ref[...]), value, 0.0)
    out_ref[:, 0:row_count] = jnp.sum(own, axis=0, keepdims=True)


def fold_rows(rows, block_ref, slots_ref, out_ref):
    row_count, count = slots_ref.shape[1], block_ref.shape[1]
    weight = jnp.where(slot_mask(slots_ref[...]), rows, 0.0)
    out_ref[:, 0:count] = product(
        stack2(weight), block_ref[0:row_count, :], block_ref[row_count:, :]
    )
    square = row_sum(weight * weight)
    out_ref[:, count : count + EXTRA] = spread(square)


def first_apply_body(parts, scale_over_root, *refs):
    first_refs = refs[:parts]
    scale_ref, slots_ref, turned_ref, target_ref, out_ref = refs[parts:]
    scale = scale_ref[...]
    target = scale * total_of(first_refs) * scale_over_root
    target_ref[...] = target
    out_ref[:, turned_ref.shape[1] :] = to_lanes(row_sum(target * target), 0)
    apply_rows(scale * target, turned_ref, slots_ref, out_ref)


def first_fold_body(parts, *refs):
    row_refs = refs[:parts]
    slots_ref, block_ref, rows_ref, norm_ref, out_ref = refs[parts:]
    row_count = slots_ref.shape[1]
    rows = total_of(row_refs)
    rows_ref[...] = rows
    norm_ref[...] = spread(from_lanes(rows[:, row_count:], 0))
    fold_rows(rows[:, 0:row_count], block_ref, slots_ref, out_ref)


def second_apply_body(parts, inv_rows, *refs):
    fold_refs = refs[:parts]
    (scale_ref, slots_ref, turned_ref, target_ref, norm_ref,
     residual_ref, step_ref, out_ref) = refs[parts:]
    row_count, count = turned_ref.shape[1], scale_ref.shape[1]
    folded = total_of(fold_refs)
    scale = scale_ref[...]
    target = target_ref[...]
    norm = norm_ref[...]
    applied = scale * folded[:, 0:count] * inv_rows + RIDGE * target
    step = norm / (folded[:, count:] * inv_rows + RIDGE * norm)
    residual = target - wide(step, count) * applied
    residual_ref[...] = residual
    step_ref[...] = step
    out_ref[:, row_count:] = to_lanes(row_sum(residual * residual), 0) + to_lanes(
        row_sum(residual * target), SLOTS
    )
    apply_rows(scale * residual, turned_ref, slots_ref, out_ref)


def second_fold_body(parts, *refs):
    row_refs = refs[:parts]
    slots_ref, block_ref, rows_ref, norm_ref, sums_ref, out_ref = refs[parts:]
    row_count = slots_ref.shape[1]
    latest = total_of(row_refs)
    norm = spread(from_lanes(latest[:, row_count:], 0))
    ratio = norm / norm_ref[...]
    sums_ref[:, 0:EXTRA] = norm
    sums_ref[:, EXTRA:] = spread(from_lanes(latest[:, row_count:], SLOTS))
    rows = latest[:, 0:row_count] + wide(ratio, row_count) * rows_ref[:, 0:row_count]
    fold_rows(rows, block_ref, slots_ref, out_ref)


def finish_body(parts, inv_rows, *refs):
    fold_refs = refs[:parts]
    (scale_ref, target_ref, residual_ref, step_ref, norm_ref, sums_ref,
     coefficients_ref, out_ref) = refs[parts:]
    count = scale_ref.shape[1]
    folded = total_of(fold_refs)
    target = target_ref[...]
    residual = residual_ref[...]
    first_norm = norm_ref[...]
    norm, cross = sums_ref[:, 0:EXTRA], sums_ref[:, EXTRA:]
    ratio = norm / first_norm
    direction = residual + wide(ratio, count) * target
    square = norm + 2.0 * ratio * cross + ratio * ratio * first_norm
    applied = scale_ref[...] * folded[:, 0:count] * inv_rows + RIDGE * direction
    step = wide(norm / (folded[:, count:] * inv_rows + RIDGE * square), count)
    coefficients_ref[...] = wide(step_ref[...], count) * target + step * direction
    out_ref[...] = residual - step * applied


def call(body, out_shape, *args, source=VMEM, flops=0, bytes_accessed=0, **more):
    return pl.pallas_call(
        body,
        out_shape=out_shape,
        in_specs=[source] * len(args),
        out_specs=jax.tree.map(lambda _: VMEM, out_shape),
        compiler_params=pltpu.CompilerParams(vmem_limit_bytes=36 * 1024 * 1024),
        cost_estimate=pl.CostEstimate(
            flops=flops, bytes_accessed=bytes_accessed, transcendentals=0
        ),
        **more,
    )(*args)


def exchange(value, axis, near_first=False):
    size = lax.axis_size(axis)
    parts = [value]
    stride = 1
    while stride < size:
        value = pair_total(parts)
        span = min(4, size // stride)
        side = 0 if stride == 1 else 1
        parts = [value]
        for offset in range(1, span):
            pairs = [(i, i ^ (offset * stride) ^ side) for i in range(size)]
            parts.insert(0, lax.ppermute(value, axis, pairs))
        if near_first and stride == 1:
            parts = parts[-2:] + parts[:-2]
        stride *= span
    return parts


def shaped(shape, dtype=f32):
    return jax.ShapeDtypeStruct(shape, dtype)


def per_device(features, prices, slots, center_idx, center_scale):
    depth, row_count = features.shape
    count = center_idx.shape[0]
    all_rows = row_count * lax.axis_size("dp")
    row_shape = shaped((1, row_count + EXTRA))
    fold_shape = shaped((SLOTS, count + EXTRA))
    vector = shaped((SLOTS, count))
    narrow = shaped((SLOTS, EXTRA))
    pass_cost = dict(flops=64 * row_count * count, bytes_accessed=4 * row_count * count)

    inputs = [
        pltpu.with_memory_space_constraint(array, pltpu.HBM)
        for array in (
            features,
            center_idx.reshape(1, count),
            slots.reshape(1, row_count),
            prices.reshape(1, row_count),
            center_scale.reshape(1, count),
        )
    ]
    features, slots, prices, scale, picked = call(
        pick_body,
        (
            shaped(features.shape, bf16),
            shaped((1, row_count), jnp.int32),
            shaped((1, row_count)),
            shaped((1, count)),
            shaped((depth, count), bf16),
        ),
        *inputs,
        source=HBM,
        scratch_shapes=[
            pltpu.VMEM((1, count), jnp.int32),
            pltpu.VMEM((row_count, count), bf16),
            pltpu.SemaphoreType.DMA((5,)),
        ],
    )
    centers = exchange(picked, "dp")
    columns, turned_columns, weight = call(
        columns_body,
        (
            shaped((DEPTH, row_count), bf16),
            shaped((row_count, DEPTH), bf16),
            shaped((16, row_count), bf16),
        ),
        features, slots, prices,
        flops=1000 * row_count,
        bytes_accessed=1024 * row_count,
    )
    block, center, first = call(
        partial(rows_body, len(centers)),
        (shaped((2 * row_count, count), bf16), shaped((DEPTH, count), bf16), vector),
        turned_columns, weight, *centers,
        **pass_cost,
    )
    firsts = exchange(first, "dp")
    turned = call(
        turned_body, shaped((2 * count, row_count), bf16), columns, center, **pass_cost
    )
    target, rows = call(
        partial(first_apply_body, len(firsts), 1.0 / math.sqrt(all_rows)),
        (vector, row_shape),
        *firsts, scale, slots, turned,
    )
    rows = exchange(rows, "centers")
    rows, norm, folded = call(
        partial(first_fold_body, len(rows)), (row_shape, narrow, fold_shape), *rows, slots, block
    )
    folds = exchange(folded, "dp")
    residual, step, latest = call(
        partial(second_apply_body, len(folds), 1.0 / all_rows),
        (vector, narrow, row_shape),
        *folds, scale, slots, turned, target, norm,
    )
    latest = exchange(latest, "centers", True)
    sums, folded = call(
        partial(second_fold_body, len(latest)),
        (shaped((SLOTS, 2 * EXTRA)), fold_shape),
        *latest, slots, block, rows, norm,
    )
    folds = exchange(folded, "dp")
    return call(
        partial(finish_body, len(folds), 1.0 / all_rows),
        (vector, vector),
        *folds, scale, target, residual, step, norm, sums,
    )


def solution(mesh):
    return jax.shard_map(
        per_device,
        mesh=mesh,
        in_specs=(P(None, "dp"), P("dp"), P("dp"), P("centers"), P("centers")),
        out_specs=(P(None, "centers"), P(None, "centers")),
        check_vma=False,
    )
```

```python
import math
from functools import partial

import jax
import jax.numpy as jnp
from jax import lax
from jax.experimental import pallas as pl
from jax.experimental.pallas import tpu as pltpu
from jax.sharding import PartitionSpec as P

SLOTS = 8
RIDGE = 0.5
CHUNK = 512
EXTRA = 128
DEPTH = 256
STEP = 256
FACTOR = math.log2(math.e) / 64.0
f32 = jnp.float32
bf16 = jnp.bfloat16
VMEM = pl.BlockSpec(memory_space=pltpu.VMEM)
HBM = pl.BlockSpec(memory_space=pltpu.HBM)


def split3(value):
    high = value.astype(bf16).astype(f32)
    rest = value - high
    mid = rest.astype(bf16).astype(f32)
    return high, mid, rest - mid


def stack2(value):
    high = value.astype(bf16).astype(f32)
    return jnp.concatenate([high, value - high], axis=0).astype(bf16)


def product(stacked, high_block, low_block):
    main = jnp.dot(stacked, high_block, preferred_element_type=f32)
    rest = jnp.dot(stacked[0:SLOTS], low_block, preferred_element_type=f32)
    return main[0:SLOTS] + (main[SLOTS:] + rest)


def slot_lanes(first):
    lane = lax.broadcasted_iota(jnp.int32, (SLOTS, EXTRA), 1)
    return lane == lax.broadcasted_iota(jnp.int32, (SLOTS, EXTRA), 0) + first


def to_lanes(column, first):
    return jnp.sum(jnp.where(slot_lanes(first), column, 0.0), axis=0, keepdims=True)


def from_lanes(row, first):
    return jnp.sum(jnp.where(slot_lanes(first), row, 0.0), axis=1, keepdims=True)


def spread(column):
    return jnp.broadcast_to(column, (SLOTS, EXTRA))


def wide(narrow, count):
    return jnp.concatenate([narrow] * (count // EXTRA), axis=1)


def pair_total(parts):
    while len(parts) > 1:
        parts = [parts[i] + parts[i + 1] for i in range(0, len(parts), 2)]
    return parts[0]


def total_of(refs):
    return pair_total([ref[...] for ref in refs])


def row_sum(value):
    return jnp.sum(value, axis=1, keepdims=True)


def slot_mask(slots):
    row = lax.broadcasted_iota(jnp.int32, (SLOTS, slots.shape[1]), 0)
    return slots == row


def norm_rows(feat32, base):
    half = (-0.5 * FACTOR) * jnp.sum(feat32 * feat32, axis=0, keepdims=True)
    row = lax.broadcasted_iota(jnp.int32, (feat32.shape[0], feat32.shape[1]), 0)
    extra = jnp.where(row < 6, 1.0, 0.0)
    for place, part in enumerate(split3(half)):
        extra = jnp.where(row == base + place, part, extra)
    return extra


def kernel_parts(left, right):
    value = jnp.exp2(jnp.dot(left, right, preferred_element_type=f32))
    high = value.astype(bf16)
    return high, (value - high.astype(f32)).astype(bf16)


def pick_body(feat_hbm, idx_hbm, slots_hbm, prices_hbm, scale_hbm, *refs):
    feat_ref, slots_ref, prices_ref, scale_ref, out_ref, idx_ref, hit_ref, sems = refs
    row_count = feat_ref.shape[1]
    count = out_ref.shape[1]
    sources = (idx_hbm, feat_hbm, slots_hbm, prices_hbm, scale_hbm)
    targets = (idx_ref, feat_ref, slots_ref, prices_ref, scale_ref)
    copies = [
        pltpu.make_async_copy(source, target, sems.at[place])
        for place, (source, target) in enumerate(zip(sources, targets))
    ]
    for copy in copies:
        copy.start()
    copies[0].wait()
    local_idx = idx_ref[...] - lax.axis_index("dp") * row_count
    row = lax.broadcasted_iota(jnp.int32, (STEP, count), 0).astype(f32).astype(bf16)
    block = lax.div(local_idx, STEP)
    place = (local_idx - block * STEP).astype(f32)

    def hits(begin):
        own = jnp.where(block == begin // STEP, place, -1.0).astype(bf16)
        return jnp.where(row == own, jnp.ones_like(row), jnp.zeros_like(row))

    for begin in range(0, row_count, STEP):
        hit_ref[begin : begin + STEP, :] = hits(begin)
    copies[1].wait()
    out_ref[...] = jnp.dot(
        feat_ref[...], hit_ref[...], preferred_element_type=f32
    ).astype(bf16)
    for copy in copies[2:]:
        copy.wait()


def columns_body(feat_ref, slots_ref, prices_ref, columns_ref, turned_ref, weight_ref):
    for begin in range(0, feat_ref.shape[1], CHUNK):
        here = slice(begin, begin + CHUNK)
        feat32 = feat_ref[:, here].astype(f32)
        pair = jnp.concatenate([feat32, feat32], axis=0)
        last = jnp.concatenate([feat32, norm_rows(feat32, 3)], axis=0)
        columns_ref[0:128, here] = pair.astype(bf16)
        columns_ref[128:256, here] = last.astype(bf16)
        turned_ref[here, 0:128] = pair.T.astype(bf16)
        turned_ref[here, 128:256] = last.T.astype(bf16)
        weight = jnp.where(slot_mask(slots_ref[:, here]), prices_ref[:, here], 0.0)
        weight_ref[:, here] = stack2(weight)


def rows_body(parts, turned_ref, weight_ref, *refs):
    center_refs, (block_ref, center_ref, out_ref) = refs[:parts], refs[parts:]
    center = total_of(center_refs).astype(f32)
    center = jnp.concatenate(
        [*split3(center * FACTOR), norm_rows(center, 0)], axis=0
    ).astype(bf16)
    center_ref[...] = center
    row_count = turned_ref.shape[0]
    total = jnp.zeros(out_ref.shape, f32)

    def fold(begin):
        return product(
            weight_ref[:, pl.ds(begin, CHUNK)],
            block_ref[pl.ds(begin, CHUNK), :],
            block_ref[pl.ds(row_count + begin, CHUNK), :],
        )

    half = row_count // 2

    def visit(turn, total):
        first = pl.multiple_of(turn * half, half)
        for begin in range(0, half, CHUNK):
            high, low = kernel_parts(turned_ref[pl.ds(first + begin, CHUNK), :], center)
            block_ref[pl.ds(first + begin, CHUNK), :] = high
            block_ref[pl.ds(first + row_count + begin, CHUNK), :] = low
            if begin > 0:
                total += fold(first + begin - CHUNK)
        return total + fold(first + half - CHUNK)

    out_ref[...] = lax.fori_loop(0, 2, visit, total)


def turned_body(columns_ref, center_ref, block_ref):
    center = center_ref[...].astype(f32).T.astype(bf16)
    count = center.shape[0]
    half = columns_ref.shape[1] // 2

    def visit(turn, carry):
        first = pl.multiple_of(turn * half, half)
        for begin in range(0, half, CHUNK):
            here = pl.ds(first + begin, CHUNK)
            high, low = kernel_parts(center, columns_ref[:, here])
            block_ref[0:count, here] = high
            block_ref[count:, here] = low
        return carry

    lax.fori_loop(0, 2, visit, 0)


def apply_rows(scaled, turned_ref, slots_ref, out_ref):
    count, half = scaled.shape[1], turned_ref.shape[1] // 2
    stacked = stack2(scaled)

    def visit(turn, carry):
        here = pl.ds(pl.multiple_of(turn * half, half), half)
        value = product(stacked, turned_ref[0:count, here], turned_ref[count:, here])
        own = jnp.where(slot_mask(slots_ref[:, here]), value, 0.0)
        out_ref[:, here] = jnp.sum(own, axis=0, keepdims=True)
        return carry

    lax.fori_loop(0, 2, visit, 0)


def fold_rows(rows, block_ref, slots_ref, out_ref):
    row_count, count = slots_ref.shape[1], block_ref.shape[1]
    weight = jnp.where(slot_mask(slots_ref[...]), rows, 0.0)
    out_ref[:, 0:count] = product(
        stack2(weight), block_ref[0:row_count, :], block_ref[row_count:, :]
    )
    square = row_sum(weight * weight)
    out_ref[:, count : count + EXTRA] = spread(square)


def first_apply_body(parts, scale_over_root, *refs):
    first_refs = refs[:parts]
    scale_ref, slots_ref, turned_ref, target_ref, out_ref = refs[parts:]
    scale = scale_ref[...]
    target = scale * total_of(first_refs) * scale_over_root
    target_ref[...] = target
    out_ref[:, turned_ref.shape[1] :] = to_lanes(row_sum(target * target), 0)
    apply_rows(scale * target, turned_ref, slots_ref, out_ref)


def first_fold_body(parts, *refs):
    row_refs = refs[:parts]
    slots_ref, block_ref, rows_ref, norm_ref, out_ref = refs[parts:]
    row_count = slots_ref.shape[1]
    rows = total_of(row_refs)
    rows_ref[...] = rows
    norm_ref[...] = spread(from_lanes(rows[:, row_count:], 0))
    fold_rows(rows[:, 0:row_count], block_ref, slots_ref, out_ref)


def second_apply_body(parts, inv_rows, *refs):
    fold_refs = refs[:parts]
    (scale_ref, slots_ref, turned_ref, target_ref, norm_ref,
     residual_ref, step_ref, out_ref) = refs[parts:]
    row_count, count = turned_ref.shape[1], scale_ref.shape[1]
    folded = total_of(fold_refs)
    scale = scale_ref[...]
    target = target_ref[...]
    norm = norm_ref[...]
    applied = scale * folded[:, 0:count] * inv_rows + RIDGE * target
    step = norm / (folded[:, count:] * inv_rows + RIDGE * norm)
    residual = target - wide(step, count) * applied
    residual_ref[...] = residual
    step_ref[...] = step
    out_ref[:, row_count:] = to_lanes(row_sum(residual * residual), 0) + to_lanes(
        row_sum(residual * target), SLOTS
    )
    apply_rows(scale * residual, turned_ref, slots_ref, out_ref)


def second_fold_body(parts, *refs):
    row_refs = refs[:parts]
    slots_ref, block_ref, rows_ref, norm_ref, sums_ref, out_ref = refs[parts:]
    row_count = slots_ref.shape[1]
    latest = total_of(row_refs)
    norm = spread(from_lanes(latest[:, row_count:], 0))
    ratio = norm / norm_ref[...]
    sums_ref[:, 0:EXTRA] = norm
    sums_ref[:, EXTRA:] = spread(from_lanes(latest[:, row_count:], SLOTS))
    rows = latest[:, 0:row_count] + wide(ratio, row_count) * rows_ref[:, 0:row_count]
    fold_rows(rows, block_ref, slots_ref, out_ref)


def finish_body(parts, inv_rows, *refs):
    fold_refs = refs[:parts]
    (scale_ref, target_ref, residual_ref, step_ref, norm_ref, sums_ref,
     coefficients_ref, out_ref) = refs[parts:]
    count = scale_ref.shape[1]
    folded = total_of(fold_refs)
    target = target_ref[...]
    residual = residual_ref[...]
    first_norm = norm_ref[...]
    norm, cross = sums_ref[:, 0:EXTRA], sums_ref[:, EXTRA:]
    ratio = norm / first_norm
    direction = residual + wide(ratio, count) * target
    square = norm + 2.0 * ratio * cross + ratio * ratio * first_norm
    applied = scale_ref[...] * folded[:, 0:count] * inv_rows + RIDGE * direction
    step = wide(norm / (folded[:, count:] * inv_rows + RIDGE * square), count)
    coefficients_ref[...] = wide(step_ref[...], count) * target + step * direction
    out_ref[...] = residual - step * applied


def call(body, out_shape, *args, source=VMEM, flops=0, bytes_accessed=0, **more):
    return pl.pallas_call(
        body,
        out_shape=out_shape,
        in_specs=[source] * len(args),
        out_specs=jax.tree.map(lambda _: VMEM, out_shape),
        compiler_params=pltpu.CompilerParams(vmem_limit_bytes=36 * 1024 * 1024),
        cost_estimate=pl.CostEstimate(
            flops=flops, bytes_accessed=bytes_accessed, transcendentals=0
        ),
        **more,
    )(*args)


def exchange(value, axis, near_first=False):
    size = lax.axis_size(axis)
    parts = [value]
    stride = 1
    while stride < size:
        value = pair_total(parts)
        span = min(4, size // stride)
        side = 0 if stride == 1 else 1
        parts = [value]
        for offset in range(1, span):
            pairs = [(i, i ^ (offset * stride) ^ side) for i in range(size)]
            parts.insert(0, lax.ppermute(value, axis, pairs))
        if near_first and stride == 1:
            parts = parts[-2:] + parts[:-2]
        stride *= span
    return parts


def shaped(shape, dtype=f32):
    return jax.ShapeDtypeStruct(shape, dtype)


def per_device(features, prices, slots, center_idx, center_scale):
    depth, row_count = features.shape
    count = center_idx.shape[0]
    all_rows = row_count * lax.axis_size("dp")
    row_shape = shaped((1, row_count + EXTRA))
    fold_shape = shaped((SLOTS, count + EXTRA))
    vector = shaped((SLOTS, count))
    narrow = shaped((SLOTS, EXTRA))
    pass_cost = dict(flops=64 * row_count * count, bytes_accessed=4 * row_count * count)

    inputs = [
        pltpu.with_memory_space_constraint(array, pltpu.HBM)
        for array in (
            features,
            center_idx.reshape(1, count),
            slots.reshape(1, row_count),
            prices.reshape(1, row_count),
            center_scale.reshape(1, count),
        )
    ]
    features, slots, prices, scale, picked = call(
        pick_body,
        (
            shaped(features.shape, bf16),
            shaped((1, row_count), jnp.int32),
            shaped((1, row_count)),
            shaped((1, count)),
            shaped((depth, count), bf16),
        ),
        *inputs,
        source=HBM,
        scratch_shapes=[
            pltpu.VMEM((1, count), jnp.int32),
            pltpu.VMEM((row_count, count), bf16),
            pltpu.SemaphoreType.DMA((5,)),
        ],
    )
    centers = exchange(picked, "dp")
    columns, turned_columns, weight = call(
        columns_body,
        (
            shaped((DEPTH, row_count), bf16),
            shaped((row_count, DEPTH), bf16),
            shaped((16, row_count), bf16),
        ),
        features, slots, prices,
        flops=1000 * row_count,
        bytes_accessed=1024 * row_count,
    )
    block, center, first = call(
        partial(rows_body, len(centers)),
        (shaped((2 * row_count, count), bf16), shaped((DEPTH, count), bf16), vector),
        turned_columns, weight, *centers,
        **pass_cost,
    )
    firsts = exchange(first, "dp")
    turned = call(
        turned_body, shaped((2 * count, row_count), bf16), columns, center, **pass_cost
    )
    target, rows = call(
        partial(first_apply_body, len(firsts), 1.0 / math.sqrt(all_rows)),
        (vector, row_shape),
        *firsts, scale, slots, turned,
    )
    rows = exchange(rows, "centers")
    rows, norm, folded = call(
        partial(first_fold_body, len(rows)), (row_shape, narrow, fold_shape), *rows, slots, block
    )
    folds = exchange(folded, "dp")
    residual, step, latest = call(
        partial(second_apply_body, len(folds), 1.0 / all_rows),
        (vector, narrow, row_shape),
        *folds, scale, slots, turned, target, norm,
    )
    latest = exchange(latest, "centers", True)
    sums, folded = call(
        partial(second_fold_body, len(latest)),
        (shaped((SLOTS, 2 * EXTRA)), fold_shape),
        *latest, slots, block, rows, norm,
    )
    folds = exchange(folded, "dp")
    return call(
        partial(finish_body, len(folds), 1.0 / all_rows),
        (vector, vector),
        *folds, scale, target, residual, step, norm, sums,
    )


def solution(mesh):
    return jax.shard_map(
        per_device,
        mesh=mesh,
        in_specs=(P(None, "dp"), P("dp"), P("dp"), P("centers"), P("centers")),
        out_specs=(P(None, "centers"), P(None, "centers")),
        check_vma=False,
    )
```

```python
import math
from functools import partial

import jax
import jax.numpy as jnp
from jax import lax
from jax.experimental import pallas as pl
from jax.experimental.pallas import tpu as pltpu
from jax.sharding import PartitionSpec as P

SLOTS = 8
RIDGE = 0.5
CHUNK = 512
EXTRA = 128
DEPTH = 256
STEP = 256
FACTOR = math.log2(math.e) / 64.0
f32 = jnp.float32
bf16 = jnp.bfloat16
VMEM = pl.BlockSpec(memory_space=pltpu.VMEM)
HBM = pl.BlockSpec(memory_space=pltpu.HBM)


def split3(value):
    high = value.astype(bf16).astype(f32)
    rest = value - high
    mid = rest.astype(bf16).astype(f32)
    return high, mid, rest - mid


def stack2(value):
    high = value.astype(bf16).astype(f32)
    return jnp.concatenate([high, value - high], axis=0).astype(bf16)


def product(stacked, high_block, low_block):
    main = jnp.dot(stacked, high_block, preferred_element_type=f32)
    rest = jnp.dot(stacked[0:SLOTS], low_block, preferred_element_type=f32)
    return main[0:SLOTS] + (main[SLOTS:] + rest)


def slot_lanes(first):
    lane = lax.broadcasted_iota(jnp.int32, (SLOTS, EXTRA), 1)
    return lane == lax.broadcasted_iota(jnp.int32, (SLOTS, EXTRA), 0) + first


def to_lanes(column, first):
    return jnp.sum(jnp.where(slot_lanes(first), column, 0.0), axis=0, keepdims=True)


def from_lanes(row, first):
    return jnp.sum(jnp.where(slot_lanes(first), row, 0.0), axis=1, keepdims=True)


def spread(column):
    return jnp.broadcast_to(column, (SLOTS, EXTRA))


def wide(narrow, count):
    return jnp.concatenate([narrow] * (count // EXTRA), axis=1)


def pair_total(parts):
    while len(parts) > 1:
        parts = [parts[i] + parts[i + 1] for i in range(0, len(parts), 2)]
    return parts[0]


def total_of(refs):
    return pair_total([ref[...] for ref in refs])


def row_sum(value):
    return jnp.sum(value, axis=1, keepdims=True)


def slot_mask(slots):
    row = lax.broadcasted_iota(jnp.int32, (SLOTS, slots.shape[1]), 0)
    return slots == row


def norm_rows(feat32, base):
    half = (-0.5 * FACTOR) * jnp.sum(feat32 * feat32, axis=0, keepdims=True)
    row = lax.broadcasted_iota(jnp.int32, (feat32.shape[0], feat32.shape[1]), 0)
    extra = jnp.where(row < 6, 1.0, 0.0)
    for place, part in enumerate(split3(half)):
        extra = jnp.where(row == base + place, part, extra)
    return extra


def kernel_parts(exponent):
    value = jnp.exp2(exponent)
    high = value.astype(bf16)
    return high, (value - high.astype(f32)).astype(bf16)


def pick_body(feat_hbm, idx_hbm, slots_hbm, prices_hbm, scale_hbm, *refs):
    feat_ref, slots_ref, prices_ref, scale_ref, out_ref, idx_ref, hit_ref, sems = refs
    row_count = feat_ref.shape[1]
    count = out_ref.shape[1]
    sources = (idx_hbm, feat_hbm, slots_hbm, prices_hbm, scale_hbm)
    targets = (idx_ref, feat_ref, slots_ref, prices_ref, scale_ref)
    copies = [
        pltpu.make_async_copy(source, target, sems.at[place])
        for place, (source, target) in enumerate(zip(sources, targets))
    ]
    for copy in copies:
        copy.start()
    copies[0].wait()
    local_idx = idx_ref[...] - lax.axis_index("dp") * row_count
    row = lax.broadcasted_iota(jnp.int32, (STEP, count), 0).astype(f32).astype(bf16)
    block = lax.div(local_idx, STEP)
    place = (local_idx - block * STEP).astype(f32)

    def hits(begin):
        own = jnp.where(block == begin // STEP, place, -1.0).astype(bf16)
        return jnp.where(row == own, jnp.ones_like(row), jnp.zeros_like(row))

    for begin in range(0, row_count, STEP):
        hit_ref[begin : begin + STEP, :] = hits(begin)
    copies[1].wait()
    out_ref[...] = jnp.dot(
        feat_ref[...], hit_ref[...], preferred_element_type=f32
    ).astype(bf16)
    for copy in copies[2:]:
        copy.wait()


def columns_body(feat_ref, slots_ref, prices_ref, columns_ref, turned_ref, weight_ref):
    for begin in range(0, feat_ref.shape[1], CHUNK):
        here = slice(begin, begin + CHUNK)
        feat32 = feat_ref[:, here].astype(f32)
        pair = jnp.concatenate([feat32, feat32], axis=0)
        last = jnp.concatenate([feat32, norm_rows(feat32, 3)], axis=0)
        columns_ref[0:128, here] = pair.astype(bf16)
        columns_ref[128:256, here] = last.astype(bf16)
        turned_ref[here, 0:128] = pair.T.astype(bf16)
        turned_ref[here, 128:256] = last.T.astype(bf16)
        weight = jnp.where(slot_mask(slots_ref[:, here]), prices_ref[:, here], 0.0)
        weight_ref[:, here] = stack2(weight)


def rows_body(parts, turned_ref, weight_ref, *refs):
    center_refs, (block_ref, center_ref, out_ref) = refs[:parts], refs[parts:]
    center = total_of(center_refs).astype(f32)
    center = jnp.concatenate(
        [*split3(center * FACTOR), norm_rows(center, 0)], axis=0
    ).astype(bf16)
    center_ref[...] = center
    row_count = turned_ref.shape[0]
    total = jnp.zeros(out_ref.shape, f32)

    def fold(begin):
        end = begin + CHUNK
        return product(
            weight_ref[:, begin:end],
            block_ref[begin:end, :],
            block_ref[row_count + begin : row_count + end, :],
        )

    def inner(begin):
        return jnp.dot(
            turned_ref[begin : begin + CHUNK, :], center, preferred_element_type=f32
        )

    ahead = inner(0)
    for begin in range(0, row_count, CHUNK):
        exponent = ahead
        if begin + CHUNK < row_count:
            ahead = inner(begin + CHUNK)
        high, low = kernel_parts(exponent)
        block_ref[begin : begin + CHUNK, :] = high
        block_ref[row_count + begin : row_count + begin + CHUNK, :] = low
        if begin > 0:
            total += fold(begin - CHUNK)
    out_ref[...] = total + fold(row_count - CHUNK)


def turned_body(columns_ref, center_ref, block_ref):
    center = center_ref[...].astype(f32).T.astype(bf16)
    count, row_count = center.shape[0], columns_ref.shape[1]

    def inner(begin):
        return jnp.dot(
            center, columns_ref[:, begin : begin + CHUNK], preferred_element_type=f32
        )

    ahead = inner(0)
    for begin in range(0, row_count, CHUNK):
        exponent = ahead
        if begin + CHUNK < row_count:
            ahead = inner(begin + CHUNK)
        high, low = kernel_parts(exponent)
        block_ref[0:count, begin : begin + CHUNK] = high
        block_ref[count:, begin : begin + CHUNK] = low


def apply_rows(scaled, turned_ref, slots_ref, out_ref):
    count, row_count = scaled.shape[1], turned_ref.shape[1]
    value = product(stack2(scaled), turned_ref[0:count, :], turned_ref[count:, :])
    own = jnp.where(slot_mask(slots_ref[...]), value, 0.0)
    out_ref[:, 0:row_count] = jnp.sum(own, axis=0, keepdims=True)


def fold_rows(rows, block_ref, slots_ref, out_ref):
    row_count, count = slots_ref.shape[1], block_ref.shape[1]
    weight = jnp.where(slot_mask(slots_ref[...]), rows, 0.0)
    out_ref[:, 0:count] = product(
        stack2(weight), block_ref[0:row_count, :], block_ref[row_count:, :]
    )
    square = row_sum(weight * weight)
    out_ref[:, count : count + EXTRA] = spread(square)


def first_apply_body(parts, scale_over_root, *refs):
    first_refs = refs[:parts]
    scale_ref, slots_ref, turned_ref, target_ref, out_ref = refs[parts:]
    scale = scale_ref[...]
    target = scale * total_of(first_refs) * scale_over_root
    target_ref[...] = target
    out_ref[:, turned_ref.shape[1] :] = to_lanes(row_sum(target * target), 0)
    apply_rows(scale * target, turned_ref, slots_ref, out_ref)


def first_fold_body(parts, *refs):
    row_refs = refs[:parts]
    slots_ref, block_ref, rows_ref, norm_ref, out_ref = refs[parts:]
    row_count = slots_ref.shape[1]
    rows = total_of(row_refs)
    rows_ref[...] = rows
    norm_ref[...] = spread(from_lanes(rows[:, row_count:], 0))
    fold_rows(rows[:, 0:row_count], block_ref, slots_ref, out_ref)


def second_apply_body(parts, inv_rows, *refs):
    fold_refs = refs[:parts]
    (scale_ref, slots_ref, turned_ref, target_ref, norm_ref,
     residual_ref, step_ref, out_ref) = refs[parts:]
    row_count, count = turned_ref.shape[1], scale_ref.shape[1]
    folded = total_of(fold_refs)
    scale = scale_ref[...]
    target = target_ref[...]
    norm = norm_ref[...]
    applied = scale * folded[:, 0:count] * inv_rows + RIDGE * target
    step = norm / (folded[:, count:] * inv_rows + RIDGE * norm)
    residual = target - wide(step, count) * applied
    residual_ref[...] = residual
    step_ref[...] = step
    out_ref[:, row_count:] = to_lanes(row_sum(residual * residual), 0) + to_lanes(
        row_sum(residual * target), SLOTS
    )
    apply_rows(scale * residual, turned_ref, slots_ref, out_ref)


def second_fold_body(parts, *refs):
    row_refs = refs[:parts]
    slots_ref, block_ref, rows_ref, norm_ref, sums_ref, out_ref = refs[parts:]
    row_count = slots_ref.shape[1]
    latest = total_of(row_refs)
    norm = spread(from_lanes(latest[:, row_count:], 0))
    ratio = norm / norm_ref[...]
    sums_ref[:, 0:EXTRA] = norm
    sums_ref[:, EXTRA:] = spread(from_lanes(latest[:, row_count:], SLOTS))
    rows = latest[:, 0:row_count] + wide(ratio, row_count) * rows_ref[:, 0:row_count]
    fold_rows(rows, block_ref, slots_ref, out_ref)


def finish_body(parts, inv_rows, *refs):
    fold_refs = refs[:parts]
    (scale_ref, target_ref, residual_ref, step_ref, norm_ref, sums_ref,
     coefficients_ref, out_ref) = refs[parts:]
    count = scale_ref.shape[1]
    folded = total_of(fold_refs)
    target = target_ref[...]
    residual = residual_ref[...]
    first_norm = norm_ref[...]
    norm, cross = sums_ref[:, 0:EXTRA], sums_ref[:, EXTRA:]
    ratio = norm / first_norm
    direction = residual + wide(ratio, count) * target
    square = norm + 2.0 * ratio * cross + ratio * ratio * first_norm
    applied = scale_ref[...] * folded[:, 0:count] * inv_rows + RIDGE * direction
    step = wide(norm / (folded[:, count:] * inv_rows + RIDGE * square), count)
    coefficients_ref[...] = wide(step_ref[...], count) * target + step * direction
    out_ref[...] = residual - step * applied


def call(body, out_shape, *args, source=VMEM, flops=0, bytes_accessed=0, **more):
    return pl.pallas_call(
        body,
        out_shape=out_shape,
        in_specs=[source] * len(args),
        out_specs=jax.tree.map(lambda _: VMEM, out_shape),
        compiler_params=pltpu.CompilerParams(vmem_limit_bytes=36 * 1024 * 1024),
        cost_estimate=pl.CostEstimate(
            flops=flops, bytes_accessed=bytes_accessed, transcendentals=0
        ),
        **more,
    )(*args)


def exchange(value, axis, near_first=False):
    size = lax.axis_size(axis)
    parts = [value]
    stride = 1
    while stride < size:
        value = pair_total(parts)
        span = min(4, size // stride)
        side = 0 if stride == 1 else 1
        parts = [value]
        for offset in range(1, span):
            pairs = [(i, i ^ (offset * stride) ^ side) for i in range(size)]
            parts.insert(0, lax.ppermute(value, axis, pairs))
        if near_first and stride == 1:
            parts = parts[-2:] + parts[:-2]
        stride *= span
    return parts


def shaped(shape, dtype=f32):
    return jax.ShapeDtypeStruct(shape, dtype)


def per_device(features, prices, slots, center_idx, center_scale):
    depth, row_count = features.shape
    count = center_idx.shape[0]
    all_rows = row_count * lax.axis_size("dp")
    row_shape = shaped((1, row_count + EXTRA))
    fold_shape = shaped((SLOTS, count + EXTRA))
    vector = shaped((SLOTS, count))
    narrow = shaped((SLOTS, EXTRA))
    pass_cost = dict(flops=64 * row_count * count, bytes_accessed=4 * row_count * count)

    inputs = [
        pltpu.with_memory_space_constraint(array, pltpu.HBM)
        for array in (
            features,
            center_idx.reshape(1, count),
            slots.reshape(1, row_count),
            prices.reshape(1, row_count),
            center_scale.reshape(1, count),
        )
    ]
    features, slots, prices, scale, picked = call(
        pick_body,
        (
            shaped(features.shape, bf16),
            shaped((1, row_count), jnp.int32),
            shaped((1, row_count)),
            shaped((1, count)),
            shaped((depth, count), bf16),
        ),
        *inputs,
        source=HBM,
        scratch_shapes=[
            pltpu.VMEM((1, count), jnp.int32),
            pltpu.VMEM((row_count, count), bf16),
            pltpu.SemaphoreType.DMA((5,)),
        ],
    )
    centers = exchange(picked, "dp")
    columns, turned_columns, weight = call(
        columns_body,
        (
            shaped((DEPTH, row_count), bf16),
            shaped((row_count, DEPTH), bf16),
            shaped((16, row_count), bf16),
        ),
        features, slots, prices,
        flops=1000 * row_count,
        bytes_accessed=1024 * row_count,
    )
    block, center, first = call(
        partial(rows_body, len(centers)),
        (shaped((2 * row_count, count), bf16), shaped((DEPTH, count), bf16), vector),
        turned_columns, weight, *centers,
        **pass_cost,
    )
    firsts = exchange(first, "dp")
    turned = call(
        turned_body, shaped((2 * count, row_count), bf16), columns, center, **pass_cost
    )
    target, rows = call(
        partial(first_apply_body, len(firsts), 1.0 / math.sqrt(all_rows)),
        (vector, row_shape),
        *firsts, scale, slots, turned,
    )
    rows = exchange(rows, "centers")
    rows, norm, folded = call(
        partial(first_fold_body, len(rows)), (row_shape, narrow, fold_shape), *rows, slots, block
    )
    folds = exchange(folded, "dp")
    residual, step, latest = call(
        partial(second_apply_body, len(folds), 1.0 / all_rows),
        (vector, narrow, row_shape),
        *folds, scale, slots, turned, target, norm,
    )
    latest = exchange(latest, "centers", True)
    sums, folded = call(
        partial(second_fold_body, len(latest)),
        (shaped((SLOTS, 2 * EXTRA)), fold_shape),
        *latest, slots, block, rows, norm,
    )
    folds = exchange(folded, "dp")
    return call(
        partial(finish_body, len(folds), 1.0 / all_rows),
        (vector, vector),
        *folds, scale, target, residual, step, norm, sums,
    )


def solution(mesh):
    return jax.shard_map(
        per_device,
        mesh=mesh,
        in_specs=(P(None, "dp"), P("dp"), P("dp"), P("centers"), P("centers")),
        out_specs=(P(None, "centers"), P(None, "centers")),
        check_vma=False,
    )
```

```python
import math
from functools import partial

import jax
import jax.numpy as jnp
from jax import lax
from jax.experimental import pallas as pl
from jax.experimental.pallas import tpu as pltpu
from jax.sharding import PartitionSpec as P

SLOTS = 8
RIDGE = 0.5
CHUNK = 512
EXTRA = 128
DEPTH = 256
STEP = 256
FACTOR = math.log2(math.e) / 64.0
f32 = jnp.float32
bf16 = jnp.bfloat16
VMEM = pl.BlockSpec(memory_space=pltpu.VMEM)
HBM = pl.BlockSpec(memory_space=pltpu.HBM)


def split3(value):
    high = value.astype(bf16).astype(f32)
    rest = value - high
    mid = rest.astype(bf16).astype(f32)
    return high, mid, rest - mid


def stack2(value):
    high = value.astype(bf16).astype(f32)
    return jnp.concatenate([high, value - high], axis=0).astype(bf16)


def product(stacked, high_block, low_block):
    main = jnp.dot(stacked, high_block, preferred_element_type=f32)
    rest = jnp.dot(stacked[0:SLOTS], low_block, preferred_element_type=f32)
    return main[0:SLOTS] + (main[SLOTS:] + rest)


def slot_lanes(first):
    lane = lax.broadcasted_iota(jnp.int32, (SLOTS, EXTRA), 1)
    return lane == lax.broadcasted_iota(jnp.int32, (SLOTS, EXTRA), 0) + first


def to_lanes(column, first):
    return jnp.sum(jnp.where(slot_lanes(first), column, 0.0), axis=0, keepdims=True)


def from_lanes(row, first):
    return jnp.sum(jnp.where(slot_lanes(first), row, 0.0), axis=1, keepdims=True)


def spread(column):
    return jnp.broadcast_to(column, (SLOTS, EXTRA))


def wide(narrow, count):
    return jnp.concatenate([narrow] * (count // EXTRA), axis=1)


def pair_total(parts):
    while len(parts) > 1:
        parts = [parts[i] + parts[i + 1] for i in range(0, len(parts), 2)]
    return parts[0]


def total_of(refs):
    return pair_total([ref[...] for ref in refs])


def row_sum(value):
    return jnp.sum(value, axis=1, keepdims=True)


def slot_mask(slots):
    row = lax.broadcasted_iota(jnp.int32, (SLOTS, slots.shape[1]), 0)
    return slots == row


def norm_rows(feat32, base):
    half = (-0.5 * FACTOR) * jnp.sum(feat32 * feat32, axis=0, keepdims=True)
    row = lax.broadcasted_iota(jnp.int32, (feat32.shape[0], feat32.shape[1]), 0)
    extra = jnp.where(row < 6, 1.0, 0.0)
    for place, part in enumerate(split3(half)):
        extra = jnp.where(row == base + place, part, extra)
    return extra


def kernel_parts(exponent):
    value = jnp.exp2(exponent)
    high = value.astype(bf16)
    return high, (value - high.astype(f32)).astype(bf16)


def pick_body(feat_hbm, idx_hbm, slots_hbm, prices_hbm, scale_hbm, *refs):
    feat_ref, slots_ref, prices_ref, scale_ref, out_ref, idx_ref, hit_ref, sems = refs
    row_count = feat_ref.shape[1]
    count = out_ref.shape[1]
    sources = (idx_hbm, feat_hbm, slots_hbm, prices_hbm, scale_hbm)
    targets = (idx_ref, feat_ref, slots_ref, prices_ref, scale_ref)
    copies = [
        pltpu.make_async_copy(source, target, sems.at[place])
        for place, (source, target) in enumerate(zip(sources, targets))
    ]
    for copy in copies:
        copy.start()
    copies[0].wait()
    local_idx = idx_ref[...] - lax.axis_index("dp") * row_count
    row = lax.broadcasted_iota(jnp.int32, (STEP, count), 0).astype(f32).astype(bf16)
    block = lax.div(local_idx, STEP)
    place = (local_idx - block * STEP).astype(f32)

    def hits(begin):
        own = jnp.where(block == begin // STEP, place, -1.0).astype(bf16)
        return jnp.where(row == own, jnp.ones_like(row), jnp.zeros_like(row))

    for begin in range(0, row_count, STEP):
        hit_ref[begin : begin + STEP, :] = hits(begin)
    copies[1].wait()
    out_ref[...] = jnp.dot(
        feat_ref[...], hit_ref[...], preferred_element_type=f32
    ).astype(bf16)
    for copy in copies[2:]:
        copy.wait()


def columns_body(feat_ref, slots_ref, prices_ref, columns_ref, turned_ref, weight_ref):
    for begin in range(0, feat_ref.shape[1], CHUNK):
        here = slice(begin, begin + CHUNK)
        feat32 = feat_ref[:, here].astype(f32)
        pair = jnp.concatenate([feat32, feat32], axis=0)
        last = jnp.concatenate([feat32, norm_rows(feat32, 3)], axis=0)
        columns_ref[0:128, here] = pair.astype(bf16)
        columns_ref[128:256, here] = last.astype(bf16)
        turned_ref[here, 0:128] = pair.T.astype(bf16)
        turned_ref[here, 128:256] = last.T.astype(bf16)
        weight = jnp.where(slot_mask(slots_ref[:, here]), prices_ref[:, here], 0.0)
        weight_ref[:, here] = stack2(weight)


def rows_body(parts, turned_ref, weight_ref, *refs):
    center_refs, (block_ref, center_ref, out_ref) = refs[:parts], refs[parts:]
    center = total_of(center_refs).astype(f32)
    center = jnp.concatenate(
        [*split3(center * FACTOR), norm_rows(center, 0)], axis=0
    ).astype(bf16)
    center_ref[...] = center
    row_count = turned_ref.shape[0]
    total = jnp.zeros(out_ref.shape, f32)

    def fold(begin):
        end = begin + CHUNK
        return product(
            weight_ref[:, begin:end],
            block_ref[begin:end, :],
            block_ref[row_count + begin : row_count + end, :],
        )

    def inner(begin):
        return jnp.dot(
            turned_ref[begin : begin + CHUNK, :], center, preferred_element_type=f32
        )

    ahead = inner(0)
    for begin in range(0, row_count, CHUNK):
        exponent = ahead
        if begin + CHUNK < row_count:
            ahead = inner(begin + CHUNK)
        high, low = kernel_parts(exponent)
        block_ref[begin : begin + CHUNK, :] = high
        block_ref[row_count + begin : row_count + begin + CHUNK, :] = low
        if begin > 0:
            total += fold(begin - CHUNK)
    out_ref[...] = total + fold(row_count - CHUNK)


def turned_body(columns_ref, center_ref, block_ref):
    center = center_ref[...].astype(f32).T.astype(bf16)
    count, row_count = center.shape[0], columns_ref.shape[1]

    def inner(begin):
        return jnp.dot(
            center, columns_ref[:, begin : begin + CHUNK], preferred_element_type=f32
        )

    ahead = inner(0)
    for begin in range(0, row_count, CHUNK):
        exponent = ahead
        if begin + CHUNK < row_count:
            ahead = inner(begin + CHUNK)
        high, low = kernel_parts(exponent)
        block_ref[0:count, begin : begin + CHUNK] = high
        block_ref[count:, begin : begin + CHUNK] = low


def apply_rows(scaled, turned_ref, slots_ref, out_ref):
    count, row_count = scaled.shape[1], turned_ref.shape[1]
    value = product(stack2(scaled), turned_ref[0:count, :], turned_ref[count:, :])
    own = jnp.where(slot_mask(slots_ref[...]), value, 0.0)
    out_ref[:, 0:row_count] = jnp.sum(own, axis=0, keepdims=True)


def fold_rows(rows, block_ref, slots_ref, out_ref):
    row_count, count = slots_ref.shape[1], block_ref.shape[1]
    weight = jnp.where(slot_mask(slots_ref[...]), rows, 0.0)
    out_ref[:, 0:count] = product(
        stack2(weight), block_ref[0:row_count, :], block_ref[row_count:, :]
    )
    square = row_sum(weight * weight)
    out_ref[:, count : count + EXTRA] = spread(square)


def first_apply_body(parts, scale_over_root, *refs):
    first_refs = refs[:parts]
    scale_ref, slots_ref, turned_ref, target_ref, out_ref = refs[parts:]
    scale = scale_ref[...]
    target = scale * total_of(first_refs) * scale_over_root
    target_ref[...] = target
    out_ref[:, turned_ref.shape[1] :] = to_lanes(row_sum(target * target), 0)
    apply_rows(scale * target, turned_ref, slots_ref, out_ref)


def first_fold_body(parts, *refs):
    row_refs = refs[:parts]
    slots_ref, block_ref, rows_ref, norm_ref, out_ref = refs[parts:]
    row_count = slots_ref.shape[1]
    rows = total_of(row_refs)
    rows_ref[...] = rows
    norm_ref[...] = spread(from_lanes(rows[:, row_count:], 0))
    fold_rows(rows[:, 0:row_count], block_ref, slots_ref, out_ref)


def second_apply_body(parts, inv_rows, *refs):
    fold_refs = refs[:parts]
    (scale_ref, slots_ref, turned_ref, target_ref, norm_ref,
     state_ref, step_ref, out_ref) = refs[parts:]
    row_count, count = turned_ref.shape[1], scale_ref.shape[1]
    folded = total_of(fold_refs)
    scale = scale_ref[...]
    target = target_ref[...]
    norm = norm_ref[...]
    applied = scale * folded[:, 0:count] * inv_rows + RIDGE * target
    step = norm / (folded[:, count:] * inv_rows + RIDGE * norm)
    residual = target - wide(step, count) * applied
    state_ref[0:SLOTS, :] = target
    state_ref[SLOTS:, :] = residual
    step_ref[...] = step
    out_ref[:, row_count:] = to_lanes(row_sum(residual * residual), 0) + to_lanes(
        row_sum(residual * target), SLOTS
    )
    apply_rows(scale * residual, turned_ref, slots_ref, out_ref)


def second_fold_body(parts, *refs):
    row_refs = refs[:parts]
    slots_ref, block_ref, rows_ref, norm_ref, sums_ref, out_ref = refs[parts:]
    row_count = slots_ref.shape[1]
    latest = total_of(row_refs)
    norm = spread(from_lanes(latest[:, row_count:], 0))
    ratio = norm / norm_ref[...]
    sums_ref[:, 0:EXTRA] = norm
    sums_ref[:, EXTRA:] = spread(from_lanes(latest[:, row_count:], SLOTS))
    rows = latest[:, 0:row_count] + wide(ratio, row_count) * rows_ref[:, 0:row_count]
    fold_rows(rows, block_ref, slots_ref, out_ref)


def finish_body(parts, inv_rows, *refs):
    fold_refs = refs[:parts]
    (scale_ref, state_ref, step_ref, norm_ref, sums_ref,
     coefficients_ref, out_ref) = refs[parts:]
    count = scale_ref.shape[1]
    folded = total_of(fold_refs)
    target, residual = state_ref[0:SLOTS, :], state_ref[SLOTS:, :]
    first_norm = norm_ref[...]
    norm, cross = sums_ref[:, 0:EXTRA], sums_ref[:, EXTRA:]
    ratio = norm / first_norm
    direction = residual + wide(ratio, count) * target
    square = norm + 2.0 * ratio * cross + ratio * ratio * first_norm
    applied = scale_ref[...] * folded[:, 0:count] * inv_rows + RIDGE * direction
    step = wide(norm / (folded[:, count:] * inv_rows + RIDGE * square), count)
    coefficients_ref[...] = wide(step_ref[...], count) * target + step * direction
    out_ref[...] = residual - step * applied


def call(body, out_shape, *args, sources=None, flops=0, bytes_accessed=0, **more):
    return pl.pallas_call(
        body,
        out_shape=out_shape,
        in_specs=sources or [VMEM] * len(args),
        out_specs=jax.tree.map(lambda _: VMEM, out_shape),
        compiler_params=pltpu.CompilerParams(vmem_limit_bytes=36 * 1024 * 1024),
        cost_estimate=pl.CostEstimate(
            flops=flops, bytes_accessed=bytes_accessed, transcendentals=0
        ),
        **more,
    )(*args)


def exchange(value, axis):
    size = lax.axis_size(axis)
    parts = [value]
    stride = 1
    while stride < size:
        value = pair_total(parts)
        span = min(4, size // stride)
        side = 0 if stride == 1 else 1
        parts = [value]
        for offset in range(1, span):
            pairs = [(i, i ^ (offset * stride) ^ side) for i in range(size)]
            parts.insert(0, lax.ppermute(value, axis, pairs))
        stride *= span
    return parts


def pairs_over(target_of):
    groups, count = lax.axis_size("dp"), lax.axis_size("centers")
    pairs = []
    for group in range(groups):
        for place in range(count):
            to_group, to_place = target_of(group, place)
            pairs.append((group * count + place, to_group * count + to_place))
    return pairs


def moved(value, target_of):
    return lax.ppermute(value, ("dp", "centers"), pairs_over(target_of))


def across(group, place):
    return 1 - group, place ^ 1


def beside(group, place):
    return group, place ^ group


def outward(group, place):
    return 1 - group, place ^ (1 - group)


def homeward(group, place):
    return 1 - group, place ^ group


def shaped(shape, dtype=f32):
    return jax.ShapeDtypeStruct(shape, dtype)


def per_device(features, prices, slots, center_idx, center_scale):
    depth, row_count = features.shape
    count = center_idx.shape[0]
    all_rows = row_count * lax.axis_size("dp")
    row_shape = shaped((1, row_count + EXTRA))
    fold_shape = shaped((SLOTS, count + EXTRA))
    vector = shaped((SLOTS, count))
    narrow = shaped((SLOTS, EXTRA))
    pass_cost = dict(flops=64 * row_count * count, bytes_accessed=4 * row_count * count)

    crossed = lax.axis_size("dp") == 2

    def in_place(value):
        return moved(value, beside) if crossed else value

    def share(value):
        return [moved(value, across), value] if crossed else exchange(value, "dp")

    inputs = [
        pltpu.with_memory_space_constraint(array, pltpu.HBM)
        for array in (
            features,
            center_idx.reshape(1, count),
            slots.reshape(1, row_count),
            prices.reshape(1, row_count),
            center_scale.reshape(1, count),
        )
    ]
    features, slots, prices, own_scale, picked = call(
        pick_body,
        (
            shaped(features.shape, bf16),
            shaped((1, row_count), jnp.int32),
            shaped((1, row_count)),
            shaped((1, count)),
            shaped((depth, count), bf16),
        ),
        *inputs,
        sources=[HBM] * 5,
        scratch_shapes=[
            pltpu.VMEM((1, count), jnp.int32),
            pltpu.VMEM((row_count, count), bf16),
            pltpu.SemaphoreType.DMA((5,)),
        ],
    )
    if crossed:
        centers = [moved(picked, outward), moved(picked, beside)]
    else:
        centers = exchange(picked, "dp")
    scale = in_place(own_scale)
    columns, turned_columns, weight = call(
        columns_body,
        (
            shaped((DEPTH, row_count), bf16),
            shaped((row_count, DEPTH), bf16),
            shaped((16, row_count), bf16),
        ),
        features, slots, prices,
        flops=1000 * row_count,
        bytes_accessed=1024 * row_count,
    )
    block, center, first = call(
        partial(rows_body, len(centers)),
        (shaped((2 * row_count, count), bf16), shaped((DEPTH, count), bf16), vector),
        turned_columns, weight, *centers,
        **pass_cost,
    )
    firsts = share(first)
    turned = call(
        turned_body, shaped((2 * count, row_count), bf16), columns, center, **pass_cost
    )
    target, rows = call(
        partial(first_apply_body, len(firsts), 1.0 / math.sqrt(all_rows)),
        (vector, row_shape),
        *firsts, scale, slots, turned,
    )
    rows = exchange(rows, "centers")
    rows, norm, folded = call(
        partial(first_fold_body, len(rows)), (row_shape, narrow, fold_shape), *rows, slots, block
    )
    folds = share(folded)
    state, step, latest = call(
        partial(second_apply_body, len(folds), 1.0 / all_rows),
        (shaped((2 * SLOTS, count)), narrow, row_shape),
        *folds, scale, slots, turned, target, norm,
    )
    latest = exchange(latest, "centers")
    sums, folded = call(
        partial(second_fold_body, len(latest)),
        (shaped((SLOTS, 2 * EXTRA)), fold_shape),
        *latest, slots, block, rows, norm,
    )
    if crossed:
        folds = [moved(folded, homeward), moved(folded, beside)]
    else:
        folds = exchange(folded, "dp")
    return call(
        partial(finish_body, len(folds), 1.0 / all_rows),
        (vector, vector),
        *folds, own_scale, in_place(state), step, norm, sums,
    )


def solution(mesh):
    return jax.shard_map(
        per_device,
        mesh=mesh,
        in_specs=(P(None, "dp"), P("dp"), P("dp"), P("centers"), P("centers")),
        out_specs=(P(None, "centers"), P(None, "centers")),
        check_vma=False,
    )
```

```python
import math
from functools import partial

import jax
import jax.numpy as jnp
from jax import lax
from jax.experimental import pallas as pl
from jax.experimental.pallas import tpu as pltpu
from jax.sharding import PartitionSpec as P

SLOTS = 8
RIDGE = 0.5
CHUNK = 512
EXTRA = 128
DEPTH = 256
STEP = 256
FACTOR = math.log2(math.e) / 64.0
f32 = jnp.float32
bf16 = jnp.bfloat16
VMEM = pl.BlockSpec(memory_space=pltpu.VMEM)
HBM = pl.BlockSpec(memory_space=pltpu.HBM)


def split3(value):
    high = value.astype(bf16).astype(f32)
    rest = value - high
    mid = rest.astype(bf16).astype(f32)
    return high, mid, rest - mid


def stack2(value):
    high = value.astype(bf16).astype(f32)
    return jnp.concatenate([high, value - high], axis=0).astype(bf16)


def product(stacked, high_block, low_block):
    main = jnp.dot(stacked, high_block, preferred_element_type=f32)
    rest = jnp.dot(stacked[0:SLOTS], low_block, preferred_element_type=f32)
    return main[0:SLOTS] + (main[SLOTS:] + rest)


def slot_lanes(first):
    lane = lax.broadcasted_iota(jnp.int32, (SLOTS, EXTRA), 1)
    return lane == lax.broadcasted_iota(jnp.int32, (SLOTS, EXTRA), 0) + first


def to_lanes(column, first):
    return jnp.sum(jnp.where(slot_lanes(first), column, 0.0), axis=0, keepdims=True)


def from_lanes(row, first):
    return jnp.sum(jnp.where(slot_lanes(first), row, 0.0), axis=1, keepdims=True)


def spread(column):
    return jnp.broadcast_to(column, (SLOTS, EXTRA))


def wide(narrow, count):
    return jnp.concatenate([narrow] * (count // EXTRA), axis=1)


def pair_total(parts):
    while len(parts) > 1:
        parts = [parts[i] + parts[i + 1] for i in range(0, len(parts), 2)]
    return parts[0]


def total_of(refs):
    return pair_total([ref[...] for ref in refs])


def resident(moved, own):
    return moved + own * (lax.axis_index("dp") == 0).astype(own.dtype)


def home_total(refs):
    far, moved, own = (ref[...].astype(f32) for ref in refs)
    return far + resident(moved, own)


def row_sum(value):
    return jnp.sum(value, axis=1, keepdims=True)


def slot_mask(slots):
    row = lax.broadcasted_iota(jnp.int32, (SLOTS, slots.shape[1]), 0)
    return slots == row


def norm_rows(feat32, base):
    half = (-0.5 * FACTOR) * jnp.sum(feat32 * feat32, axis=0, keepdims=True)
    row = lax.broadcasted_iota(jnp.int32, (feat32.shape[0], feat32.shape[1]), 0)
    extra = jnp.where(row < 6, 1.0, 0.0)
    for place, part in enumerate(split3(half)):
        extra = jnp.where(row == base + place, part, extra)
    return extra


def kernel_parts(exponent):
    value = jnp.exp2(exponent)
    high = value.astype(bf16)
    return high, (value - high.astype(f32)).astype(bf16)


def pick_body(feat_hbm, idx_hbm, slots_hbm, prices_hbm, scale_hbm, *refs):
    feat_ref, slots_ref, prices_ref, scale_ref, out_ref, idx_ref, hit_ref, sems = refs
    row_count = feat_ref.shape[1]
    count = out_ref.shape[1]
    sources = (idx_hbm, feat_hbm, slots_hbm, prices_hbm, scale_hbm)
    targets = (idx_ref, feat_ref, slots_ref, prices_ref, scale_ref)
    copies = [
        pltpu.make_async_copy(source, target, sems.at[place])
        for place, (source, target) in enumerate(zip(sources, targets))
    ]
    for copy in copies:
        copy.start()
    copies[0].wait()
    local_idx = idx_ref[...] - lax.axis_index("dp") * row_count
    row = lax.broadcasted_iota(jnp.int32, (STEP, count), 0).astype(f32).astype(bf16)
    block = lax.div(local_idx, STEP)
    place = (local_idx - block * STEP).astype(f32)

    def hits(begin):
        own = jnp.where(block == begin // STEP, place, -1.0).astype(bf16)
        return jnp.where(row == own, jnp.ones_like(row), jnp.zeros_like(row))

    for begin in range(0, row_count, STEP):
        hit_ref[begin : begin + STEP, :] = hits(begin)
    copies[1].wait()
    picked = jnp.dot(feat_ref[...], hit_ref[...], preferred_element_type=f32)
    for copy in copies[2:]:
        copy.wait()
    row = lax.broadcasted_iota(jnp.int32, (16, count), 0)
    extra = jnp.zeros((16, count), f32)
    for place, part in enumerate(split3(scale_ref[...])):
        extra = jnp.where(row == place, part, extra)
    out_ref[...] = jnp.concatenate([picked, extra], axis=0).astype(bf16)


def columns_body(feat_ref, slots_ref, prices_ref, columns_ref, turned_ref, weight_ref):
    for begin in range(0, feat_ref.shape[1], CHUNK):
        here = slice(begin, begin + CHUNK)
        feat32 = feat_ref[:, here].astype(f32)
        pair = jnp.concatenate([feat32, feat32], axis=0)
        last = jnp.concatenate([feat32, norm_rows(feat32, 3)], axis=0)
        columns_ref[0:128, here] = pair.astype(bf16)
        columns_ref[128:256, here] = last.astype(bf16)
        turned_ref[here, 0:128] = pair.T.astype(bf16)
        turned_ref[here, 128:256] = last.T.astype(bf16)
        weight = jnp.where(slot_mask(slots_ref[:, here]), prices_ref[:, here], 0.0)
        weight_ref[:, here] = stack2(weight)


def rows_body(crossed, parts, turned_ref, weight_ref, *refs):
    center_refs, (block_ref, center_ref, scale_ref, out_ref) = refs[:parts], refs[parts:]
    arrived = home_total(center_refs) if crossed else total_of(center_refs).astype(f32)
    rows = arrived[-16:] * (1.0 / lax.axis_size("dp"))
    scale_ref[...] = rows[0:1] + (rows[1:2] + rows[2:3])
    center = arrived[:-16]
    center = jnp.concatenate(
        [*split3(center * FACTOR), norm_rows(center, 0)], axis=0
    ).astype(bf16)
    center_ref[...] = center
    row_count = turned_ref.shape[0]
    total = jnp.zeros(out_ref.shape, f32)

    def fold(begin):
        end = begin + CHUNK
        return product(
            weight_ref[:, begin:end],
            block_ref[begin:end, :],
            block_ref[row_count + begin : row_count + end, :],
        )

    def inner(begin):
        return jnp.dot(
            turned_ref[begin : begin + CHUNK, :], center, preferred_element_type=f32
        )

    ahead = inner(0)
    for begin in range(0, row_count, CHUNK):
        exponent = ahead
        if begin + CHUNK < row_count:
            ahead = inner(begin + CHUNK)
        high, low = kernel_parts(exponent)
        block_ref[begin : begin + CHUNK, :] = high
        block_ref[row_count + begin : row_count + begin + CHUNK, :] = low
        if begin > 0:
            total += fold(begin - CHUNK)
    out_ref[...] = total + fold(row_count - CHUNK)


def turned_body(columns_ref, center_ref, block_ref):
    center = center_ref[...].astype(f32).T.astype(bf16)
    count, row_count = center.shape[0], columns_ref.shape[1]

    def inner(begin):
        return jnp.dot(
            center, columns_ref[:, begin : begin + CHUNK], preferred_element_type=f32
        )

    ahead = inner(0)
    for begin in range(0, row_count, CHUNK):
        exponent = ahead
        if begin + CHUNK < row_count:
            ahead = inner(begin + CHUNK)
        high, low = kernel_parts(exponent)
        block_ref[0:count, begin : begin + CHUNK] = high
        block_ref[count:, begin : begin + CHUNK] = low


def apply_rows(scaled, turned_ref, slots_ref, out_ref):
    count, row_count = scaled.shape[1], turned_ref.shape[1]
    value = product(stack2(scaled), turned_ref[0:count, :], turned_ref[count:, :])
    own = jnp.where(slot_mask(slots_ref[...]), value, 0.0)
    out_ref[:, 0:row_count] = jnp.sum(own, axis=0, keepdims=True)


def fold_rows(rows, block_ref, slots_ref, out_ref):
    row_count, count = slots_ref.shape[1], block_ref.shape[1]
    weight = jnp.where(slot_mask(slots_ref[...]), rows, 0.0)
    out_ref[:, 0:count] = product(
        stack2(weight), block_ref[0:row_count, :], block_ref[row_count:, :]
    )
    square = row_sum(weight * weight)
    out_ref[:, count : count + EXTRA] = spread(square)


def first_apply_body(parts, scale_over_root, *refs):
    first_refs = refs[:parts]
    scale_ref, slots_ref, turned_ref, target_ref, out_ref = refs[parts:]
    scale = scale_ref[...]
    target = scale * total_of(first_refs) * scale_over_root
    target_ref[...] = target
    out_ref[:, turned_ref.shape[1] :] = to_lanes(row_sum(target * target), 0)
    apply_rows(scale * target, turned_ref, slots_ref, out_ref)


def first_fold_body(parts, *refs):
    row_refs = refs[:parts]
    slots_ref, block_ref, rows_ref, norm_ref, out_ref = refs[parts:]
    row_count = slots_ref.shape[1]
    rows = total_of(row_refs)
    rows_ref[...] = rows
    norm_ref[...] = spread(from_lanes(rows[:, row_count:], 0))
    fold_rows(rows[:, 0:row_count], block_ref, slots_ref, out_ref)


def second_apply_body(parts, inv_rows, *refs):
    fold_refs = refs[:parts]
    (scale_ref, slots_ref, turned_ref, target_ref, norm_ref,
     state_ref, step_ref, out_ref) = refs[parts:]
    row_count, count = turned_ref.shape[1], scale_ref.shape[1]
    folded = total_of(fold_refs)
    scale = scale_ref[...]
    target = target_ref[...]
    norm = norm_ref[...]
    applied = scale * folded[:, 0:count] * inv_rows + RIDGE * target
    step = norm / (folded[:, count:] * inv_rows + RIDGE * norm)
    residual = target - wide(step, count) * applied
    state_ref[0:SLOTS, :] = target
    state_ref[SLOTS:, :] = residual
    step_ref[...] = step
    out_ref[:, row_count:] = to_lanes(row_sum(residual * residual), 0) + to_lanes(
        row_sum(residual * target), SLOTS
    )
    apply_rows(scale * residual, turned_ref, slots_ref, out_ref)


def second_fold_body(parts, *refs):
    row_refs = refs[:parts]
    slots_ref, block_ref, rows_ref, norm_ref, sums_ref, out_ref = refs[parts:]
    row_count = slots_ref.shape[1]
    latest = total_of(row_refs)
    norm = spread(from_lanes(latest[:, row_count:], 0))
    ratio = norm / norm_ref[...]
    sums_ref[:, 0:EXTRA] = norm
    sums_ref[:, EXTRA:] = spread(from_lanes(latest[:, row_count:], SLOTS))
    rows = latest[:, 0:row_count] + wide(ratio, row_count) * rows_ref[:, 0:row_count]
    fold_rows(rows, block_ref, slots_ref, out_ref)


def finish_body(crossed, parts, inv_rows, *refs):
    fold_refs = refs[:parts]
    (moved_ref, state_ref, scale_ref, step_ref, norm_ref, sums_ref,
     coefficients_ref, out_ref) = refs[parts:]
    count = scale_ref.shape[1]
    state = state_ref[...]
    if crossed:
        folded = home_total(fold_refs)
        state = resident(moved_ref[...], state)
    else:
        folded = total_of(fold_refs)
    target, residual = state[0:SLOTS], state[SLOTS:]
    first_norm = norm_ref[...]
    norm, cross = sums_ref[:, 0:EXTRA], sums_ref[:, EXTRA:]
    ratio = norm / first_norm
    direction = residual + wide(ratio, count) * target
    square = norm + 2.0 * ratio * cross + ratio * ratio * first_norm
    applied = scale_ref[...] * folded[:, 0:count] * inv_rows + RIDGE * direction
    step = wide(norm / (folded[:, count:] * inv_rows + RIDGE * square), count)
    coefficients_ref[...] = wide(step_ref[...], count) * target + step * direction
    out_ref[...] = residual - step * applied


def call(body, out_shape, *args, sources=None, flops=0, bytes_accessed=0, **more):
    return pl.pallas_call(
        body,
        out_shape=out_shape,
        in_specs=sources or [VMEM] * len(args),
        out_specs=jax.tree.map(lambda _: VMEM, out_shape),
        compiler_params=pltpu.CompilerParams(vmem_limit_bytes=36 * 1024 * 1024),
        cost_estimate=pl.CostEstimate(
            flops=flops, bytes_accessed=bytes_accessed, transcendentals=0
        ),
        **more,
    )(*args)


def exchange(value, axis):
    size = lax.axis_size(axis)
    parts = [value]
    stride = 1
    while stride < size:
        value = pair_total(parts)
        span = min(4, size // stride)
        side = 0 if stride == 1 else 1
        parts = [value]
        for offset in range(1, span):
            pairs = [(i, i ^ (offset * stride) ^ side) for i in range(size)]
            parts.insert(0, lax.ppermute(value, axis, pairs))
        stride *= span
    return parts


def pairs_over(target_of):
    groups, count = lax.axis_size("dp"), lax.axis_size("centers")
    pairs = []
    for group in range(groups):
        for place in range(count):
            to_group, to_place = target_of(group, place)
            if (to_group, to_place) != (group, place):
                pairs.append((group * count + place, to_group * count + to_place))
    return pairs


def moved(value, target_of):
    return lax.ppermute(value, ("dp", "centers"), pairs_over(target_of))


def across(group, place):
    return 1 - group, place ^ 1


def beside(group, place):
    return group, place ^ group


def outward(group, place):
    return 1 - group, place ^ (1 - group)


def homeward(group, place):
    return 1 - group, place ^ group


def shaped(shape, dtype=f32):
    return jax.ShapeDtypeStruct(shape, dtype)


def per_device(features, prices, slots, center_idx, center_scale):
    depth, row_count = features.shape
    count = center_idx.shape[0]
    all_rows = row_count * lax.axis_size("dp")
    row_shape = shaped((1, row_count + EXTRA))
    fold_shape = shaped((SLOTS, count + EXTRA))
    vector = shaped((SLOTS, count))
    narrow = shaped((SLOTS, EXTRA))
    pass_cost = dict(flops=64 * row_count * count, bytes_accessed=4 * row_count * count)

    crossed = lax.axis_size("dp") == 2

    def share(value):
        return [moved(value, across), value] if crossed else exchange(value, "dp")

    inputs = [
        pltpu.with_memory_space_constraint(array, pltpu.HBM)
        for array in (
            features,
            center_idx.reshape(1, count),
            slots.reshape(1, row_count),
            prices.reshape(1, row_count),
            center_scale.reshape(1, count),
        )
    ]
    features, slots, prices, own_scale, picked = call(
        pick_body,
        (
            shaped(features.shape, bf16),
            shaped((1, row_count), jnp.int32),
            shaped((1, row_count)),
            shaped((1, count)),
            shaped((depth + 16, count), bf16),
        ),
        *inputs,
        sources=[HBM] * 5,
        scratch_shapes=[
            pltpu.VMEM((1, count), jnp.int32),
            pltpu.VMEM((row_count, count), bf16),
            pltpu.SemaphoreType.DMA((5,)),
        ],
    )
    if crossed:
        centers = [moved(picked, outward), moved(picked, beside), picked]
    else:
        centers = exchange(picked, "dp")
    columns, turned_columns, weight = call(
        columns_body,
        (
            shaped((DEPTH, row_count), bf16),
            shaped((row_count, DEPTH), bf16),
            shaped((16, row_count), bf16),
        ),
        features, slots, prices,
        flops=1000 * row_count,
        bytes_accessed=1024 * row_count,
    )
    block, center, scale, first = call(
        partial(rows_body, crossed, len(centers)),
        (
            shaped((2 * row_count, count), bf16),
            shaped((DEPTH, count), bf16),
            shaped((1, count)),
            vector,
        ),
        turned_columns, weight, *centers,
        **pass_cost,
    )
    firsts = share(first)
    turned = call(
        turned_body, shaped((2 * count, row_count), bf16), columns, center, **pass_cost
    )
    target, rows = call(
        partial(first_apply_body, len(firsts), 1.0 / math.sqrt(all_rows)),
        (vector, row_shape),
        *firsts, scale, slots, turned,
    )
    rows = exchange(rows, "centers")
    rows, norm, folded = call(
        partial(first_fold_body, len(rows)), (row_shape, narrow, fold_shape), *rows, slots, block
    )
    folds = share(folded)
    state, step, latest = call(
        partial(second_apply_body, len(folds), 1.0 / all_rows),
        (shaped((2 * SLOTS, count)), narrow, row_shape),
        *folds, scale, slots, turned, target, norm,
    )
    latest = exchange(latest, "centers")
    sums, folded = call(
        partial(second_fold_body, len(latest)),
        (shaped((SLOTS, 2 * EXTRA)), fold_shape),
        *latest, slots, block, rows, norm,
    )
    if crossed:
        folds = [moved(folded, homeward), moved(folded, beside), folded]
        moved_state = moved(state, beside)
    else:
        folds = exchange(folded, "dp")
        moved_state = state
    return call(
        partial(finish_body, crossed, len(folds), 1.0 / all_rows),
        (vector, vector),
        *folds, moved_state, state, own_scale, step, norm, sums,
    )


def solution(mesh):
    return jax.shard_map(
        per_device,
        mesh=mesh,
        in_specs=(P(None, "dp"), P("dp"), P("dp"), P("centers"), P("centers")),
        out_specs=(P(None, "centers"), P(None, "centers")),
        check_vma=False,
    )
```

```python
import math
from functools import partial

import jax
import jax.numpy as jnp
from jax import lax
from jax.experimental import pallas as pl
from jax.experimental.pallas import tpu as pltpu
from jax.sharding import PartitionSpec as P

SLOTS = 8
RIDGE = 0.5
CHUNK = 512
EXTRA = 128
DEPTH = 256
STEP = 256
FACTOR = math.log2(math.e) / 64.0
f32 = jnp.float32
bf16 = jnp.bfloat16
VMEM = pl.BlockSpec(memory_space=pltpu.VMEM)
HBM = pl.BlockSpec(memory_space=pltpu.HBM)


def split3(value):
    high = value.astype(bf16).astype(f32)
    rest = value - high
    mid = rest.astype(bf16).astype(f32)
    return high, mid, rest - mid


def stack2(value):
    high = value.astype(bf16).astype(f32)
    return jnp.concatenate([high, value - high], axis=0).astype(bf16)


def product(stacked, high_block, low_block):
    main = jnp.dot(stacked, high_block, preferred_element_type=f32)
    rest = jnp.dot(stacked[0:SLOTS], low_block, preferred_element_type=f32)
    return main[0:SLOTS] + (main[SLOTS:] + rest)


def slot_lanes(first):
    lane = lax.broadcasted_iota(jnp.int32, (SLOTS, EXTRA), 1)
    return lane == lax.broadcasted_iota(jnp.int32, (SLOTS, EXTRA), 0) + first


def to_lanes(column, first):
    return jnp.sum(jnp.where(slot_lanes(first), column, 0.0), axis=0, keepdims=True)


def from_lanes(row, first):
    return jnp.sum(jnp.where(slot_lanes(first), row, 0.0), axis=1, keepdims=True)


def spread(column):
    return jnp.broadcast_to(column, (SLOTS, EXTRA))


def wide(narrow, count):
    return jnp.concatenate([narrow] * (count // EXTRA), axis=1)


def pair_total(parts):
    while len(parts) > 1:
        parts = [parts[i] + parts[i + 1] for i in range(0, len(parts), 2)]
    return parts[0]


def total_of(refs):
    return pair_total([ref[...] for ref in refs])


def resident(moved, own):
    return jnp.where(lax.axis_index("dp") == 0, own, moved)


def home_total(refs):
    far, moved, own = (ref[...].astype(f32) for ref in refs)
    return far + resident(moved, own)


def row_sum(value):
    return jnp.sum(value, axis=1, keepdims=True)


def slot_mask(slots):
    row = lax.broadcasted_iota(jnp.int32, (SLOTS, slots.shape[1]), 0)
    return slots == row


def norm_rows(feat32, base):
    half = (-0.5 * FACTOR) * jnp.sum(feat32 * feat32, axis=0, keepdims=True)
    row = lax.broadcasted_iota(jnp.int32, (feat32.shape[0], feat32.shape[1]), 0)
    extra = jnp.where(row < 6, 1.0, 0.0)
    for place, part in enumerate(split3(half)):
        extra = jnp.where(row == base + place, part, extra)
    return extra


def kernel_parts(exponent):
    value = jnp.exp2(exponent)
    high = value.astype(bf16)
    return high, (value - high.astype(f32)).astype(bf16)


def pick_body(feat_hbm, idx_hbm, slots_hbm, prices_hbm, scale_hbm, *refs):
    feat_ref, slots_ref, prices_ref, scale_ref, out_ref, idx_ref, hit_ref, sems = refs
    row_count = feat_ref.shape[1]
    count = out_ref.shape[1]
    sources = (idx_hbm, feat_hbm, slots_hbm, prices_hbm, scale_hbm)
    targets = (idx_ref, feat_ref, slots_ref, prices_ref, scale_ref)
    copies = [
        pltpu.make_async_copy(source, target, sems.at[place])
        for place, (source, target) in enumerate(zip(sources, targets))
    ]
    for copy in copies:
        copy.start()
    copies[0].wait()
    local_idx = idx_ref[...] - lax.axis_index("dp") * row_count
    row = lax.broadcasted_iota(jnp.int32, (STEP, count), 0).astype(f32).astype(bf16)
    block = lax.div(local_idx, STEP)
    place = (local_idx - block * STEP).astype(f32)

    def hits(begin):
        own = jnp.where(block == begin // STEP, place, -1.0).astype(bf16)
        return jnp.where(row == own, jnp.ones_like(row), jnp.zeros_like(row))

    for begin in range(0, row_count, STEP):
        hit_ref[begin : begin + STEP, :] = hits(begin)
    copies[1].wait()
    picked = jnp.dot(feat_ref[...], hit_ref[...], preferred_element_type=f32)
    for copy in copies[2:]:
        copy.wait()
    row = lax.broadcasted_iota(jnp.int32, (16, count), 0)
    extra = jnp.zeros((16, count), f32)
    for place, part in enumerate(split3(scale_ref[...])):
        extra = jnp.where(row == place, part, extra)
    out_ref[...] = jnp.concatenate([picked, extra], axis=0).astype(bf16)


def columns_body(feat_ref, slots_ref, prices_ref, columns_ref, turned_ref, weight_ref):
    for begin in range(0, feat_ref.shape[1], CHUNK):
        here = slice(begin, begin + CHUNK)
        feat32 = feat_ref[:, here].astype(f32)
        pair = jnp.concatenate([feat32, feat32], axis=0)
        last = jnp.concatenate([feat32, norm_rows(feat32, 3)], axis=0)
        columns_ref[0:128, here] = pair.astype(bf16)
        columns_ref[128:256, here] = last.astype(bf16)
        turned_ref[here, 0:128] = pair.T.astype(bf16)
        turned_ref[here, 128:256] = last.T.astype(bf16)
        weight = jnp.where(slot_mask(slots_ref[:, here]), prices_ref[:, here], 0.0)
        weight_ref[:, here] = stack2(weight)


def rows_body(crossed, parts, turned_ref, weight_ref, *refs):
    center_refs, (block_ref, center_ref, scale_ref, out_ref) = refs[:parts], refs[parts:]
    arrived = home_total(center_refs) if crossed else total_of(center_refs).astype(f32)
    rows = arrived[-16:] * (1.0 / lax.axis_size("dp"))
    scale_ref[...] = rows[0:1] + (rows[1:2] + rows[2:3])
    center = arrived[:-16]
    center = jnp.concatenate(
        [*split3(center * FACTOR), norm_rows(center, 0)], axis=0
    ).astype(bf16)
    center_ref[...] = center
    row_count = turned_ref.shape[0]
    total = jnp.zeros(out_ref.shape, f32)

    def fold(begin):
        end = begin + CHUNK
        return product(
            weight_ref[:, begin:end],
            block_ref[begin:end, :],
            block_ref[row_count + begin : row_count + end, :],
        )

    def inner(begin):
        return jnp.dot(
            turned_ref[begin : begin + CHUNK, :], center, preferred_element_type=f32
        )

    ahead = inner(0)
    for begin in range(0, row_count, CHUNK):
        exponent = ahead
        if begin + CHUNK < row_count:
            ahead = inner(begin + CHUNK)
        high, low = kernel_parts(exponent)
        block_ref[begin : begin + CHUNK, :] = high
        block_ref[row_count + begin : row_count + begin + CHUNK, :] = low
        if begin > 0:
            total += fold(begin - CHUNK)
    out_ref[...] = total + fold(row_count - CHUNK)


def turned_body(columns_ref, center_ref, block_ref):
    center = center_ref[...].astype(f32).T.astype(bf16)
    count, row_count = center.shape[0], columns_ref.shape[1]

    def inner(begin):
        return jnp.dot(
            center, columns_ref[:, begin : begin + CHUNK], preferred_element_type=f32
        )

    ahead = inner(0)
    for begin in range(0, row_count, CHUNK):
        exponent = ahead
        if begin + CHUNK < row_count:
            ahead = inner(begin + CHUNK)
        high, low = kernel_parts(exponent)
        block_ref[0:count, begin : begin + CHUNK] = high
        block_ref[count:, begin : begin + CHUNK] = low


def apply_rows(scaled, turned_ref, slots_ref, out_ref):
    count, row_count = scaled.shape[1], turned_ref.shape[1]
    value = product(stack2(scaled), turned_ref[0:count, :], turned_ref[count:, :])
    own = jnp.where(slot_mask(slots_ref[...]), value, 0.0)
    out_ref[:, 0:row_count] = jnp.sum(own, axis=0, keepdims=True)


def fold_rows(rows, block_ref, slots_ref, out_ref):
    row_count, count = slots_ref.shape[1], block_ref.shape[1]
    weight = jnp.where(slot_mask(slots_ref[...]), rows, 0.0)
    out_ref[:, 0:count] = product(
        stack2(weight), block_ref[0:row_count, :], block_ref[row_count:, :]
    )
    square = row_sum(weight * weight)
    out_ref[:, count : count + EXTRA] = spread(square)


def first_apply_body(parts, scale_over_root, *refs):
    first_refs = refs[:parts]
    scale_ref, slots_ref, turned_ref, target_ref, out_ref = refs[parts:]
    scale = scale_ref[...]
    target = scale * total_of(first_refs) * scale_over_root
    target_ref[...] = target
    out_ref[:, turned_ref.shape[1] :] = to_lanes(row_sum(target * target), 0)
    apply_rows(scale * target, turned_ref, slots_ref, out_ref)


def first_fold_body(parts, *refs):
    row_refs = refs[:parts]
    slots_ref, block_ref, rows_ref, norm_ref, out_ref = refs[parts:]
    row_count = slots_ref.shape[1]
    rows = total_of(row_refs)
    rows_ref[...] = rows
    norm_ref[...] = spread(from_lanes(rows[:, row_count:], 0))
    fold_rows(rows[:, 0:row_count], block_ref, slots_ref, out_ref)


def second_apply_body(parts, inv_rows, *refs):
    fold_refs = refs[:parts]
    (scale_ref, slots_ref, turned_ref, target_ref, norm_ref,
     state_ref, step_ref, out_ref) = refs[parts:]
    row_count, count = turned_ref.shape[1], scale_ref.shape[1]
    folded = total_of(fold_refs)
    scale = scale_ref[...]
    target = target_ref[...]
    norm = norm_ref[...]
    applied = scale * folded[:, 0:count] * inv_rows + RIDGE * target
    step = norm / (folded[:, count:] * inv_rows + RIDGE * norm)
    residual = target - wide(step, count) * applied
    state_ref[0:SLOTS, :] = target
    state_ref[SLOTS:, :] = residual
    step_ref[...] = step
    out_ref[:, row_count:] = to_lanes(row_sum(residual * residual), 0) + to_lanes(
        row_sum(residual * target), SLOTS
    )
    apply_rows(scale * residual, turned_ref, slots_ref, out_ref)


def second_fold_body(parts, *refs):
    row_refs = refs[:parts]
    slots_ref, block_ref, rows_ref, norm_ref, sums_ref, out_ref = refs[parts:]
    row_count = slots_ref.shape[1]
    latest = total_of(row_refs)
    norm = spread(from_lanes(latest[:, row_count:], 0))
    ratio = norm / norm_ref[...]
    sums_ref[:, 0:EXTRA] = norm
    sums_ref[:, EXTRA:] = spread(from_lanes(latest[:, row_count:], SLOTS))
    rows = latest[:, 0:row_count] + wide(ratio, row_count) * rows_ref[:, 0:row_count]
    fold_rows(rows, block_ref, slots_ref, out_ref)


def finish_body(crossed, parts, inv_rows, *refs):
    fold_refs = refs[:parts]
    (moved_ref, state_ref, scale_ref, step_ref, norm_ref, sums_ref,
     coefficients_ref, out_ref) = refs[parts:]
    count = scale_ref.shape[1]
    state = state_ref[...]
    if crossed:
        folded = home_total(fold_refs)
        state = resident(moved_ref[...], state)
    else:
        folded = total_of(fold_refs)
    target, residual = state[0:SLOTS], state[SLOTS:]
    first_norm = norm_ref[...]
    norm, cross = sums_ref[:, 0:EXTRA], sums_ref[:, EXTRA:]
    ratio = norm / first_norm
    direction = residual + wide(ratio, count) * target
    square = norm + 2.0 * ratio * cross + ratio * ratio * first_norm
    applied = scale_ref[...] * folded[:, 0:count] * inv_rows + RIDGE * direction
    step = wide(norm / (folded[:, count:] * inv_rows + RIDGE * square), count)
    coefficients_ref[...] = wide(step_ref[...], count) * target + step * direction
    out_ref[...] = residual - step * applied


def call(body, out_shape, *args, sources=None, flops=0, bytes_accessed=0, **more):
    return pl.pallas_call(
        body,
        out_shape=out_shape,
        in_specs=sources or [VMEM] * len(args),
        out_specs=jax.tree.map(lambda _: VMEM, out_shape),
        compiler_params=pltpu.CompilerParams(vmem_limit_bytes=36 * 1024 * 1024),
        cost_estimate=pl.CostEstimate(
            flops=flops, bytes_accessed=bytes_accessed, transcendentals=0
        ),
        **more,
    )(*args)


def exchange(value, axis):
    size = lax.axis_size(axis)
    parts = [value]
    stride = 1
    while stride < size:
        value = pair_total(parts)
        span = min(4, size // stride)
        side = 0 if stride == 1 else 1
        parts = [value]
        for offset in range(1, span):
            pairs = [(i, i ^ (offset * stride) ^ side) for i in range(size)]
            parts.insert(0, lax.ppermute(value, axis, pairs))
        stride *= span
    return parts


def pairs_over(target_of):
    groups, count = lax.axis_size("dp"), lax.axis_size("centers")
    pairs = []
    for group in range(groups):
        for place in range(count):
            to_group, to_place = target_of(group, place)
            pairs.append((group * count + place, to_group * count + to_place))
    return pairs


def moved(value, target_of):
    return lax.ppermute(value, ("dp", "centers"), pairs_over(target_of))


def across(group, place):
    return 1 - group, place ^ 1


def beside(group, place):
    return group, place ^ 1


def outward(group, place):
    return 1 - group, place ^ (1 - group)


def homeward(group, place):
    return 1 - group, place ^ group


def shaped(shape, dtype=f32):
    return jax.ShapeDtypeStruct(shape, dtype)


def per_device(features, prices, slots, center_idx, center_scale):
    depth, row_count = features.shape
    count = center_idx.shape[0]
    all_rows = row_count * lax.axis_size("dp")
    row_shape = shaped((1, row_count + EXTRA))
    fold_shape = shaped((SLOTS, count + EXTRA))
    vector = shaped((SLOTS, count))
    narrow = shaped((SLOTS, EXTRA))
    pass_cost = dict(flops=64 * row_count * count, bytes_accessed=4 * row_count * count)

    crossed = lax.axis_size("dp") == 2

    def share(value):
        return [moved(value, across), value] if crossed else exchange(value, "dp")

    inputs = [
        pltpu.with_memory_space_constraint(array, pltpu.HBM)
        for array in (
            features,
            center_idx.reshape(1, count),
            slots.reshape(1, row_count),
            prices.reshape(1, row_count),
            center_scale.reshape(1, count),
        )
    ]
    features, slots, prices, own_scale, picked = call(
        pick_body,
        (
            shaped(features.shape, bf16),
            shaped((1, row_count), jnp.int32),
            shaped((1, row_count)),
            shaped((1, count)),
            shaped((depth + 16, count), bf16),
        ),
        *inputs,
        sources=[HBM] * 5,
        scratch_shapes=[
            pltpu.VMEM((1, count), jnp.int32),
            pltpu.VMEM((row_count, count), bf16),
            pltpu.SemaphoreType.DMA((5,)),
        ],
    )
    if crossed:
        centers = [moved(picked, outward), moved(picked, beside), picked]
    else:
        centers = exchange(picked, "dp")
    columns, turned_columns, weight = call(
        columns_body,
        (
            shaped((DEPTH, row_count), bf16),
            shaped((row_count, DEPTH), bf16),
            shaped((16, row_count), bf16),
        ),
        features, slots, prices,
        flops=1000 * row_count,
        bytes_accessed=1024 * row_count,
    )
    block, center, scale, first = call(
        partial(rows_body, crossed, len(centers)),
        (
            shaped((2 * row_count, count), bf16),
            shaped((DEPTH, count), bf16),
            shaped((1, count)),
            vector,
        ),
        turned_columns, weight, *centers,
        **pass_cost,
    )
    firsts = share(first)
    turned = call(
        turned_body, shaped((2 * count, row_count), bf16), columns, center, **pass_cost
    )
    target, rows = call(
        partial(first_apply_body, len(firsts), 1.0 / math.sqrt(all_rows)),
        (vector, row_shape),
        *firsts, scale, slots, turned,
    )
    rows = exchange(rows, "centers")
    rows, norm, folded = call(
        partial(first_fold_body, len(rows)), (row_shape, narrow, fold_shape), *rows, slots, block
    )
    folds = share(folded)
    state, step, latest = call(
        partial(second_apply_body, len(folds), 1.0 / all_rows),
        (shaped((2 * SLOTS, count)), narrow, row_shape),
        *folds, scale, slots, turned, target, norm,
    )
    latest = exchange(latest, "centers")
    sums, folded = call(
        partial(second_fold_body, len(latest)),
        (shaped((SLOTS, 2 * EXTRA)), fold_shape),
        *latest, slots, block, rows, norm,
    )
    if crossed:
        folds = [moved(folded, homeward), moved(folded, beside), folded]
        moved_state = moved(state, beside)
    else:
        folds = exchange(folded, "dp")
        moved_state = state
    return call(
        partial(finish_body, crossed, len(folds), 1.0 / all_rows),
        (vector, vector),
        *folds, moved_state, state, own_scale, step, norm, sums,
    )


def solution(mesh):
    return jax.shard_map(
        per_device,
        mesh=mesh,
        in_specs=(P(None, "dp"), P("dp"), P("dp"), P("centers"), P("centers")),
        out_specs=(P(None, "centers"), P(None, "centers")),
        check_vma=False,
    )
```

```python
import math
from functools import partial

import jax
import jax.numpy as jnp
from jax import lax
from jax.experimental import pallas as pl
from jax.experimental.pallas import tpu as pltpu
from jax.sharding import PartitionSpec as P

SLOTS = 8
RIDGE = 0.5
CHUNK = 512
EXTRA = 128
DEPTH = 256
STEP = 256
FACTOR = math.log2(math.e) / 64.0
f32 = jnp.float32
bf16 = jnp.bfloat16
VMEM = pl.BlockSpec(memory_space=pltpu.VMEM)
HBM = pl.BlockSpec(memory_space=pltpu.HBM)


def split3(value):
    high = value.astype(bf16).astype(f32)
    rest = value - high
    mid = rest.astype(bf16).astype(f32)
    return high, mid, rest - mid


def stack2(value):
    high = value.astype(bf16).astype(f32)
    return jnp.concatenate([high, value - high], axis=0).astype(bf16)


def product(stacked, high_block, low_block):
    main = jnp.dot(stacked, high_block, preferred_element_type=f32)
    rest = jnp.dot(stacked[0:SLOTS], low_block, preferred_element_type=f32)
    return main[0:SLOTS] + (main[SLOTS:] + rest)


def slot_lanes(first):
    lane = lax.broadcasted_iota(jnp.int32, (SLOTS, EXTRA), 1)
    return lane == lax.broadcasted_iota(jnp.int32, (SLOTS, EXTRA), 0) + first


def to_lanes(column, first):
    return jnp.sum(jnp.where(slot_lanes(first), column, 0.0), axis=0, keepdims=True)


def from_lanes(row, first):
    return jnp.sum(jnp.where(slot_lanes(first), row, 0.0), axis=1, keepdims=True)


def spread(column):
    return jnp.broadcast_to(column, (SLOTS, EXTRA))


def wide(narrow, count):
    return jnp.concatenate([narrow] * (count // EXTRA), axis=1)


def pair_total(parts):
    while len(parts) > 1:
        parts = [parts[i] + parts[i + 1] for i in range(0, len(parts), 2)]
    return parts[0]


def total_of(refs):
    return pair_total([ref[...] for ref in refs])


def resident(moved, own):
    return jnp.where(lax.axis_index("dp") == 0, own, moved)


def home_total(refs):
    far, moved, own = (ref[...].astype(f32) for ref in refs)
    return far + resident(moved, own)


def row_sum(value):
    return jnp.sum(value, axis=1, keepdims=True)


def slot_mask(slots):
    row = lax.broadcasted_iota(jnp.int32, (SLOTS, slots.shape[1]), 0)
    return slots == row


def norm_rows(feat32, base):
    half = (-0.5 * FACTOR) * jnp.sum(feat32 * feat32, axis=0, keepdims=True)
    row = lax.broadcasted_iota(jnp.int32, (feat32.shape[0], feat32.shape[1]), 0)
    extra = jnp.where(row < 6, 1.0, 0.0)
    for place, part in enumerate(split3(half)):
        extra = jnp.where(row == base + place, part, extra)
    return extra


def kernel_parts(exponent):
    value = jnp.exp2(exponent)
    high = value.astype(bf16)
    return high, (value - high.astype(f32)).astype(bf16)


def pick_body(feat_hbm, idx_hbm, slots_hbm, prices_hbm, scale_hbm, *refs):
    feat_ref, slots_ref, prices_ref, scale_ref, out_ref, idx_ref, hit_ref, sems = refs
    row_count = feat_ref.shape[1]
    count = out_ref.shape[1]
    sources = (idx_hbm, feat_hbm, slots_hbm, prices_hbm, scale_hbm)
    targets = (idx_ref, feat_ref, slots_ref, prices_ref, scale_ref)
    copies = [
        pltpu.make_async_copy(source, target, sems.at[place])
        for place, (source, target) in enumerate(zip(sources, targets))
    ]
    for copy in copies:
        copy.start()
    copies[0].wait()
    local_idx = idx_ref[...] - lax.axis_index("dp") * row_count
    row = lax.broadcasted_iota(jnp.int32, (STEP, count), 0).astype(f32).astype(bf16)
    block = lax.div(local_idx, STEP)
    place = (local_idx - block * STEP).astype(f32)

    def hits(begin):
        own = jnp.where(block == begin // STEP, place, -1.0).astype(bf16)
        return jnp.where(row == own, jnp.ones_like(row), jnp.zeros_like(row))

    for begin in range(0, row_count, STEP):
        hit_ref[begin : begin + STEP, :] = hits(begin)
    copies[1].wait()
    picked = jnp.dot(feat_ref[...], hit_ref[...], preferred_element_type=f32)
    for copy in copies[2:]:
        copy.wait()
    row = lax.broadcasted_iota(jnp.int32, (16, count), 0)
    extra = jnp.zeros((16, count), f32)
    for place, part in enumerate(split3(scale_ref[...])):
        extra = jnp.where(row == place, part, extra)
    out_ref[...] = jnp.concatenate([picked, extra], axis=0).astype(bf16)


def columns_body(feat_ref, slots_ref, prices_ref, columns_ref, turned_ref, weight_ref):
    for begin in range(0, feat_ref.shape[1], CHUNK):
        here = slice(begin, begin + CHUNK)
        feat32 = feat_ref[:, here].astype(f32)
        pair = jnp.concatenate([feat32, feat32], axis=0)
        last = jnp.concatenate([feat32, norm_rows(feat32, 3)], axis=0)
        columns_ref[0:128, here] = pair.astype(bf16)
        columns_ref[128:256, here] = last.astype(bf16)
        turned_ref[here, 0:128] = pair.T.astype(bf16)
        turned_ref[here, 128:256] = last.T.astype(bf16)
        weight = jnp.where(slot_mask(slots_ref[:, here]), prices_ref[:, here], 0.0)
        weight_ref[:, here] = stack2(weight)


def rows_body(crossed, parts, turned_ref, weight_ref, *refs):
    center_refs, (block_ref, center_ref, scale_ref, out_ref) = refs[:parts], refs[parts:]
    arrived = home_total(center_refs) if crossed else total_of(center_refs).astype(f32)
    rows = arrived[-16:] * (1.0 / lax.axis_size("dp"))
    scale_ref[...] = rows[0:1] + (rows[1:2] + rows[2:3])
    center = arrived[:-16]
    center = jnp.concatenate(
        [*split3(center * FACTOR), norm_rows(center, 0)], axis=0
    ).astype(bf16)
    center_ref[...] = center
    row_count = turned_ref.shape[0]
    total = jnp.zeros(out_ref.shape, f32)

    def fold(begin):
        end = begin + CHUNK
        return product(
            weight_ref[:, begin:end],
            block_ref[begin:end, :],
            block_ref[row_count + begin : row_count + end, :],
        )

    def inner(begin):
        return jnp.dot(
            turned_ref[begin : begin + CHUNK, :], center, preferred_element_type=f32
        )

    ahead = inner(0)
    for begin in range(0, row_count, CHUNK):
        exponent = ahead
        if begin + CHUNK < row_count:
            ahead = inner(begin + CHUNK)
        high, low = kernel_parts(exponent)
        block_ref[begin : begin + CHUNK, :] = high
        block_ref[row_count + begin : row_count + begin + CHUNK, :] = low
        if begin > 0:
            total += fold(begin - CHUNK)
    out_ref[...] = total + fold(row_count - CHUNK)


def turned_body(columns_ref, center_ref, block_ref):
    center = center_ref[...].astype(f32).T.astype(bf16)
    count, row_count = center.shape[0], columns_ref.shape[1]

    def inner(begin):
        return jnp.dot(
            center, columns_ref[:, begin : begin + CHUNK], preferred_element_type=f32
        )

    ahead = inner(0)
    for begin in range(0, row_count, CHUNK):
        exponent = ahead
        if begin + CHUNK < row_count:
            ahead = inner(begin + CHUNK)
        high, low = kernel_parts(exponent)
        block_ref[0:count, begin : begin + CHUNK] = high
        block_ref[count:, begin : begin + CHUNK] = low


def apply_rows(scaled, turned_ref, slots_ref, out_ref):
    count, row_count = scaled.shape[1], turned_ref.shape[1]
    value = product(stack2(scaled), turned_ref[0:count, :], turned_ref[count:, :])
    own = jnp.where(slot_mask(slots_ref[...]), value, 0.0)
    out_ref[:, 0:row_count] = jnp.sum(own, axis=0, keepdims=True)


def fold_rows(rows, block_ref, slots_ref, out_ref):
    row_count, count = slots_ref.shape[1], block_ref.shape[1]
    weight = jnp.where(slot_mask(slots_ref[...]), rows, 0.0)
    out_ref[:, 0:count] = product(
        stack2(weight), block_ref[0:row_count, :], block_ref[row_count:, :]
    )
    square = row_sum(weight * weight)
    out_ref[:, count : count + EXTRA] = spread(square)


def first_apply_body(parts, scale_over_root, *refs):
    first_refs = refs[:parts]
    scale_ref, slots_ref, turned_ref, target_ref, out_ref = refs[parts:]
    scale = scale_ref[...]
    target = scale * total_of(first_refs) * scale_over_root
    target_ref[...] = target
    out_ref[:, turned_ref.shape[1] :] = to_lanes(row_sum(target * target), 0)
    apply_rows(scale * target, turned_ref, slots_ref, out_ref)


def first_fold_body(parts, *refs):
    row_refs = refs[:parts]
    slots_ref, block_ref, rows_ref, norm_ref, out_ref = refs[parts:]
    row_count = slots_ref.shape[1]
    rows = total_of(row_refs)
    rows_ref[...] = rows
    norm_ref[...] = spread(from_lanes(rows[:, row_count:], 0))
    fold_rows(rows[:, 0:row_count], block_ref, slots_ref, out_ref)


def second_apply_body(parts, inv_rows, *refs):
    fold_refs = refs[:parts]
    (scale_ref, slots_ref, turned_ref, target_ref, norm_ref,
     state_ref, step_ref, out_ref) = refs[parts:]
    row_count, count = turned_ref.shape[1], scale_ref.shape[1]
    folded = total_of(fold_refs)
    scale = scale_ref[...]
    target = target_ref[...]
    norm = norm_ref[...]
    applied = scale * folded[:, 0:count] * inv_rows + RIDGE * target
    step = norm / (folded[:, count:] * inv_rows + RIDGE * norm)
    residual = target - wide(step, count) * applied
    state_ref[0:SLOTS, :] = target
    state_ref[SLOTS:, :] = residual
    step_ref[...] = step
    out_ref[:, row_count:] = to_lanes(row_sum(residual * residual), 0) + to_lanes(
        row_sum(residual * target), SLOTS
    )
    apply_rows(scale * residual, turned_ref, slots_ref, out_ref)


def second_fold_body(parts, *refs):
    row_refs = refs[:parts]
    slots_ref, block_ref, rows_ref, norm_ref, state_ref, sums_ref, out_ref, bundle_ref = refs[parts:]
    row_count = slots_ref.shape[1]
    bundle_ref[SLOTS:, 0 : state_ref.shape[1]] = state_ref[...]
    bundle_ref[SLOTS:, state_ref.shape[1] :] = jnp.zeros((2 * SLOTS, EXTRA), f32)
    latest = total_of(row_refs)
    norm = spread(from_lanes(latest[:, row_count:], 0))
    ratio = norm / norm_ref[...]
    sums_ref[:, 0:EXTRA] = norm
    sums_ref[:, EXTRA:] = spread(from_lanes(latest[:, row_count:], SLOTS))
    rows = latest[:, 0:row_count] + wide(ratio, row_count) * rows_ref[:, 0:row_count]
    fold_rows(rows, block_ref, slots_ref, out_ref)
    bundle_ref[0:SLOTS, :] = out_ref[...]


def finish_body(crossed, parts, inv_rows, *refs):
    fold_refs = refs[:parts]
    (scale_ref, step_ref, norm_ref, sums_ref,
     coefficients_ref, out_ref) = refs[parts:]
    count = scale_ref.shape[1]
    bundle = fold_refs[-1][...]
    if crossed:
        far_ref, moved_ref = fold_refs[:-1]
        bundle = resident(moved_ref[...], bundle)
        folded = far_ref[...] + bundle[0:SLOTS]
    else:
        folded = total_of(fold_refs[:-1])
    target, residual = bundle[SLOTS : 2 * SLOTS, 0:count], bundle[2 * SLOTS :, 0:count]
    first_norm = norm_ref[...]
    norm, cross = sums_ref[:, 0:EXTRA], sums_ref[:, EXTRA:]
    ratio = norm / first_norm
    direction = residual + wide(ratio, count) * target
    square = norm + 2.0 * ratio * cross + ratio * ratio * first_norm
    applied = scale_ref[...] * folded[:, 0:count] * inv_rows + RIDGE * direction
    step = wide(norm / (folded[:, count:] * inv_rows + RIDGE * square), count)
    coefficients_ref[...] = wide(step_ref[...], count) * target + step * direction
    out_ref[...] = residual - step * applied


def call(body, out_shape, *args, sources=None, flops=0, bytes_accessed=0, **more):
    return pl.pallas_call(
        body,
        out_shape=out_shape,
        in_specs=sources or [VMEM] * len(args),
        out_specs=jax.tree.map(lambda _: VMEM, out_shape),
        compiler_params=pltpu.CompilerParams(vmem_limit_bytes=36 * 1024 * 1024),
        cost_estimate=pl.CostEstimate(
            flops=flops, bytes_accessed=bytes_accessed, transcendentals=0
        ),
        **more,
    )(*args)


def exchange(value, axis):
    size = lax.axis_size(axis)
    parts = [value]
    stride = 1
    while stride < size:
        value = pair_total(parts)
        span = min(4, size // stride)
        side = 0 if stride == 1 else 1
        parts = [value]
        offsets = (1, 3, 2) if stride == 1 else (1, 2, 3)
        for offset in offsets[: span - 1]:
            pairs = [(i, i ^ (offset * stride) ^ side) for i in range(size)]
            parts.insert(0, lax.ppermute(value, axis, pairs))
        stride *= span
    return parts


def pairs_over(target_of):
    groups, count = lax.axis_size("dp"), lax.axis_size("centers")
    pairs = []
    for group in range(groups):
        for place in range(count):
            to_group, to_place = target_of(group, place)
            pairs.append((group * count + place, to_group * count + to_place))
    return pairs


def moved(value, target_of):
    return lax.ppermute(value, ("dp", "centers"), pairs_over(target_of))


def across(group, place):
    return 1 - group, place ^ 1


def beside(group, place):
    return group, place ^ 1


def outward(group, place):
    return 1 - group, place ^ (1 - group)


def homeward(group, place):
    return 1 - group, place ^ group


def shaped(shape, dtype=f32):
    return jax.ShapeDtypeStruct(shape, dtype)


def per_device(features, prices, slots, center_idx, center_scale):
    depth, row_count = features.shape
    count = center_idx.shape[0]
    all_rows = row_count * lax.axis_size("dp")
    row_shape = shaped((1, row_count + EXTRA))
    fold_shape = shaped((SLOTS, count + EXTRA))
    vector = shaped((SLOTS, count))
    narrow = shaped((SLOTS, EXTRA))
    pass_cost = dict(flops=64 * row_count * count, bytes_accessed=4 * row_count * count)

    crossed = lax.axis_size("dp") == 2

    def share(value):
        return [moved(value, across), value] if crossed else exchange(value, "dp")

    inputs = [
        pltpu.with_memory_space_constraint(array, pltpu.HBM)
        for array in (
            features,
            center_idx.reshape(1, count),
            slots.reshape(1, row_count),
            prices.reshape(1, row_count),
            center_scale.reshape(1, count),
        )
    ]
    features, slots, prices, own_scale, picked = call(
        pick_body,
        (
            shaped(features.shape, bf16),
            shaped((1, row_count), jnp.int32),
            shaped((1, row_count)),
            shaped((1, count)),
            shaped((depth + 16, count), bf16),
        ),
        *inputs,
        sources=[HBM] * 5,
        scratch_shapes=[
            pltpu.VMEM((1, count), jnp.int32),
            pltpu.VMEM((row_count, count), bf16),
            pltpu.SemaphoreType.DMA((5,)),
        ],
    )
    if crossed:
        centers = [moved(picked, outward), moved(picked, beside), picked]
    else:
        centers = exchange(picked, "dp")
    columns, turned_columns, weight = call(
        columns_body,
        (
            shaped((DEPTH, row_count), bf16),
            shaped((row_count, DEPTH), bf16),
            shaped((16, row_count), bf16),
        ),
        features, slots, prices,
        flops=1000 * row_count,
        bytes_accessed=1024 * row_count,
    )
    block, center, scale, first = call(
        partial(rows_body, crossed, len(centers)),
        (
            shaped((2 * row_count, count), bf16),
            shaped((DEPTH, count), bf16),
            shaped((1, count)),
            vector,
        ),
        turned_columns, weight, *centers,
        **pass_cost,
    )
    firsts = share(first)
    turned = call(
        turned_body, shaped((2 * count, row_count), bf16), columns, center, **pass_cost
    )
    target, rows = call(
        partial(first_apply_body, len(firsts), 1.0 / math.sqrt(all_rows)),
        (vector, row_shape),
        *firsts, scale, slots, turned,
    )
    rows = exchange(rows, "centers")
    rows, norm, folded = call(
        partial(first_fold_body, len(rows)), (row_shape, narrow, fold_shape), *rows, slots, block
    )
    folds = share(folded)
    state, step, latest = call(
        partial(second_apply_body, len(folds), 1.0 / all_rows),
        (shaped((2 * SLOTS, count)), narrow, row_shape),
        *folds, scale, slots, turned, target, norm,
    )
    latest = exchange(latest, "centers")
    sums, folded, bundle = call(
        partial(second_fold_body, len(latest)),
        (
            shaped((SLOTS, 2 * EXTRA)),
            fold_shape,
            shaped((3 * SLOTS, count + EXTRA)),
        ),
        *latest, slots, block, rows, norm, state,
    )
    if crossed:
        folds = [moved(folded, homeward), moved(bundle, beside), bundle]
    else:
        folds = exchange(folded, "dp") + [bundle]
    return call(
        partial(finish_body, crossed, len(folds), 1.0 / all_rows),
        (vector, vector),
        *folds, own_scale, step, norm, sums,
    )


def solution(mesh):
    return jax.shard_map(
        per_device,
        mesh=mesh,
        in_specs=(P(None, "dp"), P("dp"), P("dp"), P("centers"), P("centers")),
        out_specs=(P(None, "centers"), P(None, "centers")),
        check_vma=False,
    )
```

```python
import math
from functools import partial

import jax
import jax.numpy as jnp
from jax import lax
from jax.experimental import pallas as pl
from jax.experimental.pallas import tpu as pltpu
from jax.sharding import PartitionSpec as P

SLOTS = 8
RIDGE = 0.5
CHUNK = 512
EXTRA = 128
DEPTH = 256
STEP = 256
FACTOR = math.log2(math.e) / 64.0
f32 = jnp.float32
bf16 = jnp.bfloat16
VMEM = pl.BlockSpec(memory_space=pltpu.VMEM)
HBM = pl.BlockSpec(memory_space=pltpu.HBM)


def split3(value):
    high = value.astype(bf16).astype(f32)
    rest = value - high
    mid = rest.astype(bf16).astype(f32)
    return high, mid, rest - mid


def stack2(value):
    high = value.astype(bf16).astype(f32)
    return jnp.concatenate([high, value - high], axis=0).astype(bf16)


def product(stacked, high_block, low_block):
    total = jnp.dot(stacked, high_block, preferred_element_type=f32)
    total += jnp.dot(stacked, low_block, preferred_element_type=f32)
    return total[0:SLOTS] + total[SLOTS:]


def slot_lanes(first):
    lane = lax.broadcasted_iota(jnp.int32, (SLOTS, EXTRA), 1)
    return lane == lax.broadcasted_iota(jnp.int32, (SLOTS, EXTRA), 0) + first


def to_lanes(column, first):
    return jnp.sum(jnp.where(slot_lanes(first), column, 0.0), axis=0, keepdims=True)


def from_lanes(row, first):
    return jnp.sum(jnp.where(slot_lanes(first), row, 0.0), axis=1, keepdims=True)


def spread(column):
    return jnp.broadcast_to(column, (SLOTS, EXTRA))


def wide(narrow, count):
    return jnp.concatenate([narrow] * (count // EXTRA), axis=1)


def pair_total(parts):
    while len(parts) > 1:
        parts = [parts[i] + parts[i + 1] for i in range(0, len(parts), 2)]
    return parts[0]


def total_of(refs):
    return pair_total([ref[...] for ref in refs])


def row_sum(value):
    return jnp.sum(value, axis=1, keepdims=True)


def slot_mask(slots):
    row = lax.broadcasted_iota(jnp.int32, (SLOTS, slots.shape[1]), 0)
    return slots == row


def norm_rows(feat32, base):
    half = (-0.5 * FACTOR) * jnp.sum(feat32 * feat32, axis=0, keepdims=True)
    row = lax.broadcasted_iota(jnp.int32, (feat32.shape[0], feat32.shape[1]), 0)
    extra = jnp.where(row < 6, 1.0, 0.0)
    for place, part in enumerate(split3(half)):
        extra = jnp.where(row == base + place, part, extra)
    return extra


def kernel_parts(exponent):
    value = jnp.exp2(exponent)
    high = value.astype(bf16)
    return high, (value - high.astype(f32)).astype(bf16)


def pick_body(feat_hbm, idx_hbm, slots_hbm, prices_hbm, scale_hbm, *refs):
    feat_ref, slots_ref, prices_ref, scale_ref, out_ref, idx_ref, hit_ref, sems = refs
    row_count = feat_ref.shape[1]
    count = out_ref.shape[1]
    sources = (idx_hbm, feat_hbm, slots_hbm, prices_hbm, scale_hbm)
    targets = (idx_ref, feat_ref, slots_ref, prices_ref, scale_ref)
    copies = [
        pltpu.make_async_copy(source, target, sems.at[place])
        for place, (source, target) in enumerate(zip(sources, targets))
    ]
    for copy in copies:
        copy.start()
    copies[0].wait()
    local_idx = idx_ref[...] - lax.axis_index("dp") * row_count
    row = lax.broadcasted_iota(jnp.int32, (STEP, count), 0).astype(f32).astype(bf16)
    block = lax.div(local_idx, STEP)
    place = (local_idx - block * STEP).astype(f32)

    def hits(begin):
        own = jnp.where(block == begin // STEP, place, -1.0).astype(bf16)
        return jnp.where(row == own, jnp.ones_like(row), jnp.zeros_like(row))

    for begin in range(0, row_count, STEP):
        hit_ref[begin : begin + STEP, :] = hits(begin)
    copies[1].wait()
    out_ref[...] = jnp.dot(
        feat_ref[...], hit_ref[...], preferred_element_type=f32
    ).astype(bf16)
    for copy in copies[2:]:
        copy.wait()


def columns_body(feat_ref, slots_ref, prices_ref, columns_ref, turned_ref, weight_ref):
    for begin in range(0, feat_ref.shape[1], CHUNK):
        here = slice(begin, begin + CHUNK)
        feat32 = feat_ref[:, here].astype(f32)
        pair = jnp.concatenate([feat32, feat32], axis=0)
        last = jnp.concatenate([feat32, norm_rows(feat32, 3)], axis=0)
        columns_ref[0:128, here] = pair.astype(bf16)
        columns_ref[128:256, here] = last.astype(bf16)
        turned_ref[here, 0:128] = pair.T.astype(bf16)
        turned_ref[here, 128:256] = last.T.astype(bf16)
        weight = jnp.where(slot_mask(slots_ref[:, here]), prices_ref[:, here], 0.0)
        weight_ref[:, here] = stack2(weight)


def rows_body(parts, turned_ref, weight_ref, *refs):
    center_refs, (block_ref, center_ref, out_ref) = refs[:parts], refs[parts:]
    center = total_of(center_refs).astype(f32)
    center = jnp.concatenate(
        [*split3(center * FACTOR), norm_rows(center, 0)], axis=0
    ).astype(bf16)
    center_ref[...] = center
    row_count = turned_ref.shape[0]
    total = jnp.zeros(out_ref.shape, f32)

    def fold(begin):
        end = begin + CHUNK
        return product(
            weight_ref[:, begin:end],
            block_ref[begin:end, :],
            block_ref[row_count + begin : row_count + end, :],
        )

    def inner(begin):
        return jnp.dot(
            turned_ref[begin : begin + CHUNK, :], center, preferred_element_type=f32
        )

    ahead = inner(0)
    for begin in range(0, row_count, CHUNK):
        exponent = ahead
        if begin + CHUNK < row_count:
            ahead = inner(begin + CHUNK)
        high, low = kernel_parts(exponent)
        block_ref[begin : begin + CHUNK, :] = high
        block_ref[row_count + begin : row_count + begin + CHUNK, :] = low
        if begin > 0:
            total += fold(begin - CHUNK)
    out_ref[...] = total + fold(row_count - CHUNK)


def turned_body(columns_ref, center_ref, block_ref):
    center = center_ref[...].astype(f32).T.astype(bf16)
    count, row_count = center.shape[0], columns_ref.shape[1]

    def inner(begin):
        return jnp.dot(
            center, columns_ref[:, begin : begin + CHUNK], preferred_element_type=f32
        )

    ahead = inner(0)
    for begin in range(0, row_count, CHUNK):
        exponent = ahead
        if begin + CHUNK < row_count:
            ahead = inner(begin + CHUNK)
        high, low = kernel_parts(exponent)
        block_ref[0:count, begin : begin + CHUNK] = high
        block_ref[count:, begin : begin + CHUNK] = low


def apply_rows(scaled, turned_ref, slots_ref, out_ref):
    count, row_count = scaled.shape[1], turned_ref.shape[1]
    value = product(stack2(scaled), turned_ref[0:count, :], turned_ref[count:, :])
    own = jnp.where(slot_mask(slots_ref[...]), value, 0.0)
    out_ref[:, 0:row_count] = jnp.sum(own, axis=0, keepdims=True)


def fold_rows(rows, block_ref, slots_ref, out_ref):
    row_count, count = slots_ref.shape[1], block_ref.shape[1]
    weight = jnp.where(slot_mask(slots_ref[...]), rows, 0.0)
    out_ref[:, 0:count] = product(
        stack2(weight), block_ref[0:row_count, :], block_ref[row_count:, :]
    )
    square = row_sum(weight * weight)
    out_ref[:, count : count + EXTRA] = spread(square)


def first_apply_body(parts, scale_over_root, *refs):
    first_refs = refs[:parts]
    scale_ref, slots_ref, turned_ref, target_ref, out_ref = refs[parts:]
    scale = scale_ref[...]
    target = scale * total_of(first_refs) * scale_over_root
    target_ref[...] = target
    out_ref[:, turned_ref.shape[1] :] = to_lanes(row_sum(target * target), 0)
    apply_rows(scale * target, turned_ref, slots_ref, out_ref)


def first_fold_body(parts, *refs):
    row_refs = refs[:parts]
    slots_ref, block_ref, rows_ref, norm_ref, out_ref = refs[parts:]
    row_count = slots_ref.shape[1]
    rows = total_of(row_refs)
    rows_ref[...] = rows
    norm_ref[...] = spread(from_lanes(rows[:, row_count:], 0))
    fold_rows(rows[:, 0:row_count], block_ref, slots_ref, out_ref)


def second_apply_body(parts, inv_rows, *refs):
    fold_refs = refs[:parts]
    (scale_ref, slots_ref, turned_ref, target_ref, norm_ref,
     residual_ref, step_ref, out_ref) = refs[parts:]
    row_count, count = turned_ref.shape[1], scale_ref.shape[1]
    folded = total_of(fold_refs)
    scale = scale_ref[...]
    target = target_ref[...]
    norm = norm_ref[...]
    applied = scale * folded[:, 0:count] * inv_rows + RIDGE * target
    step = norm / (folded[:, count:] * inv_rows + RIDGE * norm)
    residual = target - wide(step, count) * applied
    residual_ref[...] = residual
    step_ref[...] = step
    out_ref[:, row_count:] = to_lanes(row_sum(residual * residual), 0) + to_lanes(
        row_sum(residual * target), SLOTS
    )
    apply_rows(scale * residual, turned_ref, slots_ref, out_ref)


def second_fold_body(parts, *refs):
    row_refs = refs[:parts]
    slots_ref, block_ref, rows_ref, norm_ref, sums_ref, out_ref = refs[parts:]
    row_count = slots_ref.shape[1]
    latest = total_of(row_refs)
    norm = spread(from_lanes(latest[:, row_count:], 0))
    ratio = norm / norm_ref[...]
    sums_ref[:, 0:EXTRA] = norm
    sums_ref[:, EXTRA:] = spread(from_lanes(latest[:, row_count:], SLOTS))
    rows = latest[:, 0:row_count] + wide(ratio, row_count) * rows_ref[:, 0:row_count]
    fold_rows(rows, block_ref, slots_ref, out_ref)


def finish_body(parts, inv_rows, *refs):
    fold_refs = refs[:parts]
    (scale_ref, target_ref, residual_ref, step_ref, norm_ref, sums_ref,
     coefficients_ref, out_ref) = refs[parts:]
    count = scale_ref.shape[1]
    folded = total_of(fold_refs)
    target = target_ref[...]
    residual = residual_ref[...]
    first_norm = norm_ref[...]
    norm, cross = sums_ref[:, 0:EXTRA], sums_ref[:, EXTRA:]
    ratio = norm / first_norm
    direction = residual + wide(ratio, count) * target
    square = norm + 2.0 * ratio * cross + ratio * ratio * first_norm
    applied = scale_ref[...] * folded[:, 0:count] * inv_rows + RIDGE * direction
    step = wide(norm / (folded[:, count:] * inv_rows + RIDGE * square), count)
    coefficients_ref[...] = wide(step_ref[...], count) * target + step * direction
    out_ref[...] = residual - step * applied


def call(body, out_shape, *args, source=VMEM, flops=0, bytes_accessed=0, **more):
    return pl.pallas_call(
        body,
        out_shape=out_shape,
        in_specs=[source] * len(args),
        out_specs=jax.tree.map(lambda _: VMEM, out_shape),
        compiler_params=pltpu.CompilerParams(vmem_limit_bytes=36 * 1024 * 1024),
        cost_estimate=pl.CostEstimate(
            flops=flops, bytes_accessed=bytes_accessed, transcendentals=0
        ),
        **more,
    )(*args)


def exchange(value, axis, near_first=False):
    size = lax.axis_size(axis)
    parts = [value]
    stride = 1
    while stride < size:
        value = pair_total(parts)
        span = min(4, size // stride)
        side = 0 if stride == 1 else 1
        parts = [value]
        for offset in range(1, span):
            pairs = [(i, i ^ (offset * stride) ^ side) for i in range(size)]
            parts.insert(0, lax.ppermute(value, axis, pairs))
        if near_first and stride == 1:
            parts = parts[-2:] + parts[:-2]
        stride *= span
    return parts


def shaped(shape, dtype=f32):
    return jax.ShapeDtypeStruct(shape, dtype)


def per_device(features, prices, slots, center_idx, center_scale):
    depth, row_count = features.shape
    count = center_idx.shape[0]
    all_rows = row_count * lax.axis_size("dp")
    row_shape = shaped((1, row_count + EXTRA))
    fold_shape = shaped((SLOTS, count + EXTRA))
    vector = shaped((SLOTS, count))
    narrow = shaped((SLOTS, EXTRA))
    pass_cost = dict(flops=64 * row_count * count, bytes_accessed=4 * row_count * count)

    inputs = [
        pltpu.with_memory_space_constraint(array, pltpu.HBM)
        for array in (
            features,
            center_idx.reshape(1, count),
            slots.reshape(1, row_count),
            prices.reshape(1, row_count),
            center_scale.reshape(1, count),
        )
    ]
    features, slots, prices, scale, picked = call(
        pick_body,
        (
            shaped(features.shape, bf16),
            shaped((1, row_count), jnp.int32),
            shaped((1, row_count)),
            shaped((1, count)),
            shaped((depth, count), bf16),
        ),
        *inputs,
        source=HBM,
        scratch_shapes=[
            pltpu.VMEM((1, count), jnp.int32),
            pltpu.VMEM((row_count, count), bf16),
            pltpu.SemaphoreType.DMA((5,)),
        ],
    )
    centers = exchange(picked, "dp")
    columns, turned_columns, weight = call(
        columns_body,
        (
            shaped((DEPTH, row_count), bf16),
            shaped((row_count, DEPTH), bf16),
            shaped((16, row_count), bf16),
        ),
        features, slots, prices,
        flops=1000 * row_count,
        bytes_accessed=1024 * row_count,
    )
    block, center, first = call(
        partial(rows_body, len(centers)),
        (shaped((2 * row_count, count), bf16), shaped((DEPTH, count), bf16), vector),
        turned_columns, weight, *centers,
        **pass_cost,
    )
    firsts = exchange(first, "dp")
    turned = call(
        turned_body, shaped((2 * count, row_count), bf16), columns, center, **pass_cost
    )
    target, rows = call(
        partial(first_apply_body, len(firsts), 1.0 / math.sqrt(all_rows)),
        (vector, row_shape),
        *firsts, scale, slots, turned,
    )
    rows = exchange(rows, "centers")
    rows, norm, folded = call(
        partial(first_fold_body, len(rows)), (row_shape, narrow, fold_shape), *rows, slots, block
    )
    folds = exchange(folded, "dp")
    residual, step, latest = call(
        partial(second_apply_body, len(folds), 1.0 / all_rows),
        (vector, narrow, row_shape),
        *folds, scale, slots, turned, target, norm,
    )
    latest = exchange(latest, "centers", True)
    sums, folded = call(
        partial(second_fold_body, len(latest)),
        (shaped((SLOTS, 2 * EXTRA)), fold_shape),
        *latest, slots, block, rows, norm,
    )
    folds = exchange(folded, "dp")
    return call(
        partial(finish_body, len(folds), 1.0 / all_rows),
        (vector, vector),
        *folds, scale, target, residual, step, norm, sums,
    )


def solution(mesh):
    return jax.shard_map(
        per_device,
        mesh=mesh,
        in_specs=(P(None, "dp"), P("dp"), P("dp"), P("centers"), P("centers")),
        out_specs=(P(None, "centers"), P(None, "centers")),
        check_vma=False,
    )
```

```python
import math
from functools import partial

import jax
import jax.numpy as jnp
from jax import lax
from jax.experimental import pallas as pl
from jax.experimental.pallas import tpu as pltpu
from jax.sharding import PartitionSpec as P

SLOTS = 8
RIDGE = 0.5
CHUNK = 512
EXTRA = 128
DEPTH = 256
STEP = 256
FACTOR = math.log2(math.e) / 64.0
f32 = jnp.float32
bf16 = jnp.bfloat16
VMEM = pl.BlockSpec(memory_space=pltpu.VMEM)
HBM = pl.BlockSpec(memory_space=pltpu.HBM)


def split3(value):
    high = value.astype(bf16).astype(f32)
    rest = value - high
    mid = rest.astype(bf16).astype(f32)
    return high, mid, rest - mid


def stack2(value):
    high = value.astype(bf16).astype(f32)
    return jnp.concatenate([high, value - high], axis=0).astype(bf16)


def product(stacked, high_block, low_block):
    main = jnp.dot(stacked, high_block, preferred_element_type=f32)
    rest = jnp.dot(stacked[0:SLOTS], low_block, preferred_element_type=f32)
    return main[0:SLOTS] + (main[SLOTS:] + rest)


def slot_lanes(first):
    lane = lax.broadcasted_iota(jnp.int32, (SLOTS, EXTRA), 1)
    return lane == lax.broadcasted_iota(jnp.int32, (SLOTS, EXTRA), 0) + first


def to_lanes(column, first):
    return jnp.sum(jnp.where(slot_lanes(first), column, 0.0), axis=0, keepdims=True)


def from_lanes(row, first):
    return jnp.sum(jnp.where(slot_lanes(first), row, 0.0), axis=1, keepdims=True)


def spread(column):
    return jnp.broadcast_to(column, (SLOTS, EXTRA))


def wide(narrow, count):
    return jnp.concatenate([narrow] * (count // EXTRA), axis=1)


def pair_total(parts):
    while len(parts) > 1:
        parts = [parts[i] + parts[i + 1] for i in range(0, len(parts), 2)]
    return parts[0]


def total_of(refs):
    return pair_total([ref[...] for ref in refs])


def row_sum(value):
    return jnp.sum(value, axis=1, keepdims=True)


def slot_mask(slots):
    row = lax.broadcasted_iota(jnp.int32, (SLOTS, slots.shape[1]), 0)
    return slots == row


def norm_rows(feat32, base):
    half = (-0.5 * FACTOR) * jnp.sum(feat32 * feat32, axis=0, keepdims=True)
    row = lax.broadcasted_iota(jnp.int32, (feat32.shape[0], feat32.shape[1]), 0)
    extra = jnp.where(row < 6, 1.0, 0.0)
    for place, part in enumerate(split3(half)):
        extra = jnp.where(row == base + place, part, extra)
    return extra


def kernel_parts(exponent):
    value = jnp.exp2(exponent)
    high = value.astype(bf16)
    return high, (value - high.astype(f32)).astype(bf16)


def pick_body(feat_hbm, idx_hbm, slots_hbm, prices_hbm, scale_hbm, *refs):
    feat_ref, slots_ref, prices_ref, scale_ref, out_ref, idx_ref, hit_ref, sems = refs
    row_count = feat_ref.shape[1]
    count = out_ref.shape[1]
    sources = (idx_hbm, feat_hbm, slots_hbm, prices_hbm, scale_hbm)
    targets = (idx_ref, feat_ref, slots_ref, prices_ref, scale_ref)
    copies = [
        pltpu.make_async_copy(source, target, sems.at[place])
        for place, (source, target) in enumerate(zip(sources, targets))
    ]
    for copy in copies:
        copy.start()
    copies[0].wait()
    local_idx = idx_ref[...] - lax.axis_index("dp") * row_count
    row = lax.broadcasted_iota(jnp.int32, (STEP, count), 0).astype(f32).astype(bf16)
    block = lax.div(local_idx, STEP)
    place = (local_idx - block * STEP).astype(f32)

    def hits(begin):
        own = jnp.where(block == begin // STEP, place, -1.0).astype(bf16)
        return jnp.where(row == own, jnp.ones_like(row), jnp.zeros_like(row))

    for begin in range(0, row_count, STEP):
        hit_ref[begin : begin + STEP, :] = hits(begin)
    copies[1].wait()
    out_ref[...] = jnp.dot(
        feat_ref[...], hit_ref[...], preferred_element_type=f32
    ).astype(bf16)
    for copy in copies[2:]:
        copy.wait()


def columns_body(feat_ref, slots_ref, prices_ref, columns_ref, turned_ref, weight_ref):
    for begin in range(0, feat_ref.shape[1], CHUNK):
        here = slice(begin, begin + CHUNK)
        feat32 = feat_ref[:, here].astype(f32)
        pair = jnp.concatenate([feat32, feat32], axis=0)
        last = jnp.concatenate([feat32, norm_rows(feat32, 3)], axis=0)
        columns_ref[0:128, here] = pair.astype(bf16)
        columns_ref[128:256, here] = last.astype(bf16)
        turned_ref[here, 0:128] = pair.T.astype(bf16)
        turned_ref[here, 128:256] = last.T.astype(bf16)
        weight = jnp.where(slot_mask(slots_ref[:, here]), prices_ref[:, here], 0.0)
        weight_ref[:, here] = stack2(weight)


def rows_body(parts, turned_ref, weight_ref, *refs):
    center_refs, (block_ref, center_ref, out_ref) = refs[:parts], refs[parts:]
    center = total_of(center_refs).astype(f32)
    center = jnp.concatenate(
        [*split3(center * FACTOR), norm_rows(center, 0)], axis=0
    ).astype(bf16)
    center_ref[...] = center
    row_count = turned_ref.shape[0]
    total = jnp.zeros(out_ref.shape, f32)

    def fold(begin):
        end = begin + CHUNK
        return product(
            weight_ref[:, begin:end],
            block_ref[begin:end, :],
            block_ref[row_count + begin : row_count + end, :],
        )

    def inner(begin):
        return jnp.dot(
            turned_ref[begin : begin + CHUNK, :], center, preferred_element_type=f32
        )

    ahead = inner(0)
    for begin in range(0, row_count, CHUNK):
        exponent = ahead
        if begin + CHUNK < row_count:
            ahead = inner(begin + CHUNK)
        high, low = kernel_parts(exponent)
        block_ref[begin : begin + CHUNK, :] = high
        block_ref[row_count + begin : row_count + begin + CHUNK, :] = low
        if begin > 0:
            total += fold(begin - CHUNK)
    out_ref[...] = total + fold(row_count - CHUNK)


def turned_body(columns_ref, center_ref, block_ref):
    center = center_ref[...].astype(f32).T.astype(bf16)
    count, row_count = center.shape[0], columns_ref.shape[1]

    def inner(begin):
        return jnp.dot(
            center, columns_ref[:, begin : begin + CHUNK], preferred_element_type=f32
        )

    ahead = inner(0)
    for begin in range(0, row_count, CHUNK):
        exponent = ahead
        if begin + CHUNK < row_count:
            ahead = inner(begin + CHUNK)
        high, low = kernel_parts(exponent)
        block_ref[0:count, begin : begin + CHUNK] = high
        block_ref[count:, begin : begin + CHUNK] = low


def apply_rows(scaled, turned_ref, slots_ref, out_ref):
    count, row_count = scaled.shape[1], turned_ref.shape[1]
    value = product(stack2(scaled), turned_ref[0:count, :], turned_ref[count:, :])
    own = jnp.where(slot_mask(slots_ref[...]), value, 0.0)
    out_ref[:, 0:row_count] = jnp.sum(own, axis=0, keepdims=True)


def fold_rows(rows, block_ref, slots_ref, out_ref):
    row_count, count = slots_ref.shape[1], block_ref.shape[1]
    weight = jnp.where(slot_mask(slots_ref[...]), rows, 0.0)
    out_ref[:, 0:count] = product(
        stack2(weight), block_ref[0:row_count, :], block_ref[row_count:, :]
    )
    square = row_sum(weight * weight)
    out_ref[:, count : count + EXTRA] = spread(square)


def first_apply_body(parts, scale_over_root, *refs):
    first_refs = refs[:parts]
    scale_ref, slots_ref, turned_ref, target_ref, out_ref = refs[parts:]
    scale = scale_ref[...]
    target = scale * total_of(first_refs) * scale_over_root
    target_ref[...] = target
    out_ref[:, turned_ref.shape[1] :] = to_lanes(row_sum(target * target), 0)
    apply_rows(scale * target, turned_ref, slots_ref, out_ref)


def first_fold_body(parts, *refs):
    row_refs = refs[:parts]
    slots_ref, block_ref, rows_ref, norm_ref, out_ref = refs[parts:]
    row_count = slots_ref.shape[1]
    rows = total_of(row_refs)
    rows_ref[...] = rows
    norm_ref[...] = spread(from_lanes(rows[:, row_count:], 0))
    fold_rows(rows[:, 0:row_count], block_ref, slots_ref, out_ref)


def second_apply_body(parts, inv_rows, *refs):
    fold_refs = refs[:parts]
    (scale_ref, slots_ref, turned_ref, target_ref, norm_ref,
     residual_ref, step_ref, out_ref) = refs[parts:]
    row_count, count = turned_ref.shape[1], scale_ref.shape[1]
    folded = total_of(fold_refs)
    scale = scale_ref[...]
    target = target_ref[...]
    norm = norm_ref[...]
    applied = scale * folded[:, 0:count] * inv_rows + RIDGE * target
    step = norm / (folded[:, count:] * inv_rows + RIDGE * norm)
    residual = target - wide(step, count) * applied
    residual_ref[...] = residual
    step_ref[...] = step
    out_ref[:, row_count:] = to_lanes(row_sum(residual * residual), 0) + to_lanes(
        row_sum(residual * target), SLOTS
    )
    apply_rows(scale * residual, turned_ref, slots_ref, out_ref)


def second_fold_body(parts, *refs):
    row_refs = refs[:parts]
    slots_ref, block_ref, rows_ref, norm_ref, sums_ref, out_ref = refs[parts:]
    row_count = slots_ref.shape[1]
    latest = total_of(row_refs)
    norm = spread(from_lanes(latest[:, row_count:], 0))
    ratio = norm / norm_ref[...]
    sums_ref[:, 0:EXTRA] = norm
    sums_ref[:, EXTRA:] = spread(from_lanes(latest[:, row_count:], SLOTS))
    rows = latest[:, 0:row_count] + wide(ratio, row_count) * rows_ref[:, 0:row_count]
    fold_rows(rows, block_ref, slots_ref, out_ref)


def finish_body(parts, inv_rows, *refs):
    fold_refs = refs[:parts]
    (scale_ref, target_ref, residual_ref, step_ref, norm_ref, sums_ref,
     first_hbm, second_hbm, first_ref, second_ref, sems) = refs[parts:]
    count = scale_ref.shape[1]
    folded = total_of(fold_refs)
    target = target_ref[...]
    residual = residual_ref[...]
    first_norm = norm_ref[...]
    norm, cross = sums_ref[:, 0:EXTRA], sums_ref[:, EXTRA:]
    ratio = norm / first_norm
    direction = residual + wide(ratio, count) * target
    square = norm + 2.0 * ratio * cross + ratio * ratio * first_norm
    applied = scale_ref[...] * folded[:, 0:count] * inv_rows + RIDGE * direction
    step = wide(norm / (folded[:, count:] * inv_rows + RIDGE * square), count)
    first_ref[...] = wide(step_ref[...], count) * target + step * direction
    first_copy = pltpu.make_async_copy(first_ref, first_hbm, sems.at[0])
    first_copy.start()
    second_ref[...] = residual - step * applied
    second_copy = pltpu.make_async_copy(second_ref, second_hbm, sems.at[1])
    second_copy.start()
    first_copy.wait()
    second_copy.wait()


def call(body, out_shape, *args, source=VMEM, target=VMEM, flops=0, bytes_accessed=0, **more):
    return pl.pallas_call(
        body,
        out_shape=out_shape,
        in_specs=[source] * len(args),
        out_specs=jax.tree.map(lambda _: target, out_shape),
        compiler_params=pltpu.CompilerParams(vmem_limit_bytes=36 * 1024 * 1024),
        cost_estimate=pl.CostEstimate(
            flops=flops, bytes_accessed=bytes_accessed, transcendentals=0
        ),
        **more,
    )(*args)


def exchange(value, axis, near_first=False):
    size = lax.axis_size(axis)
    parts = [value]
    stride = 1
    while stride < size:
        value = pair_total(parts)
        span = min(4, size // stride)
        side = 0 if stride == 1 else 1
        parts = [value]
        for offset in range(1, span):
            pairs = [(i, i ^ (offset * stride) ^ side) for i in range(size)]
            parts.insert(0, lax.ppermute(value, axis, pairs))
        if near_first and stride == 1:
            parts = parts[-2:] + parts[:-2]
        stride *= span
    return parts


def shaped(shape, dtype=f32):
    return jax.ShapeDtypeStruct(shape, dtype)


def per_device(features, prices, slots, center_idx, center_scale):
    depth, row_count = features.shape
    count = center_idx.shape[0]
    all_rows = row_count * lax.axis_size("dp")
    row_shape = shaped((1, row_count + EXTRA))
    fold_shape = shaped((SLOTS, count + EXTRA))
    vector = shaped((SLOTS, count))
    narrow = shaped((SLOTS, EXTRA))
    pass_cost = dict(flops=64 * row_count * count, bytes_accessed=4 * row_count * count)

    inputs = [
        pltpu.with_memory_space_constraint(array, pltpu.HBM)
        for array in (
            features,
            center_idx.reshape(1, count),
            slots.reshape(1, row_count),
            prices.reshape(1, row_count),
            center_scale.reshape(1, count),
        )
    ]
    features, slots, prices, scale, picked = call(
        pick_body,
        (
            shaped(features.shape, bf16),
            shaped((1, row_count), jnp.int32),
            shaped((1, row_count)),
            shaped((1, count)),
            shaped((depth, count), bf16),
        ),
        *inputs,
        source=HBM,
        scratch_shapes=[
            pltpu.VMEM((1, count), jnp.int32),
            pltpu.VMEM((row_count, count), bf16),
            pltpu.SemaphoreType.DMA((5,)),
        ],
    )
    centers = exchange(picked, "dp")
    columns, turned_columns, weight = call(
        columns_body,
        (
            shaped((DEPTH, row_count), bf16),
            shaped((row_count, DEPTH), bf16),
            shaped((16, row_count), bf16),
        ),
        features, slots, prices,
        flops=1000 * row_count,
        bytes_accessed=1024 * row_count,
    )
    block, center, first = call(
        partial(rows_body, len(centers)),
        (shaped((2 * row_count, count), bf16), shaped((DEPTH, count), bf16), vector),
        turned_columns, weight, *centers,
        **pass_cost,
    )
    firsts = exchange(first, "dp")
    turned = call(
        turned_body, shaped((2 * count, row_count), bf16), columns, center, **pass_cost
    )
    target, rows = call(
        partial(first_apply_body, len(firsts), 1.0 / math.sqrt(all_rows)),
        (vector, row_shape),
        *firsts, scale, slots, turned,
    )
    rows = exchange(rows, "centers")
    rows, norm, folded = call(
        partial(first_fold_body, len(rows)), (row_shape, narrow, fold_shape), *rows, slots, block
    )
    folds = exchange(folded, "dp")
    residual, step, latest = call(
        partial(second_apply_body, len(folds), 1.0 / all_rows),
        (vector, narrow, row_shape),
        *folds, scale, slots, turned, target, norm,
    )
    latest = exchange(latest, "centers", True)
    sums, folded = call(
        partial(second_fold_body, len(latest)),
        (shaped((SLOTS, 2 * EXTRA)), fold_shape),
        *latest, slots, block, rows, norm,
    )
    folds = exchange(folded, "dp")
    return call(
        partial(finish_body, len(folds), 1.0 / all_rows),
        (vector, vector),
        *folds, scale, target, residual, step, norm, sums,
        target=HBM,
        scratch_shapes=[
            pltpu.VMEM((SLOTS, count), f32),
            pltpu.VMEM((SLOTS, count), f32),
            pltpu.SemaphoreType.DMA((2,)),
        ],
    )


def solution(mesh):
    return jax.shard_map(
        per_device,
        mesh=mesh,
        in_specs=(P(None, "dp"), P("dp"), P("dp"), P("centers"), P("centers")),
        out_specs=(P(None, "centers"), P(None, "centers")),
        check_vma=False,
    )
```

```python
import math
from functools import partial

import jax
import jax.numpy as jnp
from jax import lax
from jax.experimental import pallas as pl
from jax.experimental.pallas import tpu as pltpu
from jax.sharding import PartitionSpec as P

SLOTS = 8
RIDGE = 0.5
CHUNK = 512
BUILD = 1024
EXTRA = 128
DEPTH = 256
STEP = 256
FACTOR = math.log2(math.e) / 64.0
f32 = jnp.float32
bf16 = jnp.bfloat16
VMEM = pl.BlockSpec(memory_space=pltpu.VMEM)
HBM = pl.BlockSpec(memory_space=pltpu.HBM)


def split3(value):
    high = value.astype(bf16).astype(f32)
    rest = value - high
    mid = rest.astype(bf16).astype(f32)
    return high, mid, rest - mid


def stack2(value):
    high = value.astype(bf16).astype(f32)
    return jnp.concatenate([high, value - high], axis=0).astype(bf16)


def product(stacked, high_block, low_block):
    main = jnp.dot(stacked, high_block, preferred_element_type=f32)
    rest = jnp.dot(stacked[0:SLOTS], low_block, preferred_element_type=f32)
    return main[0:SLOTS] + (main[SLOTS:] + rest)


def slot_lanes(first):
    lane = lax.broadcasted_iota(jnp.int32, (SLOTS, EXTRA), 1)
    return lane == lax.broadcasted_iota(jnp.int32, (SLOTS, EXTRA), 0) + first


def to_lanes(column, first):
    return jnp.sum(jnp.where(slot_lanes(first), column, 0.0), axis=0, keepdims=True)


def from_lanes(row, first):
    return jnp.sum(jnp.where(slot_lanes(first), row, 0.0), axis=1, keepdims=True)


def spread(column):
    return jnp.broadcast_to(column, (SLOTS, EXTRA))


def wide(narrow, count):
    return jnp.concatenate([narrow] * (count // EXTRA), axis=1)


def pair_total(parts):
    while len(parts) > 1:
        parts = [parts[i] + parts[i + 1] for i in range(0, len(parts), 2)]
    return parts[0]


def total_of(refs):
    return pair_total([ref[...] for ref in refs])


def row_sum(value):
    return jnp.sum(value, axis=1, keepdims=True)


def slot_mask(slots):
    row = lax.broadcasted_iota(jnp.int32, (SLOTS, slots.shape[1]), 0)
    return slots == row


def norm_rows(feat32, base):
    half = (-0.5 * FACTOR) * jnp.sum(feat32 * feat32, axis=0, keepdims=True)
    row = lax.broadcasted_iota(jnp.int32, (feat32.shape[0], feat32.shape[1]), 0)
    extra = jnp.where(row < 6, 1.0, 0.0)
    for place, part in enumerate(split3(half)):
        extra = jnp.where(row == base + place, part, extra)
    return extra


def kernel_parts(exponent):
    value = jnp.exp2(exponent)
    high = value.astype(bf16)
    return high, (value - high.astype(f32)).astype(bf16)


def pick_body(feat_hbm, idx_hbm, slots_hbm, prices_hbm, scale_hbm, *refs):
    feat_ref, slots_ref, prices_ref, scale_ref, out_ref, idx_ref, hit_ref, sems = refs
    row_count = feat_ref.shape[1]
    count = out_ref.shape[1]
    sources = (idx_hbm, feat_hbm, slots_hbm, prices_hbm, scale_hbm)
    targets = (idx_ref, feat_ref, slots_ref, prices_ref, scale_ref)
    copies = [
        pltpu.make_async_copy(source, target, sems.at[place])
        for place, (source, target) in enumerate(zip(sources, targets))
    ]
    for copy in copies:
        copy.start()
    copies[0].wait()
    local_idx = idx_ref[...] - lax.axis_index("dp") * row_count
    row = lax.broadcasted_iota(jnp.int32, (STEP, count), 0).astype(f32).astype(bf16)
    block = lax.div(local_idx, STEP)
    place = (local_idx - block * STEP).astype(f32)

    def hits(begin):
        own = jnp.where(block == begin // STEP, place, -1.0).astype(bf16)
        return jnp.where(row == own, jnp.ones_like(row), jnp.zeros_like(row))

    for begin in range(0, row_count, STEP):
        hit_ref[begin : begin + STEP, :] = hits(begin)
    copies[1].wait()
    out_ref[...] = jnp.dot(
        feat_ref[...], hit_ref[...], preferred_element_type=f32
    ).astype(bf16)
    for copy in copies[2:]:
        copy.wait()


def columns_body(feat_ref, slots_ref, prices_ref, columns_ref, turned_ref, weight_ref):
    for begin in range(0, feat_ref.shape[1], CHUNK):
        here = slice(begin, begin + CHUNK)
        feat32 = feat_ref[:, here].astype(f32)
        pair = jnp.concatenate([feat32, feat32], axis=0)
        last = jnp.concatenate([feat32, norm_rows(feat32, 3)], axis=0)
        columns_ref[0:128, here] = pair.astype(bf16)
        columns_ref[128:256, here] = last.astype(bf16)
        turned_ref[here, 0:128] = pair.T.astype(bf16)
        turned_ref[here, 128:256] = last.T.astype(bf16)
        weight = jnp.where(slot_mask(slots_ref[:, here]), prices_ref[:, here], 0.0)
        weight_ref[:, here] = stack2(weight)


def rows_body(parts, turned_ref, weight_ref, *refs):
    center_refs, (block_ref, center_ref, out_ref) = refs[:parts], refs[parts:]
    center = total_of(center_refs).astype(f32)
    center = jnp.concatenate(
        [*split3(center * FACTOR), norm_rows(center, 0)], axis=0
    ).astype(bf16)
    center_ref[...] = center
    row_count = turned_ref.shape[0]
    total = jnp.zeros(out_ref.shape, f32)

    def fold(begin):
        end = begin + BUILD
        return product(
            weight_ref[:, begin:end],
            block_ref[begin:end, :],
            block_ref[row_count + begin : row_count + end, :],
        )

    def inner(begin):
        return jnp.dot(
            turned_ref[begin : begin + BUILD, :], center, preferred_element_type=f32
        )

    ahead = inner(0)
    for begin in range(0, row_count, BUILD):
        exponent = ahead
        if begin + BUILD < row_count:
            ahead = inner(begin + BUILD)
        high, low = kernel_parts(exponent)
        block_ref[begin : begin + BUILD, :] = high
        block_ref[row_count + begin : row_count + begin + BUILD, :] = low
        if begin > 0:
            total += fold(begin - BUILD)
    out_ref[...] = total + fold(row_count - BUILD)


def turned_body(columns_ref, center_ref, block_ref):
    center = center_ref[...].astype(f32).T.astype(bf16)
    count, row_count = center.shape[0], columns_ref.shape[1]

    def inner(begin):
        return jnp.dot(
            center, columns_ref[:, begin : begin + BUILD], preferred_element_type=f32
        )

    ahead = inner(0)
    for begin in range(0, row_count, BUILD):
        exponent = ahead
        if begin + BUILD < row_count:
            ahead = inner(begin + BUILD)
        high, low = kernel_parts(exponent)
        block_ref[0:count, begin : begin + BUILD] = high
        block_ref[count:, begin : begin + BUILD] = low


def apply_rows(scaled, turned_ref, slots_ref, out_ref):
    count, row_count = scaled.shape[1], turned_ref.shape[1]
    value = product(stack2(scaled), turned_ref[0:count, :], turned_ref[count:, :])
    own = jnp.where(slot_mask(slots_ref[...]), value, 0.0)
    out_ref[:, 0:row_count] = jnp.sum(own, axis=0, keepdims=True)


def fold_rows(rows, block_ref, slots_ref, out_ref):
    row_count, count = slots_ref.shape[1], block_ref.shape[1]
    weight = jnp.where(slot_mask(slots_ref[...]), rows, 0.0)
    out_ref[:, 0:count] = product(
        stack2(weight), block_ref[0:row_count, :], block_ref[row_count:, :]
    )
    square = row_sum(weight * weight)
    out_ref[:, count : count + EXTRA] = spread(square)


def first_apply_body(parts, scale_over_root, *refs):
    first_refs = refs[:parts]
    scale_ref, slots_ref, turned_ref, target_ref, out_ref = refs[parts:]
    scale = scale_ref[...]
    target = scale * total_of(first_refs) * scale_over_root
    target_ref[...] = target
    out_ref[:, turned_ref.shape[1] :] = to_lanes(row_sum(target * target), 0)
    apply_rows(scale * target, turned_ref, slots_ref, out_ref)


def first_fold_body(parts, *refs):
    row_refs = refs[:parts]
    slots_ref, block_ref, rows_ref, norm_ref, out_ref = refs[parts:]
    row_count = slots_ref.shape[1]
    rows = total_of(row_refs)
    rows_ref[...] = rows
    norm_ref[...] = spread(from_lanes(rows[:, row_count:], 0))
    fold_rows(rows[:, 0:row_count], block_ref, slots_ref, out_ref)


def second_apply_body(parts, inv_rows, *refs):
    fold_refs = refs[:parts]
    (scale_ref, slots_ref, turned_ref, target_ref, norm_ref,
     residual_ref, step_ref, out_ref) = refs[parts:]
    row_count, count = turned_ref.shape[1], scale_ref.shape[1]
    folded = total_of(fold_refs)
    scale = scale_ref[...]
    target = target_ref[...]
    norm = norm_ref[...]
    applied = scale * folded[:, 0:count] * inv_rows + RIDGE * target
    step = norm / (folded[:, count:] * inv_rows + RIDGE * norm)
    residual = target - wide(step, count) * applied
    residual_ref[...] = residual
    step_ref[...] = step
    out_ref[:, row_count:] = to_lanes(row_sum(residual * residual), 0) + to_lanes(
        row_sum(residual * target), SLOTS
    )
    apply_rows(scale * residual, turned_ref, slots_ref, out_ref)


def second_fold_body(parts, *refs):
    row_refs = refs[:parts]
    slots_ref, block_ref, rows_ref, norm_ref, sums_ref, out_ref = refs[parts:]
    row_count = slots_ref.shape[1]
    latest = total_of(row_refs)
    norm = spread(from_lanes(latest[:, row_count:], 0))
    ratio = norm / norm_ref[...]
    sums_ref[:, 0:EXTRA] = norm
    sums_ref[:, EXTRA:] = spread(from_lanes(latest[:, row_count:], SLOTS))
    rows = latest[:, 0:row_count] + wide(ratio, row_count) * rows_ref[:, 0:row_count]
    fold_rows(rows, block_ref, slots_ref, out_ref)


def finish_body(parts, inv_rows, *refs):
    fold_refs = refs[:parts]
    (scale_ref, target_ref, residual_ref, step_ref, norm_ref, sums_ref,
     coefficients_ref, out_ref) = refs[parts:]
    count = scale_ref.shape[1]
    folded = total_of(fold_refs)
    target = target_ref[...]
    residual = residual_ref[...]
    first_norm = norm_ref[...]
    norm, cross = sums_ref[:, 0:EXTRA], sums_ref[:, EXTRA:]
    ratio = norm / first_norm
    direction = residual + wide(ratio, count) * target
    square = norm + 2.0 * ratio * cross + ratio * ratio * first_norm
    applied = scale_ref[...] * folded[:, 0:count] * inv_rows + RIDGE * direction
    step = wide(norm / (folded[:, count:] * inv_rows + RIDGE * square), count)
    coefficients_ref[...] = wide(step_ref[...], count) * target + step * direction
    out_ref[...] = residual - step * applied


def call(body, out_shape, *args, source=VMEM, flops=0, bytes_accessed=0, **more):
    return pl.pallas_call(
        body,
        out_shape=out_shape,
        in_specs=[source] * len(args),
        out_specs=jax.tree.map(lambda _: VMEM, out_shape),
        compiler_params=pltpu.CompilerParams(vmem_limit_bytes=36 * 1024 * 1024),
        cost_estimate=pl.CostEstimate(
            flops=flops, bytes_accessed=bytes_accessed, transcendentals=0
        ),
        **more,
    )(*args)


def exchange(value, axis, near_first=False):
    size = lax.axis_size(axis)
    parts = [value]
    stride = 1
    while stride < size:
        value = pair_total(parts)
        span = min(4, size // stride)
        side = 0 if stride == 1 else 1
        parts = [value]
        for offset in range(1, span):
            pairs = [(i, i ^ (offset * stride) ^ side) for i in range(size)]
            parts.insert(0, lax.ppermute(value, axis, pairs))
        if near_first and stride == 1:
            parts = parts[-2:] + parts[:-2]
        stride *= span
    return parts


def shaped(shape, dtype=f32):
    return jax.ShapeDtypeStruct(shape, dtype)


def per_device(features, prices, slots, center_idx, center_scale):
    depth, row_count = features.shape
    count = center_idx.shape[0]
    all_rows = row_count * lax.axis_size("dp")
    row_shape = shaped((1, row_count + EXTRA))
    fold_shape = shaped((SLOTS, count + EXTRA))
    vector = shaped((SLOTS, count))
    narrow = shaped((SLOTS, EXTRA))
    pass_cost = dict(flops=64 * row_count * count, bytes_accessed=4 * row_count * count)

    inputs = [
        pltpu.with_memory_space_constraint(array, pltpu.HBM)
        for array in (
            features,
            center_idx.reshape(1, count),
            slots.reshape(1, row_count),
            prices.reshape(1, row_count),
            center_scale.reshape(1, count),
        )
    ]
    features, slots, prices, scale, picked = call(
        pick_body,
        (
            shaped(features.shape, bf16),
            shaped((1, row_count), jnp.int32),
            shaped((1, row_count)),
            shaped((1, count)),
            shaped((depth, count), bf16),
        ),
        *inputs,
        source=HBM,
        scratch_shapes=[
            pltpu.VMEM((1, count), jnp.int32),
            pltpu.VMEM((row_count, count), bf16),
            pltpu.SemaphoreType.DMA((5,)),
        ],
    )
    centers = exchange(picked, "dp")
    columns, turned_columns, weight = call(
        columns_body,
        (
            shaped((DEPTH, row_count), bf16),
            shaped((row_count, DEPTH), bf16),
            shaped((16, row_count), bf16),
        ),
        features, slots, prices,
        flops=1000 * row_count,
        bytes_accessed=1024 * row_count,
    )
    block, center, first = call(
        partial(rows_body, len(centers)),
        (shaped((2 * row_count, count), bf16), shaped((DEPTH, count), bf16), vector),
        turned_columns, weight, *centers,
        **pass_cost,
    )
    firsts = exchange(first, "dp")
    turned = call(
        turned_body, shaped((2 * count, row_count), bf16), columns, center, **pass_cost
    )
    target, rows = call(
        partial(first_apply_body, len(firsts), 1.0 / math.sqrt(all_rows)),
        (vector, row_shape),
        *firsts, scale, slots, turned,
    )
    rows = exchange(rows, "centers")
    rows, norm, folded = call(
        partial(first_fold_body, len(rows)), (row_shape, narrow, fold_shape), *rows, slots, block
    )
    folds = exchange(folded, "dp")
    residual, step, latest = call(
        partial(second_apply_body, len(folds), 1.0 / all_rows),
        (vector, narrow, row_shape),
        *folds, scale, slots, turned, target, norm,
    )
    latest = exchange(latest, "centers", True)
    sums, folded = call(
        partial(second_fold_body, len(latest)),
        (shaped((SLOTS, 2 * EXTRA)), fold_shape),
        *latest, slots, block, rows, norm,
    )
    folds = exchange(folded, "dp")
    return call(
        partial(finish_body, len(folds), 1.0 / all_rows),
        (vector, vector),
        *folds, scale, target, residual, step, norm, sums,
    )


def solution(mesh):
    return jax.shard_map(
        per_device,
        mesh=mesh,
        in_specs=(P(None, "dp"), P("dp"), P("dp"), P("centers"), P("centers")),
        out_specs=(P(None, "centers"), P(None, "centers")),
        check_vma=False,
    )
```

```python
import math
from functools import partial

import jax
import jax.numpy as jnp
from jax import lax
from jax.experimental import pallas as pl
from jax.experimental.pallas import tpu as pltpu
from jax.sharding import PartitionSpec as P

SLOTS = 8
RIDGE = 0.5
CHUNK = 512
EXTRA = 128
DEPTH = 256
STEP = 256
FACTOR = math.log2(math.e) / 64.0
f32 = jnp.float32
bf16 = jnp.bfloat16
VMEM = pl.BlockSpec(memory_space=pltpu.VMEM)
HBM = pl.BlockSpec(memory_space=pltpu.HBM)


def split3(value):
    high = value.astype(bf16).astype(f32)
    rest = value - high
    mid = rest.astype(bf16).astype(f32)
    return high, mid, rest - mid


def stack2(value):
    high = value.astype(bf16).astype(f32)
    return jnp.concatenate([high, value - high], axis=0).astype(bf16)


def product(stacked, high_block, low_block):
    main = jnp.dot(stacked, high_block, preferred_element_type=f32)
    rest = jnp.dot(stacked[0:SLOTS], low_block, preferred_element_type=f32)
    return main[0:SLOTS] + (main[SLOTS:] + rest)


def slot_lanes(first):
    lane = lax.broadcasted_iota(jnp.int32, (SLOTS, EXTRA), 1)
    return lane == lax.broadcasted_iota(jnp.int32, (SLOTS, EXTRA), 0) + first


def to_lanes(column, first):
    return jnp.sum(jnp.where(slot_lanes(first), column, 0.0), axis=0, keepdims=True)


def from_lanes(row, first):
    return jnp.sum(jnp.where(slot_lanes(first), row, 0.0), axis=1, keepdims=True)


def spread(column):
    return jnp.broadcast_to(column, (SLOTS, EXTRA))


def wide(narrow, count):
    return jnp.concatenate([narrow] * (count // EXTRA), axis=1)


def pair_total(parts):
    while len(parts) > 1:
        parts = [parts[i] + parts[i + 1] for i in range(0, len(parts), 2)]
    return parts[0]


def total_of(refs):
    return pair_total([ref[...] for ref in refs])


def row_sum(value):
    return jnp.sum(value, axis=1, keepdims=True)


def slot_mask(slots):
    row = lax.broadcasted_iota(jnp.int32, (SLOTS, slots.shape[1]), 0)
    return slots == row


def norm_rows(feat32, base):
    half = (-0.5 * FACTOR) * jnp.sum(feat32 * feat32, axis=0, keepdims=True)
    row = lax.broadcasted_iota(jnp.int32, (feat32.shape[0], feat32.shape[1]), 0)
    extra = jnp.where(row < 6, 1.0, 0.0)
    for place, part in enumerate(split3(half)):
        extra = jnp.where(row == base + place, part, extra)
    return extra


def kernel_parts(exponent):
    value = jnp.exp2(exponent)
    high = value.astype(bf16)
    return high, (value - high.astype(f32)).astype(bf16)


def pick_body(feat_hbm, idx_hbm, slots_hbm, prices_hbm, scale_hbm, *refs):
    feat_ref, slots_ref, prices_ref, scale_ref, out_ref, idx_ref, hit_ref, sems = refs
    row_count = feat_ref.shape[1]
    count = out_ref.shape[1]
    bands = [pl.ds(first, 16) for first in range(0, feat_ref.shape[0], 16)]
    sources = [idx_hbm, *(feat_hbm.at[band, :] for band in bands)]
    targets = [idx_ref, *(feat_ref.at[band, :] for band in bands)]
    sources += [slots_hbm, prices_hbm, scale_hbm]
    targets += [slots_ref, prices_ref, scale_ref]
    copies = [
        pltpu.make_async_copy(source, target, sems.at[place])
        for place, (source, target) in enumerate(zip(sources, targets))
    ]
    for copy in copies:
        copy.start()
    copies[0].wait()
    local_idx = idx_ref[...] - lax.axis_index("dp") * row_count
    row = lax.broadcasted_iota(jnp.int32, (STEP, count), 0).astype(f32).astype(bf16)
    block = lax.div(local_idx, STEP)
    place = (local_idx - block * STEP).astype(f32)

    def hits(begin):
        own = jnp.where(block == begin // STEP, place, -1.0).astype(bf16)
        return jnp.where(row == own, jnp.ones_like(row), jnp.zeros_like(row))

    for begin in range(0, row_count, STEP):
        hit_ref[begin : begin + STEP, :] = hits(begin)
    for copy in copies[1 : 1 + len(bands)]:
        copy.wait()
    out_ref[...] = jnp.dot(
        feat_ref[...], hit_ref[...], preferred_element_type=f32
    ).astype(bf16)
    for copy in copies[1 + len(bands) :]:
        copy.wait()


def columns_body(feat_ref, slots_ref, prices_ref, columns_ref, turned_ref, weight_ref):
    for begin in range(0, feat_ref.shape[1], CHUNK):
        here = slice(begin, begin + CHUNK)
        feat32 = feat_ref[:, here].astype(f32)
        pair = jnp.concatenate([feat32, feat32], axis=0)
        last = jnp.concatenate([feat32, norm_rows(feat32, 3)], axis=0)
        columns_ref[0:128, here] = pair.astype(bf16)
        columns_ref[128:256, here] = last.astype(bf16)
        turned_ref[here, 0:128] = pair.T.astype(bf16)
        turned_ref[here, 128:256] = last.T.astype(bf16)
        weight = jnp.where(slot_mask(slots_ref[:, here]), prices_ref[:, here], 0.0)
        weight_ref[:, here] = stack2(weight)


def rows_body(parts, turned_ref, weight_ref, *refs):
    center_refs, (block_ref, center_ref, out_ref) = refs[:parts], refs[parts:]
    center = total_of(center_refs).astype(f32)
    center = jnp.concatenate(
        [*split3(center * FACTOR), norm_rows(center, 0)], axis=0
    ).astype(bf16)
    center_ref[...] = center
    row_count = turned_ref.shape[0]
    total = jnp.zeros(out_ref.shape, f32)

    def fold(begin):
        end = begin + CHUNK
        return product(
            weight_ref[:, begin:end],
            block_ref[begin:end, :],
            block_ref[row_count + begin : row_count + end, :],
        )

    def inner(begin):
        return jnp.dot(
            turned_ref[begin : begin + CHUNK, :], center, preferred_element_type=f32
        )

    ahead = inner(0)
    for begin in range(0, row_count, CHUNK):
        exponent = ahead
        if begin + CHUNK < row_count:
            ahead = inner(begin + CHUNK)
        high, low = kernel_parts(exponent)
        block_ref[begin : begin + CHUNK, :] = high
        block_ref[row_count + begin : row_count + begin + CHUNK, :] = low
        if begin > 0:
            total += fold(begin - CHUNK)
    out_ref[...] = total + fold(row_count - CHUNK)


def turned_body(columns_ref, center_ref, block_ref):
    center = center_ref[...].astype(f32).T.astype(bf16)
    count, row_count = center.shape[0], columns_ref.shape[1]

    def inner(begin):
        return jnp.dot(
            center, columns_ref[:, begin : begin + CHUNK], preferred_element_type=f32
        )

    ahead = inner(0)
    for begin in range(0, row_count, CHUNK):
        exponent = ahead
        if begin + CHUNK < row_count:
            ahead = inner(begin + CHUNK)
        high, low = kernel_parts(exponent)
        block_ref[0:count, begin : begin + CHUNK] = high
        block_ref[count:, begin : begin + CHUNK] = low


def apply_rows(scaled, turned_ref, slots_ref, out_ref):
    count, row_count = scaled.shape[1], turned_ref.shape[1]
    value = product(stack2(scaled), turned_ref[0:count, :], turned_ref[count:, :])
    own = jnp.where(slot_mask(slots_ref[...]), value, 0.0)
    out_ref[:, 0:row_count] = jnp.sum(own, axis=0, keepdims=True)


def fold_rows(rows, block_ref, slots_ref, out_ref):
    row_count, count = slots_ref.shape[1], block_ref.shape[1]
    weight = jnp.where(slot_mask(slots_ref[...]), rows, 0.0)
    out_ref[:, 0:count] = product(
        stack2(weight), block_ref[0:row_count, :], block_ref[row_count:, :]
    )
    square = row_sum(weight * weight)
    out_ref[:, count : count + EXTRA] = spread(square)


def first_apply_body(parts, scale_over_root, *refs):
    first_refs = refs[:parts]
    scale_ref, slots_ref, turned_ref, target_ref, out_ref = refs[parts:]
    scale = scale_ref[...]
    target = scale * total_of(first_refs) * scale_over_root
    target_ref[...] = target
    out_ref[:, turned_ref.shape[1] :] = to_lanes(row_sum(target * target), 0)
    apply_rows(scale * target, turned_ref, slots_ref, out_ref)


def first_fold_body(parts, *refs):
    row_refs = refs[:parts]
    slots_ref, block_ref, rows_ref, norm_ref, out_ref = refs[parts:]
    row_count = slots_ref.shape[1]
    rows = total_of(row_refs)
    rows_ref[...] = rows
    norm_ref[...] = spread(from_lanes(rows[:, row_count:], 0))
    fold_rows(rows[:, 0:row_count], block_ref, slots_ref, out_ref)


def second_apply_body(parts, inv_rows, *refs):
    fold_refs = refs[:parts]
    (scale_ref, slots_ref, turned_ref, target_ref, norm_ref,
     residual_ref, step_ref, out_ref) = refs[parts:]
    row_count, count = turned_ref.shape[1], scale_ref.shape[1]
    folded = total_of(fold_refs)
    scale = scale_ref[...]
    target = target_ref[...]
    norm = norm_ref[...]
    applied = scale * folded[:, 0:count] * inv_rows + RIDGE * target
    step = norm / (folded[:, count:] * inv_rows + RIDGE * norm)
    residual = target - wide(step, count) * applied
    residual_ref[...] = residual
    step_ref[...] = step
    out_ref[:, row_count:] = to_lanes(row_sum(residual * residual), 0) + to_lanes(
        row_sum(residual * target), SLOTS
    )
    apply_rows(scale * residual, turned_ref, slots_ref, out_ref)


def second_fold_body(parts, *refs):
    row_refs = refs[:parts]
    slots_ref, block_ref, rows_ref, norm_ref, sums_ref, out_ref = refs[parts:]
    row_count = slots_ref.shape[1]
    latest = total_of(row_refs)
    norm = spread(from_lanes(latest[:, row_count:], 0))
    ratio = norm / norm_ref[...]
    sums_ref[:, 0:EXTRA] = norm
    sums_ref[:, EXTRA:] = spread(from_lanes(latest[:, row_count:], SLOTS))
    rows = latest[:, 0:row_count] + wide(ratio, row_count) * rows_ref[:, 0:row_count]
    fold_rows(rows, block_ref, slots_ref, out_ref)


def finish_body(parts, inv_rows, *refs):
    fold_refs = refs[:parts]
    (scale_ref, target_ref, residual_ref, step_ref, norm_ref, sums_ref,
     coefficients_ref, out_ref) = refs[parts:]
    count = scale_ref.shape[1]
    folded = total_of(fold_refs)
    target = target_ref[...]
    residual = residual_ref[...]
    first_norm = norm_ref[...]
    norm, cross = sums_ref[:, 0:EXTRA], sums_ref[:, EXTRA:]
    ratio = norm / first_norm
    direction = residual + wide(ratio, count) * target
    square = norm + 2.0 * ratio * cross + ratio * ratio * first_norm
    applied = scale_ref[...] * folded[:, 0:count] * inv_rows + RIDGE * direction
    step = wide(norm / (folded[:, count:] * inv_rows + RIDGE * square), count)
    coefficients_ref[...] = wide(step_ref[...], count) * target + step * direction
    out_ref[...] = residual - step * applied


def call(body, out_shape, *args, source=VMEM, flops=0, bytes_accessed=0, **more):
    return pl.pallas_call(
        body,
        out_shape=out_shape,
        in_specs=[source] * len(args),
        out_specs=jax.tree.map(lambda _: VMEM, out_shape),
        compiler_params=pltpu.CompilerParams(vmem_limit_bytes=36 * 1024 * 1024),
        cost_estimate=pl.CostEstimate(
            flops=flops, bytes_accessed=bytes_accessed, transcendentals=0
        ),
        **more,
    )(*args)


def exchange(value, axis, near_first=False):
    size = lax.axis_size(axis)
    parts = [value]
    stride = 1
    while stride < size:
        value = pair_total(parts)
        span = min(4, size // stride)
        side = 0 if stride == 1 else 1
        parts = [value]
        for offset in range(1, span):
            pairs = [(i, i ^ (offset * stride) ^ side) for i in range(size)]
            parts.insert(0, lax.ppermute(value, axis, pairs))
        if near_first and stride == 1:
            parts = parts[-2:] + parts[:-2]
        stride *= span
    return parts


def shaped(shape, dtype=f32):
    return jax.ShapeDtypeStruct(shape, dtype)


def per_device(features, prices, slots, center_idx, center_scale):
    depth, row_count = features.shape
    count = center_idx.shape[0]
    all_rows = row_count * lax.axis_size("dp")
    row_shape = shaped((1, row_count + EXTRA))
    fold_shape = shaped((SLOTS, count + EXTRA))
    vector = shaped((SLOTS, count))
    narrow = shaped((SLOTS, EXTRA))
    pass_cost = dict(flops=64 * row_count * count, bytes_accessed=4 * row_count * count)

    inputs = [
        pltpu.with_memory_space_constraint(array, pltpu.HBM)
        for array in (
            features,
            center_idx.reshape(1, count),
            slots.reshape(1, row_count),
            prices.reshape(1, row_count),
            center_scale.reshape(1, count),
        )
    ]
    features, slots, prices, scale, picked = call(
        pick_body,
        (
            shaped(features.shape, bf16),
            shaped((1, row_count), jnp.int32),
            shaped((1, row_count)),
            shaped((1, count)),
            shaped((depth, count), bf16),
        ),
        *inputs,
        source=HBM,
        scratch_shapes=[
            pltpu.VMEM((1, count), jnp.int32),
            pltpu.VMEM((row_count, count), bf16),
            pltpu.SemaphoreType.DMA((4 + depth // 16,)),
        ],
    )
    centers = exchange(picked, "dp")
    columns, turned_columns, weight = call(
        columns_body,
        (
            shaped((DEPTH, row_count), bf16),
            shaped((row_count, DEPTH), bf16),
            shaped((16, row_count), bf16),
        ),
        features, slots, prices,
        flops=1000 * row_count,
        bytes_accessed=1024 * row_count,
    )
    block, center, first = call(
        partial(rows_body, len(centers)),
        (shaped((2 * row_count, count), bf16), shaped((DEPTH, count), bf16), vector),
        turned_columns, weight, *centers,
        **pass_cost,
    )
    firsts = exchange(first, "dp")
    turned = call(
        turned_body, shaped((2 * count, row_count), bf16), columns, center, **pass_cost
    )
    target, rows = call(
        partial(first_apply_body, len(firsts), 1.0 / math.sqrt(all_rows)),
        (vector, row_shape),
        *firsts, scale, slots, turned,
    )
    rows = exchange(rows, "centers")
    rows, norm, folded = call(
        partial(first_fold_body, len(rows)), (row_shape, narrow, fold_shape), *rows, slots, block
    )
    folds = exchange(folded, "dp")
    residual, step, latest = call(
        partial(second_apply_body, len(folds), 1.0 / all_rows),
        (vector, narrow, row_shape),
        *folds, scale, slots, turned, target, norm,
    )
    latest = exchange(latest, "centers", True)
    sums, folded = call(
        partial(second_fold_body, len(latest)),
        (shaped((SLOTS, 2 * EXTRA)), fold_shape),
        *latest, slots, block, rows, norm,
    )
    folds = exchange(folded, "dp")
    return call(
        partial(finish_body, len(folds), 1.0 / all_rows),
        (vector, vector),
        *folds, scale, target, residual, step, norm, sums,
    )


def solution(mesh):
    return jax.shard_map(
        per_device,
        mesh=mesh,
        in_specs=(P(None, "dp"), P("dp"), P("dp"), P("centers"), P("centers")),
        out_specs=(P(None, "centers"), P(None, "centers")),
        check_vma=False,
    )
```

```python
import math
from functools import partial

import jax
import jax.numpy as jnp
from jax import lax
from jax.experimental import pallas as pl
from jax.experimental.pallas import tpu as pltpu
from jax.sharding import PartitionSpec as P

SLOTS = 8
RIDGE = 0.5
CHUNK = 512
EXTRA = 128
DEPTH = 256
STEP = 256
FACTOR = math.log2(math.e) / 64.0
f32 = jnp.float32
bf16 = jnp.bfloat16
VMEM = pl.BlockSpec(memory_space=pltpu.VMEM)
HBM = pl.BlockSpec(memory_space=pltpu.HBM)


def split3(value):
    high = value.astype(bf16).astype(f32)
    rest = value - high
    mid = rest.astype(bf16).astype(f32)
    return high, mid, rest - mid


def stack2(value):
    high = value.astype(bf16).astype(f32)
    return jnp.concatenate([high, value - high], axis=0).astype(bf16)


def product(stacked, high_block, low_block):
    main = jnp.dot(stacked, high_block, preferred_element_type=f32)
    rest = jnp.dot(stacked[0:SLOTS], low_block, preferred_element_type=f32)
    return main[0:SLOTS] + (main[SLOTS:] + rest)


def slot_lanes(first):
    lane = lax.broadcasted_iota(jnp.int32, (SLOTS, EXTRA), 1)
    return lane == lax.broadcasted_iota(jnp.int32, (SLOTS, EXTRA), 0) + first


def to_lanes(column, first):
    return jnp.sum(jnp.where(slot_lanes(first), column, 0.0), axis=0, keepdims=True)


def from_lanes(row, first):
    return jnp.sum(jnp.where(slot_lanes(first), row, 0.0), axis=1, keepdims=True)


def spread(column):
    return jnp.broadcast_to(column, (SLOTS, EXTRA))


def wide(narrow, count):
    return jnp.concatenate([narrow] * (count // EXTRA), axis=1)


def pair_total(parts):
    while len(parts) > 1:
        parts = [parts[i] + parts[i + 1] for i in range(0, len(parts), 2)]
    return parts[0]


def total_of(refs):
    return pair_total([ref[...] for ref in refs])


def resident(moved, own):
    return jnp.where(lax.axis_index("dp") == 0, own, moved)


def row_sum(value):
    return jnp.sum(value, axis=1, keepdims=True)


def slot_mask(slots):
    row = lax.broadcasted_iota(jnp.int32, (SLOTS, slots.shape[1]), 0)
    return slots == row


def norm_rows(feat32, base):
    half = (-0.5 * FACTOR) * jnp.sum(feat32 * feat32, axis=0, keepdims=True)
    row = lax.broadcasted_iota(jnp.int32, (feat32.shape[0], feat32.shape[1]), 0)
    extra = jnp.where(row < 6, 1.0, 0.0)
    for place, part in enumerate(split3(half)):
        extra = jnp.where(row == base + place, part, extra)
    return extra


def kernel_parts(exponent):
    value = jnp.exp2(exponent)
    high = value.astype(bf16)
    return high, (value - high.astype(f32)).astype(bf16)


def pick(feat_ref, idx, hit_ref):
    row_count, count = hit_ref.shape
    local_idx = idx - lax.axis_index("dp") * row_count
    row = lax.broadcasted_iota(jnp.int32, (STEP, count), 0).astype(f32).astype(bf16)
    block = lax.div(local_idx, STEP)
    place = (local_idx - block * STEP).astype(f32)
    for begin in range(0, row_count, STEP):
        own = jnp.where(block == begin // STEP, place, -1.0).astype(bf16)
        hit = jnp.where(row == own, jnp.ones_like(row), jnp.zeros_like(row))
        hit_ref[begin : begin + STEP, :] = hit


def pick_body(feat_hbm, idx_hbm, slots_hbm, prices_hbm, scale_hbm, *refs):
    feat_ref, idx_ref, slots_ref, prices_ref, scale_ref, out_ref, hit_ref, sems = refs
    sources = (idx_hbm, feat_hbm, slots_hbm, prices_hbm, scale_hbm)
    targets = (idx_ref, feat_ref, slots_ref, prices_ref, scale_ref)
    copies = [
        pltpu.make_async_copy(source, target, sems.at[place])
        for place, (source, target) in enumerate(zip(sources, targets))
    ]
    for copy in copies:
        copy.start()
    copies[0].wait()
    pick(feat_ref, idx_ref[...], hit_ref)
    copies[1].wait()
    picked = jnp.dot(feat_ref[...], hit_ref[...], preferred_element_type=f32)
    for copy in copies[2:]:
        copy.wait()
    row = lax.broadcasted_iota(jnp.int32, (16, picked.shape[1]), 0)
    extra = jnp.zeros(row.shape, f32)
    for place, part in enumerate(split3(scale_ref[...])):
        extra = jnp.where(row == place, part, extra)
    out_ref[...] = jnp.concatenate([picked, extra], axis=0).astype(bf16)


def pick_beside_body(feat_ref, moved_idx_ref, idx_ref, picked_ref, out_ref, hit_ref):
    first = lax.axis_index("dp") == 0
    pick(feat_ref, jnp.where(first, idx_ref[...], moved_idx_ref[...]), hit_ref)
    out_ref[0:-16, :] = jnp.dot(
        feat_ref[...], hit_ref[...], preferred_element_type=f32
    ).astype(bf16)
    own = picked_ref[-16:, :].astype(f32)
    out_ref[-16:, :] = jnp.where(first, own, 0.0).astype(bf16)


def columns_body(feat_ref, slots_ref, prices_ref, columns_ref, turned_ref, weight_ref):
    for begin in range(0, feat_ref.shape[1], CHUNK):
        here = slice(begin, begin + CHUNK)
        feat32 = feat_ref[:, here].astype(f32)
        pair = jnp.concatenate([feat32, feat32], axis=0)
        last = jnp.concatenate([feat32, norm_rows(feat32, 3)], axis=0)
        columns_ref[0:128, here] = pair.astype(bf16)
        columns_ref[128:256, here] = last.astype(bf16)
        turned_ref[here, 0:128] = pair.T.astype(bf16)
        turned_ref[here, 128:256] = last.T.astype(bf16)
        weight = jnp.where(slot_mask(slots_ref[:, here]), prices_ref[:, here], 0.0)
        weight_ref[:, here] = stack2(weight)


def rows_body(crossed, parts, turned_ref, weight_ref, *refs):
    center_refs, (block_ref, center_ref, scale_ref, out_ref) = refs[:parts], refs[parts:]
    arrived = total_of(center_refs).astype(f32)
    rows = arrived[-16:] * (1.0 / lax.axis_size("dp"))
    if crossed:
        rows = jnp.where(lax.axis_index("dp") == 0, rows, arrived[-16:])
    scale_ref[...] = rows[0:1] + (rows[1:2] + rows[2:3])
    center = arrived[:-16]
    center = jnp.concatenate(
        [*split3(center * FACTOR), norm_rows(center, 0)], axis=0
    ).astype(bf16)
    center_ref[...] = center
    row_count = turned_ref.shape[0]
    total = jnp.zeros(out_ref.shape, f32)

    def fold(begin):
        end = begin + CHUNK
        return product(
            weight_ref[:, begin:end],
            block_ref[begin:end, :],
            block_ref[row_count + begin : row_count + end, :],
        )

    def inner(begin):
        return jnp.dot(
            turned_ref[begin : begin + CHUNK, :], center, preferred_element_type=f32
        )

    ahead = inner(0)
    for begin in range(0, row_count, CHUNK):
        exponent = ahead
        if begin + CHUNK < row_count:
            ahead = inner(begin + CHUNK)
        high, low = kernel_parts(exponent)
        block_ref[begin : begin + CHUNK, :] = high
        block_ref[row_count + begin : row_count + begin + CHUNK, :] = low
        if begin > 0:
            total += fold(begin - CHUNK)
    out_ref[...] = total + fold(row_count - CHUNK)


def turned_body(columns_ref, center_ref, block_ref):
    center = center_ref[...].astype(f32).T.astype(bf16)
    count, row_count = center.shape[0], columns_ref.shape[1]

    def inner(begin):
        return jnp.dot(
            center, columns_ref[:, begin : begin + CHUNK], preferred_element_type=f32
        )

    ahead = inner(0)
    for begin in range(0, row_count, CHUNK):
        exponent = ahead
        if begin + CHUNK < row_count:
            ahead = inner(begin + CHUNK)
        high, low = kernel_parts(exponent)
        block_ref[0:count, begin : begin + CHUNK] = high
        block_ref[count:, begin : begin + CHUNK] = low


def apply_rows(scaled, turned_ref, slots_ref, out_ref):
    count, row_count = scaled.shape[1], turned_ref.shape[1]
    value = product(stack2(scaled), turned_ref[0:count, :], turned_ref[count:, :])
    own = jnp.where(slot_mask(slots_ref[...]), value, 0.0)
    out_ref[:, 0:row_count] = jnp.sum(own, axis=0, keepdims=True)


def fold_rows(rows, block_ref, slots_ref, out_ref):
    row_count, count = slots_ref.shape[1], block_ref.shape[1]
    weight = jnp.where(slot_mask(slots_ref[...]), rows, 0.0)
    out_ref[:, 0:count] = product(
        stack2(weight), block_ref[0:row_count, :], block_ref[row_count:, :]
    )
    square = row_sum(weight * weight)
    out_ref[:, count : count + EXTRA] = spread(square)


def first_apply_body(parts, scale_over_root, *refs):
    first_refs = refs[:parts]
    scale_ref, slots_ref, turned_ref, target_ref, out_ref = refs[parts:]
    scale = scale_ref[...]
    target = scale * total_of(first_refs) * scale_over_root
    target_ref[...] = target
    out_ref[:, turned_ref.shape[1] :] = to_lanes(row_sum(target * target), 0)
    apply_rows(scale * target, turned_ref, slots_ref, out_ref)


def first_fold_body(parts, *refs):
    row_refs = refs[:parts]
    slots_ref, block_ref, rows_ref, norm_ref, out_ref = refs[parts:]
    row_count = slots_ref.shape[1]
    rows = total_of(row_refs)
    rows_ref[...] = rows
    norm_ref[...] = spread(from_lanes(rows[:, row_count:], 0))
    fold_rows(rows[:, 0:row_count], block_ref, slots_ref, out_ref)


def second_apply_body(parts, inv_rows, *refs):
    fold_refs = refs[:parts]
    (scale_ref, slots_ref, turned_ref, target_ref, norm_ref,
     state_ref, step_ref, out_ref) = refs[parts:]
    row_count, count = turned_ref.shape[1], scale_ref.shape[1]
    folded = total_of(fold_refs)
    scale = scale_ref[...]
    target = target_ref[...]
    norm = norm_ref[...]
    applied = scale * folded[:, 0:count] * inv_rows + RIDGE * target
    step = norm / (folded[:, count:] * inv_rows + RIDGE * norm)
    residual = target - wide(step, count) * applied
    state_ref[0:SLOTS, :] = target
    state_ref[SLOTS:, :] = residual
    step_ref[...] = step
    out_ref[:, row_count:] = to_lanes(row_sum(residual * residual), 0) + to_lanes(
        row_sum(residual * target), SLOTS
    )
    apply_rows(scale * residual, turned_ref, slots_ref, out_ref)


def second_fold_body(parts, *refs):
    row_refs = refs[:parts]
    slots_ref, block_ref, rows_ref, norm_ref, state_ref, sums_ref, out_ref, bundle_ref = refs[parts:]
    row_count = slots_ref.shape[1]
    bundle_ref[SLOTS:, 0 : state_ref.shape[1]] = state_ref[...]
    bundle_ref[SLOTS:, state_ref.shape[1] :] = jnp.zeros((2 * SLOTS, EXTRA), f32)
    latest = total_of(row_refs)
    norm = spread(from_lanes(latest[:, row_count:], 0))
    ratio = norm / norm_ref[...]
    sums_ref[:, 0:EXTRA] = norm
    sums_ref[:, EXTRA:] = spread(from_lanes(latest[:, row_count:], SLOTS))
    rows = latest[:, 0:row_count] + wide(ratio, row_count) * rows_ref[:, 0:row_count]
    fold_rows(rows, block_ref, slots_ref, out_ref)
    bundle_ref[0:SLOTS, :] = out_ref[...]


def finish_body(crossed, parts, inv_rows, *refs):
    fold_refs = refs[:parts]
    (scale_ref, step_ref, norm_ref, sums_ref,
     coefficients_ref, out_ref) = refs[parts:]
    count = scale_ref.shape[1]
    bundle = fold_refs[-1][...]
    if crossed:
        far_ref, moved_ref = fold_refs[:-1]
        bundle = resident(moved_ref[...], bundle)
        folded = far_ref[...] + bundle[0:SLOTS]
    else:
        folded = total_of(fold_refs[:-1])
    target, residual = bundle[SLOTS : 2 * SLOTS, 0:count], bundle[2 * SLOTS :, 0:count]
    first_norm = norm_ref[...]
    norm, cross = sums_ref[:, 0:EXTRA], sums_ref[:, EXTRA:]
    ratio = norm / first_norm
    direction = residual + wide(ratio, count) * target
    square = norm + 2.0 * ratio * cross + ratio * ratio * first_norm
    applied = scale_ref[...] * folded[:, 0:count] * inv_rows + RIDGE * direction
    step = wide(norm / (folded[:, count:] * inv_rows + RIDGE * square), count)
    coefficients_ref[...] = wide(step_ref[...], count) * target + step * direction
    out_ref[...] = residual - step * applied


def call(body, out_shape, *args, sources=None, flops=0, bytes_accessed=0, **more):
    return pl.pallas_call(
        body,
        out_shape=out_shape,
        in_specs=sources or [VMEM] * len(args),
        out_specs=jax.tree.map(lambda _: VMEM, out_shape),
        compiler_params=pltpu.CompilerParams(vmem_limit_bytes=36 * 1024 * 1024),
        cost_estimate=pl.CostEstimate(
            flops=flops, bytes_accessed=bytes_accessed, transcendentals=0
        ),
        **more,
    )(*args)


def exchange(value, axis):
    size = lax.axis_size(axis)
    parts = [value]
    stride = 1
    while stride < size:
        value = pair_total(parts)
        span = min(4, size // stride)
        side = 0 if stride == 1 else 1
        parts = [value]
        offsets = (1, 3, 2) if stride == 1 else (1, 2, 3)
        for offset in offsets[: span - 1]:
            pairs = [(i, i ^ (offset * stride) ^ side) for i in range(size)]
            parts.insert(0, lax.ppermute(value, axis, pairs))
        stride *= span
    return parts


def pairs_over(target_of):
    groups, count = lax.axis_size("dp"), lax.axis_size("centers")
    pairs = []
    for group in range(groups):
        for place in range(count):
            to_group, to_place = target_of(group, place)
            pairs.append((group * count + place, to_group * count + to_place))
    return pairs


def moved(value, target_of):
    return lax.ppermute(value, ("dp", "centers"), pairs_over(target_of))


def across(group, place):
    return 1 - group, place ^ 1


def beside(group, place):
    return group, place ^ 1


def outward(group, place):
    return 1 - group, place ^ (1 - group)


def homeward(group, place):
    return 1 - group, place ^ group


def shaped(shape, dtype=f32):
    return jax.ShapeDtypeStruct(shape, dtype)


def per_device(features, prices, slots, center_idx, center_scale):
    depth, row_count = features.shape
    count = center_idx.shape[0]
    all_rows = row_count * lax.axis_size("dp")
    row_shape = shaped((1, row_count + EXTRA))
    fold_shape = shaped((SLOTS, count + EXTRA))
    vector = shaped((SLOTS, count))
    narrow = shaped((SLOTS, EXTRA))
    pass_cost = dict(flops=64 * row_count * count, bytes_accessed=4 * row_count * count)

    crossed = lax.axis_size("dp") == 2

    def share(value):
        return [moved(value, across), value] if crossed else exchange(value, "dp")

    moved_idx = moved(center_idx, beside) if crossed else center_idx
    inputs = [
        pltpu.with_memory_space_constraint(array, pltpu.HBM)
        for array in (
            features,
            center_idx.reshape(1, count),
            slots.reshape(1, row_count),
            prices.reshape(1, row_count),
            center_scale.reshape(1, count),
        )
    ]
    features, idx, slots, prices, own_scale, picked = call(
        pick_body,
        (
            shaped(features.shape, bf16),
            shaped((1, count), jnp.int32),
            shaped((1, row_count), jnp.int32),
            shaped((1, row_count)),
            shaped((1, count)),
            shaped((depth + 16, count), bf16),
        ),
        *inputs,
        sources=[HBM] * 5,
        scratch_shapes=[
            pltpu.VMEM((row_count, count), bf16),
            pltpu.SemaphoreType.DMA((5,)),
        ],
    )
    if crossed:
        resident_picks = call(
            pick_beside_body,
            shaped((depth + 16, count), bf16),
            features, moved_idx.reshape(1, count), idx, picked,
            flops=128 * row_count * count,
            bytes_accessed=128 * row_count,
            scratch_shapes=[pltpu.VMEM((row_count, count), bf16)],
        )
        centers = [moved(picked, outward), resident_picks]
    else:
        centers = exchange(picked, "dp")
    columns, turned_columns, weight = call(
        columns_body,
        (
            shaped((DEPTH, row_count), bf16),
            shaped((row_count, DEPTH), bf16),
            shaped((16, row_count), bf16),
        ),
        features, slots, prices,
        flops=1000 * row_count,
        bytes_accessed=1024 * row_count,
    )
    block, center, scale, first = call(
        partial(rows_body, crossed, len(centers)),
        (
            shaped((2 * row_count, count), bf16),
            shaped((DEPTH, count), bf16),
            shaped((1, count)),
            vector,
        ),
        turned_columns, weight, *centers,
        **pass_cost,
    )
    firsts = share(first)
    turned = call(
        turned_body, shaped((2 * count, row_count), bf16), columns, center, **pass_cost
    )
    target, rows = call(
        partial(first_apply_body, len(firsts), 1.0 / math.sqrt(all_rows)),
        (vector, row_shape),
        *firsts, scale, slots, turned,
    )
    rows = exchange(rows, "centers")
    rows, norm, folded = call(
        partial(first_fold_body, len(rows)), (row_shape, narrow, fold_shape), *rows, slots, block
    )
    folds = share(folded)
    state, step, latest = call(
        partial(second_apply_body, len(folds), 1.0 / all_rows),
        (shaped((2 * SLOTS, count)), narrow, row_shape),
        *folds, scale, slots, turned, target, norm,
    )
    latest = exchange(latest, "centers")
    sums, folded, bundle = call(
        partial(second_fold_body, len(latest)),
        (
            shaped((SLOTS, 2 * EXTRA)),
            fold_shape,
            shaped((3 * SLOTS, count + EXTRA)),
        ),
        *latest, slots, block, rows, norm, state,
    )
    if crossed:
        folds = [moved(folded, homeward), moved(bundle, beside), bundle]
    else:
        folds = exchange(folded, "dp") + [bundle]
    return call(
        partial(finish_body, crossed, len(folds), 1.0 / all_rows),
        (vector, vector),
        *folds, own_scale, step, norm, sums,
    )


def solution(mesh):
    return jax.shard_map(
        per_device,
        mesh=mesh,
        in_specs=(P(None, "dp"), P("dp"), P("dp"), P("centers"), P("centers")),
        out_specs=(P(None, "centers"), P(None, "centers")),
        check_vma=False,
    )
```

```python
import math
from functools import partial

import jax
import jax.numpy as jnp
from jax import lax
from jax.experimental import pallas as pl
from jax.experimental.pallas import tpu as pltpu
from jax.sharding import PartitionSpec as P

SLOTS = 8
RIDGE = 0.5
CHUNK = 512
EXTRA = 128
DEPTH = 256
STEP = 256
FACTOR = math.log2(math.e) / 64.0
f32 = jnp.float32
bf16 = jnp.bfloat16
VMEM = pl.BlockSpec(memory_space=pltpu.VMEM)
HBM = pl.BlockSpec(memory_space=pltpu.HBM)


def split3(value):
    high = value.astype(bf16).astype(f32)
    rest = value - high
    mid = rest.astype(bf16).astype(f32)
    return high, mid, rest - mid


def stack2(value):
    high = value.astype(bf16).astype(f32)
    return jnp.concatenate([high, value - high], axis=0).astype(bf16)


def product(stacked, high_block, low_block):
    main = jnp.dot(stacked, high_block, preferred_element_type=f32)
    rest = jnp.dot(stacked[0:SLOTS], low_block, preferred_element_type=f32)
    return main[0:SLOTS] + (main[SLOTS:] + rest)


def slot_lanes(first):
    lane = lax.broadcasted_iota(jnp.int32, (SLOTS, EXTRA), 1)
    return lane == lax.broadcasted_iota(jnp.int32, (SLOTS, EXTRA), 0) + first


def to_lanes(column, first):
    return jnp.sum(jnp.where(slot_lanes(first), column, 0.0), axis=0, keepdims=True)


def from_lanes(row, first):
    return jnp.sum(jnp.where(slot_lanes(first), row, 0.0), axis=1, keepdims=True)


def spread(column):
    return jnp.broadcast_to(column, (SLOTS, EXTRA))


def wide(narrow, count):
    return jnp.concatenate([narrow] * (count // EXTRA), axis=1)


def pair_total(parts):
    while len(parts) > 1:
        parts = [parts[i] + parts[i + 1] for i in range(0, len(parts), 2)]
    return parts[0]


def total_of(refs):
    return pair_total([ref[...] for ref in refs])


def resident(moved, own):
    return jnp.where(lax.axis_index("dp") == 0, own, moved)


def row_sum(value):
    return jnp.sum(value, axis=1, keepdims=True)


def slot_mask(slots):
    row = lax.broadcasted_iota(jnp.int32, (SLOTS, slots.shape[1]), 0)
    return slots == row


def norm_rows(feat32, base):
    half = (-0.5 * FACTOR) * jnp.sum(feat32 * feat32, axis=0, keepdims=True)
    row = lax.broadcasted_iota(jnp.int32, (feat32.shape[0], feat32.shape[1]), 0)
    extra = jnp.where(row < 6, 1.0, 0.0)
    for place, part in enumerate(split3(half)):
        extra = jnp.where(row == base + place, part, extra)
    return extra


def kernel_parts(exponent):
    value = jnp.exp2(exponent)
    high = value.astype(bf16)
    return high, (value - high.astype(f32)).astype(bf16)


def pick(feat_ref, idx, hit_ref):
    row_count, count = hit_ref.shape
    local_idx = idx - lax.axis_index("dp") * row_count
    row = lax.broadcasted_iota(jnp.int32, (STEP, count), 0).astype(f32).astype(bf16)
    block = lax.div(local_idx, STEP)
    place = (local_idx - block * STEP).astype(f32)
    for begin in range(0, row_count, STEP):
        own = jnp.where(block == begin // STEP, place, -1.0).astype(bf16)
        hit = jnp.where(row == own, jnp.ones_like(row), jnp.zeros_like(row))
        hit_ref[begin : begin + STEP, :] = hit


def pick_body(feat_hbm, idx_hbm, slots_hbm, prices_hbm, scale_hbm, *refs):
    feat_ref, idx_ref, slots_ref, prices_ref, scale_ref, out_ref, hit_ref, sems = refs
    sources = (idx_hbm, feat_hbm, slots_hbm, prices_hbm, scale_hbm)
    targets = (idx_ref, feat_ref, slots_ref, prices_ref, scale_ref)
    copies = [
        pltpu.make_async_copy(source, target, sems.at[place])
        for place, (source, target) in enumerate(zip(sources, targets))
    ]
    for copy in copies:
        copy.start()
    copies[0].wait()
    pick(feat_ref, idx_ref[...], hit_ref)
    copies[1].wait()
    picked = jnp.dot(feat_ref[...], hit_ref[...], preferred_element_type=f32)
    for copy in copies[2:]:
        copy.wait()
    out_ref[...] = picked.astype(bf16)


def pick_beside_body(feat_ref, moved_idx_ref, idx_ref, out_ref, hit_ref):
    first = lax.axis_index("dp") == 0
    pick(feat_ref, jnp.where(first, idx_ref[...], moved_idx_ref[...]), hit_ref)
    out_ref[...] = jnp.dot(
        feat_ref[...], hit_ref[...], preferred_element_type=f32
    ).astype(bf16)


def columns_body(feat_ref, slots_ref, prices_ref, columns_ref, turned_ref, weight_ref):
    for begin in range(0, feat_ref.shape[1], CHUNK):
        here = slice(begin, begin + CHUNK)
        feat32 = feat_ref[:, here].astype(f32)
        pair = jnp.concatenate([feat32, feat32], axis=0)
        last = jnp.concatenate([feat32, norm_rows(feat32, 3)], axis=0)
        columns_ref[0:128, here] = pair.astype(bf16)
        columns_ref[128:256, here] = last.astype(bf16)
        turned_ref[here, 0:128] = pair.T.astype(bf16)
        turned_ref[here, 128:256] = last.T.astype(bf16)
        weight = jnp.where(slot_mask(slots_ref[:, here]), prices_ref[:, here], 0.0)
        weight_ref[:, here] = stack2(weight)


def rows_body(parts, turned_ref, weight_ref, moved_scale_ref, own_scale_ref, *refs):
    center_refs, (block_ref, center_ref, scale_ref, out_ref) = refs[:parts], refs[parts:]
    scale_ref[...] = resident(moved_scale_ref[...], own_scale_ref[...])
    center = total_of(center_refs).astype(f32)
    center = jnp.concatenate(
        [*split3(center * FACTOR), norm_rows(center, 0)], axis=0
    ).astype(bf16)
    center_ref[...] = center
    row_count = turned_ref.shape[0]
    total = jnp.zeros(out_ref.shape, f32)

    def fold(begin):
        end = begin + CHUNK
        return product(
            weight_ref[:, begin:end],
            block_ref[begin:end, :],
            block_ref[row_count + begin : row_count + end, :],
        )

    def inner(begin):
        return jnp.dot(
            turned_ref[begin : begin + CHUNK, :], center, preferred_element_type=f32
        )

    ahead = inner(0)
    for begin in range(0, row_count, CHUNK):
        exponent = ahead
        if begin + CHUNK < row_count:
            ahead = inner(begin + CHUNK)
        high, low = kernel_parts(exponent)
        block_ref[begin : begin + CHUNK, :] = high
        block_ref[row_count + begin : row_count + begin + CHUNK, :] = low
        if begin > 0:
            total += fold(begin - CHUNK)
    out_ref[...] = total + fold(row_count - CHUNK)


def turned_body(columns_ref, center_ref, block_ref):
    center = center_ref[...].astype(f32).T.astype(bf16)
    count, row_count = center.shape[0], columns_ref.shape[1]

    def inner(begin):
        return jnp.dot(
            center, columns_ref[:, begin : begin + CHUNK], preferred_element_type=f32
        )

    ahead = inner(0)
    for begin in range(0, row_count, CHUNK):
        exponent = ahead
        if begin + CHUNK < row_count:
            ahead = inner(begin + CHUNK)
        high, low = kernel_parts(exponent)
        block_ref[0:count, begin : begin + CHUNK] = high
        block_ref[count:, begin : begin + CHUNK] = low


def apply_rows(scaled, turned_ref, slots_ref, out_ref):
    count, row_count = scaled.shape[1], turned_ref.shape[1]
    value = product(stack2(scaled), turned_ref[0:count, :], turned_ref[count:, :])
    own = jnp.where(slot_mask(slots_ref[...]), value, 0.0)
    out_ref[:, 0:row_count] = jnp.sum(own, axis=0, keepdims=True)


def fold_rows(rows, block_ref, slots_ref, out_ref):
    row_count, count = slots_ref.shape[1], block_ref.shape[1]
    weight = jnp.where(slot_mask(slots_ref[...]), rows, 0.0)
    out_ref[:, 0:count] = product(
        stack2(weight), block_ref[0:row_count, :], block_ref[row_count:, :]
    )
    square = row_sum(weight * weight)
    out_ref[:, count : count + EXTRA] = spread(square)


def first_apply_body(parts, scale_over_root, *refs):
    first_refs = refs[:parts]
    scale_ref, slots_ref, turned_ref, target_ref, out_ref = refs[parts:]
    scale = scale_ref[...]
    target = scale * total_of(first_refs) * scale_over_root
    target_ref[...] = target
    out_ref[:, turned_ref.shape[1] :] = to_lanes(row_sum(target * target), 0)
    apply_rows(scale * target, turned_ref, slots_ref, out_ref)


def first_fold_body(parts, *refs):
    row_refs = refs[:parts]
    slots_ref, block_ref, rows_ref, norm_ref, out_ref = refs[parts:]
    row_count = slots_ref.shape[1]
    rows = total_of(row_refs)
    rows_ref[...] = rows
    norm_ref[...] = spread(from_lanes(rows[:, row_count:], 0))
    fold_rows(rows[:, 0:row_count], block_ref, slots_ref, out_ref)


def second_apply_body(parts, inv_rows, *refs):
    fold_refs = refs[:parts]
    (scale_ref, slots_ref, turned_ref, target_ref, norm_ref,
     state_ref, step_ref, out_ref) = refs[parts:]
    row_count, count = turned_ref.shape[1], scale_ref.shape[1]
    folded = total_of(fold_refs)
    scale = scale_ref[...]
    target = target_ref[...]
    norm = norm_ref[...]
    applied = scale * folded[:, 0:count] * inv_rows + RIDGE * target
    step = norm / (folded[:, count:] * inv_rows + RIDGE * norm)
    residual = target - wide(step, count) * applied
    state_ref[0:SLOTS, :] = target
    state_ref[SLOTS:, :] = residual
    step_ref[...] = step
    out_ref[:, row_count:] = to_lanes(row_sum(residual * residual), 0) + to_lanes(
        row_sum(residual * target), SLOTS
    )
    apply_rows(scale * residual, turned_ref, slots_ref, out_ref)


def second_fold_body(parts, *refs):
    row_refs = refs[:parts]
    slots_ref, block_ref, rows_ref, norm_ref, sums_ref, out_ref = refs[parts:]
    row_count = slots_ref.shape[1]
    latest = total_of(row_refs)
    norm = spread(from_lanes(latest[:, row_count:], 0))
    ratio = norm / norm_ref[...]
    sums_ref[:, 0:EXTRA] = norm
    sums_ref[:, EXTRA:] = spread(from_lanes(latest[:, row_count:], SLOTS))
    rows = latest[:, 0:row_count] + wide(ratio, row_count) * rows_ref[:, 0:row_count]
    fold_rows(rows, block_ref, slots_ref, out_ref)


def finish_body(crossed, parts, inv_rows, *refs):
    fold_refs = refs[:parts]
    (moved_ref, state_ref, scale_ref, step_ref, norm_ref, sums_ref,
     coefficients_ref, out_ref) = refs[parts:]
    count = scale_ref.shape[1]
    if crossed:
        far, moved, own = (ref[...] for ref in fold_refs)
        folded = far + resident(moved, own)
        state = resident(moved_ref[...], state_ref[...])
    else:
        folded = total_of(fold_refs)
        state = state_ref[...]
    target, residual = state[0:SLOTS], state[SLOTS:]
    first_norm = norm_ref[...]
    norm, cross = sums_ref[:, 0:EXTRA], sums_ref[:, EXTRA:]
    ratio = norm / first_norm
    direction = residual + wide(ratio, count) * target
    square = norm + 2.0 * ratio * cross + ratio * ratio * first_norm
    applied = scale_ref[...] * folded[:, 0:count] * inv_rows + RIDGE * direction
    step = wide(norm / (folded[:, count:] * inv_rows + RIDGE * square), count)
    coefficients_ref[...] = wide(step_ref[...], count) * target + step * direction
    out_ref[...] = residual - step * applied


def call(body, out_shape, *args, sources=None, flops=0, bytes_accessed=0, **more):
    return pl.pallas_call(
        body,
        out_shape=out_shape,
        in_specs=sources or [VMEM] * len(args),
        out_specs=jax.tree.map(lambda _: VMEM, out_shape),
        compiler_params=pltpu.CompilerParams(vmem_limit_bytes=36 * 1024 * 1024),
        cost_estimate=pl.CostEstimate(
            flops=flops, bytes_accessed=bytes_accessed, transcendentals=0
        ),
        **more,
    )(*args)


def exchange(value, axis):
    size = lax.axis_size(axis)
    parts = [value]
    stride = 1
    while stride < size:
        value = pair_total(parts)
        span = min(4, size // stride)
        side = 0 if stride == 1 else 1
        parts = [value]
        offsets = (1, 3, 2) if stride == 1 else (1, 2, 3)
        for offset in offsets[: span - 1]:
            pairs = [(i, i ^ (offset * stride) ^ side) for i in range(size)]
            parts.insert(0, lax.ppermute(value, axis, pairs))
        stride *= span
    return parts


def pairs_over(target_of):
    groups, count = lax.axis_size("dp"), lax.axis_size("centers")
    pairs = []
    for group in range(groups):
        for place in range(count):
            to_group, to_place = target_of(group, place)
            pairs.append((group * count + place, to_group * count + to_place))
    return pairs


def moved(value, target_of):
    return lax.ppermute(value, ("dp", "centers"), pairs_over(target_of))


def across(group, place):
    return 1 - group, place ^ 1


def beside(group, place):
    return group, place ^ 1


def outward(group, place):
    return 1 - group, place ^ (1 - group)


def homeward(group, place):
    return 1 - group, place ^ group


def shaped(shape, dtype=f32):
    return jax.ShapeDtypeStruct(shape, dtype)


def per_device(features, prices, slots, center_idx, center_scale):
    depth, row_count = features.shape
    count = center_idx.shape[0]
    all_rows = row_count * lax.axis_size("dp")
    row_shape = shaped((1, row_count + EXTRA))
    fold_shape = shaped((SLOTS, count + EXTRA))
    vector = shaped((SLOTS, count))
    narrow = shaped((SLOTS, EXTRA))
    pass_cost = dict(flops=64 * row_count * count, bytes_accessed=4 * row_count * count)

    crossed = lax.axis_size("dp") == 2

    def share(value):
        return [moved(value, across), value] if crossed else exchange(value, "dp")

    inputs = [
        pltpu.with_memory_space_constraint(array, pltpu.HBM)
        for array in (
            features,
            center_idx.reshape(1, count),
            slots.reshape(1, row_count),
            prices.reshape(1, row_count),
            center_scale.reshape(1, count),
        )
    ]
    features, idx, slots, prices, own_scale, picked = call(
        pick_body,
        (
            shaped(features.shape, bf16),
            shaped((1, count), jnp.int32),
            shaped((1, row_count), jnp.int32),
            shaped((1, row_count)),
            shaped((1, count)),
            shaped((depth, count), bf16),
        ),
        *inputs,
        sources=[HBM] * 5,
        scratch_shapes=[
            pltpu.VMEM((row_count, count), bf16),
            pltpu.SemaphoreType.DMA((5,)),
        ],
    )
    if crossed:
        moved_idx = moved(center_idx, beside)
        resident_picks = call(
            pick_beside_body,
            shaped((depth, count), bf16),
            features, moved_idx.reshape(1, count), idx,
            flops=128 * row_count * count,
            bytes_accessed=128 * row_count,
            scratch_shapes=[pltpu.VMEM((row_count, count), bf16)],
        )
        centers = [moved(picked, outward), resident_picks]
        moved_scale = moved(center_scale, beside).reshape(1, count)
    else:
        centers = exchange(picked, "dp")
        moved_scale = own_scale
    columns, turned_columns, weight = call(
        columns_body,
        (
            shaped((DEPTH, row_count), bf16),
            shaped((row_count, DEPTH), bf16),
            shaped((16, row_count), bf16),
        ),
        features, slots, prices,
        flops=1000 * row_count,
        bytes_accessed=1024 * row_count,
    )
    block, center, scale, first = call(
        partial(rows_body, len(centers)),
        (
            shaped((2 * row_count, count), bf16),
            shaped((DEPTH, count), bf16),
            shaped((1, count)),
            vector,
        ),
        turned_columns, weight, moved_scale, own_scale, *centers,
        **pass_cost,
    )
    firsts = share(first)
    turned = call(
        turned_body, shaped((2 * count, row_count), bf16), columns, center, **pass_cost
    )
    target, rows = call(
        partial(first_apply_body, len(firsts), 1.0 / math.sqrt(all_rows)),
        (vector, row_shape),
        *firsts, scale, slots, turned,
    )
    rows = exchange(rows, "centers")
    rows, norm, folded = call(
        partial(first_fold_body, len(rows)), (row_shape, narrow, fold_shape), *rows, slots, block
    )
    folds = share(folded)
    state, step, latest = call(
        partial(second_apply_body, len(folds), 1.0 / all_rows),
        (shaped((2 * SLOTS, count)), narrow, row_shape),
        *folds, scale, slots, turned, target, norm,
    )
    latest = exchange(latest, "centers")
    sums, folded = call(
        partial(second_fold_body, len(latest)),
        (shaped((SLOTS, 2 * EXTRA)), fold_shape),
        *latest, slots, block, rows, norm,
    )
    if crossed:
        folds = [moved(folded, homeward), moved(folded, beside), folded]
        moved_state = moved(state, beside)
    else:
        folds = exchange(folded, "dp")
        moved_state = state
    return call(
        partial(finish_body, crossed, len(folds), 1.0 / all_rows),
        (vector, vector),
        *folds, moved_state, state, own_scale, step, norm, sums,
    )


def solution(mesh):
    return jax.shard_map(
        per_device,
        mesh=mesh,
        in_specs=(P(None, "dp"), P("dp"), P("dp"), P("centers"), P("centers")),
        out_specs=(P(None, "centers"), P(None, "centers")),
        check_vma=False,
    )
```

```python
import math
from functools import partial

import jax
import jax.numpy as jnp
from jax import lax
from jax.experimental import pallas as pl
from jax.experimental.pallas import tpu as pltpu
from jax.sharding import PartitionSpec as P

SLOTS = 8
RIDGE = 0.5
CHUNK = 512
EXTRA = 128
DEPTH = 256
STEP = 256
FACTOR = math.log2(math.e) / 64.0
f32 = jnp.float32
bf16 = jnp.bfloat16
VMEM = pl.BlockSpec(memory_space=pltpu.VMEM)
HBM = pl.BlockSpec(memory_space=pltpu.HBM)


def split3(value):
    high = value.astype(bf16).astype(f32)
    rest = value - high
    mid = rest.astype(bf16).astype(f32)
    return high, mid, rest - mid


def stack2(value):
    high = value.astype(bf16).astype(f32)
    return jnp.concatenate([high, value - high], axis=0).astype(bf16)


def product(stacked, high_block, low_block):
    main = jnp.dot(stacked, high_block, preferred_element_type=f32)
    rest = jnp.dot(stacked[0:SLOTS], low_block, preferred_element_type=f32)
    return main[0:SLOTS] + (main[SLOTS:] + rest)


def slot_lanes(first):
    lane = lax.broadcasted_iota(jnp.int32, (SLOTS, EXTRA), 1)
    return lane == lax.broadcasted_iota(jnp.int32, (SLOTS, EXTRA), 0) + first


def to_lanes(column, first):
    return jnp.sum(jnp.where(slot_lanes(first), column, 0.0), axis=0, keepdims=True)


def from_lanes(row, first):
    return jnp.sum(jnp.where(slot_lanes(first), row, 0.0), axis=1, keepdims=True)


def spread(column):
    return jnp.broadcast_to(column, (SLOTS, EXTRA))


def wide(narrow, count):
    return jnp.concatenate([narrow] * (count // EXTRA), axis=1)


def pair_total(parts):
    while len(parts) > 1:
        parts = [parts[i] + parts[i + 1] for i in range(0, len(parts), 2)]
    return parts[0]


def total_of(refs):
    return pair_total([ref[...] for ref in refs])


def resident(moved, own):
    return jnp.where(lax.axis_index("dp") == 0, own, moved)


def row_sum(value):
    return jnp.sum(value, axis=1, keepdims=True)


def slot_mask(slots):
    row = lax.broadcasted_iota(jnp.int32, (SLOTS, slots.shape[1]), 0)
    return slots == row


def norm_rows(feat32, base):
    half = (-0.5 * FACTOR) * jnp.sum(feat32 * feat32, axis=0, keepdims=True)
    row = lax.broadcasted_iota(jnp.int32, (feat32.shape[0], feat32.shape[1]), 0)
    extra = jnp.where(row < 6, 1.0, 0.0)
    for place, part in enumerate(split3(half)):
        extra = jnp.where(row == base + place, part, extra)
    return extra


def kernel_parts(exponent):
    value = jnp.exp2(exponent)
    high = value.astype(bf16)
    return high, (value - high.astype(f32)).astype(bf16)


def pick(feat_ref, idx, hit_ref):
    row_count, count = hit_ref.shape
    local_idx = idx - lax.axis_index("dp") * row_count
    row = lax.broadcasted_iota(jnp.int32, (STEP, count), 0).astype(f32).astype(bf16)
    block = lax.div(local_idx, STEP)
    place = (local_idx - block * STEP).astype(f32)
    for begin in range(0, row_count, STEP):
        own = jnp.where(block == begin // STEP, place, -1.0).astype(bf16)
        hit = jnp.where(row == own, jnp.ones_like(row), jnp.zeros_like(row))
        hit_ref[begin : begin + STEP, :] = hit


def store_halves(picked, left_ref, right_ref):
    half = left_ref.shape[1]
    left_ref[...] = picked[:, :half].astype(bf16)
    right_ref[...] = picked[:, half:].astype(bf16)


def pick_body(feat_hbm, idx_hbm, slots_hbm, prices_hbm, scale_hbm, *refs):
    feat_ref, idx_ref, slots_ref, prices_ref, scale_ref, left_ref, right_ref, hit_ref, sems = refs
    sources = (idx_hbm, feat_hbm, slots_hbm, prices_hbm, scale_hbm)
    targets = (idx_ref, feat_ref, slots_ref, prices_ref, scale_ref)
    copies = [
        pltpu.make_async_copy(source, target, sems.at[place])
        for place, (source, target) in enumerate(zip(sources, targets))
    ]
    for copy in copies:
        copy.start()
    copies[0].wait()
    pick(feat_ref, idx_ref[...], hit_ref)
    copies[1].wait()
    picked = jnp.dot(feat_ref[...], hit_ref[...], preferred_element_type=f32)
    for copy in copies[2:]:
        copy.wait()
    store_halves(picked, left_ref, right_ref)


def pick_beside_body(feat_ref, moved_idx_ref, idx_ref, left_ref, right_ref, hit_ref):
    first = lax.axis_index("dp") == 0
    pick(feat_ref, jnp.where(first, idx_ref[...], moved_idx_ref[...]), hit_ref)
    picked = jnp.dot(feat_ref[...], hit_ref[...], preferred_element_type=f32)
    store_halves(picked, left_ref, right_ref)


def columns_body(feat_ref, slots_ref, prices_ref, columns_ref, turned_ref, weight_ref):
    for begin in range(0, feat_ref.shape[1], CHUNK):
        here = slice(begin, begin + CHUNK)
        feat32 = feat_ref[:, here].astype(f32)
        pair = jnp.concatenate([feat32, feat32], axis=0)
        last = jnp.concatenate([feat32, norm_rows(feat32, 3)], axis=0)
        columns_ref[0:128, here] = pair.astype(bf16)
        columns_ref[128:256, here] = last.astype(bf16)
        turned_ref[here, 0:128] = pair.T.astype(bf16)
        turned_ref[here, 128:256] = last.T.astype(bf16)
        weight = jnp.where(slot_mask(slots_ref[:, here]), prices_ref[:, here], 0.0)
        weight_ref[:, here] = stack2(weight)


def rows_body(parts, turned_ref, weight_ref, moved_scale_ref, own_scale_ref, *refs):
    left_refs, right_refs = refs[:parts], refs[parts : 2 * parts]
    block_ref, center_ref, scale_ref, out_ref = refs[2 * parts :]
    scale_ref[...] = resident(moved_scale_ref[...], own_scale_ref[...])
    center = jnp.concatenate([total_of(left_refs), total_of(right_refs)], axis=1)
    center = center.astype(f32)
    center = jnp.concatenate(
        [*split3(center * FACTOR), norm_rows(center, 0)], axis=0
    ).astype(bf16)
    center_ref[...] = center
    row_count = turned_ref.shape[0]
    total = jnp.zeros(out_ref.shape, f32)

    def fold(begin):
        end = begin + CHUNK
        return product(
            weight_ref[:, begin:end],
            block_ref[begin:end, :],
            block_ref[row_count + begin : row_count + end, :],
        )

    def inner(begin):
        return jnp.dot(
            turned_ref[begin : begin + CHUNK, :], center, preferred_element_type=f32
        )

    ahead = inner(0)
    for begin in range(0, row_count, CHUNK):
        exponent = ahead
        if begin + CHUNK < row_count:
            ahead = inner(begin + CHUNK)
        high, low = kernel_parts(exponent)
        block_ref[begin : begin + CHUNK, :] = high
        block_ref[row_count + begin : row_count + begin + CHUNK, :] = low
        if begin > 0:
            total += fold(begin - CHUNK)
    out_ref[...] = total + fold(row_count - CHUNK)


def turned_body(columns_ref, center_ref, block_ref):
    center = center_ref[...].astype(f32).T.astype(bf16)
    count, row_count = center.shape[0], columns_ref.shape[1]

    def inner(begin):
        return jnp.dot(
            center, columns_ref[:, begin : begin + CHUNK], preferred_element_type=f32
        )

    ahead = inner(0)
    for begin in range(0, row_count, CHUNK):
        exponent = ahead
        if begin + CHUNK < row_count:
            ahead = inner(begin + CHUNK)
        high, low = kernel_parts(exponent)
        block_ref[0:count, begin : begin + CHUNK] = high
        block_ref[count:, begin : begin + CHUNK] = low


def apply_rows(scaled, turned_ref, slots_ref, out_ref):
    count, row_count = scaled.shape[1], turned_ref.shape[1]
    value = product(stack2(scaled), turned_ref[0:count, :], turned_ref[count:, :])
    own = jnp.where(slot_mask(slots_ref[...]), value, 0.0)
    out_ref[:, 0:row_count] = jnp.sum(own, axis=0, keepdims=True)


def fold_rows(rows, block_ref, slots_ref, out_ref):
    row_count, count = slots_ref.shape[1], block_ref.shape[1]
    weight = jnp.where(slot_mask(slots_ref[...]), rows, 0.0)
    out_ref[:, 0:count] = product(
        stack2(weight), block_ref[0:row_count, :], block_ref[row_count:, :]
    )
    square = row_sum(weight * weight)
    out_ref[:, count : count + EXTRA] = spread(square)


def first_apply_body(parts, scale_over_root, *refs):
    first_refs = refs[:parts]
    scale_ref, slots_ref, turned_ref, target_ref, out_ref = refs[parts:]
    scale = scale_ref[...]
    target = scale * total_of(first_refs) * scale_over_root
    target_ref[...] = target
    out_ref[:, turned_ref.shape[1] :] = to_lanes(row_sum(target * target), 0)
    apply_rows(scale * target, turned_ref, slots_ref, out_ref)


def first_fold_body(parts, *refs):
    row_refs = refs[:parts]
    slots_ref, block_ref, rows_ref, norm_ref, out_ref = refs[parts:]
    row_count = slots_ref.shape[1]
    rows = total_of(row_refs)
    rows_ref[...] = rows
    norm_ref[...] = spread(from_lanes(rows[:, row_count:], 0))
    fold_rows(rows[:, 0:row_count], block_ref, slots_ref, out_ref)


def second_apply_body(parts, inv_rows, *refs):
    fold_refs = refs[:parts]
    (scale_ref, slots_ref, turned_ref, target_ref, norm_ref,
     state_ref, step_ref, out_ref) = refs[parts:]
    row_count, count = turned_ref.shape[1], scale_ref.shape[1]
    folded = total_of(fold_refs)
    scale = scale_ref[...]
    target = target_ref[...]
    norm = norm_ref[...]
    applied = scale * folded[:, 0:count] * inv_rows + RIDGE * target
    step = norm / (folded[:, count:] * inv_rows + RIDGE * norm)
    residual = target - wide(step, count) * applied
    state_ref[0:SLOTS, :] = target
    state_ref[SLOTS:, :] = residual
    step_ref[...] = step
    out_ref[:, row_count:] = to_lanes(row_sum(residual * residual), 0) + to_lanes(
        row_sum(residual * target), SLOTS
    )
    apply_rows(scale * residual, turned_ref, slots_ref, out_ref)


def second_fold_body(parts, *refs):
    row_refs = refs[:parts]
    slots_ref, block_ref, rows_ref, norm_ref, sums_ref, out_ref = refs[parts:]
    row_count = slots_ref.shape[1]
    latest = total_of(row_refs)
    norm = spread(from_lanes(latest[:, row_count:], 0))
    ratio = norm / norm_ref[...]
    sums_ref[:, 0:EXTRA] = norm
    sums_ref[:, EXTRA:] = spread(from_lanes(latest[:, row_count:], SLOTS))
    rows = latest[:, 0:row_count] + wide(ratio, row_count) * rows_ref[:, 0:row_count]
    fold_rows(rows, block_ref, slots_ref, out_ref)


def finish_body(crossed, parts, inv_rows, *refs):
    fold_refs = refs[:parts]
    (moved_ref, state_ref, scale_ref, step_ref, norm_ref, sums_ref,
     coefficients_ref, out_ref) = refs[parts:]
    count = scale_ref.shape[1]
    if crossed:
        far, moved, own = (ref[...] for ref in fold_refs)
        folded = far + resident(moved, own)
        state = resident(moved_ref[...], state_ref[...])
    else:
        folded = total_of(fold_refs)
        state = state_ref[...]
    target, residual = state[0:SLOTS], state[SLOTS:]
    first_norm = norm_ref[...]
    norm, cross = sums_ref[:, 0:EXTRA], sums_ref[:, EXTRA:]
    ratio = norm / first_norm
    direction = residual + wide(ratio, count) * target
    square = norm + 2.0 * ratio * cross + ratio * ratio * first_norm
    applied = scale_ref[...] * folded[:, 0:count] * inv_rows + RIDGE * direction
    step = wide(norm / (folded[:, count:] * inv_rows + RIDGE * square), count)
    coefficients_ref[...] = wide(step_ref[...], count) * target + step * direction
    out_ref[...] = residual - step * applied


def call(body, out_shape, *args, sources=None, flops=0, bytes_accessed=0, **more):
    return pl.pallas_call(
        body,
        out_shape=out_shape,
        in_specs=sources or [VMEM] * len(args),
        out_specs=jax.tree.map(lambda _: VMEM, out_shape),
        compiler_params=pltpu.CompilerParams(vmem_limit_bytes=36 * 1024 * 1024),
        cost_estimate=pl.CostEstimate(
            flops=flops, bytes_accessed=bytes_accessed, transcendentals=0
        ),
        **more,
    )(*args)


def exchange(value, axis, later=(1, 2, 3)):
    size = lax.axis_size(axis)
    parts = [value]
    stride = 1
    while stride < size:
        value = pair_total(parts)
        span = min(4, size // stride)
        side = 0 if stride == 1 else 1
        parts = [value]
        offsets = (1, 3, 2) if stride == 1 else later
        for offset in offsets[: span - 1]:
            pairs = [(i, i ^ (offset * stride) ^ side) for i in range(size)]
            parts.insert(0, lax.ppermute(value, axis, pairs))
        stride *= span
    return parts


def pairs_over(target_of):
    groups, count = lax.axis_size("dp"), lax.axis_size("centers")
    pairs = []
    for group in range(groups):
        for place in range(count):
            to_group, to_place = target_of(group, place)
            pairs.append((group * count + place, to_group * count + to_place))
    return pairs


def moved(value, target_of):
    return lax.ppermute(value, ("dp", "centers"), pairs_over(target_of))


def across(group, place):
    return 1 - group, place ^ 1


def beside(group, place):
    return group, place ^ 1


def outward(group, place):
    return 1 - group, place ^ (1 - group)


def homeward(group, place):
    return 1 - group, place ^ group


def shaped(shape, dtype=f32):
    return jax.ShapeDtypeStruct(shape, dtype)


def per_device(features, prices, slots, center_idx, center_scale):
    depth, row_count = features.shape
    count = center_idx.shape[0]
    all_rows = row_count * lax.axis_size("dp")
    row_shape = shaped((1, row_count + EXTRA))
    fold_shape = shaped((SLOTS, count + EXTRA))
    vector = shaped((SLOTS, count))
    narrow = shaped((SLOTS, EXTRA))
    pass_cost = dict(flops=64 * row_count * count, bytes_accessed=4 * row_count * count)

    crossed = lax.axis_size("dp") == 2

    def share(value):
        return [moved(value, across), value] if crossed else exchange(value, "dp")

    inputs = [
        pltpu.with_memory_space_constraint(array, pltpu.HBM)
        for array in (
            features,
            center_idx.reshape(1, count),
            slots.reshape(1, row_count),
            prices.reshape(1, row_count),
            center_scale.reshape(1, count),
        )
    ]
    picked_half = shaped((depth, count // 2), bf16)
    features, idx, slots, prices, own_scale, *picked = call(
        pick_body,
        (
            shaped(features.shape, bf16),
            shaped((1, count), jnp.int32),
            shaped((1, row_count), jnp.int32),
            shaped((1, row_count)),
            shaped((1, count)),
            picked_half,
            picked_half,
        ),
        *inputs,
        sources=[HBM] * 5,
        scratch_shapes=[
            pltpu.VMEM((row_count, count), bf16),
            pltpu.SemaphoreType.DMA((5,)),
        ],
    )
    if crossed:
        moved_idx = moved(center_idx, beside)
        resident_picks = call(
            pick_beside_body,
            (picked_half, picked_half),
            features, moved_idx.reshape(1, count), idx,
            flops=128 * row_count * count,
            bytes_accessed=128 * row_count,
            scratch_shapes=[pltpu.VMEM((row_count, count), bf16)],
        )
        centers = [
            [moved(part, outward), other] for part, other in zip(picked, resident_picks)
        ]
        moved_scale = moved(center_scale, beside).reshape(1, count)
    else:
        centers = [exchange(part, "dp") for part in picked]
        moved_scale = own_scale
    columns, turned_columns, weight = call(
        columns_body,
        (
            shaped((DEPTH, row_count), bf16),
            shaped((row_count, DEPTH), bf16),
            shaped((16, row_count), bf16),
        ),
        features, slots, prices,
        flops=1000 * row_count,
        bytes_accessed=1024 * row_count,
    )
    block, center, scale, first = call(
        partial(rows_body, len(centers[0])),
        (
            shaped((2 * row_count, count), bf16),
            shaped((DEPTH, count), bf16),
            shaped((1, count)),
            vector,
        ),
        turned_columns, weight, moved_scale, own_scale, *centers[0], *centers[1],
        **pass_cost,
    )
    firsts = share(first)
    turned = call(
        turned_body, shaped((2 * count, row_count), bf16), columns, center, **pass_cost
    )
    target, rows = call(
        partial(first_apply_body, len(firsts), 1.0 / math.sqrt(all_rows)),
        (vector, row_shape),
        *firsts, scale, slots, turned,
    )
    rows = exchange(rows, "centers", (3, 1, 2))
    rows, norm, folded = call(
        partial(first_fold_body, len(rows)), (row_shape, narrow, fold_shape), *rows, slots, block
    )
    folds = share(folded)
    state, step, latest = call(
        partial(second_apply_body, len(folds), 1.0 / all_rows),
        (shaped((2 * SLOTS, count)), narrow, row_shape),
        *folds, scale, slots, turned, target, norm,
    )
    latest = exchange(latest, "centers")
    sums, folded = call(
        partial(second_fold_body, len(latest)),
        (shaped((SLOTS, 2 * EXTRA)), fold_shape),
        *latest, slots, block, rows, norm,
    )
    if crossed:
        folds = [moved(folded, homeward), moved(folded, beside), folded]
        moved_state = moved(state, beside)
    else:
        folds = exchange(folded, "dp")
        moved_state = state
    return call(
        partial(finish_body, crossed, len(folds), 1.0 / all_rows),
        (vector, vector),
        *folds, moved_state, state, own_scale, step, norm, sums,
    )


def solution(mesh):
    return jax.shard_map(
        per_device,
        mesh=mesh,
        in_specs=(P(None, "dp"), P("dp"), P("dp"), P("centers"), P("centers")),
        out_specs=(P(None, "centers"), P(None, "centers")),
        check_vma=False,
    )
```

```python
import math
from functools import partial

import jax
import jax.numpy as jnp
from jax import lax
from jax.experimental import pallas as pl
from jax.experimental.pallas import tpu as pltpu
from jax.sharding import PartitionSpec as P

SLOTS = 8
RIDGE = 0.5
CHUNK = 512
EXTRA = 128
DEPTH = 256
STEP = 256
FACTOR = math.log2(math.e) / 64.0
f32 = jnp.float32
bf16 = jnp.bfloat16
VMEM = pl.BlockSpec(memory_space=pltpu.VMEM)
HBM = pl.BlockSpec(memory_space=pltpu.HBM)


def split3(value):
    high = value.astype(bf16).astype(f32)
    rest = value - high
    mid = rest.astype(bf16).astype(f32)
    return high, mid, rest - mid


def stack2(value):
    high = value.astype(bf16).astype(f32)
    return jnp.concatenate([high, value - high], axis=0).astype(bf16)


def product(stacked, high_block, low_block):
    main = jnp.dot(stacked, high_block, preferred_element_type=f32)
    rest = jnp.dot(stacked[0:SLOTS], low_block, preferred_element_type=f32)
    return main[0:SLOTS] + (main[SLOTS:] + rest)


def slot_lanes(first):
    lane = lax.broadcasted_iota(jnp.int32, (SLOTS, EXTRA), 1)
    return lane == lax.broadcasted_iota(jnp.int32, (SLOTS, EXTRA), 0) + first


def to_lanes(column, first):
    return jnp.sum(jnp.where(slot_lanes(first), column, 0.0), axis=0, keepdims=True)


def from_lanes(row, first):
    return jnp.sum(jnp.where(slot_lanes(first), row, 0.0), axis=1, keepdims=True)


def spread(column):
    return jnp.broadcast_to(column, (SLOTS, EXTRA))


def wide(narrow, count):
    return jnp.concatenate([narrow] * (count // EXTRA), axis=1)


def pair_total(parts):
    while len(parts) > 1:
        parts = [parts[i] + parts[i + 1] for i in range(0, len(parts), 2)]
    return parts[0]


def total_of(refs):
    return pair_total([ref[...] for ref in refs])


def resident(moved, own):
    return jnp.where(lax.axis_index("dp") == 0, own, moved)


def row_sum(value):
    return jnp.sum(value, axis=1, keepdims=True)


def slot_mask(slots):
    row = lax.broadcasted_iota(jnp.int32, (SLOTS, slots.shape[1]), 0)
    return slots == row


def norm_rows(feat32, base):
    half = (-0.5 * FACTOR) * jnp.sum(feat32 * feat32, axis=0, keepdims=True)
    row = lax.broadcasted_iota(jnp.int32, (feat32.shape[0], feat32.shape[1]), 0)
    extra = jnp.where(row < 6, 1.0, 0.0)
    for place, part in enumerate(split3(half)):
        extra = jnp.where(row == base + place, part, extra)
    return extra


def kernel_parts(exponent):
    value = jnp.exp2(exponent)
    high = value.astype(bf16)
    return high, (value - high.astype(f32)).astype(bf16)


def place_of(idx, row_count):
    local_idx = idx - lax.axis_index("dp") * row_count
    block = lax.div(local_idx, STEP)
    place = (local_idx - block * STEP).astype(f32).astype(bf16)
    row = lax.broadcasted_iota(jnp.int32, (STEP, idx.shape[1]), 0).astype(f32).astype(bf16)
    return block, jnp.where(row == place, jnp.ones_like(row), jnp.zeros_like(row))


def pick(feat_ref, block, hit):
    depth, row_count = feat_ref.shape
    blocks = range(row_count // STEP)
    stacked = jnp.concatenate(
        [feat_ref[:, turn * STEP : (turn + 1) * STEP] for turn in blocks], axis=0
    )
    product = jnp.dot(stacked, hit, preferred_element_type=f32)
    picked = jnp.zeros((depth, hit.shape[1]), f32)
    for turn in blocks:
        picked = jnp.where(block == turn, product[turn * depth : (turn + 1) * depth], picked)
    return picked


def pick_body(feat_hbm, idx_hbm, slots_hbm, prices_hbm, scale_hbm, *refs):
    feat_ref, idx_ref, slots_ref, prices_ref, scale_ref, out_ref, sems = refs
    sources = (idx_hbm, feat_hbm, slots_hbm, prices_hbm, scale_hbm)
    targets = (idx_ref, feat_ref, slots_ref, prices_ref, scale_ref)
    copies = [
        pltpu.make_async_copy(source, target, sems.at[place])
        for place, (source, target) in enumerate(zip(sources, targets))
    ]
    for copy in copies:
        copy.start()
    copies[0].wait()
    block, hit = place_of(idx_ref[...], feat_ref.shape[1])
    copies[1].wait()
    picked = pick(feat_ref, block, hit)
    for copy in copies[2:]:
        copy.wait()
    out_ref[...] = picked.astype(bf16)


def pick_beside_body(feat_ref, moved_idx_ref, idx_ref, out_ref):
    idx = jnp.where(lax.axis_index("dp") == 0, idx_ref[...], moved_idx_ref[...])
    block, hit = place_of(idx, feat_ref.shape[1])
    out_ref[...] = pick(feat_ref, block, hit).astype(bf16)


def columns_body(feat_ref, slots_ref, prices_ref, columns_ref, turned_ref, weight_ref):
    for begin in range(0, feat_ref.shape[1], CHUNK):
        here = slice(begin, begin + CHUNK)
        feat32 = feat_ref[:, here].astype(f32)
        pair = jnp.concatenate([feat32, feat32], axis=0)
        last = jnp.concatenate([feat32, norm_rows(feat32, 3)], axis=0)
        columns_ref[0:128, here] = pair.astype(bf16)
        columns_ref[128:256, here] = last.astype(bf16)
        turned_ref[here, 0:128] = pair.T.astype(bf16)
        turned_ref[here, 128:256] = last.T.astype(bf16)
        weight = jnp.where(slot_mask(slots_ref[:, here]), prices_ref[:, here], 0.0)
        weight_ref[:, here] = stack2(weight)


def rows_body(parts, turned_ref, weight_ref, moved_scale_ref, own_scale_ref, *refs):
    center_refs, (block_ref, center_ref, scale_ref, out_ref) = refs[:parts], refs[parts:]
    scale_ref[...] = resident(moved_scale_ref[...], own_scale_ref[...])
    center = total_of(center_refs).astype(f32)
    center = jnp.concatenate(
        [*split3(center * FACTOR), norm_rows(center, 0)], axis=0
    ).astype(bf16)
    center_ref[...] = center
    row_count = turned_ref.shape[0]
    total = jnp.zeros(out_ref.shape, f32)

    def fold(begin):
        end = begin + CHUNK
        return product(
            weight_ref[:, begin:end],
            block_ref[begin:end, :],
            block_ref[row_count + begin : row_count + end, :],
        )

    def inner(begin):
        return jnp.dot(
            turned_ref[begin : begin + CHUNK, :], center, preferred_element_type=f32
        )

    ahead = inner(0)
    for begin in range(0, row_count, CHUNK):
        exponent = ahead
        if begin + CHUNK < row_count:
            ahead = inner(begin + CHUNK)
        high, low = kernel_parts(exponent)
        block_ref[begin : begin + CHUNK, :] = high
        block_ref[row_count + begin : row_count + begin + CHUNK, :] = low
        if begin > 0:
            total += fold(begin - CHUNK)
    out_ref[...] = total + fold(row_count - CHUNK)


def turned_body(columns_ref, center_ref, block_ref):
    center = center_ref[...].astype(f32).T.astype(bf16)
    count, row_count = center.shape[0], columns_ref.shape[1]

    def inner(begin):
        return jnp.dot(
            center, columns_ref[:, begin : begin + CHUNK], preferred_element_type=f32
        )

    ahead = inner(0)
    for begin in range(0, row_count, CHUNK):
        exponent = ahead
        if begin + CHUNK < row_count:
            ahead = inner(begin + CHUNK)
        high, low = kernel_parts(exponent)
        block_ref[0:count, begin : begin + CHUNK] = high
        block_ref[count:, begin : begin + CHUNK] = low


def apply_rows(scaled, turned_ref, slots_ref, out_ref):
    count, row_count = scaled.shape[1], turned_ref.shape[1]
    value = product(stack2(scaled), turned_ref[0:count, :], turned_ref[count:, :])
    own = jnp.where(slot_mask(slots_ref[...]), value, 0.0)
    out_ref[:, 0:row_count] = jnp.sum(own, axis=0, keepdims=True)


def fold_rows(rows, block_ref, slots_ref, out_ref):
    row_count, count = slots_ref.shape[1], block_ref.shape[1]
    weight = jnp.where(slot_mask(slots_ref[...]), rows, 0.0)
    out_ref[:, 0:count] = product(
        stack2(weight), block_ref[0:row_count, :], block_ref[row_count:, :]
    )
    square = row_sum(weight * weight)
    out_ref[:, count : count + EXTRA] = spread(square)


def first_apply_body(parts, scale_over_root, *refs):
    first_refs = refs[:parts]
    scale_ref, slots_ref, turned_ref, target_ref, out_ref = refs[parts:]
    scale = scale_ref[...]
    target = scale * total_of(first_refs) * scale_over_root
    target_ref[...] = target
    out_ref[:, turned_ref.shape[1] :] = to_lanes(row_sum(target * target), 0)
    apply_rows(scale * target, turned_ref, slots_ref, out_ref)


def first_fold_body(parts, *refs):
    row_refs = refs[:parts]
    slots_ref, block_ref, rows_ref, norm_ref, out_ref = refs[parts:]
    row_count = slots_ref.shape[1]
    rows = total_of(row_refs)
    rows_ref[...] = rows
    norm_ref[...] = spread(from_lanes(rows[:, row_count:], 0))
    fold_rows(rows[:, 0:row_count], block_ref, slots_ref, out_ref)


def second_apply_body(parts, inv_rows, *refs):
    fold_refs = refs[:parts]
    (scale_ref, slots_ref, turned_ref, target_ref, norm_ref,
     state_ref, step_ref, out_ref) = refs[parts:]
    row_count, count = turned_ref.shape[1], scale_ref.shape[1]
    folded = total_of(fold_refs)
    scale = scale_ref[...]
    target = target_ref[...]
    norm = norm_ref[...]
    applied = scale * folded[:, 0:count] * inv_rows + RIDGE * target
    step = norm / (folded[:, count:] * inv_rows + RIDGE * norm)
    residual = target - wide(step, count) * applied
    state_ref[0:SLOTS, :] = target
    state_ref[SLOTS:, :] = residual
    step_ref[...] = step
    out_ref[:, row_count:] = to_lanes(row_sum(residual * residual), 0) + to_lanes(
        row_sum(residual * target), SLOTS
    )
    apply_rows(scale * residual, turned_ref, slots_ref, out_ref)


def second_fold_body(parts, *refs):
    row_refs = refs[:parts]
    slots_ref, block_ref, rows_ref, norm_ref, sums_ref, out_ref = refs[parts:]
    row_count = slots_ref.shape[1]
    latest = total_of(row_refs)
    norm = spread(from_lanes(latest[:, row_count:], 0))
    ratio = norm / norm_ref[...]
    sums_ref[:, 0:EXTRA] = norm
    sums_ref[:, EXTRA:] = spread(from_lanes(latest[:, row_count:], SLOTS))
    rows = latest[:, 0:row_count] + wide(ratio, row_count) * rows_ref[:, 0:row_count]
    fold_rows(rows, block_ref, slots_ref, out_ref)


def finish_body(crossed, parts, inv_rows, *refs):
    fold_refs = refs[:parts]
    (moved_ref, state_ref, scale_ref, step_ref, norm_ref, sums_ref,
     coefficients_ref, out_ref) = refs[parts:]
    count = scale_ref.shape[1]
    if crossed:
        far, moved, own = (ref[...] for ref in fold_refs)
        folded = far + resident(moved, own)
        state = resident(moved_ref[...], state_ref[...])
    else:
        folded = total_of(fold_refs)
        state = state_ref[...]
    target, residual = state[0:SLOTS], state[SLOTS:]
    first_norm = norm_ref[...]
    norm, cross = sums_ref[:, 0:EXTRA], sums_ref[:, EXTRA:]
    ratio = norm / first_norm
    direction = residual + wide(ratio, count) * target
    square = norm + 2.0 * ratio * cross + ratio * ratio * first_norm
    applied = scale_ref[...] * folded[:, 0:count] * inv_rows + RIDGE * direction
    step = wide(norm / (folded[:, count:] * inv_rows + RIDGE * square), count)
    coefficients_ref[...] = wide(step_ref[...], count) * target + step * direction
    out_ref[...] = residual - step * applied


def call(body, out_shape, *args, sources=None, flops=0, bytes_accessed=0, **more):
    return pl.pallas_call(
        body,
        out_shape=out_shape,
        in_specs=sources or [VMEM] * len(args),
        out_specs=jax.tree.map(lambda _: VMEM, out_shape),
        compiler_params=pltpu.CompilerParams(vmem_limit_bytes=36 * 1024 * 1024),
        cost_estimate=pl.CostEstimate(
            flops=flops, bytes_accessed=bytes_accessed, transcendentals=0
        ),
        **more,
    )(*args)


def exchange(value, axis):
    size = lax.axis_size(axis)
    parts = [value]
    stride = 1
    while stride < size:
        value = pair_total(parts)
        span = min(4, size // stride)
        side = 0 if stride == 1 else 1
        parts = [value]
        offsets = (1, 3, 2) if stride == 1 else (1, 2, 3)
        for offset in offsets[: span - 1]:
            pairs = [(i, i ^ (offset * stride) ^ side) for i in range(size)]
            parts.insert(0, lax.ppermute(value, axis, pairs))
        stride *= span
    return parts


def pairs_over(target_of):
    groups, count = lax.axis_size("dp"), lax.axis_size("centers")
    pairs = []
    for group in range(groups):
        for place in range(count):
            to_group, to_place = target_of(group, place)
            pairs.append((group * count + place, to_group * count + to_place))
    return pairs


def moved(value, target_of):
    return lax.ppermute(value, ("dp", "centers"), pairs_over(target_of))


def across(group, place):
    return 1 - group, place ^ 1


def beside(group, place):
    return group, place ^ 1


def outward(group, place):
    return 1 - group, place ^ (1 - group)


def homeward(group, place):
    return 1 - group, place ^ group


def shaped(shape, dtype=f32):
    return jax.ShapeDtypeStruct(shape, dtype)


def per_device(features, prices, slots, center_idx, center_scale):
    depth, row_count = features.shape
    count = center_idx.shape[0]
    all_rows = row_count * lax.axis_size("dp")
    row_shape = shaped((1, row_count + EXTRA))
    fold_shape = shaped((SLOTS, count + EXTRA))
    vector = shaped((SLOTS, count))
    narrow = shaped((SLOTS, EXTRA))
    pass_cost = dict(flops=64 * row_count * count, bytes_accessed=4 * row_count * count)

    crossed = lax.axis_size("dp") == 2

    def share(value):
        return [moved(value, across), value] if crossed else exchange(value, "dp")

    inputs = [
        pltpu.with_memory_space_constraint(array, pltpu.HBM)
        for array in (
            features,
            center_idx.reshape(1, count),
            slots.reshape(1, row_count),
            prices.reshape(1, row_count),
            center_scale.reshape(1, count),
        )
    ]
    features, idx, slots, prices, own_scale, picked = call(
        pick_body,
        (
            shaped(features.shape, bf16),
            shaped((1, count), jnp.int32),
            shaped((1, row_count), jnp.int32),
            shaped((1, row_count)),
            shaped((1, count)),
            shaped((depth, count), bf16),
        ),
        *inputs,
        sources=[HBM] * 5,
        scratch_shapes=[pltpu.SemaphoreType.DMA((5,))],
    )
    if crossed:
        moved_idx = moved(center_idx, beside)
        resident_picks = call(
            pick_beside_body,
            shaped((depth, count), bf16),
            features, moved_idx.reshape(1, count), idx,
            flops=128 * row_count * count,
            bytes_accessed=128 * row_count,
        )
        centers = [moved(picked, outward), resident_picks]
        moved_scale = moved(center_scale, beside).reshape(1, count)
    else:
        centers = exchange(picked, "dp")
        moved_scale = own_scale
    columns, turned_columns, weight = call(
        columns_body,
        (
            shaped((DEPTH, row_count), bf16),
            shaped((row_count, DEPTH), bf16),
            shaped((16, row_count), bf16),
        ),
        features, slots, prices,
        flops=1000 * row_count,
        bytes_accessed=1024 * row_count,
    )
    block, center, scale, first = call(
        partial(rows_body, len(centers)),
        (
            shaped((2 * row_count, count), bf16),
            shaped((DEPTH, count), bf16),
            shaped((1, count)),
            vector,
        ),
        turned_columns, weight, moved_scale, own_scale, *centers,
        **pass_cost,
    )
    firsts = share(first)
    turned = call(
        turned_body, shaped((2 * count, row_count), bf16), columns, center, **pass_cost
    )
    target, rows = call(
        partial(first_apply_body, len(firsts), 1.0 / math.sqrt(all_rows)),
        (vector, row_shape),
        *firsts, scale, slots, turned,
    )
    rows = exchange(rows, "centers")
    rows, norm, folded = call(
        partial(first_fold_body, len(rows)), (row_shape, narrow, fold_shape), *rows, slots, block
    )
    folds = share(folded)
    state, step, latest = call(
        partial(second_apply_body, len(folds), 1.0 / all_rows),
        (shaped((2 * SLOTS, count)), narrow, row_shape),
        *folds, scale, slots, turned, target, norm,
    )
    latest = exchange(latest, "centers")
    sums, folded = call(
        partial(second_fold_body, len(latest)),
        (shaped((SLOTS, 2 * EXTRA)), fold_shape),
        *latest, slots, block, rows, norm,
    )
    if crossed:
        folds = [moved(folded, homeward), moved(folded, beside), folded]
        moved_state = moved(state, beside)
    else:
        folds = exchange(folded, "dp")
        moved_state = state
    return call(
        partial(finish_body, crossed, len(folds), 1.0 / all_rows),
        (vector, vector),
        *folds, moved_state, state, own_scale, step, norm, sums,
    )


def solution(mesh):
    return jax.shard_map(
        per_device,
        mesh=mesh,
        in_specs=(P(None, "dp"), P("dp"), P("dp"), P("centers"), P("centers")),
        out_specs=(P(None, "centers"), P(None, "centers")),
        check_vma=False,
    )
```

```python
import math
from functools import partial

import jax
import jax.numpy as jnp
from jax import lax
from jax.experimental import pallas as pl
from jax.experimental.pallas import tpu as pltpu
from jax.sharding import PartitionSpec as P

SLOTS = 8
RIDGE = 0.5
CHUNK = 512
EXTRA = 128
DEPTH = 256
STEP = 256
FACTOR = math.log2(math.e) / 64.0
f32 = jnp.float32
bf16 = jnp.bfloat16
VMEM = pl.BlockSpec(memory_space=pltpu.VMEM)
HBM = pl.BlockSpec(memory_space=pltpu.HBM)


def split3(value):
    high = value.astype(bf16).astype(f32)
    rest = value - high
    mid = rest.astype(bf16).astype(f32)
    return high, mid, rest - mid


def stack2(value):
    high = value.astype(bf16).astype(f32)
    return jnp.concatenate([high, value - high], axis=0).astype(bf16)


def product(stacked, high_block, low_block):
    main = jnp.dot(stacked, high_block, preferred_element_type=f32)
    rest = jnp.dot(stacked[0:SLOTS], low_block, preferred_element_type=f32)
    return main[0:SLOTS] + (main[SLOTS:] + rest)


def slot_lanes(first):
    lane = lax.broadcasted_iota(jnp.int32, (SLOTS, EXTRA), 1)
    return lane == lax.broadcasted_iota(jnp.int32, (SLOTS, EXTRA), 0) + first


def to_lanes(column, first):
    return jnp.sum(jnp.where(slot_lanes(first), column, 0.0), axis=0, keepdims=True)


def from_lanes(row, first):
    return jnp.sum(jnp.where(slot_lanes(first), row, 0.0), axis=1, keepdims=True)


def spread(column):
    return jnp.broadcast_to(column, (SLOTS, EXTRA))


def wide(narrow, count):
    return jnp.concatenate([narrow] * (count // EXTRA), axis=1)


def pair_total(parts):
    while len(parts) > 1:
        parts = [parts[i] + parts[i + 1] for i in range(0, len(parts), 2)]
    return parts[0]


def total_of(refs):
    return pair_total([ref[...] for ref in refs])


def resident(moved, own):
    return jnp.where(lax.axis_index("dp") == 0, own, moved)


def row_sum(value):
    return jnp.sum(value, axis=1, keepdims=True)


def slot_mask(slots):
    row = lax.broadcasted_iota(jnp.int32, (SLOTS, slots.shape[1]), 0)
    return slots == row


def norm_rows(feat32, base):
    half = (-0.5 * FACTOR) * jnp.sum(feat32 * feat32, axis=0, keepdims=True)
    row = lax.broadcasted_iota(jnp.int32, (feat32.shape[0], feat32.shape[1]), 0)
    extra = jnp.where(row < 6, 1.0, 0.0)
    for place, part in enumerate(split3(half)):
        extra = jnp.where(row == base + place, part, extra)
    return extra


def kernel_parts(exponent):
    value = jnp.exp2(exponent)
    high = value.astype(bf16)
    return high, (value - high.astype(f32)).astype(bf16)


def place_of(idx, row_count):
    local_idx = idx - lax.axis_index("dp") * row_count
    block = lax.div(local_idx, STEP)
    place = (local_idx - block * STEP).astype(f32).astype(bf16)
    row = lax.broadcasted_iota(jnp.int32, (STEP, idx.shape[1]), 0).astype(f32).astype(bf16)
    return block, jnp.where(row == place, jnp.ones_like(row), jnp.zeros_like(row))


def pick(feat_ref, block, hit, picked, blocks):
    depth = feat_ref.shape[0]
    stacked = jnp.concatenate(
        [feat_ref[:, turn * STEP : (turn + 1) * STEP] for turn in blocks], axis=0
    )
    product = jnp.dot(stacked, hit, preferred_element_type=f32)
    for step, turn in enumerate(blocks):
        picked = jnp.where(block == turn, product[step * depth : (step + 1) * depth], picked)
    return picked


def pick_body(feat_hbm, idx_hbm, slots_hbm, prices_hbm, scale_hbm, *refs):
    feat_ref, idx_ref, slots_ref, prices_ref, scale_ref, out_ref, sems = refs
    blocks = feat_ref.shape[1] // STEP
    left = pl.ds(0, blocks // 2 * STEP)
    right = pl.ds(blocks // 2 * STEP, (blocks - blocks // 2) * STEP)
    sources = (
        idx_hbm, feat_hbm.at[:, left], feat_hbm.at[:, right], slots_hbm, prices_hbm, scale_hbm
    )
    targets = (
        idx_ref, feat_ref.at[:, left], feat_ref.at[:, right], slots_ref, prices_ref, scale_ref
    )
    copies = [
        pltpu.make_async_copy(source, target, sems.at[place])
        for place, (source, target) in enumerate(zip(sources, targets))
    ]
    for copy in copies:
        copy.start()
    copies[0].wait()
    block, hit = place_of(idx_ref[...], feat_ref.shape[1])
    picked = jnp.zeros(out_ref.shape, f32)
    copies[1].wait()
    picked = pick(feat_ref, block, hit, picked, range(blocks // 2))
    copies[2].wait()
    picked = pick(feat_ref, block, hit, picked, range(blocks // 2, blocks))
    for copy in copies[3:]:
        copy.wait()
    out_ref[...] = picked.astype(bf16)


def pick_beside_body(feat_ref, moved_idx_ref, idx_ref, out_ref):
    idx = jnp.where(lax.axis_index("dp") == 0, idx_ref[...], moved_idx_ref[...])
    block, hit = place_of(idx, feat_ref.shape[1])
    picked = jnp.zeros(out_ref.shape, f32)
    blocks = range(feat_ref.shape[1] // STEP)
    out_ref[...] = pick(feat_ref, block, hit, picked, blocks).astype(bf16)


def columns_body(feat_ref, slots_ref, prices_ref, columns_ref, turned_ref, weight_ref):
    for begin in range(0, feat_ref.shape[1], CHUNK):
        here = slice(begin, begin + CHUNK)
        feat32 = feat_ref[:, here].astype(f32)
        pair = jnp.concatenate([feat32, feat32], axis=0)
        last = jnp.concatenate([feat32, norm_rows(feat32, 3)], axis=0)
        columns_ref[0:128, here] = pair.astype(bf16)
        columns_ref[128:256, here] = last.astype(bf16)
        turned_ref[here, 0:128] = pair.T.astype(bf16)
        turned_ref[here, 128:256] = last.T.astype(bf16)
        weight = jnp.where(slot_mask(slots_ref[:, here]), prices_ref[:, here], 0.0)
        weight_ref[:, here] = stack2(weight)


def rows_body(parts, turned_ref, weight_ref, moved_scale_ref, own_scale_ref, *refs):
    center_refs, (block_ref, center_ref, scale_ref, out_ref) = refs[:parts], refs[parts:]
    scale_ref[...] = resident(moved_scale_ref[...], own_scale_ref[...])
    center = total_of(center_refs).astype(f32)
    center = jnp.concatenate(
        [*split3(center * FACTOR), norm_rows(center, 0)], axis=0
    ).astype(bf16)
    center_ref[...] = center
    row_count = turned_ref.shape[0]
    total = jnp.zeros(out_ref.shape, f32)

    def fold(begin):
        end = begin + CHUNK
        return product(
            weight_ref[:, begin:end],
            block_ref[begin:end, :],
            block_ref[row_count + begin : row_count + end, :],
        )

    def inner(begin):
        return jnp.dot(
            turned_ref[begin : begin + CHUNK, :], center, preferred_element_type=f32
        )

    ahead = inner(0)
    for begin in range(0, row_count, CHUNK):
        exponent = ahead
        if begin + CHUNK < row_count:
            ahead = inner(begin + CHUNK)
        high, low = kernel_parts(exponent)
        block_ref[begin : begin + CHUNK, :] = high
        block_ref[row_count + begin : row_count + begin + CHUNK, :] = low
        if begin > 0:
            total += fold(begin - CHUNK)
    out_ref[...] = total + fold(row_count - CHUNK)


def turned_body(columns_ref, center_ref, block_ref):
    center = center_ref[...].astype(f32).T.astype(bf16)
    count, row_count = center.shape[0], columns_ref.shape[1]

    def inner(begin):
        return jnp.dot(
            center, columns_ref[:, begin : begin + CHUNK], preferred_element_type=f32
        )

    ahead = inner(0)
    for begin in range(0, row_count, CHUNK):
        exponent = ahead
        if begin + CHUNK < row_count:
            ahead = inner(begin + CHUNK)
        high, low = kernel_parts(exponent)
        block_ref[0:count, begin : begin + CHUNK] = high
        block_ref[count:, begin : begin + CHUNK] = low


def apply_rows(scaled, turned_ref, slots_ref, out_ref):
    count, row_count = scaled.shape[1], turned_ref.shape[1]
    value = product(stack2(scaled), turned_ref[0:count, :], turned_ref[count:, :])
    own = jnp.where(slot_mask(slots_ref[...]), value, 0.0)
    out_ref[:, 0:row_count] = jnp.sum(own, axis=0, keepdims=True)


def fold_rows(rows, block_ref, slots_ref, out_ref):
    row_count, count = slots_ref.shape[1], block_ref.shape[1]
    weight = jnp.where(slot_mask(slots_ref[...]), rows, 0.0)
    out_ref[:, 0:count] = product(
        stack2(weight), block_ref[0:row_count, :], block_ref[row_count:, :]
    )
    square = row_sum(weight * weight)
    out_ref[:, count : count + EXTRA] = spread(square)


def first_apply_body(parts, scale_over_root, *refs):
    first_refs = refs[:parts]
    scale_ref, slots_ref, turned_ref, target_ref, out_ref = refs[parts:]
    scale = scale_ref[...]
    target = scale * total_of(first_refs) * scale_over_root
    target_ref[...] = target
    out_ref[:, turned_ref.shape[1] :] = to_lanes(row_sum(target * target), 0)
    apply_rows(scale * target, turned_ref, slots_ref, out_ref)


def first_fold_body(parts, *refs):
    row_refs = refs[:parts]
    slots_ref, block_ref, rows_ref, norm_ref, out_ref = refs[parts:]
    row_count = slots_ref.shape[1]
    rows = total_of(row_refs)
    rows_ref[...] = rows
    norm_ref[...] = spread(from_lanes(rows[:, row_count:], 0))
    fold_rows(rows[:, 0:row_count], block_ref, slots_ref, out_ref)


def second_apply_body(parts, inv_rows, *refs):
    fold_refs = refs[:parts]
    (scale_ref, slots_ref, turned_ref, target_ref, norm_ref,
     state_ref, step_ref, out_ref) = refs[parts:]
    row_count, count = turned_ref.shape[1], scale_ref.shape[1]
    folded = total_of(fold_refs)
    scale = scale_ref[...]
    target = target_ref[...]
    norm = norm_ref[...]
    applied = scale * folded[:, 0:count] * inv_rows + RIDGE * target
    step = norm / (folded[:, count:] * inv_rows + RIDGE * norm)
    residual = target - wide(step, count) * applied
    state_ref[0:SLOTS, :] = target
    state_ref[SLOTS:, :] = residual
    step_ref[...] = step
    out_ref[:, row_count:] = to_lanes(row_sum(residual * residual), 0) + to_lanes(
        row_sum(residual * target), SLOTS
    )
    apply_rows(scale * residual, turned_ref, slots_ref, out_ref)


def second_fold_body(parts, *refs):
    row_refs = refs[:parts]
    slots_ref, block_ref, rows_ref, norm_ref, sums_ref, out_ref = refs[parts:]
    row_count = slots_ref.shape[1]
    latest = total_of(row_refs)
    norm = spread(from_lanes(latest[:, row_count:], 0))
    ratio = norm / norm_ref[...]
    sums_ref[:, 0:EXTRA] = norm
    sums_ref[:, EXTRA:] = spread(from_lanes(latest[:, row_count:], SLOTS))
    rows = latest[:, 0:row_count] + wide(ratio, row_count) * rows_ref[:, 0:row_count]
    fold_rows(rows, block_ref, slots_ref, out_ref)


def finish_body(crossed, parts, inv_rows, *refs):
    fold_refs = refs[:parts]
    (moved_ref, state_ref, scale_ref, step_ref, norm_ref, sums_ref,
     coefficients_ref, out_ref) = refs[parts:]
    count = scale_ref.shape[1]
    if crossed:
        far, moved, own = (ref[...] for ref in fold_refs)
        folded = far + resident(moved, own)
        state = resident(moved_ref[...], state_ref[...])
    else:
        folded = total_of(fold_refs)
        state = state_ref[...]
    target, residual = state[0:SLOTS], state[SLOTS:]
    first_norm = norm_ref[...]
    norm, cross = sums_ref[:, 0:EXTRA], sums_ref[:, EXTRA:]
    ratio = norm / first_norm
    direction = residual + wide(ratio, count) * target
    square = norm + 2.0 * ratio * cross + ratio * ratio * first_norm
    applied = scale_ref[...] * folded[:, 0:count] * inv_rows + RIDGE * direction
    step = wide(norm / (folded[:, count:] * inv_rows + RIDGE * square), count)
    coefficients_ref[...] = wide(step_ref[...], count) * target + step * direction
    out_ref[...] = residual - step * applied


def call(body, out_shape, *args, sources=None, flops=0, bytes_accessed=0, **more):
    return pl.pallas_call(
        body,
        out_shape=out_shape,
        in_specs=sources or [VMEM] * len(args),
        out_specs=jax.tree.map(lambda _: VMEM, out_shape),
        compiler_params=pltpu.CompilerParams(vmem_limit_bytes=36 * 1024 * 1024),
        cost_estimate=pl.CostEstimate(
            flops=flops, bytes_accessed=bytes_accessed, transcendentals=0
        ),
        **more,
    )(*args)


def exchange(value, axis):
    size = lax.axis_size(axis)
    parts = [value]
    stride = 1
    while stride < size:
        value = pair_total(parts)
        span = min(4, size // stride)
        side = 0 if stride == 1 else 1
        parts = [value]
        offsets = (1, 3, 2) if stride == 1 else (1, 2, 3)
        for offset in offsets[: span - 1]:
            pairs = [(i, i ^ (offset * stride) ^ side) for i in range(size)]
            parts.insert(0, lax.ppermute(value, axis, pairs))
        stride *= span
    return parts


def pairs_over(target_of):
    groups, count = lax.axis_size("dp"), lax.axis_size("centers")
    pairs = []
    for group in range(groups):
        for place in range(count):
            to_group, to_place = target_of(group, place)
            pairs.append((group * count + place, to_group * count + to_place))
    return pairs


def moved(value, target_of):
    return lax.ppermute(value, ("dp", "centers"), pairs_over(target_of))


def across(group, place):
    return 1 - group, place ^ 1


def beside(group, place):
    return group, place ^ 1


def outward(group, place):
    return 1 - group, place ^ (1 - group)


def homeward(group, place):
    return 1 - group, place ^ group


def shaped(shape, dtype=f32):
    return jax.ShapeDtypeStruct(shape, dtype)


def per_device(features, prices, slots, center_idx, center_scale):
    depth, row_count = features.shape
    count = center_idx.shape[0]
    all_rows = row_count * lax.axis_size("dp")
    row_shape = shaped((1, row_count + EXTRA))
    fold_shape = shaped((SLOTS, count + EXTRA))
    vector = shaped((SLOTS, count))
    narrow = shaped((SLOTS, EXTRA))
    pass_cost = dict(flops=64 * row_count * count, bytes_accessed=4 * row_count * count)

    crossed = lax.axis_size("dp") == 2

    def share(value):
        return [moved(value, across), value] if crossed else exchange(value, "dp")

    inputs = [
        pltpu.with_memory_space_constraint(array, pltpu.HBM)
        for array in (
            features,
            center_idx.reshape(1, count),
            slots.reshape(1, row_count),
            prices.reshape(1, row_count),
            center_scale.reshape(1, count),
        )
    ]
    features, idx, slots, prices, own_scale, picked = call(
        pick_body,
        (
            shaped(features.shape, bf16),
            shaped((1, count), jnp.int32),
            shaped((1, row_count), jnp.int32),
            shaped((1, row_count)),
            shaped((1, count)),
            shaped((depth, count), bf16),
        ),
        *inputs,
        sources=[HBM] * 5,
        scratch_shapes=[pltpu.SemaphoreType.DMA((6,))],
    )
    if crossed:
        moved_idx = moved(center_idx, beside)
        resident_picks = call(
            pick_beside_body,
            shaped((depth, count), bf16),
            features, moved_idx.reshape(1, count), idx,
            flops=128 * row_count * count,
            bytes_accessed=128 * row_count,
        )
        centers = [moved(picked, outward), resident_picks]
        moved_scale = moved(center_scale, beside).reshape(1, count)
    else:
        centers = exchange(picked, "dp")
        moved_scale = own_scale
    columns, turned_columns, weight = call(
        columns_body,
        (
            shaped((DEPTH, row_count), bf16),
            shaped((row_count, DEPTH), bf16),
            shaped((16, row_count), bf16),
        ),
        features, slots, prices,
        flops=1000 * row_count,
        bytes_accessed=1024 * row_count,
    )
    block, center, scale, first = call(
        partial(rows_body, len(centers)),
        (
            shaped((2 * row_count, count), bf16),
            shaped((DEPTH, count), bf16),
            shaped((1, count)),
            vector,
        ),
        turned_columns, weight, moved_scale, own_scale, *centers,
        **pass_cost,
    )
    firsts = share(first)
    turned = call(
        turned_body, shaped((2 * count, row_count), bf16), columns, center, **pass_cost
    )
    target, rows = call(
        partial(first_apply_body, len(firsts), 1.0 / math.sqrt(all_rows)),
        (vector, row_shape),
        *firsts, scale, slots, turned,
    )
    rows = exchange(rows, "centers")
    rows, norm, folded = call(
        partial(first_fold_body, len(rows)), (row_shape, narrow, fold_shape), *rows, slots, block
    )
    folds = share(folded)
    state, step, latest = call(
        partial(second_apply_body, len(folds), 1.0 / all_rows),
        (shaped((2 * SLOTS, count)), narrow, row_shape),
        *folds, scale, slots, turned, target, norm,
    )
    latest = exchange(latest, "centers")
    sums, folded = call(
        partial(second_fold_body, len(latest)),
        (shaped((SLOTS, 2 * EXTRA)), fold_shape),
        *latest, slots, block, rows, norm,
    )
    if crossed:
        folds = [moved(folded, homeward), moved(folded, beside), folded]
        moved_state = moved(state, beside)
    else:
        folds = exchange(folded, "dp")
        moved_state = state
    return call(
        partial(finish_body, crossed, len(folds), 1.0 / all_rows),
        (vector, vector),
        *folds, moved_state, state, own_scale, step, norm, sums,
    )


def solution(mesh):
    return jax.shard_map(
        per_device,
        mesh=mesh,
        in_specs=(P(None, "dp"), P("dp"), P("dp"), P("centers"), P("centers")),
        out_specs=(P(None, "centers"), P(None, "centers")),
        check_vma=False,
    )
```

```python
import math
from functools import partial

import jax
import jax.numpy as jnp
from jax import lax
from jax.experimental import pallas as pl
from jax.experimental.pallas import tpu as pltpu
from jax.sharding import PartitionSpec as P

SLOTS = 8
RIDGE = 0.5
CHUNK = 512
EXTRA = 128
DEPTH = 256
STEP = 256
FACTOR = math.log2(math.e) / 64.0
f32 = jnp.float32
bf16 = jnp.bfloat16
VMEM = pl.BlockSpec(memory_space=pltpu.VMEM)
HBM = pl.BlockSpec(memory_space=pltpu.HBM)


def split3(value):
    high = value.astype(bf16).astype(f32)
    rest = value - high
    mid = rest.astype(bf16).astype(f32)
    return high, mid, rest - mid


def stack2(value):
    high = value.astype(bf16).astype(f32)
    return jnp.concatenate([high, value - high], axis=0).astype(bf16)


def product(stacked, high_block, low_block):
    main = jnp.dot(stacked, high_block, preferred_element_type=f32)
    rest = jnp.dot(stacked[0:SLOTS], low_block, preferred_element_type=f32)
    return main[0:SLOTS] + (main[SLOTS:] + rest)


def slot_lanes(first):
    lane = lax.broadcasted_iota(jnp.int32, (SLOTS, EXTRA), 1)
    return lane == lax.broadcasted_iota(jnp.int32, (SLOTS, EXTRA), 0) + first


def to_lanes(column, first):
    return jnp.sum(jnp.where(slot_lanes(first), column, 0.0), axis=0, keepdims=True)


def from_lanes(row, first):
    return jnp.sum(jnp.where(slot_lanes(first), row, 0.0), axis=1, keepdims=True)


def spread(column):
    return jnp.broadcast_to(column, (SLOTS, EXTRA))


def wide(narrow, count):
    return jnp.concatenate([narrow] * (count // EXTRA), axis=1)


def pair_total(parts):
    while len(parts) > 1:
        parts = [parts[i] + parts[i + 1] for i in range(0, len(parts), 2)]
    return parts[0]


def total_of(refs):
    return pair_total([ref[...] for ref in refs])


def resident(moved, own):
    return jnp.where(lax.axis_index("dp") == 0, own, moved)


def row_sum(value):
    return jnp.sum(value, axis=1, keepdims=True)


def slot_mask(slots):
    row = lax.broadcasted_iota(jnp.int32, (SLOTS, slots.shape[1]), 0)
    return slots == row


def norm_rows(feat32, base):
    half = (-0.5 * FACTOR) * jnp.sum(feat32 * feat32, axis=0, keepdims=True)
    row = lax.broadcasted_iota(jnp.int32, (feat32.shape[0], feat32.shape[1]), 0)
    extra = jnp.where(row < 6, 1.0, 0.0)
    for place, part in enumerate(split3(half)):
        extra = jnp.where(row == base + place, part, extra)
    return extra


def kernel_parts(exponent):
    value = jnp.exp2(exponent)
    high = value.astype(bf16)
    return high, (value - high.astype(f32)).astype(bf16)


def place_of(idx, row_count):
    local_idx = idx - lax.axis_index("dp") * row_count
    block = lax.div(local_idx, STEP)
    place = (local_idx - block * STEP).astype(f32).astype(bf16)
    row = lax.broadcasted_iota(jnp.int32, (STEP, idx.shape[1]), 0).astype(f32).astype(bf16)
    return block, jnp.where(row == place, jnp.ones_like(row), jnp.zeros_like(row))


def pick(feat_ref, block, hit):
    depth, row_count = feat_ref.shape
    blocks = range(row_count // STEP)
    stacked = jnp.concatenate(
        [feat_ref[:, turn * STEP : (turn + 1) * STEP] for turn in blocks], axis=0
    )
    product = jnp.dot(stacked, hit, preferred_element_type=f32)
    picked = jnp.zeros((depth, hit.shape[1]), f32)
    for turn in blocks:
        picked = jnp.where(block == turn, product[turn * depth : (turn + 1) * depth], picked)
    return picked


def pick_body(feat_hbm, idx_hbm, slots_hbm, prices_hbm, scale_hbm, *refs):
    feat_ref, idx_ref, slots_ref, prices_ref, scale_ref, out_ref, sems = refs
    sources = (idx_hbm, feat_hbm, slots_hbm, prices_hbm, scale_hbm)
    targets = (idx_ref, feat_ref, slots_ref, prices_ref, scale_ref)
    copies = [
        pltpu.make_async_copy(source, target, sems.at[place])
        for place, (source, target) in enumerate(zip(sources, targets))
    ]
    for copy in copies:
        copy.start()
    copies[0].wait()
    block, hit = place_of(idx_ref[...], feat_ref.shape[1])
    copies[1].wait()
    picked = pick(feat_ref, block, hit)
    for copy in copies[2:]:
        copy.wait()
    out_ref[...] = picked.astype(bf16)


def pick_beside_body(feat_ref, moved_idx_ref, idx_ref, out_ref):
    idx = jnp.where(lax.axis_index("dp") == 0, idx_ref[...], moved_idx_ref[...])
    block, hit = place_of(idx, feat_ref.shape[1])
    out_ref[...] = pick(feat_ref, block, hit).astype(bf16)


def columns_body(feat_ref, slots_ref, prices_ref, columns_ref, turned_ref, weight_ref):
    for begin in range(0, feat_ref.shape[1], CHUNK):
        here = slice(begin, begin + CHUNK)
        feat32 = feat_ref[:, here].astype(f32)
        pair = jnp.concatenate([feat32, feat32], axis=0)
        last = jnp.concatenate([feat32, norm_rows(feat32, 3)], axis=0)
        columns_ref[0:128, here] = pair.astype(bf16)
        columns_ref[128:256, here] = last.astype(bf16)
        turned_ref[here, 0:128] = pair.T.astype(bf16)
        turned_ref[here, 128:256] = last.T.astype(bf16)
        weight = jnp.where(slot_mask(slots_ref[:, here]), prices_ref[:, here], 0.0)
        weight_ref[:, here] = stack2(weight)


def rows_body(parts, turned_ref, weight_ref, moved_scale_ref, own_scale_ref, *refs):
    center_refs, (block_ref, center_ref, scale_ref, out_ref) = refs[:parts], refs[parts:]
    scale_ref[...] = resident(moved_scale_ref[...], own_scale_ref[...])
    center = total_of(center_refs).astype(f32)
    center = jnp.concatenate(
        [*split3(center * FACTOR), norm_rows(center, 0)], axis=0
    ).astype(bf16)
    center_ref[...] = center
    row_count = turned_ref.shape[0]
    total = jnp.zeros(out_ref.shape, f32)

    def fold(begin):
        end = begin + CHUNK
        return product(
            weight_ref[:, begin:end],
            block_ref[begin:end, :],
            block_ref[row_count + begin : row_count + end, :],
        )

    def inner(begin):
        return jnp.dot(
            turned_ref[begin : begin + CHUNK, :], center, preferred_element_type=f32
        )

    ahead = inner(0)
    for begin in range(0, row_count, CHUNK):
        exponent = ahead
        if begin + CHUNK < row_count:
            ahead = inner(begin + CHUNK)
        high, low = kernel_parts(exponent)
        block_ref[begin : begin + CHUNK, :] = high
        block_ref[row_count + begin : row_count + begin + CHUNK, :] = low
        if begin > 0:
            total += fold(begin - CHUNK)
    out_ref[...] = total + fold(row_count - CHUNK)


def turned_body(columns_ref, center_ref, block_ref):
    center = center_ref[...].astype(f32).T.astype(bf16)
    count, row_count = center.shape[0], columns_ref.shape[1]

    def inner(begin):
        return jnp.dot(
            center, columns_ref[:, begin : begin + CHUNK], preferred_element_type=f32
        )

    ahead = inner(0)
    for begin in range(0, row_count, CHUNK):
        exponent = ahead
        if begin + CHUNK < row_count:
            ahead = inner(begin + CHUNK)
        high, low = kernel_parts(exponent)
        block_ref[0:count, begin : begin + CHUNK] = high
        block_ref[count:, begin : begin + CHUNK] = low


def apply_rows(scaled, turned_ref, slots_ref, out_ref):
    count, row_count = scaled.shape[1], turned_ref.shape[1]
    value = product(stack2(scaled), turned_ref[0:count, :], turned_ref[count:, :])
    own = jnp.where(slot_mask(slots_ref[...]), value, 0.0)
    out_ref[:, 0:row_count] = jnp.sum(own, axis=0, keepdims=True)


def fold_rows(rows, block_ref, slots_ref, out_ref):
    row_count, count = slots_ref.shape[1], block_ref.shape[1]
    weight = jnp.where(slot_mask(slots_ref[...]), rows, 0.0)
    folded = product(
        stack2(weight), block_ref[0:row_count, :], block_ref[row_count:, :]
    )
    for slot in range(SLOTS):
        out_ref[:, slot * count : (slot + 1) * count] = folded[slot : slot + 1]
    out_ref[:, SLOTS * count :] = to_lanes(row_sum(weight * weight), 0)


def unfold(row, count):
    folded = [row[:, slot * count : (slot + 1) * count] for slot in range(SLOTS)]
    square = spread(from_lanes(row[:, SLOTS * count :], 0))
    return jnp.concatenate([*folded], axis=0), square


def first_apply_body(parts, scale_over_root, *refs):
    first_refs = refs[:parts]
    scale_ref, slots_ref, turned_ref, target_ref, out_ref = refs[parts:]
    scale = scale_ref[...]
    target = scale * total_of(first_refs) * scale_over_root
    target_ref[...] = target
    out_ref[:, turned_ref.shape[1] :] = to_lanes(row_sum(target * target), 0)
    apply_rows(scale * target, turned_ref, slots_ref, out_ref)


def first_fold_body(parts, *refs):
    row_refs = refs[:parts]
    slots_ref, block_ref, rows_ref, norm_ref, out_ref = refs[parts:]
    row_count = slots_ref.shape[1]
    rows = total_of(row_refs)
    rows_ref[...] = rows
    norm_ref[...] = spread(from_lanes(rows[:, row_count:], 0))
    fold_rows(rows[:, 0:row_count], block_ref, slots_ref, out_ref)


def second_apply_body(parts, inv_rows, *refs):
    fold_refs = refs[:parts]
    (scale_ref, slots_ref, turned_ref, target_ref, norm_ref,
     state_ref, step_ref, out_ref) = refs[parts:]
    row_count, count = turned_ref.shape[1], scale_ref.shape[1]
    folded, square = unfold(total_of(fold_refs), count)
    scale = scale_ref[...]
    target = target_ref[...]
    norm = norm_ref[...]
    applied = scale * folded * inv_rows + RIDGE * target
    step = norm / (square * inv_rows + RIDGE * norm)
    residual = target - wide(step, count) * applied
    state_ref[0:SLOTS, :] = target
    state_ref[SLOTS:, :] = residual
    step_ref[...] = step
    out_ref[:, row_count:] = to_lanes(row_sum(residual * residual), 0) + to_lanes(
        row_sum(residual * target), SLOTS
    )
    apply_rows(scale * residual, turned_ref, slots_ref, out_ref)


def second_fold_body(parts, *refs):
    row_refs = refs[:parts]
    slots_ref, block_ref, rows_ref, norm_ref, sums_ref, out_ref = refs[parts:]
    row_count = slots_ref.shape[1]
    latest = total_of(row_refs)
    norm = spread(from_lanes(latest[:, row_count:], 0))
    ratio = norm / norm_ref[...]
    sums_ref[:, 0:EXTRA] = norm
    sums_ref[:, EXTRA:] = spread(from_lanes(latest[:, row_count:], SLOTS))
    rows = latest[:, 0:row_count] + wide(ratio, row_count) * rows_ref[:, 0:row_count]
    fold_rows(rows, block_ref, slots_ref, out_ref)


def finish_body(crossed, parts, inv_rows, *refs):
    fold_refs = refs[:parts]
    (moved_ref, state_ref, scale_ref, step_ref, norm_ref, sums_ref,
     coefficients_ref, out_ref) = refs[parts:]
    count = scale_ref.shape[1]
    if crossed:
        far, moved, own = (ref[...] for ref in fold_refs)
        folded = far + resident(moved, own)
        state = resident(moved_ref[...], state_ref[...])
    else:
        folded = total_of(fold_refs)
        state = state_ref[...]
    folded, rows_square = unfold(folded, count)
    target, residual = state[0:SLOTS], state[SLOTS:]
    first_norm = norm_ref[...]
    norm, cross = sums_ref[:, 0:EXTRA], sums_ref[:, EXTRA:]
    ratio = norm / first_norm
    direction = residual + wide(ratio, count) * target
    square = norm + 2.0 * ratio * cross + ratio * ratio * first_norm
    applied = scale_ref[...] * folded * inv_rows + RIDGE * direction
    step = wide(norm / (rows_square * inv_rows + RIDGE * square), count)
    coefficients_ref[...] = wide(step_ref[...], count) * target + step * direction
    out_ref[...] = residual - step * applied


def call(body, out_shape, *args, sources=None, flops=0, bytes_accessed=0, **more):
    return pl.pallas_call(
        body,
        out_shape=out_shape,
        in_specs=sources or [VMEM] * len(args),
        out_specs=jax.tree.map(lambda _: VMEM, out_shape),
        compiler_params=pltpu.CompilerParams(vmem_limit_bytes=36 * 1024 * 1024),
        cost_estimate=pl.CostEstimate(
            flops=flops, bytes_accessed=bytes_accessed, transcendentals=0
        ),
        **more,
    )(*args)


def exchange(value, axis):
    size = lax.axis_size(axis)
    parts = [value]
    stride = 1
    while stride < size:
        value = pair_total(parts)
        span = min(4, size // stride)
        side = 0 if stride == 1 else 1
        parts = [value]
        offsets = (1, 3, 2) if stride == 1 else (1, 2, 3)
        for offset in offsets[: span - 1]:
            pairs = [(i, i ^ (offset * stride) ^ side) for i in range(size)]
            parts.insert(0, lax.ppermute(value, axis, pairs))
        stride *= span
    return parts


def pairs_over(target_of):
    groups, count = lax.axis_size("dp"), lax.axis_size("centers")
    pairs = []
    for group in range(groups):
        for place in range(count):
            to_group, to_place = target_of(group, place)
            pairs.append((group * count + place, to_group * count + to_place))
    return pairs


def moved(value, target_of):
    return lax.ppermute(value, ("dp", "centers"), pairs_over(target_of))


def across(group, place):
    return 1 - group, place ^ 1


def beside(group, place):
    return group, place ^ 1


def outward(group, place):
    return 1 - group, place ^ (1 - group)


def homeward(group, place):
    return 1 - group, place ^ group


def shaped(shape, dtype=f32):
    return jax.ShapeDtypeStruct(shape, dtype)


def per_device(features, prices, slots, center_idx, center_scale):
    depth, row_count = features.shape
    count = center_idx.shape[0]
    all_rows = row_count * lax.axis_size("dp")
    row_shape = shaped((1, row_count + EXTRA))
    fold_shape = shaped((1, SLOTS * count + EXTRA))
    vector = shaped((SLOTS, count))
    narrow = shaped((SLOTS, EXTRA))
    pass_cost = dict(flops=64 * row_count * count, bytes_accessed=4 * row_count * count)

    crossed = lax.axis_size("dp") == 2

    def share(value):
        return [moved(value, across), value] if crossed else exchange(value, "dp")

    inputs = [
        pltpu.with_memory_space_constraint(array, pltpu.HBM)
        for array in (
            features,
            center_idx.reshape(1, count),
            slots.reshape(1, row_count),
            prices.reshape(1, row_count),
            center_scale.reshape(1, count),
        )
    ]
    features, idx, slots, prices, own_scale, picked = call(
        pick_body,
        (
            shaped(features.shape, bf16),
            shaped((1, count), jnp.int32),
            shaped((1, row_count), jnp.int32),
            shaped((1, row_count)),
            shaped((1, count)),
            shaped((depth, count), bf16),
        ),
        *inputs,
        sources=[HBM] * 5,
        scratch_shapes=[pltpu.SemaphoreType.DMA((5,))],
    )
    if crossed:
        moved_idx = moved(center_idx, beside)
        resident_picks = call(
            pick_beside_body,
            shaped((depth, count), bf16),
            features, moved_idx.reshape(1, count), idx,
            flops=128 * row_count * count,
            bytes_accessed=128 * row_count,
        )
        centers = [moved(picked, outward), resident_picks]
        moved_scale = moved(center_scale, beside).reshape(1, count)
    else:
        centers = exchange(picked, "dp")
        moved_scale = own_scale
    columns, turned_columns, weight = call(
        columns_body,
        (
            shaped((DEPTH, row_count), bf16),
            shaped((row_count, DEPTH), bf16),
            shaped((16, row_count), bf16),
        ),
        features, slots, prices,
        flops=1000 * row_count,
        bytes_accessed=1024 * row_count,
    )
    block, center, scale, first = call(
        partial(rows_body, len(centers)),
        (
            shaped((2 * row_count, count), bf16),
            shaped((DEPTH, count), bf16),
            shaped((1, count)),
            vector,
        ),
        turned_columns, weight, moved_scale, own_scale, *centers,
        **pass_cost,
    )
    firsts = share(first)
    turned = call(
        turned_body, shaped((2 * count, row_count), bf16), columns, center, **pass_cost
    )
    target, rows = call(
        partial(first_apply_body, len(firsts), 1.0 / math.sqrt(all_rows)),
        (vector, row_shape),
        *firsts, scale, slots, turned,
    )
    rows = exchange(rows, "centers")
    rows, norm, folded = call(
        partial(first_fold_body, len(rows)), (row_shape, narrow, fold_shape), *rows, slots, block
    )
    folds = share(folded)
    state, step, latest = call(
        partial(second_apply_body, len(folds), 1.0 / all_rows),
        (shaped((2 * SLOTS, count)), narrow, row_shape),
        *folds, scale, slots, turned, target, norm,
    )
    latest = exchange(latest, "centers")
    sums, folded = call(
        partial(second_fold_body, len(latest)),
        (shaped((SLOTS, 2 * EXTRA)), fold_shape),
        *latest, slots, block, rows, norm,
    )
    if crossed:
        folds = [moved(folded, homeward), moved(folded, beside), folded]
        moved_state = moved(state, beside)
    else:
        folds = exchange(folded, "dp")
        moved_state = state
    return call(
        partial(finish_body, crossed, len(folds), 1.0 / all_rows),
        (vector, vector),
        *folds, moved_state, state, own_scale, step, norm, sums,
    )


def solution(mesh):
    return jax.shard_map(
        per_device,
        mesh=mesh,
        in_specs=(P(None, "dp"), P("dp"), P("dp"), P("centers"), P("centers")),
        out_specs=(P(None, "centers"), P(None, "centers")),
        check_vma=False,
    )
```

```python
import math
from functools import partial

import jax
import jax.numpy as jnp
from jax import lax
from jax.experimental import pallas as pl
from jax.experimental.pallas import tpu as pltpu
from jax.sharding import PartitionSpec as P

SLOTS = 8
RIDGE = 0.5
CHUNK = 512
EXTRA = 128
DEPTH = 256
STEP = 256
FACTOR = math.log2(math.e) / 64.0
f32 = jnp.float32
bf16 = jnp.bfloat16
VMEM = pl.BlockSpec(memory_space=pltpu.VMEM)
HBM = pl.BlockSpec(memory_space=pltpu.HBM)


def split3(value):
    high = value.astype(bf16).astype(f32)
    rest = value - high
    mid = rest.astype(bf16).astype(f32)
    return high, mid, rest - mid


def stack2(value):
    high = value.astype(bf16).astype(f32)
    return jnp.concatenate([high, value - high], axis=0).astype(bf16)


def product(stacked, high_block, low_block):
    main = jnp.dot(stacked, high_block, preferred_element_type=f32)
    rest = jnp.dot(stacked[0:SLOTS], low_block, preferred_element_type=f32)
    return main[0:SLOTS] + (main[SLOTS:] + rest)


def slot_lanes(first):
    lane = lax.broadcasted_iota(jnp.int32, (SLOTS, EXTRA), 1)
    return lane == lax.broadcasted_iota(jnp.int32, (SLOTS, EXTRA), 0) + first


def to_lanes(column, first):
    return jnp.sum(jnp.where(slot_lanes(first), column, 0.0), axis=0, keepdims=True)


def from_lanes(row, first):
    return jnp.sum(jnp.where(slot_lanes(first), row, 0.0), axis=1, keepdims=True)


def spread(column):
    return jnp.broadcast_to(column, (SLOTS, EXTRA))


def wide(narrow, count):
    return jnp.concatenate([narrow] * (count // EXTRA), axis=1)


def pair_total(parts):
    while len(parts) > 1:
        parts = [parts[i] + parts[i + 1] for i in range(0, len(parts), 2)]
    return parts[0]


def total_of(refs):
    return pair_total([ref[...] for ref in refs])


def resident(moved, own):
    return jnp.where(lax.axis_index("dp") == 0, own, moved)


def row_sum(value):
    return jnp.sum(value, axis=1, keepdims=True)


def slot_mask(slots):
    row = lax.broadcasted_iota(jnp.int32, (SLOTS, slots.shape[1]), 0)
    return slots == row


def norm_rows(feat32, base):
    half = (-0.5 * FACTOR) * jnp.sum(feat32 * feat32, axis=0, keepdims=True)
    row = lax.broadcasted_iota(jnp.int32, (feat32.shape[0], feat32.shape[1]), 0)
    extra = jnp.where(row < 6, 1.0, 0.0)
    for place, part in enumerate(split3(half)):
        extra = jnp.where(row == base + place, part, extra)
    return extra


def kernel_parts(exponent):
    value = jnp.exp2(exponent)
    high = value.astype(bf16)
    return high, (value - high.astype(f32)).astype(bf16)


def place_of(idx, row_count):
    local_idx = idx - lax.axis_index("dp") * row_count
    block = lax.div(local_idx, STEP)
    place = (local_idx - block * STEP).astype(f32).astype(bf16)
    row = lax.broadcasted_iota(jnp.int32, (STEP, idx.shape[1]), 0).astype(f32).astype(bf16)
    return block, jnp.where(row == place, jnp.ones_like(row), jnp.zeros_like(row))


def pick(feat_ref, block, hit):
    depth, row_count = feat_ref.shape
    blocks = range(row_count // STEP)
    stacked = jnp.concatenate(
        [feat_ref[:, turn * STEP : (turn + 1) * STEP] for turn in blocks], axis=0
    )
    product = jnp.dot(stacked, hit, preferred_element_type=f32)
    picked = jnp.zeros((depth, hit.shape[1]), f32)
    for turn in blocks:
        picked = jnp.where(block == turn, product[turn * depth : (turn + 1) * depth], picked)
    return picked


def pick_body(feat_hbm, idx_hbm, slots_hbm, prices_hbm, scale_hbm, *refs):
    feat_ref, idx_ref, slots_ref, prices_ref, scale_ref, out_ref, sems = refs
    sources = (idx_hbm, feat_hbm, slots_hbm, prices_hbm, scale_hbm)
    targets = (idx_ref, feat_ref, slots_ref, prices_ref, scale_ref)
    copies = [
        pltpu.make_async_copy(source, target, sems.at[place])
        for place, (source, target) in enumerate(zip(sources, targets))
    ]
    for copy in copies:
        copy.start()
    copies[0].wait()
    block, hit = place_of(idx_ref[...], feat_ref.shape[1])
    copies[1].wait()
    picked = pick(feat_ref, block, hit)
    for copy in copies[2:]:
        copy.wait()
    out_ref[...] = picked.astype(bf16)


def pick_beside_body(feat_ref, moved_idx_ref, idx_ref, out_ref):
    idx = jnp.where(lax.axis_index("dp") == 0, idx_ref[...], moved_idx_ref[...])
    block, hit = place_of(idx, feat_ref.shape[1])
    out_ref[...] = pick(feat_ref, block, hit).astype(bf16)


def columns_body(feat_ref, slots_ref, prices_ref, columns_ref, turned_ref, weight_ref):
    for begin in range(0, feat_ref.shape[1], CHUNK):
        here = slice(begin, begin + CHUNK)
        feat32 = feat_ref[:, here].astype(f32)
        pair = jnp.concatenate([feat32, feat32], axis=0)
        last = jnp.concatenate([feat32, norm_rows(feat32, 3)], axis=0)
        columns_ref[0:128, here] = pair.astype(bf16)
        columns_ref[128:256, here] = last.astype(bf16)
        turned_ref[here, 0:128] = pair.T.astype(bf16)
        turned_ref[here, 128:256] = last.T.astype(bf16)
        weight = jnp.where(slot_mask(slots_ref[:, here]), prices_ref[:, here], 0.0)
        weight_ref[:, here] = stack2(weight)


def rows_body(parts, turned_ref, weight_ref, moved_scale_ref, own_scale_ref, *refs):
    center_refs, (block_ref, center_ref, scale_ref, out_ref) = refs[:parts], refs[parts:]
    scale_ref[...] = resident(moved_scale_ref[...], own_scale_ref[...])
    center = total_of(center_refs).astype(f32)
    center = jnp.concatenate(
        [*split3(center * FACTOR), norm_rows(center, 0)], axis=0
    ).astype(bf16)
    center_ref[...] = center
    row_count = turned_ref.shape[0]
    total = jnp.zeros(out_ref.shape, f32)

    def fold(begin):
        end = begin + CHUNK
        return product(
            weight_ref[:, begin:end],
            block_ref[begin:end, :],
            block_ref[row_count + begin : row_count + end, :],
        )

    def inner(begin):
        return jnp.dot(
            turned_ref[begin : begin + CHUNK, :], center, preferred_element_type=f32
        )

    ahead = inner(0)
    for begin in range(0, row_count, CHUNK):
        exponent = ahead
        if begin + CHUNK < row_count:
            ahead = inner(begin + CHUNK)
        high, low = kernel_parts(exponent)
        block_ref[begin : begin + CHUNK, :] = high
        block_ref[row_count + begin : row_count + begin + CHUNK, :] = low
        if begin > 0:
            total += fold(begin - CHUNK)
    out_ref[...] = total + fold(row_count - CHUNK)


def turned_body(columns_ref, center_ref, block_ref):
    center = center_ref[...].astype(f32).T.astype(bf16)
    count, row_count = center.shape[0], columns_ref.shape[1]

    def inner(begin):
        return jnp.dot(
            center, columns_ref[:, begin : begin + CHUNK], preferred_element_type=f32
        )

    ahead = inner(0)
    for begin in range(0, row_count, CHUNK):
        exponent = ahead
        if begin + CHUNK < row_count:
            ahead = inner(begin + CHUNK)
        high, low = kernel_parts(exponent)
        block_ref[0:count, begin : begin + CHUNK] = high
        block_ref[count:, begin : begin + CHUNK] = low


def apply_rows(scaled, turned_ref, slots_ref, out_ref):
    count, row_count = scaled.shape[1], turned_ref.shape[1]
    value = product(stack2(scaled), turned_ref[0:count, :], turned_ref[count:, :])
    own = jnp.where(slot_mask(slots_ref[...]), value, 0.0)
    out_ref[:, 0:row_count] = jnp.sum(own, axis=0, keepdims=True)


def fold_rows(rows, block_ref, slots_ref, out_ref):
    row_count, count = slots_ref.shape[1], block_ref.shape[1]
    weight = jnp.where(slot_mask(slots_ref[...]), rows, 0.0)
    out_ref[:, 0:count] = product(
        stack2(weight), block_ref[0:row_count, :], block_ref[row_count:, :]
    )
    square = row_sum(weight * weight)
    out_ref[:, count : count + EXTRA] = spread(square)


def first_apply_body(parts, scale_over_root, *refs):
    first_refs = refs[:parts]
    scale_ref, slots_ref, turned_ref, target_ref, out_ref = refs[parts:]
    scale = scale_ref[...]
    target = scale * total_of(first_refs) * scale_over_root
    target_ref[...] = target
    out_ref[:, turned_ref.shape[1] :] = to_lanes(row_sum(target * target), 0)
    apply_rows(scale * target, turned_ref, slots_ref, out_ref)


def first_fold_body(parts, *refs):
    row_refs = refs[:parts]
    slots_ref, block_ref, rows_ref, norm_ref, out_ref = refs[parts:]
    row_count = slots_ref.shape[1]
    rows = total_of(row_refs)
    rows_ref[...] = rows
    norm_ref[...] = spread(from_lanes(rows[:, row_count:], 0))
    fold_rows(rows[:, 0:row_count], block_ref, slots_ref, out_ref)


def second_apply_body(parts, inv_rows, *refs):
    fold_refs = refs[:parts]
    (scale_ref, slots_ref, turned_ref, target_ref, norm_ref,
     state_ref, step_ref, out_ref) = refs[parts:]
    row_count, count = turned_ref.shape[1], scale_ref.shape[1]
    folded = total_of(fold_refs)
    scale = scale_ref[...]
    target = target_ref[...]
    norm = norm_ref[...]
    applied = scale * folded[:, 0:count] * inv_rows + RIDGE * target
    step = norm / (folded[:, count:] * inv_rows + RIDGE * norm)
    residual = target - wide(step, count) * applied
    state_ref[0:SLOTS, :] = target
    state_ref[SLOTS:, :] = residual
    step_ref[...] = step
    out_ref[:, row_count:] = to_lanes(row_sum(residual * residual), 0) + to_lanes(
        row_sum(residual * target), SLOTS
    )
    apply_rows(scale * residual, turned_ref, slots_ref, out_ref)


def second_fold_body(parts, *refs):
    row_refs = refs[:parts]
    slots_ref, block_ref, rows_ref, norm_ref, sums_ref, out_ref = refs[parts:]
    row_count = slots_ref.shape[1]
    latest = total_of(row_refs)
    norm = spread(from_lanes(latest[:, row_count:], 0))
    ratio = norm / norm_ref[...]
    sums_ref[:, 0:EXTRA] = norm
    sums_ref[:, EXTRA:] = spread(from_lanes(latest[:, row_count:], SLOTS))
    rows = latest[:, 0:row_count] + wide(ratio, row_count) * rows_ref[:, 0:row_count]
    fold_rows(rows, block_ref, slots_ref, out_ref)


def finish_body(crossed, parts, inv_rows, *refs):
    fold_refs = refs[:parts]
    (moved_ref, state_ref, scale_ref, step_ref, norm_ref, sums_ref,
     coefficients_ref, out_ref) = refs[parts:]
    count = scale_ref.shape[1]
    if crossed:
        far, moved, own = (ref[...] for ref in fold_refs)
        folded = far + resident(moved, own)
        state = resident(moved_ref[...], state_ref[...])
    else:
        folded = total_of(fold_refs)
        state = state_ref[...]
    target, residual = state[0:SLOTS], state[SLOTS:]
    first_norm = norm_ref[...]
    norm, cross = sums_ref[:, 0:EXTRA], sums_ref[:, EXTRA:]
    ratio = norm / first_norm
    direction = residual + wide(ratio, count) * target
    square = norm + 2.0 * ratio * cross + ratio * ratio * first_norm
    applied = scale_ref[...] * folded[:, 0:count] * inv_rows + RIDGE * direction
    step = wide(norm / (folded[:, count:] * inv_rows + RIDGE * square), count)
    coefficients_ref[...] = wide(step_ref[...], count) * target + step * direction
    out_ref[...] = residual - step * applied


def call(body, out_shape, *args, sources=None, flops=0, bytes_accessed=0, **more):
    return pl.pallas_call(
        body,
        out_shape=out_shape,
        in_specs=sources or [VMEM] * len(args),
        out_specs=jax.tree.map(lambda _: VMEM, out_shape),
        compiler_params=pltpu.CompilerParams(vmem_limit_bytes=36 * 1024 * 1024),
        cost_estimate=pl.CostEstimate(
            flops=flops, bytes_accessed=bytes_accessed, transcendentals=0
        ),
        **more,
    )(*args)


def exchange(value, axis):
    size = lax.axis_size(axis)
    parts = [value]
    stride = 1
    while stride < size:
        value = pair_total(parts)
        span = min(4, size // stride)
        side = 0 if stride == 1 else 1
        parts = [value]
        offsets = (3, 1, 2) if stride == 1 else (1, 2, 3)
        for offset in offsets[: span - 1]:
            pairs = [(i, i ^ (offset * stride) ^ side) for i in range(size)]
            parts.insert(0, lax.ppermute(value, axis, pairs))
        stride *= span
    return parts


def pairs_over(target_of):
    groups, count = lax.axis_size("dp"), lax.axis_size("centers")
    pairs = []
    for group in range(groups):
        for place in range(count):
            to_group, to_place = target_of(group, place)
            pairs.append((group * count + place, to_group * count + to_place))
    return pairs


def moved(value, target_of):
    return lax.ppermute(value, ("dp", "centers"), pairs_over(target_of))


def across(group, place):
    return 1 - group, place ^ 1


def beside(group, place):
    return group, place ^ 1


def outward(group, place):
    return 1 - group, place ^ (1 - group)


def homeward(group, place):
    return 1 - group, place ^ group


def shaped(shape, dtype=f32):
    return jax.ShapeDtypeStruct(shape, dtype)


def per_device(features, prices, slots, center_idx, center_scale):
    depth, row_count = features.shape
    count = center_idx.shape[0]
    all_rows = row_count * lax.axis_size("dp")
    row_shape = shaped((1, row_count + EXTRA))
    fold_shape = shaped((SLOTS, count + EXTRA))
    vector = shaped((SLOTS, count))
    narrow = shaped((SLOTS, EXTRA))
    pass_cost = dict(flops=64 * row_count * count, bytes_accessed=4 * row_count * count)

    crossed = lax.axis_size("dp") == 2

    def share(value):
        return [moved(value, across), value] if crossed else exchange(value, "dp")

    inputs = [
        pltpu.with_memory_space_constraint(array, pltpu.HBM)
        for array in (
            features,
            center_idx.reshape(1, count),
            slots.reshape(1, row_count),
            prices.reshape(1, row_count),
            center_scale.reshape(1, count),
        )
    ]
    features, idx, slots, prices, own_scale, picked = call(
        pick_body,
        (
            shaped(features.shape, bf16),
            shaped((1, count), jnp.int32),
            shaped((1, row_count), jnp.int32),
            shaped((1, row_count)),
            shaped((1, count)),
            shaped((depth, count), bf16),
        ),
        *inputs,
        sources=[HBM] * 5,
        scratch_shapes=[pltpu.SemaphoreType.DMA((5,))],
    )
    if crossed:
        moved_idx = moved(center_idx, beside)
        resident_picks = call(
            pick_beside_body,
            shaped((depth, count), bf16),
            features, moved_idx.reshape(1, count), idx,
            flops=128 * row_count * count,
            bytes_accessed=128 * row_count,
        )
        centers = [moved(picked, outward), resident_picks]
        moved_scale = moved(center_scale, beside).reshape(1, count)
    else:
        centers = exchange(picked, "dp")
        moved_scale = own_scale
    columns, turned_columns, weight = call(
        columns_body,
        (
            shaped((DEPTH, row_count), bf16),
            shaped((row_count, DEPTH), bf16),
            shaped((16, row_count), bf16),
        ),
        features, slots, prices,
        flops=1000 * row_count,
        bytes_accessed=1024 * row_count,
    )
    block, center, scale, first = call(
        partial(rows_body, len(centers)),
        (
            shaped((2 * row_count, count), bf16),
            shaped((DEPTH, count), bf16),
            shaped((1, count)),
            vector,
        ),
        turned_columns, weight, moved_scale, own_scale, *centers,
        **pass_cost,
    )
    firsts = share(first)
    turned = call(
        turned_body, shaped((2 * count, row_count), bf16), columns, center, **pass_cost
    )
    target, rows = call(
        partial(first_apply_body, len(firsts), 1.0 / math.sqrt(all_rows)),
        (vector, row_shape),
        *firsts, scale, slots, turned,
    )
    rows = exchange(rows, "centers")
    rows, norm, folded = call(
        partial(first_fold_body, len(rows)), (row_shape, narrow, fold_shape), *rows, slots, block
    )
    folds = share(folded)
    state, step, latest = call(
        partial(second_apply_body, len(folds), 1.0 / all_rows),
        (shaped((2 * SLOTS, count)), narrow, row_shape),
        *folds, scale, slots, turned, target, norm,
    )
    latest = exchange(latest, "centers")
    sums, folded = call(
        partial(second_fold_body, len(latest)),
        (shaped((SLOTS, 2 * EXTRA)), fold_shape),
        *latest, slots, block, rows, norm,
    )
    if crossed:
        folds = [moved(folded, homeward), moved(folded, beside), folded]
        moved_state = moved(state, beside)
    else:
        folds = exchange(folded, "dp")
        moved_state = state
    return call(
        partial(finish_body, crossed, len(folds), 1.0 / all_rows),
        (vector, vector),
        *folds, moved_state, state, own_scale, step, norm, sums,
    )


def solution(mesh):
    return jax.shard_map(
        per_device,
        mesh=mesh,
        in_specs=(P(None, "dp"), P("dp"), P("dp"), P("centers"), P("centers")),
        out_specs=(P(None, "centers"), P(None, "centers")),
        check_vma=False,
    )
```
